32 devices in a mesh: blk: 8 (over z, y), pair: 4 (over x, core).
Axes of the slice: x: 2, y: 2, z: 4, core: 2. Of those that a mesh axis runs over, the one named last changes fastest.
Arguments:
- basis: float32 [8, 64, 510, 128], P(None, ('blk', 'pair'))
- mie_coeffs: float32 [64, 510, 128], P(('blk', 'pair')), may hold values from -8 to 8
- rot_table: bfloat16 [8, 510, 510], replicated, may hold values from -0.25 to 0.25
- axial_table: bfloat16 [8, 2, 510, 510], replicated, may hold values from -0.1875 to 0.1875
- pair_table: int32 [8, 128, 3], P('blk'), may hold values from 0 to 23, as said below
- pair_count: int32 [8], P('blk'), may hold values from 32 to 128, as said below
Outputs:
- projections: float32 [2, 8], replicated
- next_basis: float32 [64, 510, 128], P(('blk', 'pair'))
The draws below stay inside these ranges and needn't reach their ends.
Inputs may be any that keep to these rules, and one draw needn't show every extreme that they name: `pair_table`: row p of blk index i is (a, b, g): a names one of the 8 blocks of blk index i; b counts from the first block of blk index i - 1 and is never a + 8; on blk index 0, b >= 8; on the last, b < 16; g < 8. Rows from pair_count on are ignored. `pair_count`: some blk index lists all 128 rows.
All inputs are finite; a program needn't handle non-finite values.
Results may differ from the reference program's by a relative error of at most 0.0003.
Values may be sent and summed in bfloat16 or wider, within the bound.
No kernel may reach another device: no remote copies, remote signals or barrier semaphores. Data moves between devices by JAX's collectives and lax.ppermute only.
A program may use at most 128 MiB of HBM per device.

```python
import jax
import jax.numpy as jnp
from jax import lax

MODES = 510
SPHERES = 64
BLK_DEV = 8
PAIR_MAX = 128
TABLES = 8
KRYLOV = 8
BLOCKS = 64
N_BLK = 8


def draw_basis(key, part):
    key = jax.random.fold_in(key, 11)
    keys = jax.random.split(key, 4)
    shape = (KRYLOV, BLOCKS, MODES, 2 * SPHERES)
    rise = jnp.exp(jnp.log(3.0) * jnp.arange(BLOCKS, dtype=jnp.float32) / (BLOCKS - 1))
    rise = rise[None, :, None, None]
    row_scale = jnp.exp(jnp.log(10.0) * jax.random.uniform(keys[0], (1, BLOCKS, MODES, 1), jnp.float32))
    column_scale = jnp.exp(jnp.log(10.0) * jax.random.uniform(keys[1], (1, 1, 1, 2 * SPHERES), jnp.float32))
    common = jax.random.normal(keys[2], (1, BLOCKS, MODES, 2 * SPHERES), jnp.float32)
    own = jax.random.normal(keys[3], shape, jnp.float32)
    shared_weight = 0.5
    return (0.7 * own + shared_weight * common) * rise * row_scale * column_scale


def draw_pair_count(key, part):
    key = jax.random.fold_in(key, 23)
    keys = jax.random.split(key, 2)
    uneven = jax.random.randint(keys[0], (N_BLK,), 0, 1001)
    counts = PAIR_MAX // 4 + 3 * PAIR_MAX // 4 * uneven * uneven // 1000000
    busiest = jax.random.randint(keys[1], (), 0, N_BLK)
    return jnp.where(jnp.arange(N_BLK) == busiest, PAIR_MAX, counts).astype(jnp.int32)


def draw_pair_table(key, part):
    key = jax.random.fold_in(key, 37)
    keys = jax.random.split(key, 3)
    target = jax.random.randint(keys[0], (N_BLK, PAIR_MAX), 0, BLK_DEV)
    device_row = jnp.arange(N_BLK)[:, None]
    lowest = jnp.where(device_row > 0, 0, BLK_DEV)
    highest = jnp.where(device_row < N_BLK - 1, 3 * BLK_DEV, 2 * BLK_DEV)
    raw_source = jax.random.randint(keys[1], (N_BLK, PAIR_MAX), 0, 1 << 20)
    source = lowest + raw_source % (highest - lowest)
    source = jnp.where(source == target + BLK_DEV, lowest + (source - lowest + 1) % (highest - lowest), source)
    source = source.at[0, PAIR_MAX - 1].set(3 * BLK_DEV - 1)
    entry = jax.random.randint(keys[2], (N_BLK, PAIR_MAX), 0, TABLES)
    return jnp.stack([target, source, entry], axis=-1).astype(jnp.int32)


def block_scale(stream_key, shape, cuts, least, high):
    gain, own = 1.0, jax.random.fold_in(stream_key, 6)
    for dim, shards_of in cuts:
        draws = jnp.exp(jax.random.uniform(jax.random.fold_in(own, dim), (shards_of,), jnp.float32, least / len(cuts), high / len(cuts)))
        gain = gain * jnp.repeat(draws, shape[dim] // shards_of).reshape([-1 if axis == dim else 1 for axis in range(len(shape))])
    return gain


def centred(stream_key, extent, scale, limit, pieces=(), kind=jnp.bfloat16):
    result = scale * jax.random.normal(stream_key, extent, jnp.float32)
    if pieces:
        result = result * block_scale(stream_key, extent, pieces, -0.22, 0.18)
    return jnp.clip(result, -limit, limit).astype(kind)


def setup_inputs(seed: int = 0) -> dict:
    seeds = jax.random.split(jax.random.key(seed), 7)
    basis = draw_basis(jax.random.fold_in(seeds[6], 71), 0)
    mie_coeffs = centred(seeds[1], (BLOCKS, MODES, 2 * SPHERES), 2.0, 8.0, ((0, 32),), jnp.float32)
    rot_table = centred(seeds[2], (TABLES, MODES, MODES), MODES ** -0.5, 0.25)
    axial_table = centred(seeds[3], (TABLES, 2, MODES, MODES), (2 * MODES) ** -0.5, 0.1875)
    pair_table = draw_pair_table(jax.random.fold_in(seeds[6], 71), 0)
    pair_count = draw_pair_count(jax.random.fold_in(seeds[6], 71), 0)
    return {"basis": basis, "mie_coeffs": mie_coeffs, "rot_table": rot_table, "axial_table": axial_table, "pair_table": pair_table, "pair_count": pair_count}


batch_pairs = 8

def swap_parts(packed):
    half_width = packed.shape[-1] // 2
    return jnp.concatenate([-packed[..., half_width:], packed[..., :half_width]], axis=-1)

def complex_product(left, right):
    half_width = left.shape[-1] // 2
    left_real, left_imag = (left[..., :half_width], left[..., half_width:])
    right_real, right_imag = (right[..., :half_width], right[..., half_width:])
    return jnp.concatenate([left_real * right_real - left_imag * right_imag, left_real * right_imag + left_imag * right_real], axis=-1)

def translate(rotation, axial_pair, source, transposed):
    turned = jnp.einsum('pij,pjk->pik', rotation, source)
    turned = lax.optimization_barrier(turned.astype(jnp.bfloat16)).astype(jnp.float32)
    stacked = jnp.stack([turned, swap_parts(turned)], axis=1)
    if transposed:
        moved = jnp.einsum('pcji,pcjk->pik', axial_pair, stacked)
    else:
        moved = jnp.einsum('pcij,pcjk->pik', axial_pair, stacked)
    moved = lax.optimization_barrier(moved.astype(jnp.bfloat16)).astype(jnp.float32)
    return jnp.einsum('pji,pjk->pik', rotation, moved)

def reference(basis, mie_coeffs, rot_table, axial_table, pair_table, pair_count):
    coeff = basis[KRYLOV - 1].astype(jnp.bfloat16)
    flat_rows = pair_table.reshape(-1, 3)
    position = jnp.arange(N_BLK * PAIR_MAX, dtype=jnp.int32)
    owner = position // PAIR_MAX
    live = position % PAIR_MAX < pair_count[owner]
    target = owner * BLK_DEV + flat_rows[:, 0]
    source = jnp.clip((owner - 1) * BLK_DEV + flat_rows[:, 1], 0, BLOCKS - 1)
    groups = (target.reshape(-1, batch_pairs), source.reshape(-1, batch_pairs), flat_rows[:, 2].reshape(-1, batch_pairs), live.reshape(-1, batch_pairs))

    def accumulate(scattered, group):
        target_rows, source_rows, table_rows, live_rows = group
        rotation = rot_table[table_rows].astype(jnp.float32)
        axial_pair = axial_table[table_rows].astype(jnp.float32)
        forward = translate(rotation, axial_pair, coeff[source_rows].astype(jnp.float32), False)
        backward = translate(rotation, axial_pair, coeff[target_rows].astype(jnp.float32), True)
        forward = jnp.where(live_rows[:, None, None], forward, jnp.float32(0.0))
        backward = jnp.where(live_rows[:, None, None], backward, jnp.float32(0.0))
        scattered = scattered.at[target_rows].add(forward).at[source_rows].add(backward)
        return (scattered, None)
    start_field = jnp.zeros((BLOCKS, MODES, 2 * SPHERES), jnp.float32)
    scattered, unused = lax.scan(accumulate, start_field, groups)
    image = basis[KRYLOV - 1] - complex_product(mie_coeffs, scattered)
    mean_scale = 1.0 / (BLOCKS * MODES * 2 * SPHERES)
    highest = lax.Precision.HIGHEST
    real_part = jnp.einsum('kbcs,bcs->k', basis, image, precision=highest) * mean_scale
    imag_part = -jnp.einsum('kbcs,bcs->k', basis, swap_parts(image), precision=highest) * mean_scale
    remainder = image - jnp.einsum('k,kbcs->bcs', real_part, basis, precision=highest)
    remainder = remainder - jnp.einsum('k,kbcs->bcs', imag_part, swap_parts(basis), precision=highest)
    norm_square = jnp.sum(remainder * remainder) * mean_scale
    next_basis = remainder * lax.rsqrt(norm_square)
    return (jnp.stack([real_part, imag_part]), next_basis)
```

```python
import functools

import jax
import jax.numpy as jnp
from jax import lax
from jax.experimental import pallas as pl
from jax.experimental.pallas import tpu as pltpu
from jax.sharding import PartitionSpec as P

MIB = 1024 * 1024
F32 = jnp.float32
BF16 = jnp.bfloat16


def params(mib):
    return pltpu.CompilerParams(vmem_limit_bytes=mib * MIB)


def whole():
    return pl.BlockSpec(memory_space=pltpu.VMEM)


def rounded_up(value, unit):
    return (value + unit - 1) // unit * unit


def iota(shape, dim):
    return lax.broadcasted_iota(jnp.int32, shape, dim)


def dot_nn(left, right):
    return lax.dot_general(left, right, (((1,), (0,)), ((), ())), preferred_element_type=F32)


def dot_nt(left, right):
    return lax.dot_general(left, right, (((1,), (1,)), ((), ())), preferred_element_type=F32)


def pack_kernel(quarter, modes, ways, pair_rows_ref, count_ref, basis_ref, out_ref, codes_ref, pad_ref):
    columns = pad_ref.shape[1]
    part = columns // 2 // ways
    first = basis_ref.shape[1] - quarter * modes
    pad_ref[...] = jnp.zeros_like(pad_ref)
    for j in range(quarter):
        pad_ref[0:modes, :] = basis_ref[0, pl.ds(first + j, modes, quarter), :]
        turned = jnp.transpose(pad_ref[...]).astype(BF16)
        for p in range(ways):
            for c in range(2):
                row = c * (columns // 2) + p * part
                out_ref[p, c, j] = turned[row : row + part]
    slots = pair_rows_ref.shape[2]
    live = iota((1, slots), 1) < count_ref[0]
    zero = jnp.zeros((1, slots), jnp.int32)
    codes_ref[...] = jnp.zeros_like(codes_ref)
    codes_ref[0:1, :] = jnp.where(live, pair_rows_ref[0], zero)
    codes_ref[1:2, :] = jnp.where(live, pair_rows_ref[1], zero)
    codes_ref[2:3, :] = jnp.where(live, pair_rows_ref[2] + 1, zero)


def tables_kernel(modes, tables, axial_ref, rot_ref, rot_out_ref, axial_out_ref, lines_ref):
    step = pl.program_id(0)
    size = rot_out_ref.shape[1]
    chunk = 256

    @pl.when(step == 0)
    def _():
        rot_out_ref[...] = jnp.zeros_like(rot_out_ref)
        lines_ref[...] = jnp.zeros_like(lines_ref)

    out_row, in_row = iota((chunk, chunk), 0), iota((chunk, chunk), 1)
    each = chunk // 2
    halves = (in_row == 2 * lax.rem(out_row, each) + lax.div(out_row, each)).astype(F32).astype(BF16)
    lines_ref[0 : 2 * modes, 0:modes] = axial_ref[0].reshape(2 * modes, modes)
    for q in range(2 * size // chunk):
        sorted_rows = dot_nn(halves, lines_ref[q * chunk : (q + 1) * chunk, :]).astype(BF16)
        for c in range(2):
            axial_out_ref[0, c * size + q * each : c * size + (q + 1) * each, :] = sorted_rows[c * each : (c + 1) * each]
    each = chunk // tables
    entries = (in_row == tables * lax.rem(out_row, each) + lax.div(out_row, each)).astype(F32).astype(BF16)
    block = rot_ref.shape[0]
    left = tables * modes - step * block
    rows = jnp.where(iota((block, modes), 0) < left, rot_ref[...], jnp.zeros((), BF16))
    for q in range(block // chunk):
        sorted_rows = dot_nn(entries, rows[q * chunk : (q + 1) * chunk]).astype(BF16)
        start = pl.multiple_of(step * (block // tables) + q * each, each)
        for g in range(tables):
            rot_out_ref[g, pl.ds(start, each), 0:modes] = sorted_rows[g * each : (g + 1) * each]


def weights_kernel(own, part, codes_ref, below_ref, above_ref, out_ref):
    tables = out_ref.shape[0]
    group = own * part
    slots = codes_ref.shape[1]
    stacked = jnp.concatenate([below_ref[...], codes_ref[...], above_ref[...]], axis=0).astype(F32)
    filler = jnp.zeros((slots - stacked.shape[0], slots), F32)
    columns = jnp.transpose(jnp.concatenate([stacked, filler], axis=0)).astype(jnp.int32)
    row = iota((tables * group, slots), 0)
    entry = lax.div(row, group) + 1
    block = lax.rem(lax.div(row, part), own)

    def chosen(codes, line, shift):
        hit = (codes[2:3, :] == entry) & (codes[line : line + 1, :] - shift == block)
        return jnp.where(hit, 1.0, 0.0).astype(BF16)

    def spread(column, blocks):
        lane = lax.div(iota((slots, blocks * part), 1), part)
        return jnp.where(column == lane, 1.0, 0.0).astype(BF16)

    def store(direction, first, counts):
        lanes = counts.shape[1]
        same = lax.rem(iota(counts.shape, 0), part) == lax.rem(iota(counts.shape, 1), part)
        kept = jnp.where(same, counts, 0.0).astype(BF16)
        for g in range(tables):
            out_ref[g, direction * group : (direction + 1) * group, first : first + lanes] = kept[g * group : (g + 1) * group]

    store(0, 0, dot_nn(chosen(codes_ref[...], 0, 0), spread(columns[:, 9:10], 3 * own)))
    for window, ref in enumerate((below_ref, codes_ref, above_ref)):
        shift = (2 - window) * own
        counts = dot_nn(chosen(ref[...], 1, shift), spread(columns[:, 8 * window : 8 * window + 1], own))
        store(1, window * group, counts)


def swapped(value):
    half = value.shape[0] // 2
    return jnp.concatenate([-value[half:], value[:half]], axis=0)


def field_kernel(weights_ref, rot_ref, axial_ref, below_ref, own_ref, above_ref, out_ref, window_ref, total_ref):
    step = pl.program_id(0)
    group = weights_ref.shape[1] // 2
    size = window_ref.shape[2]

    @pl.when(step == 0)
    def _():
        for w, ref in enumerate((below_ref, own_ref, above_ref)):
            for c in range(2):
                window_ref[c, w * group : (w + 1) * group, :] = ref[:, c].reshape(group, size)
        total_ref[...] = jnp.zeros_like(total_ref)

    weights = weights_ref[0]
    real = dot_nn(weights, window_ref[0]).astype(BF16)
    imag = dot_nn(weights, window_ref[1]).astype(BF16)
    sums = jnp.concatenate([real[:group], imag[:group], real[group:], imag[group:]], axis=0)
    rotation = rot_ref[0]
    turned = dot_nt(sums, rotation).astype(BF16)
    forward, backward = turned[: 2 * group], turned[2 * group :]
    moved = dot_nt(forward, axial_ref[0, :size]) + dot_nt(swapped(forward), axial_ref[0, size:])
    moved += dot_nn(jnp.concatenate([backward, swapped(backward)], axis=1), axial_ref[0])
    total_ref[...] += dot_nn(moved.astype(BF16), rotation)

    @pl.when(step == pl.num_programs(0) - 1)
    def _():
        for c in range(2):
            out_ref[:, c] = total_ref[c * group : (c + 1) * group].astype(BF16).reshape(out_ref[:, c].shape)


def lane_swap(value):
    half = value.shape[1] // 2
    rolled = pltpu.roll(value, half, axis=1)
    return jnp.where(iota(value.shape, 1) < half, -rolled, rolled)


def folded(value):
    return jnp.sum(value.reshape(value.shape[0] // 8, 8, value.shape[1]), axis=0)


def image_kernel(quarter, modes, basis_ref, mie_ref, pieces_ref, image_ref, sums_ref, lines_ref, kept_ref):
    step = pl.program_id(0)
    rows = quarter * modes
    full = kept_ref.shape[1]
    gap = full - rows
    blocks = pl.num_programs(0)

    @pl.when(step == 0)
    def _():
        ways, _, _, part, size = pieces_ref.shape
        for j in range(quarter):
            turned = jnp.concatenate([pieces_ref[:, c, j].reshape(ways * part, size) for c in range(2)], axis=0)
            lines_ref[pl.ds(j, modes, quarter), :] = jnp.transpose(turned.astype(F32))[:modes]
        field = lines_ref[0:rows, :]
        mie = mie_ref[...]
        half = mie.shape[1] // 2
        left = iota(mie.shape, 1) < half
        other = pltpu.roll(mie, half, axis=1)
        product = jnp.where(left, mie, other) * field + jnp.where(left, -other, mie) * pltpu.roll(field, half, axis=1)
        image = basis_ref[0, rows : 2 * rows, :] - product
        kept_ref[...] = jnp.zeros_like(kept_ref)
        kept_ref[0, 0:rows, :] = image
        kept_ref[1, gap:full, :] = image
        image_ref[...] = kept_ref[0]
        kept_ref[2] = lane_swap(kept_ref[0])
        kept_ref[3] = lane_swap(kept_ref[1])
        sums_ref[...] = jnp.zeros_like(sums_ref)

    tile = iota(sums_ref.shape, 0), iota(sums_ref.shape, 1)
    update = jnp.zeros(sums_ref.shape, F32)
    for side in range(2):
        first = side * (2 * rows - full)
        values = basis_ref[0, first : first + full, :]
        k = 2 * (blocks - 1 - step) + side
        real = jnp.sum(folded(values * kept_ref[side]), axis=(0, 1), keepdims=True)
        imag = -jnp.sum(folded(values * kept_ref[2 + side]), axis=(0, 1), keepdims=True)
        update += jnp.where((tile[0] == k) & (tile[1] == 0), real, 0.0)
        update += jnp.where((tile[0] == k) & (tile[1] == 1), imag, 0.0)
    sums_ref[...] += update


def remainder_kernel(quarter, modes, dots_ref, basis_ref, image_ref, out_ref, squares_ref, kept_ref):
    step = pl.program_id(0)
    rows = quarter * modes
    full = kept_ref.shape[1]
    gap = full - rows
    for side in range(2):
        first = side * (2 * rows - full)
        values = basis_ref[0, first : first + full, :]
        k = 2 * step + side
        real, imag = dots_ref[k, 0] * values, dots_ref[k, 1] * values

        @pl.when(step == 0)
        def _():
            kept_ref[side] = real
            kept_ref[2 + side] = imag

        @pl.when(step > 0)
        def _():
            kept_ref[side] += real
            kept_ref[2 + side] += imag

    @pl.when(step == pl.num_programs(0) - 1)
    def _():
        real = kept_ref[0, 0:rows, :] + kept_ref[1, gap:full, :]
        imag = kept_ref[2, 0:rows, :] + kept_ref[3, gap:full, :]
        remainder = image_ref[0:rows, :] - real - lane_swap(imag)
        out_ref[...] = remainder
        squares = jnp.sum(remainder * remainder, axis=(0, 1), keepdims=True)
        squares_ref[...] = jnp.broadcast_to(squares, squares_ref.shape)


def butterfly(value, axis):
    count = lax.axis_size(axis)
    if count & (count - 1):
        return lax.psum(value, axis)
    distance = 1
    while distance < count:
        value = value + lax.ppermute(value, axis, [(i, i ^ distance) for i in range(count)])
        distance *= 2
    return value


def exchanged(value):
    return lax.all_to_all(value, "pair", split_axis=0, concat_axis=0, tiled=True)


def neighbours(value):
    count = lax.axis_size("blk")
    up = [(i, i + 1) for i in range(count - 1)]
    down = [(j, i) for i, j in up]
    return lax.ppermute(value, "blk", up), lax.ppermute(value, "blk", down)


def shards(basis, mie_coeffs, rot_table, axial_table, pair_table, pair_count):
    vectors, quarter, modes, columns = basis.shape
    ways = lax.axis_size("pair")
    blk_ways = lax.axis_size("blk")
    tables = rot_table.shape[0]
    slots = pair_table.shape[1]
    own = quarter * ways
    part = columns // 2 // ways
    group = own * part
    size = rounded_up(modes, 128)
    rows = quarter * modes
    full = rounded_up(rows, 8)
    pairs_of_vectors = vectors // 2

    basis_rows = basis.transpose(0, 2, 1, 3).reshape(pairs_of_vectors, 2 * rows, columns)
    mie_rows = mie_coeffs.transpose(1, 0, 2).reshape(rows, columns)
    rot_rows = rot_table.transpose(1, 0, 2).reshape(modes * tables, modes)
    axial_rows = axial_table.transpose(0, 2, 1, 3)
    pair_rows = pair_table.transpose(2, 0, 1)

    pieces_shape = (ways, 2, quarter, part, size)
    pieces, codes = pl.pallas_call(
        functools.partial(pack_kernel, quarter, modes, ways),
        grid=(1,),
        in_specs=[
            whole(),
            pl.BlockSpec(memory_space=pltpu.SMEM),
            pl.BlockSpec((1, 2 * rows, columns), lambda i: (pairs_of_vectors - 1, 0, 0)),
        ],
        out_specs=[whole(), whole()],
        out_shape=[jax.ShapeDtypeStruct(pieces_shape, BF16), jax.ShapeDtypeStruct((8, slots), jnp.int32)],
        scratch_shapes=[pltpu.VMEM((size, columns), F32)],
        compiler_params=params(16),
        name="pack",
    )(pair_rows, pair_count, basis_rows)
    codes_below, codes_above = neighbours(codes)
    own_pieces = exchanged(pieces)
    below, above = neighbours(own_pieces)

    block = tables * size // tables
    rotations, axials = pl.pallas_call(
        functools.partial(tables_kernel, modes, tables),
        grid=(tables,),
        in_specs=[
            pl.BlockSpec((1, modes, 2, modes), lambda g: (g, 0, 0, 0)),
            pl.BlockSpec((block, modes), lambda g: (g, 0)),
        ],
        out_specs=[
            pl.BlockSpec((tables, size, size), lambda g: (0, 0, 0)),
            pl.BlockSpec((1, 2 * size, size), lambda g: (g, 0, 0)),
        ],
        out_shape=[
            jax.ShapeDtypeStruct((tables, size, size), BF16),
            jax.ShapeDtypeStruct((tables, 2 * size, size), BF16),
        ],
        scratch_shapes=[pltpu.VMEM((2 * size, size), BF16)],
        compiler_params=params(32),
        cost_estimate=pl.CostEstimate(flops=tables * 8 * 256 * 256 * size, bytes_accessed=6 * tables * size * size * 2, transcendentals=0),
        name="tables",
    )(axial_rows, rot_rows)

    weights = pl.pallas_call(
        functools.partial(weights_kernel, own, part),
        in_specs=[whole()] * 3,
        out_specs=whole(),
        out_shape=jax.ShapeDtypeStruct((tables, 2 * group, 3 * group), BF16),
        compiler_params=params(24),
        name="weights",
    )(codes, codes_below, codes_above)

    field = pl.pallas_call(
        field_kernel,
        grid=(tables,),
        in_specs=[
            pl.BlockSpec((1, 2 * group, 3 * group), lambda g: (g, 0, 0)),
            pl.BlockSpec((1, size, size), lambda g: (g, 0, 0)),
            pl.BlockSpec((1, 2 * size, size), lambda g: (g, 0, 0)),
            whole(),
            whole(),
            whole(),
        ],
        out_specs=whole(),
        out_shape=jax.ShapeDtypeStruct(pieces_shape, BF16),
        scratch_shapes=[pltpu.VMEM((2, 3 * group, size), BF16), pltpu.VMEM((2 * group, size), F32)],
        compiler_params=params(32),
        name="field",
    )(weights, rotations, axials, below, own_pieces, above)
    field_pieces = exchanged(field)

    pair_block = (1, 2 * rows, columns)
    image, sums = pl.pallas_call(
        functools.partial(image_kernel, quarter, modes),
        grid=(pairs_of_vectors,),
        in_specs=[
            pl.BlockSpec(pair_block, lambda i: (pairs_of_vectors - 1 - i, 0, 0)),
            whole(),
            whole(),
        ],
        out_specs=[whole(), whole()],
        out_shape=[jax.ShapeDtypeStruct((full, columns), F32), jax.ShapeDtypeStruct((8, 128), F32)],
        scratch_shapes=[pltpu.VMEM((full, columns), F32), pltpu.VMEM((4, full, columns), F32)],
        compiler_params=params(24),
        name="image",
    )(basis_rows, mie_rows, field_pieces)

    mean_scale = 1.0 / (own * blk_ways * modes * columns)
    dots = butterfly(butterfly(sums, "pair"), "blk") * mean_scale

    remainder, squares = pl.pallas_call(
        functools.partial(remainder_kernel, quarter, modes),
        grid=(pairs_of_vectors,),
        in_specs=[
            pl.BlockSpec(memory_space=pltpu.SMEM),
            pl.BlockSpec(pair_block, lambda i: (i, 0, 0)),
            whole(),
        ],
        out_specs=[whole(), whole()],
        out_shape=[jax.ShapeDtypeStruct((rows, columns), F32), jax.ShapeDtypeStruct((8, 128), F32)],
        scratch_shapes=[pltpu.VMEM((4, full, columns), F32)],
        compiler_params=params(24),
        name="remainder",
    )(dots, basis_rows, image)
    norm_square = lax.psum(lax.psum(squares[0, 0], "pair"), "blk") * mean_scale
    next_basis = (remainder * lax.rsqrt(norm_square)).reshape(modes, quarter, columns).transpose(1, 0, 2)
    return dots[:vectors, :2].T, next_basis


def solution(mesh):
    placed = (
        P(None, ("blk", "pair"), None, None),
        P(("blk", "pair"), None, None),
        P(),
        P(),
        P("blk", None, None),
        P("blk"),
    )
    return jax.shard_map(
        shards,
        mesh=mesh,
        in_specs=placed,
        out_specs=(P(), P(("blk", "pair"), None, None)),
        check_vma=False,
    )
```

```python
import functools

import jax
import jax.numpy as jnp
from jax import lax
from jax.experimental import pallas as pl
from jax.experimental.pallas import tpu as pltpu
from jax.sharding import PartitionSpec as P

MIB = 1024 * 1024
F32 = jnp.float32
BF16 = jnp.bfloat16


def params(mib):
    return pltpu.CompilerParams(vmem_limit_bytes=mib * MIB)


def whole():
    return pl.BlockSpec(memory_space=pltpu.VMEM)


def in_hbm(value):
    return pltpu.with_memory_space_constraint(value, pltpu.HBM)


def rounded_up(value, unit):
    return (value + unit - 1) // unit * unit


def iota(shape, dim):
    return lax.broadcasted_iota(jnp.int32, shape, dim)


def dot_nn(left, right):
    return lax.dot_general(left, right, (((1,), (0,)), ((), ())), preferred_element_type=F32)


def dot_nt(left, right):
    return lax.dot_general(left, right, (((1,), (1,)), ((), ())), preferred_element_type=F32)


def pack_kernel(quarter, modes, ways, own, pair_rows_ref, count_ref, basis_ref, out_ref, lines_ref, pad_ref, codes_ref, sem):
    full, columns = lines_ref.shape
    rows = quarter * modes
    part = columns // 2 // ways
    copy = pltpu.make_async_copy(basis_ref.at[basis_ref.shape[0] - 1, pl.ds(2 * rows - full, full)], lines_ref, sem)
    copy.start()
    slots = pair_rows_ref.shape[2]
    live = iota((1, slots), 1) < count_ref[0]
    marks = jnp.where(live, own * (pair_rows_ref[2] + 1) + pair_rows_ref[0], 0)
    line = iota((slots, slots), 0)
    stacked = jnp.where(line == 0, marks, jnp.where(line == 1, pair_rows_ref[1], 0))
    turned = jnp.transpose(stacked.astype(F32))
    codes_ref[0:slots, :] = turned
    codes_ref[slots : 2 * slots, :] = pltpu.roll(turned, slots - 1, axis=1)
    share = 2 * quarter * part
    mine = codes_ref[pl.ds(pl.multiple_of(lax.axis_index("pair") * share, share), share), :][:, 0:1]
    pad_ref[...] = jnp.zeros_like(pad_ref)
    copy.wait()
    for j in range(quarter):
        pad_ref[0:modes, :] = lines_ref[pl.ds(full - rows + j, modes, quarter), :]
        turned = jnp.transpose(pad_ref[...])
        for c in range(2):
            codes = mine[(c * quarter + j) * part : (c * quarter + j + 1) * part]
            for p in range(ways):
                row = c * (columns // 2) + p * part
                piece = turned[row : row + part]
                out_ref[p, c, j] = jnp.where(iota(piece.shape, 1) == modes, codes, piece).astype(BF16)


def tables_kernel(modes, tables, axial_ref, rot_ref, rot_out_ref, axial_out_ref, lines_ref):
    step = pl.program_id(0)
    size = rot_out_ref.shape[1]
    chunk = 256

    @pl.when(step == 0)
    def _():
        rot_out_ref[...] = jnp.zeros_like(rot_out_ref)
        lines_ref[...] = jnp.zeros_like(lines_ref)

    out_row, in_row = iota((chunk, chunk), 0), iota((chunk, chunk), 1)
    each = chunk // 2
    halves = (in_row == 2 * lax.rem(out_row, each) + lax.div(out_row, each)).astype(F32).astype(BF16)
    lines_ref[0 : 2 * modes, 0:modes] = axial_ref[0].reshape(2 * modes, modes)
    for q in range(2 * size // chunk):
        sorted_rows = dot_nn(halves, lines_ref[q * chunk : (q + 1) * chunk, :]).astype(BF16)
        for c in range(2):
            axial_out_ref[0, c * size + q * each : c * size + (q + 1) * each, :] = sorted_rows[c * each : (c + 1) * each]
    each = chunk // tables
    entries = (in_row == tables * lax.rem(out_row, each) + lax.div(out_row, each)).astype(F32).astype(BF16)
    block = rot_ref.shape[0]
    left = tables * modes - step * block
    rows = jnp.where(iota((block, modes), 0) < left, rot_ref[...], jnp.zeros((), BF16))
    for q in range(block // chunk):
        sorted_rows = dot_nn(entries, rows[q * chunk : (q + 1) * chunk]).astype(BF16)
        start = pl.multiple_of(step * (block // tables) + q * each, each)
        for g in range(tables):
            rot_out_ref[g, pl.ds(start, each), 0:modes] = sorted_rows[g * each : (g + 1) * each]


def weights_kernel(own, part, modes, below_ref, own_ref, above_ref, out_ref):
    tables = out_ref.shape[0]
    group = own * part
    size = own_ref.shape[4]
    lane = modes % 128
    wanted = lax.div(iota((tables * group, group), 0), part) + own

    def lists(ref):
        values = ref[:, :, :, :, size - 128 : size].reshape(2 * group, 128).astype(F32)
        marks, sources = values[:group], values[group:]
        lines = [jnp.transpose(side)[lane : lane + 1].astype(jnp.int32) for side in (marks, sources)]
        return lines, [side[:, lane : lane + 1].astype(jnp.int32) for side in (marks, sources)]

    def one_hot(hit):
        return jnp.where(hit, 1.0, 0.0).astype(BF16)

    def store(direction, first, counts):
        lanes = counts.shape[1]
        same = lax.rem(iota(counts.shape, 0), part) == lax.rem(iota(counts.shape, 1), part)
        kept = jnp.where(same, counts, 0.0).astype(BF16)
        for g in range(tables):
            out_ref[g, direction * group : (direction + 1) * group, first : first + lanes] = kept[g * group : (g + 1) * group]

    for window, ref in enumerate((below_ref, own_ref, above_ref)):
        (marks, sources), (marks_column, sources_column) = lists(ref)
        if window == 1:
            spread = one_hot(sources_column == lax.div(iota((group, 3 * group), 1), part))
            store(0, 0, dot_nn(one_hot(marks == wanted), spread))
        block = sources - (2 - window) * own
        inside = (block >= 0) & (block < own) & (marks >= own)
        hits = one_hot(jnp.where(inside, lax.div(marks, own) * own + block, -1) == wanted)
        spread = one_hot(lax.rem(marks_column, own) == lax.div(iota((group, group), 1), part))
        store(1, window * group, dot_nn(hits, spread))


def swapped(value):
    half = value.shape[0] // 2
    return jnp.concatenate([-value[half:], value[:half]], axis=0)


def field_kernel(weights_ref, rot_ref, axial_ref, below_ref, own_ref, above_ref, out_ref, window_ref, total_ref):
    step = pl.program_id(0)
    group = weights_ref.shape[1] // 2
    size = window_ref.shape[2]

    @pl.when(step == 0)
    def _():
        for w, ref in enumerate((below_ref, own_ref, above_ref)):
            for c in range(2):
                window_ref[c, w * group : (w + 1) * group, :] = ref[:, c].reshape(group, size)
        total_ref[...] = jnp.zeros_like(total_ref)

    weights = weights_ref[0]
    real = dot_nn(weights, window_ref[0]).astype(BF16)
    imag = dot_nn(weights, window_ref[1]).astype(BF16)
    sums = jnp.concatenate([real[:group], imag[:group], real[group:], imag[group:]], axis=0)
    rotation = rot_ref[0]
    turned = dot_nt(sums, rotation).astype(BF16)
    forward, backward = turned[: 2 * group], turned[2 * group :]
    moved = dot_nt(forward, axial_ref[0, :size]) + dot_nt(swapped(forward), axial_ref[0, size:])
    moved += dot_nn(jnp.concatenate([backward, swapped(backward)], axis=1), axial_ref[0])
    total_ref[...] += dot_nn(moved.astype(BF16), rotation)

    @pl.when(step == pl.num_programs(0) - 1)
    def _():
        for c in range(2):
            out_ref[:, c] = total_ref[c * group : (c + 1) * group].astype(BF16).reshape(out_ref[:, c].shape)


def lane_swap(value):
    half = value.shape[1] // 2
    rolled = pltpu.roll(value, half, axis=1)
    return jnp.where(iota(value.shape, 1) < half, -rolled, rolled)


def folded(value):
    return jnp.sum(value.reshape(value.shape[0] // 8, 8, value.shape[1]), axis=0)


def gram_kernel(quarter, modes, basis_ref, aligned_ref, gram_ref, blocks_ref, sums_ref, sems):
    vectors, full, columns = aligned_ref.shape
    rows = quarter * modes
    copies = [pltpu.make_async_copy(basis_ref.at[i], blocks_ref.at[i], sems.at[i]) for i in range(vectors // 2)]
    for copy in copies:
        copy.start()
    sums_ref[...] = jnp.zeros_like(sums_ref)
    for i, copy in enumerate(copies):
        copy.wait()
        for side in range(2):
            aligned_ref[2 * i + side, 0:rows, :] = blocks_ref[i, side * rows : (side + 1) * rows, :]
            aligned_ref[2 * i + side, rows:full, :] = jnp.zeros((full - rows, columns), F32)
    chunk = 32

    def body(i, carry):
        here = pl.ds(pl.multiple_of(i * chunk, chunk), chunk)
        values = [aligned_ref[k, here, :] for k in range(vectors)]
        for l in range(vectors):
            other = lane_swap(values[l])
            for k in range(l + 1):
                sums_ref[0, l, k] += folded(values[k] * values[l])
                if k < l:
                    sums_ref[1, l, k] -= folded(values[k] * other)
        return carry

    lax.fori_loop(0, full // chunk, body, 0)
    totals = jnp.sum(jnp.sum(sums_ref[...].reshape(2 * vectors * vectors, 8, columns), axis=1), axis=1, keepdims=True)
    lane = iota(gram_ref.shape, 1)
    tile = jnp.zeros(gram_ref.shape, F32)
    for l in range(2 * vectors):
        tile = jnp.where(lane == l, totals[l * vectors : (l + 1) * vectors], tile)
    gram_ref[...] = tile


def image_kernel(quarter, modes, aligned_ref, gram_ref, mie_ref, pieces_ref, image_ref, sums_ref, lines_ref):
    vectors, full, columns = aligned_ref.shape
    rows = quarter * modes
    ways, _, _, part, size = pieces_ref.shape
    lines_ref[rows:full, :] = jnp.zeros((full - rows, columns), F32)
    for j in range(quarter):
        turned = jnp.concatenate([pieces_ref[:, c, j].reshape(ways * part, size) for c in range(2)], axis=0)
        lines_ref[pl.ds(j, modes, quarter), :] = jnp.transpose(turned.astype(F32))[:modes]
    half = columns // 2
    chunk = 64
    totals = [jnp.zeros((8, columns), F32) for _ in range(2 * vectors + 1)]
    for first in range(0, full, chunk):
        count = min(chunk, rows - first)
        here = slice(first, first + chunk)
        field = lines_ref[here, :]
        mie = mie_ref[first : first + count, :]
        if count < chunk:
            mie = jnp.concatenate([mie, jnp.zeros((chunk - count, columns), F32)], axis=0)
        left = iota(mie.shape, 1) < half
        other = pltpu.roll(mie, half, axis=1)
        product = jnp.where(left, mie, other) * field + jnp.where(left, -other, mie) * pltpu.roll(field, half, axis=1)
        image = aligned_ref[vectors - 1, here, :] - product
        image_ref[here, :] = image
        turned = lane_swap(image)
        for k in range(vectors):
            values = aligned_ref[k, here, :]
            totals[k] += folded(values * image)
            totals[vectors + k] -= folded(values * turned)
        totals[2 * vectors] += folded(image * image)
    lane = iota(gram_ref.shape, 1)
    tile = gram_ref[...]
    for part_index in range(2):
        stacked = jnp.stack(totals[part_index * vectors : (part_index + 1) * vectors], axis=0)
        column = jnp.sum(jnp.sum(stacked, axis=1), axis=1, keepdims=True)
        tile = jnp.where(lane == 2 * vectors + part_index, column, tile)
    square = jnp.sum(totals[2 * vectors], axis=(0, 1), keepdims=True)
    tile = jnp.where((lane == 2 * vectors + 2) & (iota(tile.shape, 0) == 0), square, tile)
    sums_ref[...] = jnp.broadcast_to(tile[None], sums_ref.shape)


def remainder_kernel(quarter, modes, mean_scale, sums_ref, aligned_ref, image_ref, dots_ref, out_ref):
    vectors, full, columns = aligned_ref.shape
    rows = quarter * modes
    total = jnp.sum(sums_ref[...], axis=0)
    row, lane = iota(total.shape, 0), iota(total.shape, 1)

    def lane_at(index):
        return jnp.sum(jnp.where(lane == index, total, 0.0), axis=1, keepdims=True)

    def on_lanes(column, first):
        return jnp.sum(jnp.where(row + first == lane, column, 0.0), axis=0, keepdims=True)

    real, imag = lane_at(2 * vectors) * mean_scale, lane_at(2 * vectors + 1) * mean_scale
    real_line, imag_line = on_lanes(real, 0), on_lanes(imag, 0)
    dots_ref[0:1, :] = real_line[:, :vectors]
    dots_ref[1:2, :] = imag_line[:, :vectors]
    same = jnp.where(lane < vectors, real * real_line + imag * imag_line, 0.0)
    cross = imag * on_lanes(real, vectors) - real * on_lanes(imag, vectors)
    cross = jnp.where((lane >= vectors) & (lane < 2 * vectors), cross, 0.0)
    often = jnp.where(row == lane, 1.0, 2.0)
    spread = jnp.sum(total * often * (same + cross), axis=(0, 1), keepdims=True)
    square = lane_at(2 * vectors + 2)[0:1]
    inside = jnp.sum(real * real + imag * imag, axis=0, keepdims=True)
    norm_square = (square + spread) * mean_scale - 2.0 * inside
    scale = lax.rsqrt(norm_square)
    image_scale = jnp.broadcast_to(scale, (8, columns))
    reals = [jnp.broadcast_to(real[k : k + 1] * scale, (8, columns)) for k in range(vectors)]
    imags = [jnp.broadcast_to(imag[k : k + 1] * scale, (8, columns)) for k in range(vectors)]
    chunk = 64
    for first in range(0, full, chunk):
        here = slice(first, first + chunk)
        values = [aligned_ref[k, here, :].reshape(chunk // 8, 8, columns) for k in range(vectors)]
        along = image_ref[here, :].reshape(chunk // 8, 8, columns) * image_scale
        turned = jnp.zeros_like(along)
        for k in range(vectors):
            along -= reals[k] * values[k]
            turned += imags[k] * values[k]
        result = along.reshape(chunk, columns) - lane_swap(turned.reshape(chunk, columns))
        count = min(chunk, rows - first)
        height = out_ref.shape[1]
        out_ref[first // height : (first + count) // height] = result.reshape(chunk // height, height, columns)[: count // height]


def exchanged(value):
    return lax.all_to_all(value, "pair", split_axis=0, concat_axis=0, tiled=True)


def neighbours(value):
    count = lax.axis_size("blk")
    up = [(i, i + 1) for i in range(count - 1)]
    down = [(j, i) for i, j in up]
    return lax.ppermute(value, "blk", up), lax.ppermute(value, "blk", down)


def shards(basis, mie_coeffs, rot_table, axial_table, pair_table, pair_count):
    vectors, quarter, modes, columns = basis.shape
    ways = lax.axis_size("pair")
    blk_ways = lax.axis_size("blk")
    tables = rot_table.shape[0]
    slots = pair_table.shape[1]
    own = quarter * ways
    part = columns // 2 // ways
    group = own * part
    size = rounded_up(modes, 128)
    rows = quarter * modes
    full = rounded_up(rows, 8)
    pairs_of_vectors = vectors // 2

    basis_rows = in_hbm(basis.transpose(0, 2, 1, 3).reshape(pairs_of_vectors, 2 * rows, columns))
    mie_rows = mie_coeffs.transpose(1, 0, 2).reshape(rows, columns)
    rot_rows = in_hbm(rot_table.transpose(1, 0, 2).reshape(modes * tables, modes))
    axial_rows = in_hbm(axial_table.transpose(0, 2, 1, 3))
    pair_rows = pair_table.transpose(2, 0, 1)

    pieces_shape = (ways, 2, quarter, part, size)
    pieces = pl.pallas_call(
        functools.partial(pack_kernel, quarter, modes, ways, own),
        in_specs=[whole(), pl.BlockSpec(memory_space=pltpu.SMEM), pl.BlockSpec(memory_space=pltpu.HBM)],
        out_specs=whole(),
        out_shape=jax.ShapeDtypeStruct(pieces_shape, BF16),
        scratch_shapes=[
            pltpu.VMEM((full, columns), F32),
            pltpu.VMEM((size, columns), F32),
            pltpu.VMEM((2 * slots, slots), F32),
            pltpu.SemaphoreType.DMA,
        ],
        compiler_params=params(16),
        name="pack",
    )(pair_rows, pair_count, basis_rows)
    own_pieces = exchanged(pieces)

    rotations, axials = pl.pallas_call(
        functools.partial(tables_kernel, modes, tables),
        grid=(tables,),
        in_specs=[
            pl.BlockSpec((1, modes, 2, modes), lambda g: (g, 0, 0, 0)),
            pl.BlockSpec((size, modes), lambda g: (g, 0)),
        ],
        out_specs=[
            pl.BlockSpec((tables, size, size), lambda g: (0, 0, 0)),
            pl.BlockSpec((1, 2 * size, size), lambda g: (g, 0, 0)),
        ],
        out_shape=[
            jax.ShapeDtypeStruct((tables, size, size), BF16),
            jax.ShapeDtypeStruct((tables, 2 * size, size), BF16),
        ],
        scratch_shapes=[pltpu.VMEM((2 * size, size), BF16)],
        compiler_params=params(32),
        cost_estimate=pl.CostEstimate(flops=tables * 8 * 256 * 256 * size, bytes_accessed=6 * tables * size * size * 2, transcendentals=0),
        name="tables",
    )(axial_rows, rot_rows)
    own_pieces, rotations, axials = lax.optimization_barrier((own_pieces, rotations, axials))
    below, above = neighbours(own_pieces)

    aligned, gram = pl.pallas_call(
        functools.partial(gram_kernel, quarter, modes),
        in_specs=[pl.BlockSpec(memory_space=pltpu.HBM)],
        out_specs=[whole(), whole()],
        out_shape=[jax.ShapeDtypeStruct((vectors, full, columns), F32), jax.ShapeDtypeStruct((vectors, 128), F32)],
        scratch_shapes=[
            pltpu.VMEM((pairs_of_vectors, 2 * rows, columns), F32),
            pltpu.VMEM((2, vectors, vectors, 8, columns), F32),
            pltpu.SemaphoreType.DMA((pairs_of_vectors,)),
        ],
        compiler_params=params(16),
        name="gram",
    )(basis_rows)
    below, above, aligned, gram = lax.optimization_barrier((below, above, aligned, gram))

    weights = pl.pallas_call(
        functools.partial(weights_kernel, own, part, modes),
        in_specs=[whole()] * 3,
        out_specs=whole(),
        out_shape=jax.ShapeDtypeStruct((tables, 2 * group, 3 * group), BF16),
        compiler_params=params(24),
        name="weights",
    )(below, own_pieces, above)

    field = pl.pallas_call(
        field_kernel,
        grid=(tables,),
        in_specs=[
            pl.BlockSpec((1, 2 * group, 3 * group), lambda g: (g, 0, 0)),
            pl.BlockSpec((1, size, size), lambda g: (g, 0, 0)),
            pl.BlockSpec((1, 2 * size, size), lambda g: (g, 0, 0)),
            whole(),
            whole(),
            whole(),
        ],
        out_specs=whole(),
        out_shape=jax.ShapeDtypeStruct(pieces_shape, BF16),
        scratch_shapes=[pltpu.VMEM((2, 3 * group, size), BF16), pltpu.VMEM((2 * group, size), F32)],
        compiler_params=params(24),
        name="field",
    )(weights, rotations, axials, below, own_pieces, above)
    field_pieces = exchanged(field)

    devices = ways * blk_ways
    image, sums = pl.pallas_call(
        functools.partial(image_kernel, quarter, modes),
        in_specs=[whole()] * 4,
        out_specs=[whole(), whole()],
        out_shape=[jax.ShapeDtypeStruct((full, columns), F32), jax.ShapeDtypeStruct((devices, vectors, 128), F32)],
        scratch_shapes=[pltpu.VMEM((full, columns), F32)],
        compiler_params=params(16),
        name="image",
    )(aligned, gram, mie_rows, field_pieces)
    sums = lax.all_to_all(sums, ("blk", "pair"), split_axis=0, concat_axis=0, tiled=True)

    mean_scale = 1.0 / (own * blk_ways * modes * columns)
    height = 4
    dots, next_rows = pl.pallas_call(
        functools.partial(remainder_kernel, quarter, modes, mean_scale),
        in_specs=[whole()] * 3,
        out_specs=[whole(), whole()],
        out_shape=[jax.ShapeDtypeStruct((2, vectors), F32), jax.ShapeDtypeStruct((rows // height, height, columns), F32)],
        compiler_params=params(16),
        name="remainder",
    )(sums, aligned, image)
    return dots, next_rows.reshape(modes, quarter, columns).transpose(1, 0, 2)


def solution(mesh):
    placed = (
        P(None, ("blk", "pair"), None, None),
        P(("blk", "pair"), None, None),
        P(),
        P(),
        P("blk", None, None),
        P("blk"),
    )
    return jax.shard_map(
        shards,
        mesh=mesh,
        in_specs=placed,
        out_specs=(P(), P(("blk", "pair"), None, None)),
        check_vma=False,
    )
```

```python
import functools

import jax
import jax.numpy as jnp
from jax import lax
from jax.experimental import pallas as pl
from jax.experimental.pallas import tpu as pltpu
from jax.sharding import PartitionSpec as P

MIB = 1024 * 1024
F32 = jnp.float32
BF16 = jnp.bfloat16


def params(mib):
    return pltpu.CompilerParams(vmem_limit_bytes=mib * MIB)


def hbm():
    return pl.BlockSpec(memory_space=pltpu.HBM)


def whole():
    return pl.BlockSpec(memory_space=pltpu.VMEM)


def in_hbm(value):
    return pltpu.with_memory_space_constraint(value, pltpu.HBM)


def rounded_up(value, unit):
    return (value + unit - 1) // unit * unit


def iota(shape, dim):
    return lax.broadcasted_iota(jnp.int32, shape, dim)


def dot_nn(left, right):
    return lax.dot_general(left, right, (((1,), (0,)), ((), ())), preferred_element_type=F32)


def dot_nt(left, right):
    return lax.dot_general(left, right, (((1,), (1,)), ((), ())), preferred_element_type=F32)


def pack_kernel(quarter, modes, ways, own, list_ref, count_ref, basis_ref, out_ref, pair_rows_ref, lines_ref, pad_ref, codes_ref, sems):
    full, columns = lines_ref.shape
    rows = quarter * modes
    part = columns // 2 // ways
    copy = pltpu.make_async_copy(basis_ref.at[basis_ref.shape[0] - 1, pl.ds(2 * rows - full, full)], lines_ref, sems.at[0])
    copy.start()
    list_copy = pltpu.make_async_copy(list_ref, pair_rows_ref, sems.at[1])
    list_copy.start()
    pad_ref[...] = jnp.zeros_like(pad_ref)
    list_copy.wait()
    slots = pair_rows_ref.shape[2]
    live = iota((1, slots), 1) < count_ref[0]
    marks = jnp.where(live, own * (pair_rows_ref[2] + 1) + pair_rows_ref[0], 0)
    line = iota((slots, slots), 0)
    stacked = jnp.where(line == 0, marks, jnp.where(line == 1, pair_rows_ref[1], 0))
    turned = jnp.transpose(stacked.astype(F32))
    codes_ref[0:slots, :] = turned
    codes_ref[slots : 2 * slots, :] = pltpu.roll(turned, slots - 1, axis=1)
    share = 2 * quarter * part
    mine = codes_ref[pl.ds(pl.multiple_of(lax.axis_index("pair") * share, share), share), :][:, 0:1]
    copy.wait()
    for j in range(quarter):
        pad_ref[0:modes, :] = lines_ref[pl.ds(full - rows + j, modes, quarter), :]
        turned = jnp.transpose(pad_ref[...])
        for c in range(2):
            codes = mine[(c * quarter + j) * part : (c * quarter + j + 1) * part]
            for p in range(ways):
                row = c * (columns // 2) + p * part
                piece = turned[row : row + part]
                out_ref[p, c, j] = jnp.where(iota(piece.shape, 1) == modes, codes, piece).astype(BF16)


def tables_kernel(modes, tables, axial_ref, rot_ref, rot_out_ref, axial_out_ref, lines_ref):
    step = pl.program_id(0)
    size = rot_out_ref.shape[2]
    chunk = 256

    @pl.when(step == 0)
    def _():
        lines_ref[...] = jnp.zeros_like(lines_ref)

    out_row, in_row = iota((chunk, chunk), 0), iota((chunk, chunk), 1)
    each = chunk // 2
    halves = (in_row == 2 * lax.rem(out_row, each) + lax.div(out_row, each)).astype(F32).astype(BF16)
    lines_ref[0 : 2 * modes, 0:modes] = axial_ref[0].reshape(2 * modes, modes)
    for q in range(2 * size // chunk):
        sorted_rows = dot_nn(halves, lines_ref[q * chunk : (q + 1) * chunk, :]).astype(BF16)
        for c in range(2):
            axial_out_ref[0, c * size + q * each : c * size + (q + 1) * each, :] = sorted_rows[c * each : (c + 1) * each]
    each = chunk // tables
    entries = (in_row == tables * lax.rem(out_row, each) + lax.div(out_row, each)).astype(F32).astype(BF16)
    block = rot_ref.shape[0]
    left = tables * modes - step * block
    rows = jnp.where(iota((block, modes), 0) < left, rot_ref[...], jnp.zeros((), BF16))
    rot_out_ref[:, :, size - 128 : size] = jnp.zeros((tables, block // tables, 128), BF16)
    for q in range(block // chunk):
        sorted_rows = dot_nn(entries, rows[q * chunk : (q + 1) * chunk]).astype(BF16)
        for g in range(tables):
            rot_out_ref[g, q * each : (q + 1) * each, 0:modes] = sorted_rows[g * each : (g + 1) * each]


def weights_kernel(own, part, modes, below_ref, own_ref, above_ref, out_ref):
    tables = out_ref.shape[0]
    group = own * part
    size = own_ref.shape[4]
    lane = modes % 128
    wanted = lax.div(iota((tables * group, group), 0), part) + own

    def lists(ref):
        values = ref[:, :, :, :, size - 128 : size].reshape(2 * group, 128).astype(F32)
        marks, sources = values[:group], values[group:]
        lines = [jnp.transpose(side)[lane : lane + 1].astype(jnp.int32) for side in (marks, sources)]
        return lines, [side[:, lane : lane + 1].astype(jnp.int32) for side in (marks, sources)]

    def one_hot(hit):
        return jnp.where(hit, 1.0, 0.0).astype(BF16)

    def store(direction, first, counts):
        lanes = counts.shape[1]
        same = lax.rem(iota(counts.shape, 0), part) == lax.rem(iota(counts.shape, 1), part)
        kept = jnp.where(same, counts, 0.0).astype(BF16)
        for g in range(tables):
            out_ref[g, direction * group : (direction + 1) * group, first : first + lanes] = kept[g * group : (g + 1) * group]

    for window, ref in enumerate((below_ref, own_ref, above_ref)):
        (marks, sources), (marks_column, sources_column) = lists(ref)
        if window == 1:
            spread = one_hot(sources_column == lax.div(iota((group, 3 * group), 1), part))
            store(0, 0, dot_nn(one_hot(marks == wanted), spread))
        block = sources - (2 - window) * own
        inside = (block >= 0) & (block < own) & (marks >= own)
        hits = one_hot(jnp.where(inside, lax.div(marks, own) * own + block, -1) == wanted)
        spread = one_hot(lax.rem(marks_column, own) == lax.div(iota((group, group), 1), part))
        store(1, window * group, dot_nn(hits, spread))


def swapped(value):
    half = value.shape[0] // 2
    return jnp.concatenate([-value[half:], value[:half]], axis=0)


def field_kernel(weights_ref, rot_ref, axial_ref, below_ref, own_ref, above_ref, out_ref, window_ref, total_ref):
    step = pl.program_id(0)
    group = weights_ref.shape[1] // 2
    size = window_ref.shape[2]

    @pl.when(step == 0)
    def _():
        for w, ref in enumerate((below_ref, own_ref, above_ref)):
            for c in range(2):
                window_ref[c, w * group : (w + 1) * group, :] = ref[:, c].reshape(group, size)
        total_ref[...] = jnp.zeros_like(total_ref)

    entries = range(weights_ref.shape[0])
    real = [dot_nn(weights_ref[g], window_ref[0]).astype(BF16) for g in entries]
    imag = [dot_nn(weights_ref[g], window_ref[1]).astype(BF16) for g in entries]
    sums = [jnp.concatenate([r[:group], i[:group], r[group:], i[group:]], axis=0) for r, i in zip(real, imag)]
    turned = [dot_nt(sums[g], rot_ref[g]).astype(BF16) for g in entries]
    moved = []
    for g in entries:
        forward, backward = turned[g][: 2 * group], turned[g][2 * group :]
        result = dot_nt(forward, axial_ref[g, :size]) + dot_nt(swapped(forward), axial_ref[g, size:])
        result += dot_nn(jnp.concatenate([backward, swapped(backward)], axis=1), axial_ref[g])
        moved.append(result.astype(BF16))
    total_ref[...] += sum(dot_nn(moved[g], rot_ref[g]) for g in entries)

    @pl.when(step == pl.num_programs(0) - 1)
    def _():
        for c in range(2):
            out_ref[:, c] = total_ref[c * group : (c + 1) * group].astype(BF16).reshape(out_ref[:, c].shape)


def lane_swap(value):
    half = value.shape[1] // 2
    rolled = pltpu.roll(value, half, axis=1)
    return jnp.where(iota(value.shape, 1) < half, -rolled, rolled)


def folded(value):
    return jnp.sum(value.reshape(value.shape[0] // 8, 8, value.shape[1]), axis=0)


def gram_kernel(quarter, modes, basis_ref, gram_ref, aligned_ref, blocks_ref, sums_ref, sems):
    vectors, full, columns = aligned_ref.shape
    rows = quarter * modes
    copies = [pltpu.make_async_copy(basis_ref.at[i], blocks_ref.at[i], sems.at[i]) for i in range(vectors // 2)]
    for copy in copies:
        copy.start()
    sums_ref[...] = jnp.zeros_like(sums_ref)
    for i, copy in enumerate(copies):
        copy.wait()
        for side in range(2):
            aligned_ref[2 * i + side, 0:rows, :] = blocks_ref[i, side * rows : (side + 1) * rows, :]
            aligned_ref[2 * i + side, rows:full, :] = jnp.zeros((full - rows, columns), F32)
    chunk = 32

    def body(i, carry):
        here = pl.ds(pl.multiple_of(i * chunk, chunk), chunk)
        values = [aligned_ref[k, here, :] for k in range(vectors)]
        for l in range(vectors):
            other = lane_swap(values[l])
            for k in range(l + 1):
                sums_ref[k, l] += folded(values[k] * values[l])
                if k < l:
                    sums_ref[l, k] -= folded(values[k] * other)
        return carry

    lax.fori_loop(0, full // chunk, body, 0)
    totals = jnp.sum(jnp.sum(sums_ref[...].reshape(vectors * vectors, 8, columns), axis=1), axis=1, keepdims=True)
    row, lane = iota((vectors, 128), 0), iota((vectors, 128), 1)
    line = jnp.zeros((1, 128), F32)
    for k in range(vectors):
        column = totals[k * vectors : (k + 1) * vectors]
        line += jnp.sum(jnp.where(row + k * vectors == lane, column, 0.0), axis=0, keepdims=True)
    gram_ref[...] = line


def image_kernel(quarter, modes, basis_ref, mie_ref, gram_ref, pieces_ref, blocks_ref, image_ref, sums_ref, lines_ref, mies_ref, tile_ref, sems):
    blocks = blocks_ref.shape[0]
    vectors = 2 * blocks
    full, columns = image_ref.shape
    rows = quarter * modes
    height = mies_ref.shape[1]
    ways, _, _, part, size = pieces_ref.shape
    small = [pltpu.make_async_copy(mie_ref, mies_ref, sems.at[blocks]), pltpu.make_async_copy(gram_ref, tile_ref, sems.at[blocks + 1])]
    copies = [pltpu.make_async_copy(basis_ref.at[i], blocks_ref.at[i, pl.ds(0, 2 * rows)], sems.at[i]) for i in range(blocks)]
    for copy in [copies[-1]] + small + copies[:-1]:
        copy.start()
    for i in range(blocks):
        blocks_ref[i, 2 * rows :, :] = jnp.zeros((blocks_ref.shape[1] - 2 * rows, columns), F32)
    lines_ref[rows:full, :] = jnp.zeros((full - rows, columns), F32)
    for j in range(quarter):
        turned = jnp.concatenate([pieces_ref[:, c, j].reshape(ways * part, size) for c in range(2)], axis=0)
        lines_ref[pl.ds(j, modes, quarter), :] = jnp.transpose(turned.astype(F32))[:modes]
    half = columns // 2
    chunk = 64
    copies[-1].wait()
    for copy in small:
        copy.wait()
    square = jnp.zeros((8, columns), F32)
    for first in range(0, full, chunk):
        count = min(chunk, rows - first)
        here = slice(first, first + chunk)
        field = lines_ref[here, :]
        mie = mies_ref[first // height : (first + count) // height].reshape(count, columns)
        if count < chunk:
            mie = jnp.concatenate([mie, jnp.zeros((chunk - count, columns), F32)], axis=0)
        left = iota(mie.shape, 1) < half
        other = pltpu.roll(mie, half, axis=1)
        product = jnp.where(left, mie, other) * field + jnp.where(left, -other, mie) * pltpu.roll(field, half, axis=1)
        image = blocks_ref[blocks - 1, rows + first : rows + first + chunk, :] - product
        image_ref[here, :] = image
        square += folded(image * image)
    lane = iota(tile_ref.shape, 1)
    tile = tile_ref[...]
    for i in reversed(range(blocks)):
        if i < blocks - 1:
            copies[i].wait()
        totals = [jnp.zeros((8, columns), F32) for _ in range(4)]
        for first in range(0, full, chunk):
            image = image_ref[first : first + chunk, :]
            turned = lane_swap(image)
            for side in range(2):
                values = blocks_ref[i, side * rows + first : side * rows + first + chunk, :]
                totals[2 * side] += folded(values * image)
                totals[2 * side + 1] -= folded(values * turned)
        for index, total in enumerate(totals):
            total = jnp.sum(total, axis=(0, 1), keepdims=True)
            tile = jnp.where(lane == vectors * vectors + 4 * i + index, total, tile)
    square = jnp.sum(square, axis=(0, 1), keepdims=True)
    tile = jnp.where(lane == vectors * vectors + 2 * vectors, square, tile)
    sums_ref[...] = jnp.broadcast_to(tile[None], sums_ref.shape)


def remainder_kernel(quarter, modes, mean_scale, sums_ref, blocks_ref, image_ref, dots_ref, out_ref):
    vectors = 2 * blocks_ref.shape[0]
    full, columns = image_ref.shape
    rows = quarter * modes
    total = jnp.sum(sums_ref[...], axis=0)
    lane = iota(total.shape, 1)

    def lane_at(index):
        return jnp.sum(jnp.where(lane == index, total, 0.0), axis=1, keepdims=True)

    def on_lanes(parts, places):
        line = jnp.zeros(total.shape, F32)
        for k in range(vectors):
            line = jnp.where(places == k, parts[k], line)
        return line

    start = vectors * vectors
    real = [lane_at(start + 2 * k) * mean_scale for k in range(vectors)]
    imag = [lane_at(start + 2 * k + 1) * mean_scale for k in range(vectors)]
    real_line, imag_line = on_lanes(real, lane), on_lanes(imag, lane)
    dots_ref[0:1, :] = real_line[:, :vectors]
    dots_ref[1:2, :] = imag_line[:, :vectors]
    first_index, last_index = lax.div(lane, vectors), lax.rem(lane, vectors)
    real_first, real_last = on_lanes(real, first_index), on_lanes(real, last_index)
    imag_first, imag_last = on_lanes(imag, first_index), on_lanes(imag, last_index)
    same = real_first * real_last + imag_first * imag_last
    cross = imag_last * real_first - real_last * imag_first
    often = jnp.where(first_index == last_index, 1.0, 2.0)
    spread = jnp.where(lane < start, total * often * jnp.where(first_index <= last_index, same, cross), 0.0)
    spread = jnp.sum(spread, axis=1, keepdims=True)
    inside = jnp.sum(real_line * real_line + imag_line * imag_line, axis=1, keepdims=True)
    norm_square = (lane_at(start + 2 * vectors) + spread) * mean_scale - 2.0 * inside
    scale = lax.rsqrt(norm_square)
    image_scale = jnp.broadcast_to(scale, (8, columns))
    reals = [jnp.broadcast_to(real[k] * scale, (8, columns)) for k in range(vectors)]
    imags = [jnp.broadcast_to(imag[k] * scale, (8, columns)) for k in range(vectors)]
    chunk = 64
    for first in range(0, full, chunk):
        here = slice(first, first + chunk)
        values = []
        for k in range(vectors):
            start = k % 2 * rows + first
            values.append(blocks_ref[k // 2, start : start + chunk, :].reshape(chunk // 8, 8, columns))
        along = image_ref[here, :].reshape(chunk // 8, 8, columns) * image_scale
        turned = jnp.zeros_like(along)
        for k in range(vectors):
            along -= reals[k] * values[k]
            turned += imags[k] * values[k]
        result = along.reshape(chunk, columns) - lane_swap(turned.reshape(chunk, columns))
        count = min(chunk, rows - first)
        height = out_ref.shape[1]
        out_ref[first // height : (first + count) // height] = result.reshape(chunk // height, height, columns)[: count // height]


def exchanged(value):
    return lax.all_to_all(value, "pair", split_axis=0, concat_axis=0, tiled=True)


def neighbours(value):
    count = lax.axis_size("blk")
    up = [(i, i + 1) for i in range(count - 1)]
    down = [(j, i) for i, j in up]
    return lax.ppermute(value, "blk", up), lax.ppermute(value, "blk", down)


def shards(basis, mie_coeffs, rot_table, axial_table, pair_table, pair_count):
    vectors, quarter, modes, columns = basis.shape
    ways = lax.axis_size("pair")
    blk_ways = lax.axis_size("blk")
    tables = rot_table.shape[0]
    slots = pair_table.shape[1]
    own = quarter * ways
    part = columns // 2 // ways
    group = own * part
    size = rounded_up(modes, 128)
    rows = quarter * modes
    full = rounded_up(rows, 8)
    pairs_of_vectors = vectors // 2

    basis_rows = in_hbm(basis.transpose(0, 2, 1, 3).reshape(pairs_of_vectors, 2 * rows, columns))
    mie_rows = in_hbm(mie_coeffs.transpose(1, 0, 2).reshape(rows // 4, 4, columns))
    rot_rows = in_hbm(rot_table.transpose(1, 0, 2).reshape(modes * tables, modes))
    axial_rows = in_hbm(axial_table.transpose(0, 2, 1, 3))
    pair_rows = in_hbm(pair_table.transpose(2, 0, 1))

    pieces_shape = (ways, 2, quarter, part, size)
    pieces = pl.pallas_call(
        functools.partial(pack_kernel, quarter, modes, ways, own),
        in_specs=[hbm(), pl.BlockSpec(memory_space=pltpu.SMEM), hbm()],
        out_specs=whole(),
        out_shape=jax.ShapeDtypeStruct(pieces_shape, BF16),
        scratch_shapes=[
            pltpu.VMEM(pair_rows.shape, jnp.int32),
            pltpu.VMEM((full, columns), F32),
            pltpu.VMEM((size, columns), F32),
            pltpu.VMEM((2 * slots, slots), F32),
            pltpu.SemaphoreType.DMA((2,)),
        ],
        compiler_params=params(16),
        name="pack",
    )(pair_rows, pair_count, basis_rows)
    pieces, basis_later = lax.optimization_barrier((pieces, basis_rows))
    own_pieces = exchanged(pieces)

    gram = pl.pallas_call(
        functools.partial(gram_kernel, quarter, modes),
        grid=(1,),
        in_specs=[hbm()],
        out_specs=pl.BlockSpec((1, 128), lambda i: (0, 0)),
        out_shape=pltpu.HBM((1, 128), F32),
        scratch_shapes=[
            pltpu.VMEM((vectors, full, columns), F32),
            pltpu.VMEM((pairs_of_vectors, 2 * rows, columns), F32),
            pltpu.VMEM((vectors, vectors, 8, columns), F32),
            pltpu.SemaphoreType.DMA((pairs_of_vectors,)),
        ],
        compiler_params=params(16),
        name="gram",
    )(basis_later)
    own_pieces, gram = lax.optimization_barrier((own_pieces, gram))
    below, above = neighbours(own_pieces)

    rotations, axials = pl.pallas_call(
        functools.partial(tables_kernel, modes, tables),
        grid=(tables,),
        in_specs=[
            pl.BlockSpec((1, modes, 2, modes), lambda g: (g, 0, 0, 0)),
            pl.BlockSpec((size, modes), lambda g: (g, 0)),
        ],
        out_specs=[
            pl.BlockSpec((tables, size // tables, size), lambda g: (0, g, 0)),
            pl.BlockSpec((1, 2 * size, size), lambda g: (g, 0, 0)),
        ],
        out_shape=[pltpu.HBM((tables, size, size), BF16), pltpu.HBM((tables, 2 * size, size), BF16)],
        scratch_shapes=[pltpu.VMEM((2 * size, size), BF16)],
        compiler_params=params(32),
        cost_estimate=pl.CostEstimate(flops=tables * 8 * 256 * 256 * size, bytes_accessed=6 * tables * size * size * 2, transcendentals=0),
        name="tables",
    )(axial_rows, rot_rows)

    below, above, rotations, axials = lax.optimization_barrier((below, above, rotations, axials))
    weights = pl.pallas_call(
        functools.partial(weights_kernel, own, part, modes),
        in_specs=[whole()] * 3,
        out_specs=whole(),
        out_shape=jax.ShapeDtypeStruct((tables, 2 * group, 3 * group), BF16),
        compiler_params=params(24),
        name="weights",
    )(below, own_pieces, above)

    entries = 2 if tables % 2 == 0 else 1
    field = pl.pallas_call(
        field_kernel,
        grid=(tables // entries,),
        in_specs=[
            pl.BlockSpec((entries, 2 * group, 3 * group), lambda g: (g, 0, 0)),
            pl.BlockSpec((entries, size, size), lambda g: (g, 0, 0)),
            pl.BlockSpec((entries, 2 * size, size), lambda g: (g, 0, 0)),
            whole(),
            whole(),
            whole(),
        ],
        out_specs=whole(),
        out_shape=jax.ShapeDtypeStruct(pieces_shape, BF16),
        scratch_shapes=[pltpu.VMEM((2, 3 * group, size), BF16), pltpu.VMEM((2 * group, size), F32)],
        compiler_params=params(24),
        name="field",
    )(weights, in_hbm(rotations), in_hbm(axials), below, own_pieces, above)
    field_pieces = exchanged(field)

    height = 4
    tall = rounded_up(rows + full, 8)
    blocks, image, sums = pl.pallas_call(
        functools.partial(image_kernel, quarter, modes),
        in_specs=[hbm(), hbm(), hbm(), whole()],
        out_specs=[whole()] * 3,
        out_shape=[
            jax.ShapeDtypeStruct((pairs_of_vectors, tall, columns), F32),
            jax.ShapeDtypeStruct((full, columns), F32),
            jax.ShapeDtypeStruct((ways * blk_ways, 1, 128), F32),
        ],
        scratch_shapes=[
            pltpu.VMEM((full, columns), F32),
            pltpu.VMEM((rows // height, height, columns), F32),
            pltpu.VMEM((1, 128), F32),
            pltpu.SemaphoreType.DMA((pairs_of_vectors + 2,)),
        ],
        compiler_params=params(16),
        name="image",
    )(basis_rows, mie_rows, gram, field_pieces)
    sums = lax.all_to_all(sums, ("blk", "pair"), split_axis=0, concat_axis=0, tiled=True)

    mean_scale = 1.0 / (own * blk_ways * modes * columns)
    dots, next_rows = pl.pallas_call(
        functools.partial(remainder_kernel, quarter, modes, mean_scale),
        in_specs=[whole()] * 3,
        out_specs=[whole(), whole()],
        out_shape=[jax.ShapeDtypeStruct((2, vectors), F32), jax.ShapeDtypeStruct((rows // height, height, columns), F32)],
        compiler_params=params(16),
        name="remainder",
    )(sums, blocks, image)
    return dots, next_rows.reshape(modes, quarter, columns).transpose(1, 0, 2)


def solution(mesh):
    placed = (
        P(None, ("blk", "pair"), None, None),
        P(("blk", "pair"), None, None),
        P(),
        P(),
        P("blk", None, None),
        P("blk"),
    )
    return jax.shard_map(
        shards,
        mesh=mesh,
        in_specs=placed,
        out_specs=(P(), P(("blk", "pair"), None, None)),
        check_vma=False,
    )
```

```python
import functools

import jax
import jax.numpy as jnp
from jax import lax
from jax.experimental import pallas as pl
from jax.experimental.pallas import tpu as pltpu
from jax.sharding import PartitionSpec as P

MIB = 1024 * 1024
F32 = jnp.float32
BF16 = jnp.bfloat16


def params(mib):
    return pltpu.CompilerParams(vmem_limit_bytes=mib * MIB)


def hbm():
    return pl.BlockSpec(memory_space=pltpu.HBM)


def whole():
    return pl.BlockSpec(memory_space=pltpu.VMEM)


def in_hbm(value):
    return pltpu.with_memory_space_constraint(value, pltpu.HBM)


def rounded_up(value, unit):
    return (value + unit - 1) // unit * unit


def iota(shape, dim):
    return lax.broadcasted_iota(jnp.int32, shape, dim)


def dot_nn(left, right):
    return lax.dot_general(left, right, (((1,), (0,)), ((), ())), preferred_element_type=F32)


def dot_nt(left, right):
    return lax.dot_general(left, right, (((1,), (1,)), ((), ())), preferred_element_type=F32)


def pack_kernel(quarter, modes, ways, own, list_ref, count_ref, basis_ref, out_ref, pair_rows_ref, lines_ref, pad_ref, codes_ref, sems):
    full, columns = lines_ref.shape
    rows = quarter * modes
    part = columns // 2 // ways
    copy = pltpu.make_async_copy(basis_ref.at[basis_ref.shape[0] - 1, pl.ds(2 * rows - full, full)], lines_ref, sems.at[0])
    copy.start()
    list_copy = pltpu.make_async_copy(list_ref, pair_rows_ref, sems.at[1])
    list_copy.start()
    pad_ref[...] = jnp.zeros_like(pad_ref)
    list_copy.wait()
    slots = pair_rows_ref.shape[2]
    live = iota((1, slots), 1) < count_ref[0]
    marks = jnp.where(live, own * (pair_rows_ref[2] + 1) + pair_rows_ref[0], 0)
    line = iota((slots, slots), 0)
    stacked = jnp.where(line == 0, marks, jnp.where(line == 1, pair_rows_ref[1], 0))
    turned = jnp.transpose(stacked.astype(F32))
    codes_ref[0:slots, :] = turned
    codes_ref[slots : 2 * slots, :] = pltpu.roll(turned, slots - 1, axis=1)
    share = 2 * quarter * part
    mine = codes_ref[pl.ds(pl.multiple_of(lax.axis_index("pair") * share, share), share), :][:, 0:1]
    copy.wait()
    for j in range(quarter):
        pad_ref[0:modes, :] = lines_ref[pl.ds(full - rows + j, modes, quarter), :]
        turned = jnp.transpose(pad_ref[...])
        for c in range(2):
            codes = mine[(c * quarter + j) * part : (c * quarter + j + 1) * part]
            for p in range(ways):
                row = c * (columns // 2) + p * part
                piece = turned[row : row + part]
                out_ref[p, c, j] = jnp.where(iota(piece.shape, 1) == modes, codes, piece).astype(BF16)


def tables_kernel(modes, tables, axial_ref, rot_ref, rot_out_ref, axial_out_ref, lines_ref):
    step = pl.program_id(0)
    size = rot_out_ref.shape[2]
    chunk = 256

    @pl.when(step == 0)
    def _():
        lines_ref[...] = jnp.zeros_like(lines_ref)

    out_row, in_row = iota((chunk, chunk), 0), iota((chunk, chunk), 1)
    each = chunk // 2
    halves = (in_row == 2 * lax.rem(out_row, each) + lax.div(out_row, each)).astype(F32).astype(BF16)
    lines_ref[0 : 2 * modes, 0:modes] = axial_ref[0].reshape(2 * modes, modes)
    for q in range(2 * size // chunk):
        sorted_rows = dot_nn(halves, lines_ref[q * chunk : (q + 1) * chunk, :]).astype(BF16)
        for c in range(2):
            axial_out_ref[0, c * size + q * each : c * size + (q + 1) * each, :] = sorted_rows[c * each : (c + 1) * each]
    each = chunk // tables
    entries = (in_row == tables * lax.rem(out_row, each) + lax.div(out_row, each)).astype(F32).astype(BF16)
    block = rot_ref.shape[0]
    left = tables * modes - step * block
    rows = jnp.where(iota((block, modes), 0) < left, rot_ref[...], jnp.zeros((), BF16))
    rot_out_ref[:, :, size - 128 : size] = jnp.zeros((tables, block // tables, 128), BF16)
    for q in range(block // chunk):
        sorted_rows = dot_nn(entries, rows[q * chunk : (q + 1) * chunk]).astype(BF16)
        for g in range(tables):
            rot_out_ref[g, q * each : (q + 1) * each, 0:modes] = sorted_rows[g * each : (g + 1) * each]


def swapped(value):
    half = value.shape[0] // 2
    return jnp.concatenate([-value[half:], value[:half]], axis=0)


def pair_counts(own, tables, lane, refs):
    group, size = refs[0].shape[0] * refs[0].shape[2] * refs[0].shape[3], refs[0].shape[4]
    wanted = iota((tables * own, group), 0) + own

    def one_hot(hit):
        return jnp.where(hit, 1.0, 0.0).astype(BF16)

    forward, backward = None, []
    for window, ref in enumerate(refs):
        values = ref[:, :, :, :, size - 128 : size].reshape(2 * group, 128).astype(F32)
        marks_column, sources_column = (values[h * group : (h + 1) * group, lane : lane + 1].astype(jnp.int32) for h in range(2))
        marks, sources = (jnp.transpose(values[h * group : (h + 1) * group])[lane : lane + 1].astype(jnp.int32) for h in range(2))
        if window == 1:
            forward = dot_nn(one_hot(marks == wanted), one_hot(sources_column == iota((group, 3 * own), 1)))
        block = sources - (2 - window) * own
        inside = (block >= 0) & (block < own) & (marks >= own)
        hits = one_hot(jnp.where(inside, lax.div(marks, own) * own + block, -1) == wanted)
        place = lax.rem(marks_column, own) + window * own
        backward.append(dot_nn(hits, one_hot(place == iota((group, 3 * own), 1))))
    return jnp.concatenate([forward, sum(backward)], axis=0).astype(BF16)


def field_kernel(own, modes, together, rot_ref, axial_ref, below_ref, own_ref, above_ref, out_ref, window_ref, sums_ref, total_ref):
    tables, _, size = rot_ref.shape
    refs = (below_ref, own_ref, above_ref)
    ways, _, quarter, part, _ = own_ref.shape
    group = own * part
    counts = pair_counts(own, tables, modes % 128, refs)
    for w, ref in enumerate(refs):
        for c in range(2):
            for t in range(size // 128):
                window_ref[w, c, t] = ref[:, c, :, :, t * 128 : (t + 1) * 128].reshape(group, 128).astype(F32)
    for c in range(2):
        for s in range(0, part, 2):
            results = []
            for sphere in (s, s + 1):
                blocks = []
                for t in range(size // 128):
                    lists = [window_ref[w, c, t, pl.ds(sphere, own, part), :] for w in range(3)]
                    blocks.append(jnp.concatenate(lists, axis=0).astype(BF16))
                results.append(dot_nn(counts, jnp.concatenate(blocks, axis=1)))
            for direction in range(2):
                for g in range(tables):
                    first = (direction * tables + g) * own
                    rows = jnp.concatenate([result[first : first + own] for result in results], axis=0)
                    place = (direction * 2 + c) * group + s * own
                    sums_ref[g, place : place + 2 * own, :] = rows.astype(BF16)
    total_ref[...] = jnp.zeros_like(total_ref)

    def body(step, carry):
        entries = [step * together + i for i in range(together)]
        turned = [dot_nt(sums_ref[g], rot_ref[g]).astype(BF16) for g in entries]
        moved = []
        for g, both in zip(entries, turned):
            forward, backward = both[: 2 * group], both[2 * group :]
            result = dot_nt(forward, axial_ref[g, :size]) + dot_nt(swapped(forward), axial_ref[g, size:])
            result += dot_nn(jnp.concatenate([backward, swapped(backward)], axis=1), axial_ref[g])
            moved.append(result.astype(BF16))
        total_ref[...] += sum(dot_nn(value, rot_ref[g]) for g, value in zip(entries, moved))
        return carry

    lax.fori_loop(0, tables // together, body, 0)
    for c in range(2):
        for t in range(size // 128):
            lanes = slice(t * 128, (t + 1) * 128)
            window_ref[0, c, t] = total_ref[c * group : (c + 1) * group, lanes]
            for p in range(ways):
                for j in range(quarter):
                    rows = window_ref[0, c, t, pl.ds(p * quarter + j, part, own), :]
                    out_ref[p, c, j, :, lanes] = rows.astype(BF16)


def lane_swap(value):
    half = value.shape[1] // 2
    rolled = pltpu.roll(value, half, axis=1)
    return jnp.where(iota(value.shape, 1) < half, -rolled, rolled)


def folded(value):
    return jnp.sum(value.reshape(value.shape[0] // 8, 8, value.shape[1]), axis=0)


def gram_kernel(quarter, modes, basis_ref, gram_ref, blocks_ref, odd_ref, sums_ref, sems):
    blocks, full, columns = odd_ref.shape
    vectors = 2 * blocks
    rows = quarter * modes
    gap = full - rows
    middle = full // 2
    cuts = ((0, middle), (rows - gap, rows + middle + gap)), ((middle, rows - gap), (rows + middle + gap, 2 * rows))
    copies = []
    for h, ranges in enumerate(cuts):
        copies.append([])
        for i in range(blocks):
            for side, (first, last) in enumerate(ranges):
                here = pl.ds(first, last - first)
                copies[h].append(pltpu.make_async_copy(basis_ref.at[i, here], blocks_ref.at[i, here], sems.at[h, i, side]))
    for copy in copies[0] + copies[1]:
        copy.start()
    sums_ref[...] = jnp.zeros_like(sums_ref)
    chunk = 32

    def body(i, carry):
        here = pl.ds(pl.multiple_of(i * chunk, chunk), chunk)
        values = [odd_ref[k // 2, here, :] if k % 2 else blocks_ref[k // 2, here, :] for k in range(vectors)]
        for l in range(vectors):
            other = lane_swap(values[l])
            for k in range(l + 1):
                sums_ref[k, l] += folded(values[k] * values[l])
                if k < l:
                    sums_ref[l, k] -= folded(values[k] * other)
        return carry

    for h, (first, last) in enumerate(((0, middle), (middle, rows))):
        for copy in copies[h]:
            copy.wait()
        for i in range(blocks):
            odd_ref[i, first:last, :] = blocks_ref[i, rows + first : rows + last, :]
            if last == rows:
                blocks_ref[i, rows:full, :] = jnp.zeros((gap, columns), F32)
                odd_ref[i, rows:full, :] = jnp.zeros((gap, columns), F32)
        lax.fori_loop(first // chunk, rounded_up(last, chunk) // chunk, body, 0)
    totals = jnp.sum(jnp.sum(sums_ref[...].reshape(vectors * vectors, 8, columns), axis=1), axis=1, keepdims=True)
    row, lane = iota((vectors, 128), 0), iota((vectors, 128), 1)
    line = jnp.zeros((1, 128), F32)
    for k in range(vectors):
        column = totals[k * vectors : (k + 1) * vectors]
        line += jnp.sum(jnp.where(row + k * vectors == lane, column, 0.0), axis=0, keepdims=True)
    gram_ref[...] = line


def stage_kernel(basis_ref, mie_ref, blocks_ref, mie_out_ref, mies_ref, sems):
    blocks, _, columns = blocks_ref.shape
    rows = basis_ref.shape[1]
    mie_rows = mies_ref.shape[0] * mies_ref.shape[1]
    copies = [pltpu.make_async_copy(basis_ref.at[i], blocks_ref.at[i, pl.ds(0, rows)], sems.at[i]) for i in range(blocks)]
    mie_copy = pltpu.make_async_copy(mie_ref, mies_ref, sems.at[blocks])
    mie_copy.start()
    for i, copy in enumerate(copies):
        copy.start()
        blocks_ref[i, rows:, :] = jnp.zeros((blocks_ref.shape[1] - rows, columns), F32)
    mie_out_ref[mie_rows:, :] = jnp.zeros((mie_out_ref.shape[0] - mie_rows, columns), F32)
    mie_copy.wait()
    mie_out_ref[0:mie_rows, :] = mies_ref[...].reshape(mie_rows, columns)
    for copy in copies:
        copy.wait()


def image_kernel(quarter, modes, blocks_ref, mie_ref, gram_ref, pieces_ref, image_ref, sums_ref, lines_ref):
    vectors = 2 * blocks_ref.shape[0]
    full, columns = image_ref.shape
    rows = quarter * modes
    ways, _, _, part, size = pieces_ref.shape
    lines_ref[rows:full, :] = jnp.zeros((full - rows, columns), F32)
    for j in range(quarter):
        turned = jnp.concatenate([pieces_ref[:, c, j].reshape(ways * part, size) for c in range(2)], axis=0)
        lines_ref[pl.ds(j, modes, quarter), :] = jnp.transpose(turned.astype(F32))[:modes]
    half = columns // 2
    chunk = 64
    totals = [jnp.zeros((8, columns), F32) for _ in range(2 * vectors + 1)]
    for first in range(0, full, chunk):
        here = slice(first, first + chunk)
        field, mie = lines_ref[here, :], mie_ref[here, :]
        left = iota(mie.shape, 1) < half
        other = pltpu.roll(mie, half, axis=1)
        product = jnp.where(left, mie, other) * field + jnp.where(left, -other, mie) * pltpu.roll(field, half, axis=1)
        last = (vectors - 1) % 2 * rows + first
        image = blocks_ref[(vectors - 1) // 2, last : last + chunk, :] - product
        image_ref[here, :] = image
        turned = lane_swap(image)
        for k in range(vectors):
            start = k % 2 * rows + first
            values = blocks_ref[k // 2, start : start + chunk, :]
            totals[2 * k] += folded(values * image)
            totals[2 * k + 1] -= folded(values * turned)
        totals[2 * vectors] += folded(image * image)
    lane = iota(gram_ref.shape, 1)
    line = gram_ref[...]
    for index, total in enumerate(totals):
        line = jnp.where(lane == vectors * vectors + index, jnp.sum(total, axis=(0, 1), keepdims=True), line)
    sums_ref[...] = jnp.broadcast_to(line[None], sums_ref.shape)


def remainder_kernel(quarter, modes, mean_scale, sums_ref, blocks_ref, image_ref, dots_ref, out_ref):
    vectors = 2 * blocks_ref.shape[0]
    full, columns = image_ref.shape
    rows = quarter * modes
    total = jnp.sum(sums_ref[...], axis=0)
    lane = iota(total.shape, 1)

    def lane_at(index):
        return jnp.sum(jnp.where(lane == index, total, 0.0), axis=1, keepdims=True)

    def on_lanes(parts, places):
        line = jnp.zeros(total.shape, F32)
        for k in range(vectors):
            line = jnp.where(places == k, parts[k], line)
        return line

    start = vectors * vectors
    real = [lane_at(start + 2 * k) * mean_scale for k in range(vectors)]
    imag = [lane_at(start + 2 * k + 1) * mean_scale for k in range(vectors)]
    real_line, imag_line = on_lanes(real, lane), on_lanes(imag, lane)
    dots_ref[0:1, :] = real_line[:, :vectors]
    dots_ref[1:2, :] = imag_line[:, :vectors]
    first_index, last_index = lax.div(lane, vectors), lax.rem(lane, vectors)
    real_first, real_last = on_lanes(real, first_index), on_lanes(real, last_index)
    imag_first, imag_last = on_lanes(imag, first_index), on_lanes(imag, last_index)
    same = real_first * real_last + imag_first * imag_last
    cross = imag_last * real_first - real_last * imag_first
    often = jnp.where(first_index == last_index, 1.0, 2.0)
    spread = jnp.where(lane < start, total * often * jnp.where(first_index <= last_index, same, cross), 0.0)
    spread = jnp.sum(spread, axis=1, keepdims=True)
    inside = jnp.sum(real_line * real_line + imag_line * imag_line, axis=1, keepdims=True)
    norm_square = (lane_at(start + 2 * vectors) + spread) * mean_scale - 2.0 * inside
    scale = lax.rsqrt(norm_square)
    image_scale = jnp.broadcast_to(scale, (8, columns))
    reals = [jnp.broadcast_to(real[k] * scale, (8, columns)) for k in range(vectors)]
    imags = [jnp.broadcast_to(imag[k] * scale, (8, columns)) for k in range(vectors)]
    chunk = 64
    for first in range(0, full, chunk):
        here = slice(first, first + chunk)
        values = []
        for k in range(vectors):
            start = k % 2 * rows + first
            values.append(blocks_ref[k // 2, start : start + chunk, :].reshape(chunk // 8, 8, columns))
        along = image_ref[here, :].reshape(chunk // 8, 8, columns) * image_scale
        turned = jnp.zeros_like(along)
        for k in range(vectors):
            along -= reals[k] * values[k]
            turned += imags[k] * values[k]
        result = along.reshape(chunk, columns) - lane_swap(turned.reshape(chunk, columns))
        count = min(chunk, rows - first)
        height = out_ref.shape[1]
        out_ref[first // height : (first + count) // height] = result.reshape(chunk // height, height, columns)[: count // height]


def exchanged(value):
    return lax.all_to_all(value, "pair", split_axis=0, concat_axis=0, tiled=True)


def neighbours(value):
    count = lax.axis_size("blk")
    up = [(i, i + 1) for i in range(count - 1)]
    down = [(j, i) for i, j in up]
    return lax.ppermute(value, "blk", up), lax.ppermute(value, "blk", down)


def shards(basis, mie_coeffs, rot_table, axial_table, pair_table, pair_count):
    vectors, quarter, modes, columns = basis.shape
    ways = lax.axis_size("pair")
    blk_ways = lax.axis_size("blk")
    tables = rot_table.shape[0]
    slots = pair_table.shape[1]
    own = quarter * ways
    part = columns // 2 // ways
    group = own * part
    size = rounded_up(modes, 128)
    rows = quarter * modes
    full = rounded_up(rows, 8)
    pairs_of_vectors = vectors // 2

    basis_rows = in_hbm(basis.transpose(0, 2, 1, 3).reshape(pairs_of_vectors, 2 * rows, columns))
    mie_rows = in_hbm(mie_coeffs.transpose(1, 0, 2).reshape(rows // 4, 4, columns))
    rot_rows = in_hbm(rot_table.transpose(1, 0, 2).reshape(modes * tables, modes))
    axial_rows = in_hbm(axial_table.transpose(0, 2, 1, 3))
    pair_rows = in_hbm(pair_table.transpose(2, 0, 1))

    pieces_shape = (ways, 2, quarter, part, size)
    pieces = pl.pallas_call(
        functools.partial(pack_kernel, quarter, modes, ways, own),
        in_specs=[hbm(), pl.BlockSpec(memory_space=pltpu.SMEM), hbm()],
        out_specs=whole(),
        out_shape=jax.ShapeDtypeStruct(pieces_shape, BF16),
        scratch_shapes=[
            pltpu.VMEM(pair_rows.shape, jnp.int32),
            pltpu.VMEM((full, columns), F32),
            pltpu.VMEM((size, columns), F32),
            pltpu.VMEM((2 * slots, slots), F32),
            pltpu.SemaphoreType.DMA((2,)),
        ],
        compiler_params=params(16),
        name="pack",
    )(pair_rows, pair_count, basis_rows)
    pieces, basis_later = lax.optimization_barrier((pieces, basis_rows))
    own_pieces = exchanged(pieces)

    gram = pl.pallas_call(
        functools.partial(gram_kernel, quarter, modes),
        grid=(1,),
        in_specs=[hbm()],
        out_specs=pl.BlockSpec((1, 128), lambda i: (0, 0)),
        out_shape=pltpu.HBM((1, 128), F32),
        scratch_shapes=[
            pltpu.VMEM((pairs_of_vectors, 2 * rows, columns), F32),
            pltpu.VMEM((pairs_of_vectors, full, columns), F32),
            pltpu.VMEM((vectors, vectors, 8, columns), F32),
            pltpu.SemaphoreType.DMA((2, pairs_of_vectors, 2)),
        ],
        compiler_params=params(16),
        name="gram",
    )(basis_later)
    own_pieces, gram, *inputs = lax.optimization_barrier((own_pieces, gram, basis_rows, mie_rows, rot_rows, axial_rows))
    basis_rows, mie_rows, rot_rows, axial_rows = inputs
    below, above = neighbours(own_pieces)

    rotations, axials = pl.pallas_call(
        functools.partial(tables_kernel, modes, tables),
        grid=(tables,),
        in_specs=[
            pl.BlockSpec((1, modes, 2, modes), lambda g: (g, 0, 0, 0)),
            pl.BlockSpec((size, modes), lambda g: (g, 0)),
        ],
        out_specs=[
            pl.BlockSpec((tables, size // tables, size), lambda g: (0, g, 0)),
            pl.BlockSpec((1, 2 * size, size), lambda g: (g, 0, 0)),
        ],
        out_shape=[
            jax.ShapeDtypeStruct((tables, size, size), BF16),
            jax.ShapeDtypeStruct((tables, 2 * size, size), BF16),
        ],
        scratch_shapes=[pltpu.VMEM((2 * size, size), BF16)],
        compiler_params=params(32),
        cost_estimate=pl.CostEstimate(flops=tables * 8 * 256 * 256 * size, bytes_accessed=6 * tables * size * size * 2, transcendentals=0),
        name="tables",
    )(axial_rows, rot_rows)

    tall = rounded_up(rows + full, 8)
    blocks, mies = pl.pallas_call(
        stage_kernel,
        in_specs=[hbm(), hbm()],
        out_specs=[whole()] * 2,
        out_shape=[
            jax.ShapeDtypeStruct((pairs_of_vectors, tall, columns), F32),
            jax.ShapeDtypeStruct((full, columns), F32),
        ],
        scratch_shapes=[pltpu.VMEM(mie_rows.shape, F32), pltpu.SemaphoreType.DMA((pairs_of_vectors + 1,))],
        compiler_params=params(8),
        name="stage",
    )(basis_rows, mie_rows)
    held = lax.optimization_barrier((below, above, rotations, axials, blocks, mies))
    below, above, rotations, axials, blocks, mies = held

    together = 2 if tables % 2 == 0 else 1
    field = pl.pallas_call(
        functools.partial(field_kernel, own, modes, together),
        in_specs=[whole()] * 5,
        out_specs=whole(),
        out_shape=jax.ShapeDtypeStruct(pieces_shape, BF16),
        scratch_shapes=[
            pltpu.VMEM((3, 2, size // 128, group, 128), F32),
            pltpu.VMEM((tables, 4 * group, size), BF16),
            pltpu.VMEM((2 * group, size), F32),
        ],
        compiler_params=params(20),
        name="field",
    )(rotations, axials, below, own_pieces, above)
    field_pieces = exchanged(field)

    image, sums = pl.pallas_call(
        functools.partial(image_kernel, quarter, modes),
        in_specs=[whole()] * 4,
        out_specs=[whole()] * 2,
        out_shape=[jax.ShapeDtypeStruct((full, columns), F32), jax.ShapeDtypeStruct((ways * blk_ways, 1, 128), F32)],
        scratch_shapes=[pltpu.VMEM((full, columns), F32)],
        compiler_params=params(8),
        name="image",
    )(blocks, mies, gram, field_pieces)
    sums = lax.all_to_all(sums, ("blk", "pair"), split_axis=0, concat_axis=0, tiled=True)

    height = 4
    mean_scale = 1.0 / (own * blk_ways * modes * columns)
    dots, next_rows = pl.pallas_call(
        functools.partial(remainder_kernel, quarter, modes, mean_scale),
        in_specs=[whole()] * 3,
        out_specs=[whole(), whole()],
        out_shape=[jax.ShapeDtypeStruct((2, vectors), F32), jax.ShapeDtypeStruct((rows // height, height, columns), F32)],
        compiler_params=params(16),
        name="remainder",
    )(sums, blocks, image)
    return dots, next_rows.reshape(modes, quarter, columns).transpose(1, 0, 2)


def solution(mesh):
    placed = (
        P(None, ("blk", "pair"), None, None),
        P(("blk", "pair"), None, None),
        P(),
        P(),
        P("blk", None, None),
        P("blk"),
    )
    return jax.shard_map(
        shards,
        mesh=mesh,
        in_specs=placed,
        out_specs=(P(), P(("blk", "pair"), None, None)),
        check_vma=False,
    )
```

```python
import functools

import jax
import jax.numpy as jnp
from jax import lax
from jax.experimental import pallas as pl
from jax.experimental.pallas import tpu as pltpu
from jax.sharding import PartitionSpec as P

MIB = 1024 * 1024
F32 = jnp.float32
BF16 = jnp.bfloat16


def params(mib):
    return pltpu.CompilerParams(vmem_limit_bytes=mib * MIB)


def hbm():
    return pl.BlockSpec(memory_space=pltpu.HBM)


def whole():
    return pl.BlockSpec(memory_space=pltpu.VMEM)


def in_hbm(value):
    return pltpu.with_memory_space_constraint(value, pltpu.HBM)


def rounded_up(value, unit):
    return (value + unit - 1) // unit * unit


def iota(shape, dim):
    return lax.broadcasted_iota(jnp.int32, shape, dim)


def dot_nn(left, right):
    return lax.dot_general(left, right, (((1,), (0,)), ((), ())), preferred_element_type=F32)


def dot_nt(left, right):
    return lax.dot_general(left, right, (((1,), (1,)), ((), ())), preferred_element_type=F32)


def pack_kernel(quarter, modes, ways, own, list_ref, count_ref, basis_ref, out_ref, pair_rows_ref, lines_ref, pad_ref, codes_ref, sems):
    full, columns = lines_ref.shape
    rows = quarter * modes
    part = columns // 2 // ways
    copy = pltpu.make_async_copy(basis_ref.at[basis_ref.shape[0] - 1, pl.ds(2 * rows - full, full)], lines_ref, sems.at[0])
    copy.start()
    list_copy = pltpu.make_async_copy(list_ref, pair_rows_ref, sems.at[1])
    list_copy.start()
    pad_ref[...] = jnp.zeros_like(pad_ref)
    list_copy.wait()
    slots = pair_rows_ref.shape[2]
    live = iota((1, slots), 1) < count_ref[0]
    marks = jnp.where(live, own * (pair_rows_ref[2] + 1) + pair_rows_ref[0], 0)
    line = iota((slots, slots), 0)
    stacked = jnp.where(line == 0, marks, jnp.where(line == 1, pair_rows_ref[1], 0))
    turned = jnp.transpose(stacked.astype(F32))
    codes_ref[0:slots, :] = turned
    codes_ref[slots : 2 * slots, :] = pltpu.roll(turned, slots - 1, axis=1)
    share = 2 * quarter * part
    mine = codes_ref[pl.ds(pl.multiple_of(lax.axis_index("pair") * share, share), share), :][:, 0:1]
    copy.wait()
    for j in range(quarter):
        pad_ref[0:modes, :] = lines_ref[pl.ds(full - rows + j, modes, quarter), :]
        turned = jnp.transpose(pad_ref[...])
        for c in range(2):
            codes = mine[(c * quarter + j) * part : (c * quarter + j + 1) * part]
            for p in range(ways):
                row = c * (columns // 2) + p * part
                piece = turned[row : row + part]
                out_ref[p, c, j] = jnp.where(iota(piece.shape, 1) == modes, codes, piece).astype(BF16)


def tables_kernel(modes, tables, axial_ref, rot_ref, rot_out_ref, axial_out_ref, lines_ref):
    step = pl.program_id(0)
    size = rot_out_ref.shape[2]
    chunk = 256

    @pl.when(step == 0)
    def _():
        lines_ref[...] = jnp.zeros_like(lines_ref)

    out_row, in_row = iota((chunk, chunk), 0), iota((chunk, chunk), 1)
    each = chunk // 2
    halves = (in_row == 2 * lax.rem(out_row, each) + lax.div(out_row, each)).astype(F32).astype(BF16)
    lines_ref[0 : 2 * modes, 0:modes] = axial_ref[0].reshape(2 * modes, modes)
    for q in range(2 * size // chunk):
        sorted_rows = dot_nn(halves, lines_ref[q * chunk : (q + 1) * chunk, :]).astype(BF16)
        for c in range(2):
            axial_out_ref[0, c * size + q * each : c * size + (q + 1) * each, :] = sorted_rows[c * each : (c + 1) * each]
    each = chunk // tables
    entries = (in_row == tables * lax.rem(out_row, each) + lax.div(out_row, each)).astype(F32).astype(BF16)
    block = rot_ref.shape[0]
    left = tables * modes - step * block
    rows = jnp.where(iota((block, modes), 0) < left, rot_ref[...], jnp.zeros((), BF16))
    rot_out_ref[:, :, size - 128 : size] = jnp.zeros((tables, block // tables, 128), BF16)
    for q in range(block // chunk):
        sorted_rows = dot_nn(entries, rows[q * chunk : (q + 1) * chunk]).astype(BF16)
        for g in range(tables):
            rot_out_ref[g, q * each : (q + 1) * each, 0:modes] = sorted_rows[g * each : (g + 1) * each]


def swapped(value):
    half = value.shape[0] // 2
    return jnp.concatenate([-value[half:], value[:half]], axis=0)


def pair_counts(own, tables, lane, refs):
    group, size = refs[0].shape[0] * refs[0].shape[2] * refs[0].shape[3], refs[0].shape[4]
    wanted = iota((tables * own, group), 0) + own

    def one_hot(hit):
        return jnp.where(hit, 1.0, 0.0).astype(BF16)

    forward, backward = None, []
    for window, ref in enumerate(refs):
        values = ref[:, :, :, :, size - 128 : size].reshape(2 * group, 128).astype(F32)
        marks_column, sources_column = (values[h * group : (h + 1) * group, lane : lane + 1].astype(jnp.int32) for h in range(2))
        marks, sources = (jnp.transpose(values[h * group : (h + 1) * group])[lane : lane + 1].astype(jnp.int32) for h in range(2))
        if window == 1:
            forward = dot_nn(one_hot(marks == wanted), one_hot(sources_column == iota((group, 3 * own), 1)))
        block = sources - (2 - window) * own
        inside = (block >= 0) & (block < own) & (marks >= own)
        hits = one_hot(jnp.where(inside, lax.div(marks, own) * own + block, -1) == wanted)
        place = lax.rem(marks_column, own) + window * own
        backward.append(dot_nn(hits, one_hot(place == iota((group, 3 * own), 1))))
    return jnp.concatenate([forward, sum(backward)], axis=0).astype(BF16)


def field_kernel(
    own, modes, together, rot_ref, axial_ref, below_ref, own_ref, above_ref, basis_ref, mie_ref,
    out_ref, blocks_ref, mies_ref, window_ref, sums_ref, total_ref, sems,
):
    tables, _, size = rot_ref.shape
    vector_blocks, rows, columns = basis_ref.shape
    copies = [pltpu.make_async_copy(mie_ref, mies_ref, sems.at[vector_blocks])]
    for i in range(vector_blocks):
        copies.append(pltpu.make_async_copy(basis_ref.at[i], blocks_ref.at[i, pl.ds(0, rows)], sems.at[i]))
    for copy in copies:
        copy.start()
    for i in range(vector_blocks):
        blocks_ref[i, rows:, :] = jnp.zeros((blocks_ref.shape[1] - rows, columns), F32)
    refs = (below_ref, own_ref, above_ref)
    ways, _, quarter, part, _ = own_ref.shape
    group = own * part
    counts = pair_counts(own, tables, modes % 128, refs)
    for w, ref in enumerate(refs):
        for c in range(2):
            for t in range(size // 128):
                window_ref[w, c, t] = ref[:, c, :, :, t * 128 : (t + 1) * 128].reshape(group, 128).astype(F32)
    for c in range(2):
        for s in range(0, part, 2):
            results = []
            for sphere in (s, s + 1):
                blocks = []
                for t in range(size // 128):
                    lists = [window_ref[w, c, t, pl.ds(sphere, own, part), :] for w in range(3)]
                    blocks.append(jnp.concatenate(lists, axis=0).astype(BF16))
                results.append(dot_nn(counts, jnp.concatenate(blocks, axis=1)))
            for direction in range(2):
                for g in range(tables):
                    first = (direction * tables + g) * own
                    rows = jnp.concatenate([result[first : first + own] for result in results], axis=0)
                    place = (direction * 2 + c) * group + s * own
                    sums_ref[g, place : place + 2 * own, :] = rows.astype(BF16)
    total_ref[...] = jnp.zeros_like(total_ref)

    def body(step, carry):
        entries = [step * together + i for i in range(together)]
        turned = [dot_nt(sums_ref[g], rot_ref[g]).astype(BF16) for g in entries]
        moved = []
        for g, both in zip(entries, turned):
            forward, backward = both[: 2 * group], both[2 * group :]
            result = dot_nt(forward, axial_ref[g, :size]) + dot_nt(swapped(forward), axial_ref[g, size:])
            result += dot_nn(jnp.concatenate([backward, swapped(backward)], axis=1), axial_ref[g])
            moved.append(result.astype(BF16))
        total_ref[...] += sum(dot_nn(value, rot_ref[g]) for g, value in zip(entries, moved))
        return carry

    lax.fori_loop(0, tables // together, body, 0)
    for c in range(2):
        for t in range(size // 128):
            lanes = slice(t * 128, (t + 1) * 128)
            window_ref[0, c, t] = total_ref[c * group : (c + 1) * group, lanes]
            for p in range(ways):
                for j in range(quarter):
                    rows = window_ref[0, c, t, pl.ds(p * quarter + j, part, own), :]
                    out_ref[p, c, j, :, lanes] = rows.astype(BF16)
    for copy in copies:
        copy.wait()


def lane_swap(value):
    half = value.shape[1] // 2
    rolled = pltpu.roll(value, half, axis=1)
    return jnp.where(iota(value.shape, 1) < half, -rolled, rolled)


def folded(value):
    return jnp.sum(value.reshape(value.shape[0] // 8, 8, value.shape[1]), axis=0)


def gram_kernel(quarter, modes, basis_ref, gram_ref, blocks_ref, odd_ref, sums_ref, sems):
    blocks, full, columns = odd_ref.shape
    vectors = 2 * blocks
    rows = quarter * modes
    gap = full - rows
    middle = full // 2
    cuts = ((0, middle), (rows - gap, rows + middle + gap)), ((middle, rows - gap), (rows + middle + gap, 2 * rows))
    copies = []
    for h, ranges in enumerate(cuts):
        copies.append([])
        for i in range(blocks):
            for side, (first, last) in enumerate(ranges):
                here = pl.ds(first, last - first)
                copies[h].append(pltpu.make_async_copy(basis_ref.at[i, here], blocks_ref.at[i, here], sems.at[h, i, side]))
    for copy in copies[0] + copies[1]:
        copy.start()
    sums_ref[...] = jnp.zeros_like(sums_ref)
    chunk = 32

    def body(i, carry):
        here = pl.ds(pl.multiple_of(i * chunk, chunk), chunk)
        values = [odd_ref[k // 2, here, :] if k % 2 else blocks_ref[k // 2, here, :] for k in range(vectors)]
        for l in range(vectors):
            other = lane_swap(values[l])
            for k in range(l + 1):
                sums_ref[k, l] += folded(values[k] * values[l])
                if k < l:
                    sums_ref[l, k] -= folded(values[k] * other)
        return carry

    for h, (first, last) in enumerate(((0, middle), (middle, rows))):
        for copy in copies[h]:
            copy.wait()
        for i in range(blocks):
            odd_ref[i, first:last, :] = blocks_ref[i, rows + first : rows + last, :]
            if last == rows:
                blocks_ref[i, rows:full, :] = jnp.zeros((gap, columns), F32)
                odd_ref[i, rows:full, :] = jnp.zeros((gap, columns), F32)
        lax.fori_loop(first // chunk, rounded_up(last, chunk) // chunk, body, 0)
    totals = jnp.sum(jnp.sum(sums_ref[...].reshape(vectors * vectors, 8, columns), axis=1), axis=1, keepdims=True)
    row, lane = iota((vectors, 128), 0), iota((vectors, 128), 1)
    line = jnp.zeros((1, 128), F32)
    for k in range(vectors):
        column = totals[k * vectors : (k + 1) * vectors]
        line += jnp.sum(jnp.where(row + k * vectors == lane, column, 0.0), axis=0, keepdims=True)
    gram_ref[...] = line


def image_kernel(quarter, modes, blocks_ref, mie_ref, gram_ref, pieces_ref, image_ref, sums_ref, lines_ref):
    vectors = 2 * blocks_ref.shape[0]
    full, columns = image_ref.shape
    rows = quarter * modes
    ways, _, _, part, size = pieces_ref.shape
    lines_ref[rows:full, :] = jnp.zeros((full - rows, columns), F32)
    for j in range(quarter):
        turned = jnp.concatenate([pieces_ref[:, c, j].reshape(ways * part, size) for c in range(2)], axis=0)
        lines_ref[pl.ds(j, modes, quarter), :] = jnp.transpose(turned.astype(F32))[:modes]
    half = columns // 2
    chunk = 64
    totals = [jnp.zeros((8, columns), F32) for _ in range(2 * vectors + 1)]
    for first in range(0, full, chunk):
        here = slice(first, first + chunk)
        field = lines_ref[here, :]
        count = min(chunk, rows - first)
        height = mie_ref.shape[1]
        mie = mie_ref[first // height : (first + count) // height].reshape(count, columns)
        if count < chunk:
            mie = jnp.concatenate([mie, jnp.zeros((chunk - count, columns), F32)], axis=0)
        left = iota(mie.shape, 1) < half
        other = pltpu.roll(mie, half, axis=1)
        product = jnp.where(left, mie, other) * field + jnp.where(left, -other, mie) * pltpu.roll(field, half, axis=1)
        last = (vectors - 1) % 2 * rows + first
        image = blocks_ref[(vectors - 1) // 2, last : last + chunk, :] - product
        image_ref[here, :] = image
        turned = lane_swap(image)
        for k in range(vectors):
            start = k % 2 * rows + first
            values = blocks_ref[k // 2, start : start + chunk, :]
            totals[2 * k] += folded(values * image)
            totals[2 * k + 1] -= folded(values * turned)
        totals[2 * vectors] += folded(image * image)
    lane = iota(gram_ref.shape, 1)
    line = gram_ref[...]
    for index, total in enumerate(totals):
        line = jnp.where(lane == vectors * vectors + index, jnp.sum(total, axis=(0, 1), keepdims=True), line)
    sums_ref[...] = jnp.broadcast_to(line[None], sums_ref.shape)


def remainder_kernel(quarter, modes, mean_scale, sums_ref, blocks_ref, image_ref, dots_ref, out_ref):
    vectors = 2 * blocks_ref.shape[0]
    full, columns = image_ref.shape
    rows = quarter * modes
    total = jnp.sum(sums_ref[...], axis=0)
    lane = iota(total.shape, 1)

    def lane_at(index):
        return jnp.sum(jnp.where(lane == index, total, 0.0), axis=1, keepdims=True)

    def on_lanes(parts, places):
        line = jnp.zeros(total.shape, F32)
        for k in range(vectors):
            line = jnp.where(places == k, parts[k], line)
        return line

    start = vectors * vectors
    real = [lane_at(start + 2 * k) * mean_scale for k in range(vectors)]
    imag = [lane_at(start + 2 * k + 1) * mean_scale for k in range(vectors)]
    real_line, imag_line = on_lanes(real, lane), on_lanes(imag, lane)
    dots_ref[0:1, :] = real_line[:, :vectors]
    dots_ref[1:2, :] = imag_line[:, :vectors]
    first_index, last_index = lax.div(lane, vectors), lax.rem(lane, vectors)
    real_first, real_last = on_lanes(real, first_index), on_lanes(real, last_index)
    imag_first, imag_last = on_lanes(imag, first_index), on_lanes(imag, last_index)
    same = real_first * real_last + imag_first * imag_last
    cross = imag_last * real_first - real_last * imag_first
    often = jnp.where(first_index == last_index, 1.0, 2.0)
    spread = jnp.where(lane < start, total * often * jnp.where(first_index <= last_index, same, cross), 0.0)
    spread = jnp.sum(spread, axis=1, keepdims=True)
    inside = jnp.sum(real_line * real_line + imag_line * imag_line, axis=1, keepdims=True)
    norm_square = (lane_at(start + 2 * vectors) + spread) * mean_scale - 2.0 * inside
    scale = lax.rsqrt(norm_square)
    image_scale = jnp.broadcast_to(scale, (8, columns))
    reals = [jnp.broadcast_to(real[k] * scale, (8, columns)) for k in range(vectors)]
    imags = [jnp.broadcast_to(imag[k] * scale, (8, columns)) for k in range(vectors)]
    chunk = 64
    for first in range(0, full, chunk):
        here = slice(first, first + chunk)
        values = []
        for k in range(vectors):
            start = k % 2 * rows + first
            values.append(blocks_ref[k // 2, start : start + chunk, :].reshape(chunk // 8, 8, columns))
        along = image_ref[here, :].reshape(chunk // 8, 8, columns) * image_scale
        turned = jnp.zeros_like(along)
        for k in range(vectors):
            along -= reals[k] * values[k]
            turned += imags[k] * values[k]
        result = along.reshape(chunk, columns) - lane_swap(turned.reshape(chunk, columns))
        count = min(chunk, rows - first)
        height = out_ref.shape[1]
        out_ref[first // height : (first + count) // height] = result.reshape(chunk // height, height, columns)[: count // height]


def exchanged(value):
    return lax.all_to_all(value, "pair", split_axis=0, concat_axis=0, tiled=True)


def neighbours(value):
    count = lax.axis_size("blk")
    up = [(i, i + 1) for i in range(count - 1)]
    down = [(j, i) for i, j in up]
    return lax.ppermute(value, "blk", up), lax.ppermute(value, "blk", down)


def shards(basis, mie_coeffs, rot_table, axial_table, pair_table, pair_count):
    vectors, quarter, modes, columns = basis.shape
    ways = lax.axis_size("pair")
    blk_ways = lax.axis_size("blk")
    tables = rot_table.shape[0]
    slots = pair_table.shape[1]
    own = quarter * ways
    part = columns // 2 // ways
    group = own * part
    size = rounded_up(modes, 128)
    rows = quarter * modes
    full = rounded_up(rows, 8)
    pairs_of_vectors = vectors // 2

    basis_rows = in_hbm(basis.transpose(0, 2, 1, 3).reshape(pairs_of_vectors, 2 * rows, columns))
    mie_rows = in_hbm(mie_coeffs.transpose(1, 0, 2).reshape(rows // 4, 4, columns))
    rot_rows = in_hbm(rot_table.transpose(1, 0, 2).reshape(modes * tables, modes))
    axial_rows = in_hbm(axial_table.transpose(0, 2, 1, 3))
    pair_rows = in_hbm(pair_table.transpose(2, 0, 1))

    pieces_shape = (ways, 2, quarter, part, size)
    pieces = pl.pallas_call(
        functools.partial(pack_kernel, quarter, modes, ways, own),
        in_specs=[hbm(), pl.BlockSpec(memory_space=pltpu.SMEM), hbm()],
        out_specs=whole(),
        out_shape=jax.ShapeDtypeStruct(pieces_shape, BF16),
        scratch_shapes=[
            pltpu.VMEM(pair_rows.shape, jnp.int32),
            pltpu.VMEM((full, columns), F32),
            pltpu.VMEM((size, columns), F32),
            pltpu.VMEM((2 * slots, slots), F32),
            pltpu.SemaphoreType.DMA((2,)),
        ],
        compiler_params=params(16),
        name="pack",
    )(pair_rows, pair_count, basis_rows)
    pieces, basis_later = lax.optimization_barrier((pieces, basis_rows))
    own_pieces = exchanged(pieces)

    gram = pl.pallas_call(
        functools.partial(gram_kernel, quarter, modes),
        grid=(1,),
        in_specs=[hbm()],
        out_specs=pl.BlockSpec((1, 128), lambda i: (0, 0)),
        out_shape=pltpu.HBM((1, 128), F32),
        scratch_shapes=[
            pltpu.VMEM((pairs_of_vectors, 2 * rows, columns), F32),
            pltpu.VMEM((pairs_of_vectors, full, columns), F32),
            pltpu.VMEM((vectors, vectors, 8, columns), F32),
            pltpu.SemaphoreType.DMA((2, pairs_of_vectors, 2)),
        ],
        compiler_params=params(16),
        name="gram",
    )(basis_later)
    own_pieces, gram, *inputs = lax.optimization_barrier((own_pieces, gram, basis_rows, mie_rows, rot_rows, axial_rows))
    basis_rows, mie_rows, rot_rows, axial_rows = inputs
    below, above = neighbours(own_pieces)

    rotations, axials = pl.pallas_call(
        functools.partial(tables_kernel, modes, tables),
        grid=(tables,),
        in_specs=[
            pl.BlockSpec((1, modes, 2, modes), lambda g: (g, 0, 0, 0)),
            pl.BlockSpec((size, modes), lambda g: (g, 0)),
        ],
        out_specs=[
            pl.BlockSpec((tables, size // tables, size), lambda g: (0, g, 0)),
            pl.BlockSpec((1, 2 * size, size), lambda g: (g, 0, 0)),
        ],
        out_shape=[
            jax.ShapeDtypeStruct((tables, size, size), BF16),
            jax.ShapeDtypeStruct((tables, 2 * size, size), BF16),
        ],
        scratch_shapes=[pltpu.VMEM((2 * size, size), BF16)],
        compiler_params=params(32),
        cost_estimate=pl.CostEstimate(flops=tables * 8 * 256 * 256 * size, bytes_accessed=6 * tables * size * size * 2, transcendentals=0),
        name="tables",
    )(axial_rows, rot_rows)

    tall = rounded_up(rows + full, 8)
    below, above, rotations, axials = lax.optimization_barrier((below, above, rotations, axials))

    together = 2 if tables % 2 == 0 else 1
    field, blocks, mies = pl.pallas_call(
        functools.partial(field_kernel, own, modes, together),
        in_specs=[whole()] * 5 + [hbm()] * 2,
        out_specs=[whole()] * 3,
        out_shape=[
            jax.ShapeDtypeStruct(pieces_shape, BF16),
            jax.ShapeDtypeStruct((pairs_of_vectors, tall, columns), F32),
            jax.ShapeDtypeStruct(mie_rows.shape, F32),
        ],
        scratch_shapes=[
            pltpu.VMEM((3, 2, size // 128, group, 128), F32),
            pltpu.VMEM((tables, 4 * group, size), BF16),
            pltpu.VMEM((2 * group, size), F32),
            pltpu.SemaphoreType.DMA((pairs_of_vectors + 1,)),
        ],
        compiler_params=params(20),
        name="field",
    )(rotations, axials, below, own_pieces, above, basis_rows, mie_rows)
    field_pieces = exchanged(field)

    image, sums = pl.pallas_call(
        functools.partial(image_kernel, quarter, modes),
        in_specs=[whole()] * 4,
        out_specs=[whole()] * 2,
        out_shape=[jax.ShapeDtypeStruct((full, columns), F32), jax.ShapeDtypeStruct((ways * blk_ways, 1, 128), F32)],
        scratch_shapes=[pltpu.VMEM((full, columns), F32)],
        compiler_params=params(8),
        name="image",
    )(blocks, mies, gram, field_pieces)
    sums = lax.all_to_all(sums, ("blk", "pair"), split_axis=0, concat_axis=0, tiled=True)

    height = 4
    mean_scale = 1.0 / (own * blk_ways * modes * columns)
    dots, next_rows = pl.pallas_call(
        functools.partial(remainder_kernel, quarter, modes, mean_scale),
        in_specs=[whole()] * 3,
        out_specs=[whole(), whole()],
        out_shape=[jax.ShapeDtypeStruct((2, vectors), F32), jax.ShapeDtypeStruct((rows // height, height, columns), F32)],
        compiler_params=params(16),
        name="remainder",
    )(sums, blocks, image)
    return dots, next_rows.reshape(modes, quarter, columns).transpose(1, 0, 2)


def solution(mesh):
    placed = (
        P(None, ("blk", "pair"), None, None),
        P(("blk", "pair"), None, None),
        P(),
        P(),
        P("blk", None, None),
        P("blk"),
    )
    return jax.shard_map(
        shards,
        mesh=mesh,
        in_specs=placed,
        out_specs=(P(), P(("blk", "pair"), None, None)),
        check_vma=False,
    )
```

```python
import functools

import jax
import jax.numpy as jnp
from jax import lax
from jax.experimental import pallas as pl
from jax.experimental.pallas import tpu as pltpu
from jax.sharding import PartitionSpec as P

MIB = 1024 * 1024
F32 = jnp.float32
BF16 = jnp.bfloat16


def params(mib):
    return pltpu.CompilerParams(vmem_limit_bytes=mib * MIB)


def hbm():
    return pl.BlockSpec(memory_space=pltpu.HBM)


def whole():
    return pl.BlockSpec(memory_space=pltpu.VMEM)


def in_hbm(value):
    return pltpu.with_memory_space_constraint(value, pltpu.HBM)


def rounded_up(value, unit):
    return (value + unit - 1) // unit * unit


def iota(shape, dim):
    return lax.broadcasted_iota(jnp.int32, shape, dim)


def dot_nn(left, right):
    return lax.dot_general(left, right, (((1,), (0,)), ((), ())), preferred_element_type=F32)


def dot_nt(left, right):
    return lax.dot_general(left, right, (((1,), (1,)), ((), ())), preferred_element_type=F32)


def pack_kernel(quarter, modes, ways, own, list_ref, count_ref, basis_ref, out_ref, pair_rows_ref, lines_ref, pad_ref, codes_ref, sems):
    full, columns = lines_ref.shape
    rows = quarter * modes
    part = columns // 2 // ways
    copy = pltpu.make_async_copy(basis_ref.at[basis_ref.shape[0] - 1, pl.ds(2 * rows - full, full)], lines_ref, sems.at[0])
    copy.start()
    list_copy = pltpu.make_async_copy(list_ref, pair_rows_ref, sems.at[1])
    list_copy.start()
    pad_ref[...] = jnp.zeros_like(pad_ref)
    list_copy.wait()
    slots = pair_rows_ref.shape[2]
    live = iota((1, slots), 1) < count_ref[0]
    marks = jnp.where(live, own * (pair_rows_ref[2] + 1) + pair_rows_ref[0], 0)
    line = iota((slots, slots), 0)
    stacked = jnp.where(line == 0, marks, jnp.where(line == 1, pair_rows_ref[1], 0))
    turned = jnp.transpose(stacked.astype(F32))
    codes_ref[0:slots, :] = turned
    codes_ref[slots : 2 * slots, :] = pltpu.roll(turned, slots - 1, axis=1)
    share = 2 * quarter * part
    mine = codes_ref[pl.ds(pl.multiple_of(lax.axis_index("pair") * share, share), share), :][:, 0:1]
    copy.wait()
    for j in range(quarter):
        pad_ref[0:modes, :] = lines_ref[pl.ds(full - rows + j, modes, quarter), :]
        turned = jnp.transpose(pad_ref[...])
        for c in range(2):
            codes = mine[(c * quarter + j) * part : (c * quarter + j + 1) * part]
            for p in range(ways):
                row = c * (columns // 2) + p * part
                piece = turned[row : row + part]
                out_ref[p, c, j] = jnp.where(iota(piece.shape, 1) == modes, codes, piece).astype(BF16)


def tables_kernel(modes, tables, axial_ref, rot_ref, rot_out_ref, axial_out_ref, lines_ref):
    step = pl.program_id(0)
    size = rot_out_ref.shape[2]
    chunk = 256

    @pl.when(step == 0)
    def _():
        lines_ref[...] = jnp.zeros_like(lines_ref)

    out_row, in_row = iota((chunk, chunk), 0), iota((chunk, chunk), 1)
    each = chunk // 2
    halves = (in_row == 2 * lax.rem(out_row, each) + lax.div(out_row, each)).astype(F32).astype(BF16)
    lines_ref[0 : 2 * modes, 0:modes] = axial_ref[0].reshape(2 * modes, modes)
    for q in range(2 * size // chunk):
        sorted_rows = dot_nn(halves, lines_ref[q * chunk : (q + 1) * chunk, :]).astype(BF16)
        for c in range(2):
            axial_out_ref[0, c * size + q * each : c * size + (q + 1) * each, :] = sorted_rows[c * each : (c + 1) * each]
    each = chunk // tables
    entries = (in_row == tables * lax.rem(out_row, each) + lax.div(out_row, each)).astype(F32).astype(BF16)
    block = rot_ref.shape[0]
    left = tables * modes - step * block
    rows = jnp.where(iota((block, modes), 0) < left, rot_ref[...], jnp.zeros((), BF16))
    rot_out_ref[:, :, size - 128 : size] = jnp.zeros((tables, block // tables, 128), BF16)
    for q in range(block // chunk):
        sorted_rows = dot_nn(entries, rows[q * chunk : (q + 1) * chunk]).astype(BF16)
        for g in range(tables):
            rot_out_ref[g, q * each : (q + 1) * each, 0:modes] = sorted_rows[g * each : (g + 1) * each]


def swapped(value):
    half = value.shape[0] // 2
    return jnp.concatenate([-value[half:], value[:half]], axis=0)


def pair_counts(own, tables, lane, refs):
    group, size = refs[0].shape[0] * refs[0].shape[2] * refs[0].shape[3], refs[0].shape[4]
    wanted = iota((tables * own, group), 0) + own

    def one_hot(hit):
        return jnp.where(hit, 1.0, 0.0).astype(BF16)

    forward, backward = None, []
    for window, ref in enumerate(refs):
        values = ref[:, :, :, :, size - 128 : size].reshape(2 * group, 128).astype(F32)
        marks_column, sources_column = (values[h * group : (h + 1) * group, lane : lane + 1].astype(jnp.int32) for h in range(2))
        marks, sources = (jnp.transpose(values[h * group : (h + 1) * group])[lane : lane + 1].astype(jnp.int32) for h in range(2))
        if window == 1:
            forward = dot_nn(one_hot(marks == wanted), one_hot(sources_column == iota((group, 3 * own), 1)))
        block = sources - (2 - window) * own
        inside = (block >= 0) & (block < own) & (marks >= own)
        hits = one_hot(jnp.where(inside, lax.div(marks, own) * own + block, -1) == wanted)
        place = lax.rem(marks_column, own) + window * own
        backward.append(dot_nn(hits, one_hot(place == iota((group, 3 * own), 1))))
    return jnp.concatenate([forward, sum(backward)], axis=0).astype(BF16)


def folded(value):
    return jnp.sum(value.reshape(value.shape[0] // 8, 8, value.shape[1]), axis=0)


def add_products(blocks_ref, products_ref, rows, first, count):
    vectors = products_ref.shape[0]
    values = []
    for k in range(vectors):
        start = k % 2 * rows + first
        value = blocks_ref[k // 2, start : start + count, :]
        if k % 2 == 0 and first + count > rows:
            value = jnp.where(iota(value.shape, 0) < rows - first, value, 0.0)
        values.append(value)
    for l in range(vectors):
        other = pltpu.roll(values[l], values[l].shape[1] // 2, axis=1)
        for k in range(l + 1):
            products_ref[k, l] += folded(values[k] * values[l])
            if k < l:
                products_ref[l, k] += folded(values[k] * other)


def products_line(products_ref):
    vectors, _, _, columns = products_ref.shape
    pairs = vectors * vectors
    totals = jnp.sum(products_ref[...].reshape(pairs, 8, columns), axis=1)
    pair = iota(totals.shape, 0)
    signed = (lax.div(pair, vectors) > lax.rem(pair, vectors)) & (iota(totals.shape, 1) >= columns // 2)
    totals = jnp.sum(jnp.where(signed, -totals, totals), axis=1, keepdims=True)
    row, lane = iota((vectors, 128), 0), iota((vectors, 128), 1)
    line = jnp.zeros((1, 128), F32)
    for k in range(vectors):
        column = totals[k * vectors : (k + 1) * vectors]
        line += jnp.sum(jnp.where(row + k * vectors == lane, column, 0.0), axis=0, keepdims=True)
    return line


def field_kernel(
    own, quarter, modes, rot_ref, axial_ref, below_ref, own_ref, above_ref, basis_ref, mie_ref,
    out_ref, blocks_ref, mies_ref, line_ref, window_ref, sums_ref, total_ref, products_ref, sems,
):
    tables, _, size = rot_ref.shape
    vector_blocks, rows, columns = basis_ref.shape
    copies = [pltpu.make_async_copy(mie_ref, mies_ref, sems.at[vector_blocks])]
    for i in range(vector_blocks):
        copies.append(pltpu.make_async_copy(basis_ref.at[i], blocks_ref.at[i, pl.ds(0, rows)], sems.at[i]))
    for copy in copies:
        copy.start()
    for i in range(vector_blocks):
        blocks_ref[i, rows:, :] = jnp.zeros((blocks_ref.shape[1] - rows, columns), F32)
    refs = (below_ref, own_ref, above_ref)
    ways, part = own_ref.shape[0], own_ref.shape[3]
    group = own * part
    counts = pair_counts(own, tables, modes % 128, refs)
    for w, ref in enumerate(refs):
        for c in range(2):
            for t in range(size // 128):
                window_ref[w, c, t] = ref[:, c, :, :, t * 128 : (t + 1) * 128].reshape(group, 128).astype(F32)
    for c in range(2):
        for s in range(0, part, 2):
            results = []
            for sphere in (s, s + 1):
                blocks = []
                for t in range(size // 128):
                    lists = [window_ref[w, c, t, pl.ds(sphere, own, part), :] for w in range(3)]
                    blocks.append(jnp.concatenate(lists, axis=0).astype(BF16))
                results.append(dot_nn(counts, jnp.concatenate(blocks, axis=1)))
            for direction in range(2):
                for g in range(tables):
                    first = (direction * tables + g) * own
                    rows = jnp.concatenate([result[first : first + own] for result in results], axis=0)
                    place = (direction * 2 + c) * group + s * own
                    sums_ref[g, place : place + 2 * own, :] = rows.astype(BF16)
    products_ref[...] = jnp.zeros_like(products_ref)
    for copy in copies:
        copy.wait()
    chunk = 32
    chunks = [first * chunk for first in range(rounded_up(quarter * modes, chunk) // chunk)]
    each = (len(chunks) + tables - 1) // tables
    for g in range(tables):
        turned = dot_nt(sums_ref[g], rot_ref[g]).astype(BF16)
        forward, backward = turned[: 2 * group], turned[2 * group :]
        moved = dot_nt(forward, axial_ref[g, :size]) + dot_nt(swapped(forward), axial_ref[g, size:])
        moved += dot_nn(jnp.concatenate([backward, swapped(backward)], axis=1), axial_ref[g])
        back = dot_nn(moved.astype(BF16), rot_ref[g])
        total_ref[...] = back if g == 0 else total_ref[...] + back
        for first in chunks[g * each : (g + 1) * each]:
            add_products(blocks_ref, products_ref, quarter * modes, first, chunk)
    line_ref[...] = products_line(products_ref)
    for c in range(2):
        for t in range(size // 128):
            lanes = slice(t * 128, (t + 1) * 128)
            window_ref[0, c, t] = total_ref[c * group : (c + 1) * group, lanes]
            for p in range(ways):
                for j in range(quarter):
                    rows = window_ref[0, c, t, pl.ds(p * quarter + j, part, own), :]
                    out_ref[p, c, j, :, lanes] = rows.astype(BF16)


def lane_swap(value):
    half = value.shape[1] // 2
    rolled = pltpu.roll(value, half, axis=1)
    return jnp.where(iota(value.shape, 1) < half, -rolled, rolled)


def image_kernel(quarter, modes, blocks_ref, mie_ref, gram_ref, pieces_ref, image_ref, sums_ref, lines_ref):
    vectors = 2 * blocks_ref.shape[0]
    full, columns = image_ref.shape
    rows = quarter * modes
    ways, _, _, part, size = pieces_ref.shape
    lines_ref[rows:full, :] = jnp.zeros((full - rows, columns), F32)
    for j in range(quarter):
        turned = jnp.concatenate([pieces_ref[:, c, j].reshape(ways * part, size) for c in range(2)], axis=0)
        lines_ref[pl.ds(j, modes, quarter), :] = jnp.transpose(turned.astype(F32))[:modes]
    half = columns // 2
    chunk = 64
    totals = [jnp.zeros((8, columns), F32) for _ in range(2 * vectors + 1)]
    for first in range(0, full, chunk):
        here = slice(first, first + chunk)
        field = lines_ref[here, :]
        count = min(chunk, rows - first)
        height = mie_ref.shape[1]
        mie = mie_ref[first // height : (first + count) // height].reshape(count, columns)
        if count < chunk:
            mie = jnp.concatenate([mie, jnp.zeros((chunk - count, columns), F32)], axis=0)
        left = iota(mie.shape, 1) < half
        other = pltpu.roll(mie, half, axis=1)
        product = jnp.where(left, mie, other) * field + jnp.where(left, -other, mie) * pltpu.roll(field, half, axis=1)
        last = (vectors - 1) % 2 * rows + first
        image = blocks_ref[(vectors - 1) // 2, last : last + chunk, :] - product
        image_ref[here, :] = image
        turned = pltpu.roll(image, half, axis=1)
        for k in range(vectors):
            start = k % 2 * rows + first
            values = blocks_ref[k // 2, start : start + chunk, :]
            totals[2 * k] += folded(values * image)
            totals[2 * k + 1] += folded(values * turned)
        totals[2 * vectors] += folded(image * image)
    lane = iota(gram_ref.shape, 1)
    line = gram_ref[...]
    left = iota((8, columns), 1) < half
    for index, total in enumerate(totals):
        if index % 2 and index < 2 * vectors:
            total = jnp.where(left, total, -total)
        line = jnp.where(lane == vectors * vectors + index, jnp.sum(total, axis=(0, 1), keepdims=True), line)
    sums_ref[...] = jnp.broadcast_to(line[None], sums_ref.shape)


def remainder_kernel(quarter, modes, mean_scale, sums_ref, blocks_ref, image_ref, dots_ref, out_ref):
    vectors = 2 * blocks_ref.shape[0]
    full, columns = image_ref.shape
    rows = quarter * modes
    total = jnp.sum(sums_ref[...], axis=0)
    lane = iota(total.shape, 1)

    def lane_at(index):
        return jnp.sum(jnp.where(lane == index, total, 0.0), axis=1, keepdims=True)

    def on_lanes(parts, places):
        line = jnp.zeros(total.shape, F32)
        for k in range(vectors):
            line = jnp.where(places == k, parts[k], line)
        return line

    start = vectors * vectors
    real = [lane_at(start + 2 * k) * mean_scale for k in range(vectors)]
    imag = [lane_at(start + 2 * k + 1) * mean_scale for k in range(vectors)]
    real_line, imag_line = on_lanes(real, lane), on_lanes(imag, lane)
    dots_ref[0:1, :] = real_line[:, :vectors]
    dots_ref[1:2, :] = imag_line[:, :vectors]
    first_index, last_index = lax.div(lane, vectors), lax.rem(lane, vectors)
    real_first, real_last = on_lanes(real, first_index), on_lanes(real, last_index)
    imag_first, imag_last = on_lanes(imag, first_index), on_lanes(imag, last_index)
    same = real_first * real_last + imag_first * imag_last
    cross = imag_last * real_first - real_last * imag_first
    often = jnp.where(first_index == last_index, 1.0, 2.0)
    spread = jnp.where(lane < start, total * often * jnp.where(first_index <= last_index, same, cross), 0.0)
    spread = jnp.sum(spread, axis=1, keepdims=True)
    inside = jnp.sum(real_line * real_line + imag_line * imag_line, axis=1, keepdims=True)
    norm_square = (lane_at(start + 2 * vectors) + spread) * mean_scale - 2.0 * inside
    scale = lax.rsqrt(norm_square)
    image_scale = jnp.broadcast_to(scale, (8, columns))
    reals = [jnp.broadcast_to(real[k] * scale, (8, columns)) for k in range(vectors)]
    imags = [jnp.broadcast_to(imag[k] * scale, (8, columns)) for k in range(vectors)]
    chunk = 64
    for first in range(0, full, chunk):
        here = slice(first, first + chunk)
        values = []
        for k in range(vectors):
            start = k % 2 * rows + first
            values.append(blocks_ref[k // 2, start : start + chunk, :].reshape(chunk // 8, 8, columns))
        along = image_ref[here, :].reshape(chunk // 8, 8, columns) * image_scale
        turned = jnp.zeros_like(along)
        for k in range(vectors):
            along -= reals[k] * values[k]
            turned += imags[k] * values[k]
        result = along.reshape(chunk, columns) - lane_swap(turned.reshape(chunk, columns))
        count = min(chunk, rows - first)
        height = out_ref.shape[1]
        out_ref[first // height : (first + count) // height] = result.reshape(chunk // height, height, columns)[: count // height]


def exchanged(value):
    return lax.all_to_all(value, "pair", split_axis=0, concat_axis=0, tiled=True)


def neighbours(value):
    count = lax.axis_size("blk")
    up = [(i, i + 1) for i in range(count - 1)]
    down = [(j, i) for i, j in up]
    return lax.ppermute(value, "blk", up), lax.ppermute(value, "blk", down)


def shards(basis, mie_coeffs, rot_table, axial_table, pair_table, pair_count):
    vectors, quarter, modes, columns = basis.shape
    ways = lax.axis_size("pair")
    blk_ways = lax.axis_size("blk")
    tables = rot_table.shape[0]
    slots = pair_table.shape[1]
    own = quarter * ways
    part = columns // 2 // ways
    group = own * part
    size = rounded_up(modes, 128)
    rows = quarter * modes
    full = rounded_up(rows, 8)
    pairs_of_vectors = vectors // 2

    basis_rows = in_hbm(basis.transpose(0, 2, 1, 3).reshape(pairs_of_vectors, 2 * rows, columns))
    mie_rows = in_hbm(mie_coeffs.transpose(1, 0, 2).reshape(rows // 4, 4, columns))
    rot_rows = in_hbm(rot_table.transpose(1, 0, 2).reshape(modes * tables, modes))
    axial_rows = in_hbm(axial_table.transpose(0, 2, 1, 3))
    pair_rows = in_hbm(pair_table.transpose(2, 0, 1))

    pieces_shape = (ways, 2, quarter, part, size)
    pieces = pl.pallas_call(
        functools.partial(pack_kernel, quarter, modes, ways, own),
        in_specs=[hbm(), pl.BlockSpec(memory_space=pltpu.SMEM), hbm()],
        out_specs=whole(),
        out_shape=jax.ShapeDtypeStruct(pieces_shape, BF16),
        scratch_shapes=[
            pltpu.VMEM(pair_rows.shape, jnp.int32),
            pltpu.VMEM((full, columns), F32),
            pltpu.VMEM((size, columns), F32),
            pltpu.VMEM((2 * slots, slots), F32),
            pltpu.SemaphoreType.DMA((2,)),
        ],
        compiler_params=params(16),
        name="pack",
    )(pair_rows, pair_count, basis_rows)
    own_pieces = exchanged(pieces)
    own_pieces, basis_rows, mie_rows, rot_rows, axial_rows = lax.optimization_barrier(
        (own_pieces, basis_rows, mie_rows, rot_rows, axial_rows)
    )
    below, above = neighbours(own_pieces)

    rotations, axials = pl.pallas_call(
        functools.partial(tables_kernel, modes, tables),
        grid=(tables,),
        in_specs=[
            pl.BlockSpec((1, modes, 2, modes), lambda g: (g, 0, 0, 0)),
            pl.BlockSpec((size, modes), lambda g: (g, 0)),
        ],
        out_specs=[
            pl.BlockSpec((tables, size // tables, size), lambda g: (0, g, 0)),
            pl.BlockSpec((1, 2 * size, size), lambda g: (g, 0, 0)),
        ],
        out_shape=[
            jax.ShapeDtypeStruct((tables, size, size), BF16),
            jax.ShapeDtypeStruct((tables, 2 * size, size), BF16),
        ],
        scratch_shapes=[pltpu.VMEM((2 * size, size), BF16)],
        compiler_params=params(32),
        cost_estimate=pl.CostEstimate(flops=tables * 8 * 256 * 256 * size, bytes_accessed=6 * tables * size * size * 2, transcendentals=0),
        name="tables",
    )(axial_rows, rot_rows)

    tall = rounded_up(rows + full, 8)
    below, above, rotations, axials = lax.optimization_barrier((below, above, rotations, axials))

    field, blocks, mies, line = pl.pallas_call(
        functools.partial(field_kernel, own, quarter, modes),
        in_specs=[whole()] * 5 + [hbm()] * 2,
        out_specs=[whole()] * 4,
        out_shape=[
            jax.ShapeDtypeStruct(pieces_shape, BF16),
            jax.ShapeDtypeStruct((pairs_of_vectors, tall, columns), F32),
            jax.ShapeDtypeStruct(mie_rows.shape, F32),
            jax.ShapeDtypeStruct((1, 128), F32),
        ],
        scratch_shapes=[
            pltpu.VMEM((3, 2, size // 128, group, 128), F32),
            pltpu.VMEM((tables, 4 * group, size), BF16),
            pltpu.VMEM((2 * group, size), F32),
            pltpu.VMEM((vectors, vectors, 8, columns), F32),
            pltpu.SemaphoreType.DMA((pairs_of_vectors + 1,)),
        ],
        compiler_params=params(20),
        name="field",
    )(rotations, axials, below, own_pieces, above, basis_rows, mie_rows)
    field_pieces = exchanged(field)

    image, sums = pl.pallas_call(
        functools.partial(image_kernel, quarter, modes),
        in_specs=[whole()] * 4,
        out_specs=[whole()] * 2,
        out_shape=[jax.ShapeDtypeStruct((full, columns), F32), jax.ShapeDtypeStruct((ways * blk_ways, 1, 128), F32)],
        scratch_shapes=[pltpu.VMEM((full, columns), F32)],
        compiler_params=params(8),
        name="image",
    )(blocks, mies, line, field_pieces)
    sums = lax.all_to_all(sums, ("blk", "pair"), split_axis=0, concat_axis=0, tiled=True)

    height = 4
    mean_scale = 1.0 / (own * blk_ways * modes * columns)
    dots, next_rows = pl.pallas_call(
        functools.partial(remainder_kernel, quarter, modes, mean_scale),
        in_specs=[whole()] * 3,
        out_specs=[whole(), whole()],
        out_shape=[jax.ShapeDtypeStruct((2, vectors), F32), jax.ShapeDtypeStruct((rows // height, height, columns), F32)],
        compiler_params=params(16),
        name="remainder",
    )(sums, blocks, image)
    return dots, next_rows.reshape(modes, quarter, columns).transpose(1, 0, 2)


def solution(mesh):
    placed = (
        P(None, ("blk", "pair"), None, None),
        P(("blk", "pair"), None, None),
        P(),
        P(),
        P("blk", None, None),
        P("blk"),
    )
    return jax.shard_map(
        shards,
        mesh=mesh,
        in_specs=placed,
        out_specs=(P(), P(("blk", "pair"), None, None)),
        check_vma=False,
    )
```

```python
import functools

import jax
import jax.numpy as jnp
from jax import lax
from jax.experimental import pallas as pl
from jax.experimental.pallas import tpu as pltpu
from jax.sharding import PartitionSpec as P

MIB = 1024 * 1024
F32 = jnp.float32
BF16 = jnp.bfloat16


def params(mib):
    return pltpu.CompilerParams(vmem_limit_bytes=mib * MIB)


def hbm():
    return pl.BlockSpec(memory_space=pltpu.HBM)


def whole():
    return pl.BlockSpec(memory_space=pltpu.VMEM)


def in_hbm(value):
    return pltpu.with_memory_space_constraint(value, pltpu.HBM)


def rounded_up(value, unit):
    return (value + unit - 1) // unit * unit


def iota(shape, dim):
    return lax.broadcasted_iota(jnp.int32, shape, dim)


def dot_nn(left, right):
    return lax.dot_general(left, right, (((1,), (0,)), ((), ())), preferred_element_type=F32)


def dot_nt(left, right):
    return lax.dot_general(left, right, (((1,), (1,)), ((), ())), preferred_element_type=F32)


def pack_kernel(quarter, modes, ways, own, list_ref, count_ref, basis_ref, out_ref, pair_rows_ref, lines_ref, pad_ref, codes_ref, sems):
    full, columns = lines_ref.shape
    rows = quarter * modes
    part = columns // 2 // ways
    copy = pltpu.make_async_copy(basis_ref.at[basis_ref.shape[0] - 1, pl.ds(2 * rows - full, full)], lines_ref, sems.at[0])
    copy.start()
    list_copy = pltpu.make_async_copy(list_ref, pair_rows_ref, sems.at[1])
    list_copy.start()
    pad_ref[...] = jnp.zeros_like(pad_ref)
    list_copy.wait()
    slots = pair_rows_ref.shape[2]
    live = iota((1, slots), 1) < count_ref[0]
    marks = jnp.where(live, own * (pair_rows_ref[2] + 1) + pair_rows_ref[0], 0)
    line = iota((slots, slots), 0)
    stacked = jnp.where(line == 0, marks, jnp.where(line == 1, pair_rows_ref[1], 0))
    turned = jnp.transpose(stacked.astype(F32))
    codes_ref[0:slots, :] = turned
    codes_ref[slots : 2 * slots, :] = pltpu.roll(turned, slots - 1, axis=1)
    share = 2 * quarter * part
    mine = codes_ref[pl.ds(pl.multiple_of(lax.axis_index("pair") * share, share), share), :][:, 0:1]
    copy.wait()
    for j in range(quarter):
        pad_ref[0:modes, :] = lines_ref[pl.ds(full - rows + j, modes, quarter), :]
        turned = jnp.transpose(pad_ref[...])
        for c in range(2):
            codes = mine[(c * quarter + j) * part : (c * quarter + j + 1) * part]
            for p in range(ways):
                row = c * (columns // 2) + p * part
                piece = turned[row : row + part]
                out_ref[p, c, j] = jnp.where(iota(piece.shape, 1) == modes, codes, piece).astype(BF16)


def tables_kernel(modes, tables, axial_ref, rot_ref, rot_out_ref, axial_out_ref, lines_ref):
    step = pl.program_id(0)
    size = rot_out_ref.shape[2]
    chunk = 256

    @pl.when(step == 0)
    def _():
        lines_ref[...] = jnp.zeros_like(lines_ref)

    out_row, in_row = iota((chunk, chunk), 0), iota((chunk, chunk), 1)
    each = chunk // 2
    halves = (in_row == 2 * lax.rem(out_row, each) + lax.div(out_row, each)).astype(F32).astype(BF16)
    lines_ref[0 : 2 * modes, 0:modes] = axial_ref[0].reshape(2 * modes, modes)
    for q in range(2 * size // chunk):
        sorted_rows = dot_nn(halves, lines_ref[q * chunk : (q + 1) * chunk, :]).astype(BF16)
        for c in range(2):
            axial_out_ref[0, c * size + q * each : c * size + (q + 1) * each, :] = sorted_rows[c * each : (c + 1) * each]
    each = chunk // tables
    entries = (in_row == tables * lax.rem(out_row, each) + lax.div(out_row, each)).astype(F32).astype(BF16)
    block = rot_ref.shape[0]
    left = tables * modes - step * block
    rows = jnp.where(iota((block, modes), 0) < left, rot_ref[...], jnp.zeros((), BF16))
    rot_out_ref[:, :, size - 128 : size] = jnp.zeros((tables, block // tables, 128), BF16)
    for q in range(block // chunk):
        sorted_rows = dot_nn(entries, rows[q * chunk : (q + 1) * chunk]).astype(BF16)
        for g in range(tables):
            rot_out_ref[g, q * each : (q + 1) * each, 0:modes] = sorted_rows[g * each : (g + 1) * each]


def swapped(value):
    half = value.shape[0] // 2
    return jnp.concatenate([-value[half:], value[:half]], axis=0)


def pair_counts(own, tables, lane, refs):
    group, size = refs[0].shape[0] * refs[0].shape[2] * refs[0].shape[3], refs[0].shape[4]
    wanted = iota((tables * own, group), 0) + own

    def one_hot(hit):
        return jnp.where(hit, 1.0, 0.0).astype(BF16)

    forward, backward = None, []
    for window, ref in enumerate(refs):
        values = ref[:, :, :, :, size - 128 : size].reshape(2 * group, 128).astype(F32)
        marks_column, sources_column = (values[h * group : (h + 1) * group, lane : lane + 1].astype(jnp.int32) for h in range(2))
        marks, sources = (jnp.transpose(values[h * group : (h + 1) * group])[lane : lane + 1].astype(jnp.int32) for h in range(2))
        if window == 1:
            forward = dot_nn(one_hot(marks == wanted), one_hot(sources_column == iota((group, 3 * own), 1)))
        block = sources - (2 - window) * own
        inside = (block >= 0) & (block < own) & (marks >= own)
        hits = one_hot(jnp.where(inside, lax.div(marks, own) * own + block, -1) == wanted)
        place = lax.rem(marks_column, own) + window * own
        backward.append(dot_nn(hits, one_hot(place == iota((group, 3 * own), 1))))
    return jnp.concatenate([forward, sum(backward)], axis=0).astype(BF16)


def folded(value):
    return jnp.sum(value.reshape(value.shape[0] // 8, 8, value.shape[1]), axis=0)


def field_kernel(
    own, modes, rot_ref, axial_ref, below_ref, own_ref, above_ref, basis_ref, mie_ref,
    out_ref, blocks_ref, mies_ref, window_ref, sums_ref, total_ref, sems,
):
    tables, _, size = rot_ref.shape
    vector_blocks, rows, columns = basis_ref.shape
    copies = [pltpu.make_async_copy(mie_ref, mies_ref, sems.at[vector_blocks])]
    for i in range(vector_blocks):
        copies.append(pltpu.make_async_copy(basis_ref.at[i], blocks_ref.at[i, pl.ds(0, rows)], sems.at[i]))
    for copy in copies:
        copy.start()
    for i in range(vector_blocks):
        blocks_ref[i, rows:, :] = jnp.zeros((blocks_ref.shape[1] - rows, columns), F32)
    refs = (below_ref, own_ref, above_ref)
    ways, _, quarter, part, _ = own_ref.shape
    group = own * part
    counts = pair_counts(own, tables, modes % 128, refs)
    for w, ref in enumerate(refs):
        for c in range(2):
            for t in range(size // 128):
                window_ref[w, c, t] = ref[:, c, :, :, t * 128 : (t + 1) * 128].reshape(group, 128).astype(F32)
    for c in range(2):
        for s in range(0, part, 2):
            results = []
            for sphere in (s, s + 1):
                blocks = []
                for t in range(size // 128):
                    lists = [window_ref[w, c, t, pl.ds(sphere, own, part), :] for w in range(3)]
                    blocks.append(jnp.concatenate(lists, axis=0).astype(BF16))
                results.append(dot_nn(counts, jnp.concatenate(blocks, axis=1)))
            for direction in range(2):
                for g in range(tables):
                    first = (direction * tables + g) * own
                    rows = jnp.concatenate([result[first : first + own] for result in results], axis=0)
                    place = (direction * 2 + c) * group + s * own
                    sums_ref[g, place : place + 2 * own, :] = rows.astype(BF16)
    for g in range(tables):
        turned = dot_nt(sums_ref[g], rot_ref[g]).astype(BF16)
        forward, backward = turned[: 2 * group], turned[2 * group :]
        moved = dot_nt(forward, axial_ref[g, :size]) + dot_nt(swapped(forward), axial_ref[g, size:])
        moved += dot_nn(jnp.concatenate([backward, swapped(backward)], axis=1), axial_ref[g])
        back = dot_nn(moved.astype(BF16), rot_ref[g])
        total_ref[...] = back if g == 0 else total_ref[...] + back
    for c in range(2):
        for t in range(size // 128):
            lanes = slice(t * 128, (t + 1) * 128)
            window_ref[0, c, t] = total_ref[c * group : (c + 1) * group, lanes]
            for p in range(ways):
                for j in range(quarter):
                    rows = window_ref[0, c, t, pl.ds(p * quarter + j, part, own), :]
                    out_ref[p, c, j, :, lanes] = rows.astype(BF16)
    for copy in copies:
        copy.wait()


def lane_swap(value):
    half = value.shape[1] // 2
    rolled = pltpu.roll(value, half, axis=1)
    return jnp.where(iota(value.shape, 1) < half, -rolled, rolled)


def add_products(blocks_ref, products_ref, rows, first, count):
    vectors = products_ref.shape[0]
    values = []
    for k in range(vectors):
        start = k % 2 * rows + first
        value = blocks_ref[k // 2, start : start + count, :]
        if k % 2 == 0 and first + count > rows:
            value = jnp.where(iota(value.shape, 0) < rows - first, value, 0.0)
        values.append(value)
    for l in range(vectors):
        other = pltpu.roll(values[l], values[l].shape[1] // 2, axis=1)
        for k in range(l + 1):
            products_ref[k, l] += folded(values[k] * values[l])
            if k < l:
                products_ref[l, k] += folded(values[k] * other)


def products_line(products_ref):
    vectors, _, _, columns = products_ref.shape
    pairs = vectors * vectors
    totals = jnp.sum(products_ref[...].reshape(pairs, 8, columns), axis=1)
    pair = iota(totals.shape, 0)
    signed = (lax.div(pair, vectors) > lax.rem(pair, vectors)) & (iota(totals.shape, 1) >= columns // 2)
    totals = jnp.sum(jnp.where(signed, -totals, totals), axis=1, keepdims=True)
    row, lane = iota((vectors, 128), 0), iota((vectors, 128), 1)
    line = jnp.zeros((1, 128), F32)
    for k in range(vectors):
        column = totals[k * vectors : (k + 1) * vectors]
        line += jnp.sum(jnp.where(row + k * vectors == lane, column, 0.0), axis=0, keepdims=True)
    return line


def gram_kernel(quarter, modes, basis_ref, line_ref, blocks_ref, products_ref, sems):
    blocks, _, columns = basis_ref.shape
    rows = quarter * modes
    parts, chunk = 4, 32
    tile_end = rows // 8 * 8
    step = rounded_up(rows, 8 * parts) // parts
    even = [0] + [step * q for q in range(1, parts)] + [tile_end]
    odd = [tile_end] + [rounded_up(rows, 8) + step * q for q in range(1, parts)] + [2 * rows]
    copies = []
    for q in range(parts):
        for i in range(blocks):
            for side, cuts in enumerate((even, odd)):
                here = pl.ds(cuts[q], cuts[q + 1] - cuts[q])
                copies.append(pltpu.make_async_copy(basis_ref.at[i, here], blocks_ref.at[i, here], sems.at[q, i, side]))
    for copy in copies:
        copy.start()
    products_ref[...] = jnp.zeros_like(products_ref)
    for i in range(blocks):
        blocks_ref[i, 2 * rows :, :] = jnp.zeros((blocks_ref.shape[1] - 2 * rows, columns), F32)
    for q in range(parts):
        for copy in copies[2 * blocks * q : 2 * blocks * (q + 1)]:
            copy.wait()
        for first in range(step * q, min(step * (q + 1), rows), chunk):
            add_products(blocks_ref, products_ref, rows, first, chunk)
    line_ref[...] = products_line(products_ref)


def image_kernel(quarter, modes, blocks_ref, mie_ref, gram_ref, pieces_ref, image_ref, sums_ref, lines_ref):
    vectors = 2 * blocks_ref.shape[0]
    full, columns = image_ref.shape
    rows = quarter * modes
    ways, _, _, part, size = pieces_ref.shape
    lines_ref[rows:full, :] = jnp.zeros((full - rows, columns), F32)
    for j in range(quarter):
        turned = jnp.concatenate([pieces_ref[:, c, j].reshape(ways * part, size) for c in range(2)], axis=0)
        lines_ref[pl.ds(j, modes, quarter), :] = jnp.transpose(turned.astype(F32))[:modes]
    half = columns // 2
    chunk = 64
    totals = [jnp.zeros((8, columns), F32) for _ in range(2 * vectors + 1)]
    for first in range(0, full, chunk):
        here = slice(first, first + chunk)
        field = lines_ref[here, :]
        count = min(chunk, rows - first)
        height = mie_ref.shape[1]
        mie = mie_ref[first // height : (first + count) // height].reshape(count, columns)
        if count < chunk:
            mie = jnp.concatenate([mie, jnp.zeros((chunk - count, columns), F32)], axis=0)
        left = iota(mie.shape, 1) < half
        other = pltpu.roll(mie, half, axis=1)
        product = jnp.where(left, mie, other) * field + jnp.where(left, -other, mie) * pltpu.roll(field, half, axis=1)
        last = (vectors - 1) % 2 * rows + first
        image = blocks_ref[(vectors - 1) // 2, last : last + chunk, :] - product
        image_ref[here, :] = image
        turned = pltpu.roll(image, half, axis=1)
        for k in range(vectors):
            start = k % 2 * rows + first
            values = blocks_ref[k // 2, start : start + chunk, :]
            totals[2 * k] += folded(values * image)
            totals[2 * k + 1] += folded(values * turned)
        totals[2 * vectors] += folded(image * image)
    lane = iota(gram_ref.shape, 1)
    line = gram_ref[...]
    left = iota((8, columns), 1) < half
    for index, total in enumerate(totals):
        if index % 2 and index < 2 * vectors:
            total = jnp.where(left, total, -total)
        line = jnp.where(lane == vectors * vectors + index, jnp.sum(total, axis=(0, 1), keepdims=True), line)
    sums_ref[...] = jnp.broadcast_to(line[None], sums_ref.shape)


def remainder_kernel(quarter, modes, mean_scale, sums_ref, blocks_ref, image_ref, dots_ref, out_ref):
    vectors = 2 * blocks_ref.shape[0]
    full, columns = image_ref.shape
    rows = quarter * modes
    total = jnp.sum(sums_ref[...], axis=0)
    lane = iota(total.shape, 1)

    def lane_at(index):
        return jnp.sum(jnp.where(lane == index, total, 0.0), axis=1, keepdims=True)

    def on_lanes(parts, places):
        line = jnp.zeros(total.shape, F32)
        for k in range(vectors):
            line = jnp.where(places == k, parts[k], line)
        return line

    start = vectors * vectors
    real = [lane_at(start + 2 * k) * mean_scale for k in range(vectors)]
    imag = [lane_at(start + 2 * k + 1) * mean_scale for k in range(vectors)]
    real_line, imag_line = on_lanes(real, lane), on_lanes(imag, lane)
    dots_ref[0:1, :] = real_line[:, :vectors]
    dots_ref[1:2, :] = imag_line[:, :vectors]
    first_index, last_index = lax.div(lane, vectors), lax.rem(lane, vectors)
    real_first, real_last = on_lanes(real, first_index), on_lanes(real, last_index)
    imag_first, imag_last = on_lanes(imag, first_index), on_lanes(imag, last_index)
    same = real_first * real_last + imag_first * imag_last
    cross = imag_last * real_first - real_last * imag_first
    often = jnp.where(first_index == last_index, 1.0, 2.0)
    spread = jnp.where(lane < start, total * often * jnp.where(first_index <= last_index, same, cross), 0.0)
    spread = jnp.sum(spread, axis=1, keepdims=True)
    inside = jnp.sum(real_line * real_line + imag_line * imag_line, axis=1, keepdims=True)
    norm_square = (lane_at(start + 2 * vectors) + spread) * mean_scale - 2.0 * inside
    scale = lax.rsqrt(norm_square)
    image_scale = jnp.broadcast_to(scale, (8, columns))
    reals = [jnp.broadcast_to(real[k] * scale, (8, columns)) for k in range(vectors)]
    imags = [jnp.broadcast_to(imag[k] * scale, (8, columns)) for k in range(vectors)]
    chunk = 64
    for first in range(0, full, chunk):
        here = slice(first, first + chunk)
        values = []
        for k in range(vectors):
            start = k % 2 * rows + first
            values.append(blocks_ref[k // 2, start : start + chunk, :].reshape(chunk // 8, 8, columns))
        along = image_ref[here, :].reshape(chunk // 8, 8, columns) * image_scale
        turned = jnp.zeros_like(along)
        for k in range(vectors):
            along -= reals[k] * values[k]
            turned += imags[k] * values[k]
        result = along.reshape(chunk, columns) - lane_swap(turned.reshape(chunk, columns))
        count = min(chunk, rows - first)
        height = out_ref.shape[1]
        out_ref[first // height : (first + count) // height] = result.reshape(chunk // height, height, columns)[: count // height]


def exchanged(value):
    return lax.all_to_all(value, "pair", split_axis=0, concat_axis=0, tiled=True)


def neighbours(value):
    count = lax.axis_size("blk")
    up = [(i, i + 1) for i in range(count - 1)]
    down = [(j, i) for i, j in up]
    return lax.ppermute(value, "blk", up), lax.ppermute(value, "blk", down)


def shards(basis, mie_coeffs, rot_table, axial_table, pair_table, pair_count):
    vectors, quarter, modes, columns = basis.shape
    ways = lax.axis_size("pair")
    blk_ways = lax.axis_size("blk")
    tables = rot_table.shape[0]
    slots = pair_table.shape[1]
    own = quarter * ways
    part = columns // 2 // ways
    group = own * part
    size = rounded_up(modes, 128)
    rows = quarter * modes
    full = rounded_up(rows, 8)
    pairs_of_vectors = vectors // 2

    basis_rows = in_hbm(basis.transpose(0, 2, 1, 3).reshape(pairs_of_vectors, 2 * rows, columns))
    mie_rows = in_hbm(mie_coeffs.transpose(1, 0, 2).reshape(rows // 4, 4, columns))
    rot_rows = in_hbm(rot_table.transpose(1, 0, 2).reshape(modes * tables, modes))
    axial_rows = in_hbm(axial_table.transpose(0, 2, 1, 3))
    pair_rows = in_hbm(pair_table.transpose(2, 0, 1))

    pieces_shape = (ways, 2, quarter, part, size)
    pieces = pl.pallas_call(
        functools.partial(pack_kernel, quarter, modes, ways, own),
        in_specs=[hbm(), pl.BlockSpec(memory_space=pltpu.SMEM), hbm()],
        out_specs=whole(),
        out_shape=jax.ShapeDtypeStruct(pieces_shape, BF16),
        scratch_shapes=[
            pltpu.VMEM(pair_rows.shape, jnp.int32),
            pltpu.VMEM((full, columns), F32),
            pltpu.VMEM((size, columns), F32),
            pltpu.VMEM((2 * slots, slots), F32),
            pltpu.SemaphoreType.DMA((2,)),
        ],
        compiler_params=params(16),
        name="pack",
    )(pair_rows, pair_count, basis_rows)
    tall = rounded_up(rows + full, 8)
    pieces, basis_later = lax.optimization_barrier((pieces, basis_rows))
    own_pieces = exchanged(pieces)
    line = pl.pallas_call(
        functools.partial(gram_kernel, quarter, modes),
        grid=(1,),
        in_specs=[hbm()],
        out_specs=pl.BlockSpec((1, 128), lambda i: (0, 0)),
        out_shape=pltpu.HBM((1, 128), F32),
        scratch_shapes=[
            pltpu.VMEM((pairs_of_vectors, tall, columns), F32),
            pltpu.VMEM((vectors, vectors, 8, columns), F32),
            pltpu.SemaphoreType.DMA((4, pairs_of_vectors, 2)),
        ],
        compiler_params=params(16),
        name="gram",
    )(basis_later)
    own_pieces, line, *inputs = lax.optimization_barrier((own_pieces, line, basis_rows, mie_rows, rot_rows, axial_rows))
    basis_rows, mie_rows, rot_rows, axial_rows = inputs
    below, above = neighbours(own_pieces)

    rotations, axials = pl.pallas_call(
        functools.partial(tables_kernel, modes, tables),
        grid=(tables,),
        in_specs=[
            pl.BlockSpec((1, modes, 2, modes), lambda g: (g, 0, 0, 0)),
            pl.BlockSpec((size, modes), lambda g: (g, 0)),
        ],
        out_specs=[
            pl.BlockSpec((tables, size // tables, size), lambda g: (0, g, 0)),
            pl.BlockSpec((1, 2 * size, size), lambda g: (g, 0, 0)),
        ],
        out_shape=[
            jax.ShapeDtypeStruct((tables, size, size), BF16),
            jax.ShapeDtypeStruct((tables, 2 * size, size), BF16),
        ],
        scratch_shapes=[pltpu.VMEM((2 * size, size), BF16)],
        compiler_params=params(32),
        cost_estimate=pl.CostEstimate(flops=tables * 8 * 256 * 256 * size, bytes_accessed=6 * tables * size * size * 2, transcendentals=0),
        name="tables",
    )(axial_rows, rot_rows)

    below, above, rotations, axials = lax.optimization_barrier((below, above, rotations, axials))

    field, blocks, mies = pl.pallas_call(
        functools.partial(field_kernel, own, modes),
        in_specs=[whole()] * 5 + [hbm()] * 2,
        out_specs=[whole()] * 3,
        out_shape=[
            jax.ShapeDtypeStruct(pieces_shape, BF16),
            jax.ShapeDtypeStruct((pairs_of_vectors, tall, columns), F32),
            jax.ShapeDtypeStruct(mie_rows.shape, F32),
        ],
        scratch_shapes=[
            pltpu.VMEM((3, 2, size // 128, group, 128), F32),
            pltpu.VMEM((tables, 4 * group, size), BF16),
            pltpu.VMEM((2 * group, size), F32),
            pltpu.SemaphoreType.DMA((pairs_of_vectors + 1,)),
        ],
        compiler_params=params(20),
        name="field",
    )(rotations, axials, below, own_pieces, above, basis_rows, mie_rows)
    field_pieces = exchanged(field)

    image, sums = pl.pallas_call(
        functools.partial(image_kernel, quarter, modes),
        in_specs=[whole()] * 4,
        out_specs=[whole()] * 2,
        out_shape=[jax.ShapeDtypeStruct((full, columns), F32), jax.ShapeDtypeStruct((ways * blk_ways, 1, 128), F32)],
        scratch_shapes=[pltpu.VMEM((full, columns), F32)],
        compiler_params=params(8),
        name="image",
    )(blocks, mies, line, field_pieces)
    sums = lax.all_to_all(sums, ("blk", "pair"), split_axis=0, concat_axis=0, tiled=True)

    height = 4
    mean_scale = 1.0 / (own * blk_ways * modes * columns)
    dots, next_rows = pl.pallas_call(
        functools.partial(remainder_kernel, quarter, modes, mean_scale),
        in_specs=[whole()] * 3,
        out_specs=[whole(), whole()],
        out_shape=[jax.ShapeDtypeStruct((2, vectors), F32), jax.ShapeDtypeStruct((rows // height, height, columns), F32)],
        compiler_params=params(16),
        name="remainder",
    )(sums, blocks, image)
    return dots, next_rows.reshape(modes, quarter, columns).transpose(1, 0, 2)


def solution(mesh):
    placed = (
        P(None, ("blk", "pair"), None, None),
        P(("blk", "pair"), None, None),
        P(),
        P(),
        P("blk", None, None),
        P("blk"),
    )
    return jax.shard_map(
        shards,
        mesh=mesh,
        in_specs=placed,
        out_specs=(P(), P(("blk", "pair"), None, None)),
        check_vma=False,
    )
```

```python
import functools

import jax
import jax.numpy as jnp
from jax import lax
from jax.experimental import pallas as pl
from jax.experimental.pallas import tpu as pltpu
from jax.sharding import PartitionSpec as P

MIB = 1024 * 1024
F32 = jnp.float32
BF16 = jnp.bfloat16


def params(mib):
    return pltpu.CompilerParams(vmem_limit_bytes=mib * MIB)


def hbm():
    return pl.BlockSpec(memory_space=pltpu.HBM)


def whole():
    return pl.BlockSpec(memory_space=pltpu.VMEM)


def in_hbm(value):
    return pltpu.with_memory_space_constraint(value, pltpu.HBM)


def rounded_up(value, unit):
    return (value + unit - 1) // unit * unit


def iota(shape, dim):
    return lax.broadcasted_iota(jnp.int32, shape, dim)


def dot_nn(left, right):
    return lax.dot_general(left, right, (((1,), (0,)), ((), ())), preferred_element_type=F32)


def dot_nt(left, right):
    return lax.dot_general(left, right, (((1,), (1,)), ((), ())), preferred_element_type=F32)


def pack_kernel(quarter, modes, ways, own, list_ref, count_ref, basis_ref, out_ref, pair_rows_ref, lines_ref, pad_ref, codes_ref, sems):
    full, columns = lines_ref.shape
    rows = quarter * modes
    part = columns // 2 // ways
    copy = pltpu.make_async_copy(basis_ref.at[basis_ref.shape[0] - 1, pl.ds(2 * rows - full, full)], lines_ref, sems.at[0])
    copy.start()
    list_copy = pltpu.make_async_copy(list_ref, pair_rows_ref, sems.at[1])
    list_copy.start()
    pad_ref[...] = jnp.zeros_like(pad_ref)
    list_copy.wait()
    slots = pair_rows_ref.shape[2]
    live = iota((1, slots), 1) < count_ref[0]
    marks = jnp.where(live, own * (pair_rows_ref[2] + 1) + pair_rows_ref[0], 0)
    line = iota((slots, slots), 0)
    stacked = jnp.where(line == 0, marks, jnp.where(line == 1, pair_rows_ref[1], 0))
    turned = jnp.transpose(stacked.astype(F32))
    codes_ref[0:slots, :] = turned
    codes_ref[slots : 2 * slots, :] = pltpu.roll(turned, slots - 1, axis=1)
    share = 2 * quarter * part
    mine = codes_ref[pl.ds(pl.multiple_of(lax.axis_index("pair") * share, share), share), :][:, 0:1]
    copy.wait()
    for j in range(quarter):
        pad_ref[0:modes, :] = lines_ref[pl.ds(full - rows + j, modes, quarter), :]
        turned = jnp.transpose(pad_ref[...])
        for c in range(2):
            codes = mine[(c * quarter + j) * part : (c * quarter + j + 1) * part]
            for p in range(ways):
                row = c * (columns // 2) + p * part
                piece = turned[row : row + part]
                out_ref[p, c, j] = jnp.where(iota(piece.shape, 1) == modes, codes, piece).astype(BF16)


def tables_kernel(modes, tables, axial_ref, rot_ref, rot_out_ref, axial_out_ref, lines_ref):
    step = pl.program_id(0)
    size = rot_out_ref.shape[2]
    chunk = 256

    @pl.when(step == 0)
    def _():
        lines_ref[...] = jnp.zeros_like(lines_ref)

    out_row, in_row = iota((chunk, chunk), 0), iota((chunk, chunk), 1)
    each = chunk // 2
    halves = (in_row == 2 * lax.rem(out_row, each) + lax.div(out_row, each)).astype(F32).astype(BF16)
    lines_ref[0 : 2 * modes, 0:modes] = axial_ref[0].reshape(2 * modes, modes)
    for q in range(2 * size // chunk):
        sorted_rows = dot_nn(halves, lines_ref[q * chunk : (q + 1) * chunk, :]).astype(BF16)
        for c in range(2):
            axial_out_ref[0, c * size + q * each : c * size + (q + 1) * each, :] = sorted_rows[c * each : (c + 1) * each]
    each = chunk // tables
    entries = (in_row == tables * lax.rem(out_row, each) + lax.div(out_row, each)).astype(F32).astype(BF16)
    block = rot_ref.shape[0]
    left = tables * modes - step * block
    rows = jnp.where(iota((block, modes), 0) < left, rot_ref[...], jnp.zeros((), BF16))
    rot_out_ref[:, :, size - 128 : size] = jnp.zeros((tables, block // tables, 128), BF16)
    for q in range(block // chunk):
        sorted_rows = dot_nn(entries, rows[q * chunk : (q + 1) * chunk]).astype(BF16)
        for g in range(tables):
            rot_out_ref[g, q * each : (q + 1) * each, 0:modes] = sorted_rows[g * each : (g + 1) * each]


def swapped(value):
    half = value.shape[0] // 2
    return jnp.concatenate([-value[half:], value[:half]], axis=0)


def pair_counts(own, tables, lane, refs):
    group, size = refs[0].shape[0] * refs[0].shape[2] * refs[0].shape[3], refs[0].shape[4]
    wanted = iota((tables * own, group), 0) + own

    def one_hot(hit):
        return jnp.where(hit, 1.0, 0.0).astype(BF16)

    forward, backward = None, []
    for window, ref in enumerate(refs):
        values = ref[:, :, :, :, size - 128 : size].reshape(2 * group, 128).astype(F32)
        marks_column, sources_column = (values[h * group : (h + 1) * group, lane : lane + 1].astype(jnp.int32) for h in range(2))
        marks, sources = (jnp.transpose(values[h * group : (h + 1) * group])[lane : lane + 1].astype(jnp.int32) for h in range(2))
        if window == 1:
            forward = dot_nn(one_hot(marks == wanted), one_hot(sources_column == iota((group, 3 * own), 1)))
        block = sources - (2 - window) * own
        inside = (block >= 0) & (block < own) & (marks >= own)
        hits = one_hot(jnp.where(inside, lax.div(marks, own) * own + block, -1) == wanted)
        place = lax.rem(marks_column, own) + window * own
        backward.append(dot_nn(hits, one_hot(place == iota((group, 3 * own), 1))))
    return jnp.concatenate([forward, sum(backward)], axis=0).astype(BF16)


def folded(value):
    return jnp.sum(value.reshape(value.shape[0] // 8, 8, value.shape[1]), axis=0)


def field_kernel(
    own, modes, together, rot_ref, axial_ref, below_ref, own_ref, above_ref, basis_ref, mie_ref,
    out_ref, blocks_ref, mies_ref, window_ref, sums_ref, total_ref, sems,
):
    tables, _, size = rot_ref.shape
    vector_blocks, rows, columns = basis_ref.shape
    copies = [pltpu.make_async_copy(mie_ref, mies_ref.at[pl.ds(0, mie_ref.shape[0])], sems.at[vector_blocks])]
    mies_ref[mie_ref.shape[0] :] = jnp.zeros((mies_ref.shape[0] - mie_ref.shape[0],) + mies_ref.shape[1:], F32)
    for i in range(vector_blocks):
        copies.append(pltpu.make_async_copy(basis_ref.at[i], blocks_ref.at[i, pl.ds(0, rows)], sems.at[i]))
    for copy in copies:
        copy.start()
    for i in range(vector_blocks):
        blocks_ref[i, rows:, :] = jnp.zeros((blocks_ref.shape[1] - rows, columns), F32)
    refs = (below_ref, own_ref, above_ref)
    ways, _, quarter, part, _ = own_ref.shape
    group = own * part
    counts = pair_counts(own, tables, modes % 128, refs)
    for w, ref in enumerate(refs):
        for c in range(2):
            for t in range(size // 128):
                window_ref[w, c, t] = ref[:, c, :, :, t * 128 : (t + 1) * 128].reshape(group, 128).astype(F32)

    def sums(pair, carry):
        for c in range(2):
            results = []
            for i in range(2):
                blocks = []
                for t in range(size // 128):
                    lists = [window_ref[w, c, t, pl.ds(2 * pair + i, own, part), :] for w in range(3)]
                    blocks.append(jnp.concatenate(lists, axis=0).astype(BF16))
                results.append(dot_nn(counts, jnp.concatenate(blocks, axis=1)))
            for direction in range(2):
                for g in range(tables):
                    first = (direction * tables + g) * own
                    rows = jnp.concatenate([result[first : first + own] for result in results], axis=0)
                    place = pl.multiple_of((direction * 2 + c) * group + pair * 2 * own, 2 * own)
                    sums_ref[g, pl.ds(place, 2 * own), :] = rows.astype(BF16)
        return carry

    lax.fori_loop(0, part // 2, sums, 0)
    total_ref[...] = jnp.zeros_like(total_ref)

    def body(step, carry):
        entries = [step * together + i for i in range(together)]
        turned = [dot_nt(sums_ref[g], rot_ref[g]).astype(BF16) for g in entries]
        moved = []
        for g, both in zip(entries, turned):
            forward, backward = both[: 2 * group], both[2 * group :]
            result = dot_nt(forward, axial_ref[g, :size]) + dot_nt(swapped(forward), axial_ref[g, size:])
            result += dot_nn(jnp.concatenate([backward, swapped(backward)], axis=1), axial_ref[g])
            moved.append(result.astype(BF16))
        total_ref[...] += sum(dot_nn(value, rot_ref[g]) for g, value in zip(entries, moved))
        return carry

    lax.fori_loop(0, tables // together, body, 0)
    for c in range(2):
        for t in range(size // 128):
            lanes = slice(t * 128, (t + 1) * 128)
            window_ref[0, c, t] = total_ref[c * group : (c + 1) * group, lanes]
            for p in range(ways):
                for j in range(quarter):
                    rows = window_ref[0, c, t, pl.ds(p * quarter + j, part, own), :]
                    out_ref[p, c, j, :, lanes] = rows.astype(BF16)
    for copy in copies:
        copy.wait()


def lane_swap(value):
    half = value.shape[1] // 2
    rolled = pltpu.roll(value, half, axis=1)
    return jnp.where(iota(value.shape, 1) < half, -rolled, rolled)


def add_products(blocks_ref, products_ref, rows, first, count, ends):
    vectors = products_ref.shape[0]
    values = []
    for k in range(vectors):
        start = k % 2 * rows + first
        value = blocks_ref[k // 2, pl.ds(start, count), :]
        if k % 2 == 0 and ends:
            value = jnp.where(iota(value.shape, 0) < rows - first, value, 0.0)
        values.append(value)
    for l in range(vectors):
        other = pltpu.roll(values[l], values[l].shape[1] // 2, axis=1)
        for k in range(l + 1):
            products_ref[k, l] += folded(values[k] * values[l])
            if k < l:
                products_ref[l, k] += folded(values[k] * other)


def products_line(products_ref):
    vectors, _, _, columns = products_ref.shape
    pairs = vectors * vectors
    totals = jnp.sum(products_ref[...].reshape(pairs, 8, columns), axis=1)
    pair = iota(totals.shape, 0)
    signed = (lax.div(pair, vectors) > lax.rem(pair, vectors)) & (iota(totals.shape, 1) >= columns // 2)
    totals = jnp.sum(jnp.where(signed, -totals, totals), axis=1, keepdims=True)
    row, lane = iota((vectors, 128), 0), iota((vectors, 128), 1)
    line = jnp.zeros((1, 128), F32)
    for k in range(vectors):
        column = totals[k * vectors : (k + 1) * vectors]
        line += jnp.sum(jnp.where(row + k * vectors == lane, column, 0.0), axis=0, keepdims=True)
    return line


def gram_kernel(quarter, modes, basis_ref, line_ref, blocks_ref, products_ref, sems):
    blocks, _, columns = basis_ref.shape
    rows = quarter * modes
    parts, chunk = 4, 32
    tile_end = rows // 8 * 8
    step = rounded_up(rows, 8 * parts) // parts
    even = [0] + [step * q for q in range(1, parts)] + [tile_end]
    odd = [tile_end] + [rounded_up(rows, 8) + step * q for q in range(1, parts)] + [2 * rows]
    copies = []
    for q in range(parts):
        for i in range(blocks):
            for side, cuts in enumerate((even, odd)):
                here = pl.ds(cuts[q], cuts[q + 1] - cuts[q])
                copies.append(pltpu.make_async_copy(basis_ref.at[i, here], blocks_ref.at[i, here], sems.at[q, i, side]))
    for copy in copies:
        copy.start()
    products_ref[...] = jnp.zeros_like(products_ref)
    for i in range(blocks):
        blocks_ref[i, 2 * rows :, :] = jnp.zeros((blocks_ref.shape[1] - 2 * rows, columns), F32)
    for q in range(parts):
        for copy in copies[2 * blocks * q : 2 * blocks * (q + 1)]:
            copy.wait()
        last = min(step * (q + 1), rows) // chunk

        def body(i, carry):
            add_products(blocks_ref, products_ref, rows, pl.multiple_of(i * chunk, chunk), chunk, False)
            return carry

        lax.fori_loop(step * q // chunk, last, body, 0)
        if rows < (last + 1) * chunk and rows < step * (q + 1):
            add_products(blocks_ref, products_ref, rows, last * chunk, chunk, True)
    line_ref[...] = products_line(products_ref)


def image_kernel(quarter, modes, blocks_ref, mie_ref, gram_ref, pieces_ref, image_ref, sums_ref, lines_ref):
    vectors = 2 * blocks_ref.shape[0]
    full, columns = image_ref.shape
    rows = quarter * modes
    ways, _, _, part, size = pieces_ref.shape
    lines_ref[rows:full, :] = jnp.zeros((full - rows, columns), F32)
    for j in range(quarter):
        turned = jnp.concatenate([pieces_ref[:, c, j].reshape(ways * part, size) for c in range(2)], axis=0)
        lines_ref[pl.ds(j, modes, quarter), :] = jnp.transpose(turned.astype(F32))[:modes]
    half = columns // 2
    chunk = 64
    height = mie_ref.shape[1]

    def body(i, totals):
        first = pl.multiple_of(i * chunk, chunk)
        here = pl.ds(first, chunk)
        field = lines_ref[here, :]
        mie = mie_ref[pl.ds(i * (chunk // height), chunk // height)].reshape(chunk, columns)
        left = iota(mie.shape, 1) < half
        other = pltpu.roll(mie, half, axis=1)
        product = jnp.where(left, mie, other) * field + jnp.where(left, -other, mie) * pltpu.roll(field, half, axis=1)
        image = blocks_ref[(vectors - 1) // 2, pl.ds((vectors - 1) % 2 * rows + first, chunk), :] - product
        image_ref[here, :] = image
        turned = pltpu.roll(image, half, axis=1)
        added = []
        for k in range(vectors):
            values = blocks_ref[k // 2, pl.ds(k % 2 * rows + first, chunk), :]
            added += [folded(values * image), folded(values * turned)]
        added.append(folded(image * image))
        return [total + part_sum for total, part_sum in zip(totals, added)]

    totals = lax.fori_loop(0, full // chunk, body, [jnp.zeros((8, columns), F32)] * (2 * vectors + 1))
    lane = iota(gram_ref.shape, 1)
    line = gram_ref[...]
    left = iota((8, columns), 1) < half
    for index, total in enumerate(totals):
        if index % 2 and index < 2 * vectors:
            total = jnp.where(left, total, -total)
        line = jnp.where(lane == vectors * vectors + index, jnp.sum(total, axis=(0, 1), keepdims=True), line)
    sums_ref[...] = jnp.broadcast_to(line[None], sums_ref.shape)


def remainder_kernel(quarter, modes, mean_scale, sums_ref, blocks_ref, image_ref, dots_ref, out_ref):
    vectors = 2 * blocks_ref.shape[0]
    full, columns = image_ref.shape
    rows = quarter * modes
    total = jnp.sum(sums_ref[...], axis=0)
    lane = iota(total.shape, 1)

    def lane_at(index):
        return jnp.sum(jnp.where(lane == index, total, 0.0), axis=1, keepdims=True)

    def on_lanes(parts, places):
        line = jnp.zeros(total.shape, F32)
        for k in range(vectors):
            line = jnp.where(places == k, parts[k], line)
        return line

    start = vectors * vectors
    real = [lane_at(start + 2 * k) * mean_scale for k in range(vectors)]
    imag = [lane_at(start + 2 * k + 1) * mean_scale for k in range(vectors)]
    real_line, imag_line = on_lanes(real, lane), on_lanes(imag, lane)
    dots_ref[0:1, :] = real_line[:, :vectors]
    dots_ref[1:2, :] = imag_line[:, :vectors]
    first_index, last_index = lax.div(lane, vectors), lax.rem(lane, vectors)
    real_first, real_last = on_lanes(real, first_index), on_lanes(real, last_index)
    imag_first, imag_last = on_lanes(imag, first_index), on_lanes(imag, last_index)
    same = real_first * real_last + imag_first * imag_last
    cross = imag_last * real_first - real_last * imag_first
    often = jnp.where(first_index == last_index, 1.0, 2.0)
    spread = jnp.where(lane < start, total * often * jnp.where(first_index <= last_index, same, cross), 0.0)
    spread = jnp.sum(spread, axis=1, keepdims=True)
    inside = jnp.sum(real_line * real_line + imag_line * imag_line, axis=1, keepdims=True)
    norm_square = (lane_at(start + 2 * vectors) + spread) * mean_scale - 2.0 * inside
    scale = lax.rsqrt(norm_square)
    image_scale = jnp.broadcast_to(scale, (8, columns))
    reals = [jnp.broadcast_to(real[k] * scale, (8, columns)) for k in range(vectors)]
    imags = [jnp.broadcast_to(imag[k] * scale, (8, columns)) for k in range(vectors)]
    chunk = 64
    height = out_ref.shape[1]

    def write(first, place, count):
        values = []
        for k in range(vectors):
            value = blocks_ref[k // 2, pl.ds(k % 2 * rows + first, chunk), :]
            values.append(value.reshape(chunk // 8, 8, columns))
        along = image_ref[pl.ds(first, chunk), :].reshape(chunk // 8, 8, columns) * image_scale
        turned = jnp.zeros_like(along)
        for k in range(vectors):
            along -= reals[k] * values[k]
            turned += imags[k] * values[k]
        result = along.reshape(chunk, columns) - lane_swap(turned.reshape(chunk, columns))
        out_ref[pl.ds(place, count // height)] = result.reshape(chunk // height, height, columns)[: count // height]

    def body(i, carry):
        write(pl.multiple_of(i * chunk, chunk), i * (chunk // height), chunk)
        return carry

    lax.fori_loop(0, rows // chunk, body, 0)
    if rows % chunk:
        write(rows // chunk * chunk, rows // chunk * (chunk // height), rows % chunk)


def exchanged(value):
    return lax.all_to_all(value, "pair", split_axis=0, concat_axis=0, tiled=True)


def neighbours(value):
    count = lax.axis_size("blk")
    up = [(i, i + 1) for i in range(count - 1)]
    down = [(j, i) for i, j in up]
    return lax.ppermute(value, "blk", up), lax.ppermute(value, "blk", down)


def shards(basis, mie_coeffs, rot_table, axial_table, pair_table, pair_count):
    vectors, quarter, modes, columns = basis.shape
    ways = lax.axis_size("pair")
    blk_ways = lax.axis_size("blk")
    tables = rot_table.shape[0]
    slots = pair_table.shape[1]
    own = quarter * ways
    part = columns // 2 // ways
    group = own * part
    size = rounded_up(modes, 128)
    rows = quarter * modes
    full = rounded_up(rows, 8)
    pairs_of_vectors = vectors // 2
    height = 4

    basis_rows = in_hbm(basis.transpose(0, 2, 1, 3).reshape(pairs_of_vectors, 2 * rows, columns))
    mie_rows = in_hbm(mie_coeffs.transpose(1, 0, 2).reshape(rows // height, height, columns))
    rot_rows = in_hbm(rot_table.transpose(1, 0, 2).reshape(modes * tables, modes))
    axial_rows = in_hbm(axial_table.transpose(0, 2, 1, 3))
    pair_rows = in_hbm(pair_table.transpose(2, 0, 1))

    pieces_shape = (ways, 2, quarter, part, size)
    pieces = pl.pallas_call(
        functools.partial(pack_kernel, quarter, modes, ways, own),
        in_specs=[hbm(), pl.BlockSpec(memory_space=pltpu.SMEM), hbm()],
        out_specs=whole(),
        out_shape=jax.ShapeDtypeStruct(pieces_shape, BF16),
        scratch_shapes=[
            pltpu.VMEM(pair_rows.shape, jnp.int32),
            pltpu.VMEM((full, columns), F32),
            pltpu.VMEM((size, columns), F32),
            pltpu.VMEM((2 * slots, slots), F32),
            pltpu.SemaphoreType.DMA((2,)),
        ],
        compiler_params=params(16),
        name="pack",
    )(pair_rows, pair_count, basis_rows)
    tall = rounded_up(rows + full, 8)
    pieces, basis_later = lax.optimization_barrier((pieces, basis_rows))
    own_pieces = exchanged(pieces)
    line = pl.pallas_call(
        functools.partial(gram_kernel, quarter, modes),
        grid=(1,),
        in_specs=[hbm()],
        out_specs=pl.BlockSpec((1, 128), lambda i: (0, 0)),
        out_shape=pltpu.HBM((1, 128), F32),
        scratch_shapes=[
            pltpu.VMEM((pairs_of_vectors, tall, columns), F32),
            pltpu.VMEM((vectors, vectors, 8, columns), F32),
            pltpu.SemaphoreType.DMA((4, pairs_of_vectors, 2)),
        ],
        compiler_params=params(16),
        name="gram",
    )(basis_later)
    own_pieces, line, *inputs = lax.optimization_barrier((own_pieces, line, basis_rows, mie_rows, rot_rows, axial_rows))
    basis_rows, mie_rows, rot_rows, axial_rows = inputs
    below, above = neighbours(own_pieces)

    rotations, axials = pl.pallas_call(
        functools.partial(tables_kernel, modes, tables),
        grid=(tables,),
        in_specs=[
            pl.BlockSpec((1, modes, 2, modes), lambda g: (g, 0, 0, 0)),
            pl.BlockSpec((size, modes), lambda g: (g, 0)),
        ],
        out_specs=[
            pl.BlockSpec((tables, size // tables, size), lambda g: (0, g, 0)),
            pl.BlockSpec((1, 2 * size, size), lambda g: (g, 0, 0)),
        ],
        out_shape=[
            jax.ShapeDtypeStruct((tables, size, size), BF16),
            jax.ShapeDtypeStruct((tables, 2 * size, size), BF16),
        ],
        scratch_shapes=[pltpu.VMEM((2 * size, size), BF16)],
        compiler_params=params(32),
        cost_estimate=pl.CostEstimate(flops=tables * 8 * 256 * 256 * size, bytes_accessed=6 * tables * size * size * 2, transcendentals=0),
        name="tables",
    )(axial_rows, rot_rows)

    below, above, rotations, axials = lax.optimization_barrier((below, above, rotations, axials))

    together = 2 if tables % 2 == 0 else 1
    field, blocks, mies = pl.pallas_call(
        functools.partial(field_kernel, own, modes, together),
        in_specs=[whole()] * 5 + [hbm()] * 2,
        out_specs=[whole()] * 3,
        out_shape=[
            jax.ShapeDtypeStruct(pieces_shape, BF16),
            jax.ShapeDtypeStruct((pairs_of_vectors, tall, columns), F32),
            jax.ShapeDtypeStruct((full // height, height, columns), F32),
        ],
        scratch_shapes=[
            pltpu.VMEM((3, 2, size // 128, group, 128), F32),
            pltpu.VMEM((tables, 4 * group, size), BF16),
            pltpu.VMEM((2 * group, size), F32),
            pltpu.SemaphoreType.DMA((pairs_of_vectors + 1,)),
        ],
        compiler_params=params(20),
        name="field",
    )(rotations, axials, below, own_pieces, above, basis_rows, mie_rows)
    field_pieces = exchanged(field)

    image, sums = pl.pallas_call(
        functools.partial(image_kernel, quarter, modes),
        in_specs=[whole()] * 4,
        out_specs=[whole()] * 2,
        out_shape=[jax.ShapeDtypeStruct((full, columns), F32), jax.ShapeDtypeStruct((ways * blk_ways, 1, 128), F32)],
        scratch_shapes=[pltpu.VMEM((full, columns), F32)],
        compiler_params=params(8),
        name="image",
    )(blocks, mies, line, field_pieces)
    sums = lax.all_to_all(sums, ("blk", "pair"), split_axis=0, concat_axis=0, tiled=True)

    mean_scale = 1.0 / (own * blk_ways * modes * columns)
    dots, next_rows = pl.pallas_call(
        functools.partial(remainder_kernel, quarter, modes, mean_scale),
        in_specs=[whole()] * 3,
        out_specs=[whole(), whole()],
        out_shape=[jax.ShapeDtypeStruct((2, vectors), F32), jax.ShapeDtypeStruct((rows // height, height, columns), F32)],
        compiler_params=params(16),
        name="remainder",
    )(sums, blocks, image)
    return dots, next_rows.reshape(modes, quarter, columns).transpose(1, 0, 2)


def solution(mesh):
    placed = (
        P(None, ("blk", "pair"), None, None),
        P(("blk", "pair"), None, None),
        P(),
        P(),
        P("blk", None, None),
        P("blk"),
    )
    return jax.shard_map(
        shards,
        mesh=mesh,
        in_specs=placed,
        out_specs=(P(), P(("blk", "pair"), None, None)),
        check_vma=False,
    )
```

```python
import functools

import jax
import jax.numpy as jnp
from jax import lax
from jax.experimental import pallas as pl
from jax.experimental.pallas import tpu as pltpu
from jax.sharding import PartitionSpec as P

MIB = 1024 * 1024
F32 = jnp.float32
BF16 = jnp.bfloat16


def params(mib):
    return pltpu.CompilerParams(vmem_limit_bytes=mib * MIB)


def hbm():
    return pl.BlockSpec(memory_space=pltpu.HBM)


def whole():
    return pl.BlockSpec(memory_space=pltpu.VMEM)


def in_hbm(value):
    return pltpu.with_memory_space_constraint(value, pltpu.HBM)


def rounded_up(value, unit):
    return (value + unit - 1) // unit * unit


def iota(shape, dim):
    return lax.broadcasted_iota(jnp.int32, shape, dim)


def dot_nn(left, right):
    return lax.dot_general(left, right, (((1,), (0,)), ((), ())), preferred_element_type=F32)


def dot_nt(left, right):
    return lax.dot_general(left, right, (((1,), (1,)), ((), ())), preferred_element_type=F32)


def pack_kernel(quarter, modes, ways, own, list_ref, count_ref, basis_ref, out_ref, pair_rows_ref, lines_ref, pad_ref, codes_ref, sems):
    full, columns = lines_ref.shape
    rows = quarter * modes
    part = columns // 2 // ways
    copy = pltpu.make_async_copy(basis_ref.at[basis_ref.shape[0] - 1, pl.ds(2 * rows - full, full)], lines_ref, sems.at[0])
    copy.start()
    list_copy = pltpu.make_async_copy(list_ref, pair_rows_ref, sems.at[1])
    list_copy.start()
    pad_ref[...] = jnp.zeros_like(pad_ref)
    list_copy.wait()
    slots = pair_rows_ref.shape[2]
    live = iota((1, slots), 1) < count_ref[0]
    marks = jnp.where(live, own * (pair_rows_ref[2] + 1) + pair_rows_ref[0], 0)
    line = iota((slots, slots), 0)
    stacked = jnp.where(line == 0, marks, jnp.where(line == 1, pair_rows_ref[1], 0))
    turned = jnp.transpose(stacked.astype(F32))
    codes_ref[0:slots, :] = turned
    codes_ref[slots : 2 * slots, :] = pltpu.roll(turned, slots - 1, axis=1)
    share = 2 * quarter * part
    mine = codes_ref[pl.ds(pl.multiple_of(lax.axis_index("pair") * share, share), share), :][:, 0:1]
    copy.wait()
    turned = []
    for j in range(quarter):
        pad_ref[0:modes, :] = lines_ref[pl.ds(full - rows + j, modes, quarter), :]
        turned.append(jnp.transpose(pad_ref[...]))
    height = part * quarter // out_ref.shape[2]
    for c in range(2):
        for o in range(out_ref.shape[2]):
            place = (c * out_ref.shape[2] + o) * height
            codes = mine[place : place + height]
            for p in range(ways):
                row = c * (columns // 2) + p * part + o * (height // quarter)
                piece = jnp.concatenate([value[row : row + height // quarter] for value in turned], axis=0)
                out_ref[p, c, o] = jnp.where(iota(piece.shape, 1) == modes, codes, piece).astype(BF16)


def tables_kernel(modes, tables, axial_ref, rot_ref, rot_out_ref, axial_out_ref, lines_ref):
    step = pl.program_id(0)
    size = rot_out_ref.shape[2]
    chunk = 256

    @pl.when(step == 0)
    def _():
        lines_ref[...] = jnp.zeros_like(lines_ref)

    out_row, in_row = iota((chunk, chunk), 0), iota((chunk, chunk), 1)
    each = chunk // 2
    halves = (in_row == 2 * lax.rem(out_row, each) + lax.div(out_row, each)).astype(F32).astype(BF16)
    lines_ref[0 : 2 * modes, 0:modes] = axial_ref[0].reshape(2 * modes, modes)
    for q in range(2 * size // chunk):
        sorted_rows = dot_nn(halves, lines_ref[q * chunk : (q + 1) * chunk, :]).astype(BF16)
        for c in range(2):
            axial_out_ref[0, c * size + q * each : c * size + (q + 1) * each, :] = sorted_rows[c * each : (c + 1) * each]
    each = chunk // tables
    entries = (in_row == tables * lax.rem(out_row, each) + lax.div(out_row, each)).astype(F32).astype(BF16)
    block = rot_ref.shape[0]
    left = tables * modes - step * block
    rows = jnp.where(iota((block, modes), 0) < left, rot_ref[...], jnp.zeros((), BF16))
    rot_out_ref[:, :, size - 128 : size] = jnp.zeros((tables, block // tables, 128), BF16)
    for q in range(block // chunk):
        sorted_rows = dot_nn(entries, rows[q * chunk : (q + 1) * chunk]).astype(BF16)
        for g in range(tables):
            rot_out_ref[g, q * each : (q + 1) * each, 0:modes] = sorted_rows[g * each : (g + 1) * each]


def swapped(value):
    half = value.shape[0] // 2
    return jnp.concatenate([-value[half:], value[:half]], axis=0)


def pair_counts(own, tables, lane, refs):
    ways, parts, octets, height, size = refs[0].shape
    group = ways * octets * height
    wanted = iota((tables * own, group), 0) + own

    def one_hot(hit):
        return jnp.where(hit, 1.0, 0.0).astype(BF16)

    forward, backward = None, []
    for window, ref in enumerate(refs):
        values = ref[:, :, :, :, size - 128 : size].reshape(2 * group, 128).astype(F32)
        marks_column, sources_column = (values[h * group : (h + 1) * group, lane : lane + 1].astype(jnp.int32) for h in range(2))
        marks, sources = (jnp.transpose(values[h * group : (h + 1) * group])[lane : lane + 1].astype(jnp.int32) for h in range(2))
        if window == 1:
            forward = dot_nn(one_hot(marks == wanted), one_hot(sources_column == iota((group, 3 * own), 1)))
        block = sources - (2 - window) * own
        inside = (block >= 0) & (block < own) & (marks >= own)
        hits = one_hot(jnp.where(inside, lax.div(marks, own) * own + block, -1) == wanted)
        place = lax.rem(marks_column, own) + window * own
        backward.append(dot_nn(hits, one_hot(place == iota((group, 3 * own), 1))))
    return jnp.concatenate([forward, sum(backward)], axis=0).astype(BF16)


def folded(value):
    return jnp.sum(value.reshape(value.shape[0] // 8, 8, value.shape[1]), axis=0)


def field_kernel(
    own, modes, together, rot_ref, axial_ref, below_ref, own_ref, above_ref, basis_ref, mie_ref,
    out_ref, blocks_ref, mies_ref, sums_ref, total_ref, sems,
):
    tables, _, size = rot_ref.shape
    vector_blocks, vector_rows, columns = basis_ref.shape
    copies = [pltpu.make_async_copy(mie_ref, mies_ref, sems.at[vector_blocks])]
    for i in range(vector_blocks):
        copies.append(pltpu.make_async_copy(basis_ref.at[i], blocks_ref.at[i, pl.ds(0, vector_rows)], sems.at[i]))
    for copy in copies:
        copy.start()
    for i in range(vector_blocks):
        blocks_ref[i, vector_rows:, :] = jnp.zeros((blocks_ref.shape[1] - vector_rows, columns), F32)
    refs = (below_ref, own_ref, above_ref)
    ways, _, octets, height, _ = own_ref.shape
    quarter = own // ways
    each = height // quarter
    part = octets * each
    group = own * part
    counts = pair_counts(own, tables, modes % 128, refs)
    spread = jnp.where(iota((3 * own, 3 * own * each), 0) == lax.div(iota((3 * own, 3 * own * each), 1), each), 1.0, 0.0)
    counts = dot_nn(counts, spread.astype(BF16))
    sphere = lax.rem(iota(counts.shape, 1), each)
    chosen = jnp.concatenate([jnp.where(sphere == i, counts, 0.0).astype(BF16) for i in range(each)], axis=0)
    kinds = 2 * tables * own
    for c in range(2):
        for o in range(octets):
            blocks = jnp.concatenate([ref[:, c, o].reshape(ways * height, size) for ref in refs], axis=0)
            for i in range(0, each, 2):
                results = dot_nn(chosen[i * kinds : (i + 2) * kinds], blocks)
                for kind in range(2 * tables):
                    direction, g = kind // tables, kind % tables
                    rows = [results[start + kind * own : start + (kind + 1) * own] for start in (0, kinds)]
                    place = (direction * 2 + c) * group + (o * each + i) * own
                    sums_ref[g, place : place + 2 * own, :] = jnp.concatenate(rows, axis=0).astype(BF16)
    total_ref[...] = jnp.zeros_like(total_ref)

    def body(step, carry):
        entries = [step * together + i for i in range(together)]
        turned = [dot_nt(sums_ref[g], rot_ref[g]).astype(BF16) for g in entries]
        moved = []
        for g, both in zip(entries, turned):
            forward, backward = both[: 2 * group], both[2 * group :]
            result = dot_nt(forward, axial_ref[g, :size]) + dot_nt(swapped(forward), axial_ref[g, size:])
            result += dot_nn(jnp.concatenate([backward, swapped(backward)], axis=1), axial_ref[g])
            moved.append(result.astype(BF16))
        total_ref[...] += sum(dot_nn(value, rot_ref[g]) for g, value in zip(entries, moved))
        return carry

    lax.fori_loop(0, tables // together, body, 0)
    row, source = iota((2 * group, 2 * group), 0), iota((2 * group, 2 * group), 1)
    sphere, c = lax.rem(row, part), lax.rem(lax.div(row, quarter * part), 2)
    block = lax.div(row, 2 * quarter * part) * quarter + lax.rem(lax.div(row, part), quarter)
    order = jnp.where(source == c * group + sphere * own + block, 1.0, 0.0).astype(BF16)
    out_ref[...] = dot_nn(order, total_ref[...].astype(BF16)).astype(BF16).reshape(out_ref.shape)
    for copy in copies:
        copy.wait()


def lane_swap(value):
    half = value.shape[1] // 2
    rolled = pltpu.roll(value, half, axis=1)
    return jnp.where(iota(value.shape, 1) < half, -rolled, rolled)


def add_products(blocks_ref, products_ref, rows, first, count):
    vectors = products_ref.shape[0]
    values = []
    for k in range(vectors):
        start = k % 2 * rows + first
        value = blocks_ref[k // 2, start : start + count, :]
        if k % 2 == 0 and first + count > rows:
            value = jnp.where(iota(value.shape, 0) < rows - first, value, 0.0)
        values.append(value)
    for l in range(vectors):
        other = pltpu.roll(values[l], values[l].shape[1] // 2, axis=1)
        for k in range(l + 1):
            products_ref[k, l] += folded(values[k] * values[l])
            if k < l:
                products_ref[l, k] += folded(values[k] * other)


def products_line(products_ref):
    vectors, _, _, columns = products_ref.shape
    pairs = vectors * vectors
    totals = jnp.sum(products_ref[...].reshape(pairs, 8, columns), axis=1)
    pair = iota(totals.shape, 0)
    signed = (lax.div(pair, vectors) > lax.rem(pair, vectors)) & (iota(totals.shape, 1) >= columns // 2)
    totals = jnp.sum(jnp.where(signed, -totals, totals), axis=1, keepdims=True)
    row, lane = iota((vectors, 128), 0), iota((vectors, 128), 1)
    line = jnp.zeros((1, 128), F32)
    for k in range(vectors):
        column = totals[k * vectors : (k + 1) * vectors]
        line += jnp.sum(jnp.where(row + k * vectors == lane, column, 0.0), axis=0, keepdims=True)
    return line


def gram_kernel(quarter, modes, basis_ref, line_ref, blocks_ref, products_ref, sems):
    blocks, _, columns = basis_ref.shape
    rows = quarter * modes
    parts, chunk = 4, 32
    tile_end = rows // 8 * 8
    step = rounded_up(rows, 8 * parts) // parts
    even = [0] + [step * q for q in range(1, parts)] + [tile_end]
    odd = [tile_end] + [rounded_up(rows, 8) + step * q for q in range(1, parts)] + [2 * rows]
    copies = []
    for q in range(parts):
        for i in range(blocks):
            for side, cuts in enumerate((even, odd)):
                here = pl.ds(cuts[q], cuts[q + 1] - cuts[q])
                copies.append(pltpu.make_async_copy(basis_ref.at[i, here], blocks_ref.at[i, here], sems.at[q, i, side]))
    for copy in copies:
        copy.start()
    products_ref[...] = jnp.zeros_like(products_ref)
    for i in range(blocks):
        blocks_ref[i, 2 * rows :, :] = jnp.zeros((blocks_ref.shape[1] - 2 * rows, columns), F32)
    for q in range(parts):
        for copy in copies[2 * blocks * q : 2 * blocks * (q + 1)]:
            copy.wait()
        for first in range(step * q, min(step * (q + 1), rows), chunk):
            add_products(blocks_ref, products_ref, rows, first, chunk)
    line_ref[...] = products_line(products_ref)


def image_kernel(quarter, modes, blocks_ref, mie_ref, gram_ref, pieces_ref, image_ref, sums_ref, lines_ref):
    vectors = 2 * blocks_ref.shape[0]
    full, columns = image_ref.shape
    rows = quarter * modes
    ways, _, _, part, size = pieces_ref.shape
    lines_ref[rows:full, :] = jnp.zeros((full - rows, columns), F32)
    for j in range(quarter):
        turned = jnp.concatenate([pieces_ref[:, c, j].reshape(ways * part, size) for c in range(2)], axis=0)
        lines_ref[pl.ds(j, modes, quarter), :] = jnp.transpose(turned.astype(F32))[:modes]
    half = columns // 2
    chunk = 64
    totals = [jnp.zeros((8, columns), F32) for _ in range(2 * vectors + 1)]
    for first in range(0, full, chunk):
        here = slice(first, first + chunk)
        field = lines_ref[here, :]
        count = min(chunk, rows - first)
        height = mie_ref.shape[1]
        mie = mie_ref[first // height : (first + count) // height].reshape(count, columns)
        if count < chunk:
            mie = jnp.concatenate([mie, jnp.zeros((chunk - count, columns), F32)], axis=0)
        left = iota(mie.shape, 1) < half
        other = pltpu.roll(mie, half, axis=1)
        product = jnp.where(left, mie, other) * field + jnp.where(left, -other, mie) * pltpu.roll(field, half, axis=1)
        last = (vectors - 1) % 2 * rows + first
        image = blocks_ref[(vectors - 1) // 2, last : last + chunk, :] - product
        image_ref[here, :] = image
        turned = pltpu.roll(image, half, axis=1)
        for k in range(vectors):
            start = k % 2 * rows + first
            values = blocks_ref[k // 2, start : start + chunk, :]
            totals[2 * k] += folded(values * image)
            totals[2 * k + 1] += folded(values * turned)
        totals[2 * vectors] += folded(image * image)
    lane = iota(gram_ref.shape, 1)
    line = gram_ref[...]
    left = iota((8, columns), 1) < half
    for index, total in enumerate(totals):
        if index % 2 and index < 2 * vectors:
            total = jnp.where(left, total, -total)
        line = jnp.where(lane == vectors * vectors + index, jnp.sum(total, axis=(0, 1), keepdims=True), line)
    sums_ref[...] = jnp.broadcast_to(line[None], sums_ref.shape)


def remainder_kernel(quarter, modes, mean_scale, sums_ref, blocks_ref, image_ref, dots_ref, out_ref):
    vectors = 2 * blocks_ref.shape[0]
    full, columns = image_ref.shape
    rows = quarter * modes
    total = jnp.sum(sums_ref[...], axis=0)
    lane = iota(total.shape, 1)

    def lane_at(index):
        return jnp.sum(jnp.where(lane == index, total, 0.0), axis=1, keepdims=True)

    def on_lanes(parts, places):
        line = jnp.zeros(total.shape, F32)
        for k in range(vectors):
            line = jnp.where(places == k, parts[k], line)
        return line

    start = vectors * vectors
    real = [lane_at(start + 2 * k) * mean_scale for k in range(vectors)]
    imag = [lane_at(start + 2 * k + 1) * mean_scale for k in range(vectors)]
    real_line, imag_line = on_lanes(real, lane), on_lanes(imag, lane)
    dots_ref[0:1, :] = real_line[:, :vectors]
    dots_ref[1:2, :] = imag_line[:, :vectors]
    first_index, last_index = lax.div(lane, vectors), lax.rem(lane, vectors)
    real_first, real_last = on_lanes(real, first_index), on_lanes(real, last_index)
    imag_first, imag_last = on_lanes(imag, first_index), on_lanes(imag, last_index)
    same = real_first * real_last + imag_first * imag_last
    cross = imag_last * real_first - real_last * imag_first
    often = jnp.where(first_index == last_index, 1.0, 2.0)
    spread = jnp.where(lane < start, total * often * jnp.where(first_index <= last_index, same, cross), 0.0)
    spread = jnp.sum(spread, axis=1, keepdims=True)
    inside = jnp.sum(real_line * real_line + imag_line * imag_line, axis=1, keepdims=True)
    norm_square = (lane_at(start + 2 * vectors) + spread) * mean_scale - 2.0 * inside
    scale = lax.rsqrt(norm_square)
    image_scale = jnp.broadcast_to(scale, (8, columns))
    reals = [jnp.broadcast_to(real[k] * scale, (8, columns)) for k in range(vectors)]
    imags = [jnp.broadcast_to(imag[k] * scale, (8, columns)) for k in range(vectors)]
    chunk = 64
    for first in range(0, full, chunk):
        here = slice(first, first + chunk)
        values = []
        for k in range(vectors):
            start = k % 2 * rows + first
            values.append(blocks_ref[k // 2, start : start + chunk, :].reshape(chunk // 8, 8, columns))
        along = image_ref[here, :].reshape(chunk // 8, 8, columns) * image_scale
        turned = jnp.zeros_like(along)
        for k in range(vectors):
            along -= reals[k] * values[k]
            turned += imags[k] * values[k]
        result = along.reshape(chunk, columns) - lane_swap(turned.reshape(chunk, columns))
        count = min(chunk, rows - first)
        height = out_ref.shape[1]
        out_ref[first // height : (first + count) // height] = result.reshape(chunk // height, height, columns)[: count // height]


def exchanged(value):
    return lax.all_to_all(value, "pair", split_axis=0, concat_axis=0, tiled=True)


def neighbours(value):
    count = lax.axis_size("blk")
    up = [(i, i + 1) for i in range(count - 1)]
    down = [(j, i) for i, j in up]
    return lax.ppermute(value, "blk", up), lax.ppermute(value, "blk", down)


def shards(basis, mie_coeffs, rot_table, axial_table, pair_table, pair_count):
    vectors, quarter, modes, columns = basis.shape
    ways = lax.axis_size("pair")
    blk_ways = lax.axis_size("blk")
    tables = rot_table.shape[0]
    slots = pair_table.shape[1]
    own = quarter * ways
    part = columns // 2 // ways
    group = own * part
    size = rounded_up(modes, 128)
    rows = quarter * modes
    full = rounded_up(rows, 8)
    pairs_of_vectors = vectors // 2

    basis_rows = in_hbm(basis.transpose(0, 2, 1, 3).reshape(pairs_of_vectors, 2 * rows, columns))
    mie_rows = in_hbm(mie_coeffs.transpose(1, 0, 2).reshape(rows // 4, 4, columns))
    rot_rows = in_hbm(rot_table.transpose(1, 0, 2).reshape(modes * tables, modes))
    axial_rows = in_hbm(axial_table.transpose(0, 2, 1, 3))
    pair_rows = in_hbm(pair_table.transpose(2, 0, 1))

    pieces_shape = (ways, 2, quarter, part, size)
    octets = part * quarter // 16
    pieces = pl.pallas_call(
        functools.partial(pack_kernel, quarter, modes, ways, own),
        in_specs=[hbm(), pl.BlockSpec(memory_space=pltpu.SMEM), hbm()],
        out_specs=whole(),
        out_shape=jax.ShapeDtypeStruct((ways, 2, octets, 16, size), BF16),
        scratch_shapes=[
            pltpu.VMEM(pair_rows.shape, jnp.int32),
            pltpu.VMEM((full, columns), F32),
            pltpu.VMEM((size, columns), F32),
            pltpu.VMEM((2 * slots, slots), F32),
            pltpu.SemaphoreType.DMA((2,)),
        ],
        compiler_params=params(16),
        name="pack",
    )(pair_rows, pair_count, basis_rows)
    tall = rounded_up(rows + full, 8)
    pieces, basis_later = lax.optimization_barrier((pieces, basis_rows))
    own_pieces = exchanged(pieces)
    line = pl.pallas_call(
        functools.partial(gram_kernel, quarter, modes),
        grid=(1,),
        in_specs=[hbm()],
        out_specs=pl.BlockSpec((1, 128), lambda i: (0, 0)),
        out_shape=pltpu.HBM((1, 128), F32),
        scratch_shapes=[
            pltpu.VMEM((pairs_of_vectors, tall, columns), F32),
            pltpu.VMEM((vectors, vectors, 8, columns), F32),
            pltpu.SemaphoreType.DMA((4, pairs_of_vectors, 2)),
        ],
        compiler_params=params(16),
        name="gram",
    )(basis_later)
    own_pieces, line, *inputs = lax.optimization_barrier((own_pieces, line, basis_rows, mie_rows, rot_rows, axial_rows))
    basis_rows, mie_rows, rot_rows, axial_rows = inputs
    below, above = neighbours(own_pieces)

    rotations, axials = pl.pallas_call(
        functools.partial(tables_kernel, modes, tables),
        grid=(tables,),
        in_specs=[
            pl.BlockSpec((1, modes, 2, modes), lambda g: (g, 0, 0, 0)),
            pl.BlockSpec((size, modes), lambda g: (g, 0)),
        ],
        out_specs=[
            pl.BlockSpec((tables, size // tables, size), lambda g: (0, g, 0)),
            pl.BlockSpec((1, 2 * size, size), lambda g: (g, 0, 0)),
        ],
        out_shape=[
            jax.ShapeDtypeStruct((tables, size, size), BF16),
            jax.ShapeDtypeStruct((tables, 2 * size, size), BF16),
        ],
        scratch_shapes=[pltpu.VMEM((2 * size, size), BF16)],
        compiler_params=params(32),
        cost_estimate=pl.CostEstimate(flops=tables * 8 * 256 * 256 * size, bytes_accessed=6 * tables * size * size * 2, transcendentals=0),
        name="tables",
    )(axial_rows, rot_rows)

    below, above, rotations, axials = lax.optimization_barrier((below, above, rotations, axials))

    together = 2 if tables % 2 == 0 else 1
    field, blocks, mies = pl.pallas_call(
        functools.partial(field_kernel, own, modes, together),
        in_specs=[whole()] * 5 + [hbm()] * 2,
        out_specs=[whole()] * 3,
        out_shape=[
            jax.ShapeDtypeStruct(pieces_shape, BF16),
            jax.ShapeDtypeStruct((pairs_of_vectors, tall, columns), F32),
            jax.ShapeDtypeStruct(mie_rows.shape, F32),
        ],
        scratch_shapes=[
            pltpu.VMEM((tables, 4 * group, size), BF16),
            pltpu.VMEM((2 * group, size), F32),
            pltpu.SemaphoreType.DMA((pairs_of_vectors + 1,)),
        ],
        compiler_params=params(20),
        name="field",
    )(rotations, axials, below, own_pieces, above, basis_rows, mie_rows)
    field_pieces = exchanged(field)

    image, sums = pl.pallas_call(
        functools.partial(image_kernel, quarter, modes),
        in_specs=[whole()] * 4,
        out_specs=[whole()] * 2,
        out_shape=[jax.ShapeDtypeStruct((full, columns), F32), jax.ShapeDtypeStruct((ways * blk_ways, 1, 128), F32)],
        scratch_shapes=[pltpu.VMEM((full, columns), F32)],
        compiler_params=params(8),
        name="image",
    )(blocks, mies, line, field_pieces)
    sums = lax.all_to_all(sums, ("blk", "pair"), split_axis=0, concat_axis=0, tiled=True)

    height = 4
    mean_scale = 1.0 / (own * blk_ways * modes * columns)
    dots, next_rows = pl.pallas_call(
        functools.partial(remainder_kernel, quarter, modes, mean_scale),
        in_specs=[whole()] * 3,
        out_specs=[whole(), whole()],
        out_shape=[jax.ShapeDtypeStruct((2, vectors), F32), jax.ShapeDtypeStruct((rows // height, height, columns), F32)],
        compiler_params=params(16),
        name="remainder",
    )(sums, blocks, image)
    return dots, next_rows.reshape(modes, quarter, columns).transpose(1, 0, 2)


def solution(mesh):
    placed = (
        P(None, ("blk", "pair"), None, None),
        P(("blk", "pair"), None, None),
        P(),
        P(),
        P("blk", None, None),
        P("blk"),
    )
    return jax.shard_map(
        shards,
        mesh=mesh,
        in_specs=placed,
        out_specs=(P(), P(("blk", "pair"), None, None)),
        check_vma=False,
    )
```

```python
import functools

import jax
import jax.numpy as jnp
from jax import lax
from jax.experimental import pallas as pl
from jax.experimental.pallas import tpu as pltpu
from jax.sharding import PartitionSpec as P

MIB = 1024 * 1024
F32 = jnp.float32
BF16 = jnp.bfloat16


def params(mib):
    return pltpu.CompilerParams(vmem_limit_bytes=mib * MIB)


def hbm():
    return pl.BlockSpec(memory_space=pltpu.HBM)


def whole():
    return pl.BlockSpec(memory_space=pltpu.VMEM)


def in_hbm(value):
    return pltpu.with_memory_space_constraint(value, pltpu.HBM)


def rounded_up(value, unit):
    return (value + unit - 1) // unit * unit


def iota(shape, dim):
    return lax.broadcasted_iota(jnp.int32, shape, dim)


def dot_nn(left, right):
    return lax.dot_general(left, right, (((1,), (0,)), ((), ())), preferred_element_type=F32)


def dot_nt(left, right):
    return lax.dot_general(left, right, (((1,), (1,)), ((), ())), preferred_element_type=F32)


def pack_kernel(quarter, modes, ways, own, list_ref, count_ref, basis_ref, out_ref, pair_rows_ref, lines_ref, pad_ref, codes_ref, sems):
    full, columns = lines_ref.shape
    rows = quarter * modes
    part = columns // 2 // ways
    copy = pltpu.make_async_copy(basis_ref.at[basis_ref.shape[0] - 1, pl.ds(2 * rows - full, full)], lines_ref, sems.at[0])
    copy.start()
    list_copy = pltpu.make_async_copy(list_ref, pair_rows_ref, sems.at[1])
    list_copy.start()
    pad_ref[...] = jnp.zeros_like(pad_ref)
    list_copy.wait()
    slots = pair_rows_ref.shape[2]
    live = iota((1, slots), 1) < count_ref[0]
    marks = jnp.where(live, own * (pair_rows_ref[2] + 1) + pair_rows_ref[0], 0)
    line = iota((slots, slots), 0)
    stacked = jnp.where(line == 0, marks, jnp.where(line == 1, pair_rows_ref[1], 0))
    turned = jnp.transpose(stacked.astype(F32))
    codes_ref[0:slots, :] = turned
    codes_ref[slots : 2 * slots, :] = pltpu.roll(turned, slots - 1, axis=1)
    share = 2 * quarter * part
    mine = codes_ref[pl.ds(pl.multiple_of(lax.axis_index("pair") * share, share), share), :][:, 0:1]
    copy.wait()
    turned = []
    for j in range(quarter):
        pad_ref[0:modes, :] = lines_ref[pl.ds(full - rows + j, modes, quarter), :]
        turned.append(jnp.transpose(pad_ref[...]))
    height = part * quarter // out_ref.shape[2]
    for c in range(2):
        for o in range(out_ref.shape[2]):
            place = (c * out_ref.shape[2] + o) * height
            codes = mine[place : place + height]
            for p in range(ways):
                row = c * (columns // 2) + p * part + o * (height // quarter)
                piece = jnp.concatenate([value[row : row + height // quarter] for value in turned], axis=0)
                out_ref[p, c, o] = jnp.where(iota(piece.shape, 1) == modes, codes, piece).astype(BF16)


def tables_kernel(modes, tables, axial_ref, rot_ref, rot_out_ref, axial_out_ref, lines_ref):
    step = pl.program_id(0)
    size = rot_out_ref.shape[2]
    chunk = 256

    @pl.when(step == 0)
    def _():
        lines_ref[...] = jnp.zeros_like(lines_ref)

    out_row, in_row = iota((chunk, chunk), 0), iota((chunk, chunk), 1)
    each = chunk // 2
    halves = (in_row == 2 * lax.rem(out_row, each) + lax.div(out_row, each)).astype(F32).astype(BF16)
    lines_ref[0 : 2 * modes, 0:modes] = axial_ref[0].reshape(2 * modes, modes)
    for q in range(2 * size // chunk):
        sorted_rows = dot_nn(halves, lines_ref[q * chunk : (q + 1) * chunk, :]).astype(BF16)
        for c in range(2):
            axial_out_ref[0, c * size + q * each : c * size + (q + 1) * each, :] = sorted_rows[c * each : (c + 1) * each]
    each = chunk // tables
    entries = (in_row == tables * lax.rem(out_row, each) + lax.div(out_row, each)).astype(F32).astype(BF16)
    block = rot_ref.shape[0]
    left = tables * modes - step * block
    rows = jnp.where(iota((block, modes), 0) < left, rot_ref[...], jnp.zeros((), BF16))
    rot_out_ref[:, :, size - 128 : size] = jnp.zeros((tables, block // tables, 128), BF16)
    for q in range(block // chunk):
        sorted_rows = dot_nn(entries, rows[q * chunk : (q + 1) * chunk]).astype(BF16)
        for g in range(tables):
            rot_out_ref[g, q * each : (q + 1) * each, 0:modes] = sorted_rows[g * each : (g + 1) * each]


def swapped(value):
    half = value.shape[0] // 2
    return jnp.concatenate([-value[half:], value[:half]], axis=0)


def pair_counts(own, tables, lane, refs):
    ways, parts, octets, height, size = refs[0].shape
    group = ways * octets * height
    wanted = iota((tables * own, group), 0) + own

    def one_hot(hit):
        return jnp.where(hit, 1.0, 0.0).astype(BF16)

    forward, backward = None, []
    for window, ref in enumerate(refs):
        values = ref[:, :, :, :, size - 128 : size].reshape(2 * group, 128).astype(F32)
        marks_column, sources_column = (values[h * group : (h + 1) * group, lane : lane + 1].astype(jnp.int32) for h in range(2))
        marks, sources = (jnp.transpose(values[h * group : (h + 1) * group])[lane : lane + 1].astype(jnp.int32) for h in range(2))
        if window == 1:
            forward = dot_nn(one_hot(marks == wanted), one_hot(sources_column == iota((group, 3 * own), 1)))
        block = sources - (2 - window) * own
        inside = (block >= 0) & (block < own) & (marks >= own)
        hits = one_hot(jnp.where(inside, lax.div(marks, own) * own + block, -1) == wanted)
        place = lax.rem(marks_column, own) + window * own
        backward.append(dot_nn(hits, one_hot(place == iota((group, 3 * own), 1))))
    return jnp.concatenate([forward, sum(backward)], axis=0).astype(BF16)


def folded(value):
    return jnp.sum(value.reshape(value.shape[0] // 8, 8, value.shape[1]), axis=0)


def field_kernel(
    own, modes, together, rot_ref, axial_ref, below_ref, own_ref, above_ref, basis_ref, mie_ref,
    *rest,
):
    outs, (blocks_ref, mies_ref, sums_ref, total_ref, sems) = rest[:-5], rest[-5:]
    tables, _, size = rot_ref.shape
    vector_blocks, vector_rows, columns = basis_ref.shape
    copies = [pltpu.make_async_copy(mie_ref, mies_ref, sems.at[vector_blocks])]
    for i in range(vector_blocks):
        copies.append(pltpu.make_async_copy(basis_ref.at[i], blocks_ref.at[i, pl.ds(0, vector_rows)], sems.at[i]))
    for copy in copies:
        copy.start()
    for i in range(vector_blocks):
        blocks_ref[i, vector_rows:, :] = jnp.zeros((blocks_ref.shape[1] - vector_rows, columns), F32)
    refs = (below_ref, own_ref, above_ref)
    ways, _, octets, height, _ = own_ref.shape
    quarter = own // ways
    each = height // quarter
    part = octets * each
    group = own * part
    counts = pair_counts(own, tables, modes % 128, refs)
    spread = jnp.where(iota((3 * own, 3 * own * each), 0) == lax.div(iota((3 * own, 3 * own * each), 1), each), 1.0, 0.0)
    counts = dot_nn(counts, spread.astype(BF16))
    sphere = lax.rem(iota(counts.shape, 1), each)
    chosen = jnp.concatenate([jnp.where(sphere == i, counts, 0.0).astype(BF16) for i in range(each)], axis=0)
    kinds = 2 * tables * own
    for c in range(2):
        for o in range(octets):
            blocks = jnp.concatenate([ref[:, c, o].reshape(ways * height, size) for ref in refs], axis=0)
            for i in range(0, each, 2):
                results = dot_nn(chosen[i * kinds : (i + 2) * kinds], blocks)
                for kind in range(2 * tables):
                    direction, g = kind // tables, kind % tables
                    rows = [results[start + kind * own : start + (kind + 1) * own] for start in (0, kinds)]
                    place = (direction * 2 + c) * group + (o * each + i) * own
                    sums_ref[g, place : place + 2 * own, :] = jnp.concatenate(rows, axis=0).astype(BF16)
    total_ref[...] = jnp.zeros_like(total_ref)

    def body(step, carry):
        entries = [step * together + i for i in range(together)]
        turned = [dot_nt(sums_ref[g], rot_ref[g]).astype(BF16) for g in entries]
        moved = []
        for g, both in zip(entries, turned):
            forward, backward = both[: 2 * group], both[2 * group :]
            result = dot_nt(forward, axial_ref[g, :size]) + dot_nt(swapped(forward), axial_ref[g, size:])
            result += dot_nn(jnp.concatenate([backward, swapped(backward)], axis=1), axial_ref[g])
            moved.append(result.astype(BF16))
        total_ref[...] += sum(dot_nn(value, rot_ref[g]) for g, value in zip(entries, moved))
        return carry

    lax.fori_loop(0, tables // together, body, 0)
    row, source = iota((2 * group, 2 * group), 0), iota((2 * group, 2 * group), 1)
    sphere, c = lax.rem(row, part), lax.rem(lax.div(row, quarter * part), 2)
    owner = lax.div(row, 2 * quarter * part) ^ lax.axis_index("pair")
    block = owner * quarter + lax.rem(lax.div(row, part), quarter)
    order = jnp.where(source == c * group + sphere * own + block, 1.0, 0.0).astype(BF16)
    result = dot_nn(order, total_ref[...].astype(BF16)).astype(BF16)
    share = 2 * quarter * part
    for i, out_ref in enumerate(outs):
        out_ref[...] = result[i * share : (i + 1) * share].reshape(out_ref.shape)
    for copy in copies:
        copy.wait()


def lane_swap(value):
    half = value.shape[1] // 2
    rolled = pltpu.roll(value, half, axis=1)
    return jnp.where(iota(value.shape, 1) < half, -rolled, rolled)


def add_products(blocks_ref, products_ref, rows, first, count):
    vectors = products_ref.shape[0]
    values = []
    for k in range(vectors):
        start = k % 2 * rows + first
        value = blocks_ref[k // 2, start : start + count, :]
        if k % 2 == 0 and first + count > rows:
            value = jnp.where(iota(value.shape, 0) < rows - first, value, 0.0)
        values.append(value)
    for l in range(vectors):
        other = pltpu.roll(values[l], values[l].shape[1] // 2, axis=1)
        for k in range(l + 1):
            products_ref[k, l] += folded(values[k] * values[l])
            if k < l:
                products_ref[l, k] += folded(values[k] * other)


def products_line(products_ref):
    vectors, _, _, columns = products_ref.shape
    pairs = vectors * vectors
    totals = jnp.sum(products_ref[...].reshape(pairs, 8, columns), axis=1)
    pair = iota(totals.shape, 0)
    signed = (lax.div(pair, vectors) > lax.rem(pair, vectors)) & (iota(totals.shape, 1) >= columns // 2)
    totals = jnp.sum(jnp.where(signed, -totals, totals), axis=1, keepdims=True)
    row, lane = iota((vectors, 128), 0), iota((vectors, 128), 1)
    line = jnp.zeros((1, 128), F32)
    for k in range(vectors):
        column = totals[k * vectors : (k + 1) * vectors]
        line += jnp.sum(jnp.where(row + k * vectors == lane, column, 0.0), axis=0, keepdims=True)
    return line


def gram_kernel(quarter, modes, basis_ref, line_ref, blocks_ref, products_ref, sems):
    blocks, _, columns = basis_ref.shape
    rows = quarter * modes
    parts, chunk = 4, 32
    tile_end = rows // 8 * 8
    step = rounded_up(rows, 8 * parts) // parts
    even = [0] + [step * q for q in range(1, parts)] + [tile_end]
    odd = [tile_end] + [rounded_up(rows, 8) + step * q for q in range(1, parts)] + [2 * rows]
    copies = []
    for q in range(parts):
        for i in range(blocks):
            for side, cuts in enumerate((even, odd)):
                here = pl.ds(cuts[q], cuts[q + 1] - cuts[q])
                copies.append(pltpu.make_async_copy(basis_ref.at[i, here], blocks_ref.at[i, here], sems.at[q, i, side]))
    for copy in copies:
        copy.start()
    products_ref[...] = jnp.zeros_like(products_ref)
    for i in range(blocks):
        blocks_ref[i, 2 * rows :, :] = jnp.zeros((blocks_ref.shape[1] - 2 * rows, columns), F32)
    for q in range(parts):
        for copy in copies[2 * blocks * q : 2 * blocks * (q + 1)]:
            copy.wait()
        for first in range(step * q, min(step * (q + 1), rows), chunk):
            add_products(blocks_ref, products_ref, rows, first, chunk)
    line_ref[...] = products_line(products_ref)


def image_kernel(quarter, modes, blocks_ref, mie_ref, gram_ref, *rest):
    pieces, (image_ref, sums_ref, lines_ref, whole_ref) = rest[:-4], rest[-4:]
    vectors = 2 * blocks_ref.shape[0]
    full, columns = image_ref.shape
    rows = quarter * modes
    part = pieces[0].shape[2]
    for i, piece_ref in enumerate(pieces):
        place = pl.multiple_of((lax.axis_index("pair") ^ i) * part, part)
        for j in range(quarter):
            for c in range(2):
                whole_ref[j, pl.ds(c * (columns // 2) + place, part), :] = piece_ref[c, j]
    lines_ref[rows:full, :] = jnp.zeros((full - rows, columns), F32)
    for j in range(quarter):
        lines_ref[pl.ds(j, modes, quarter), :] = jnp.transpose(whole_ref[j].astype(F32))[:modes]
    half = columns // 2
    chunk = 64
    totals = [jnp.zeros((8, columns), F32) for _ in range(2 * vectors + 1)]
    for first in range(0, full, chunk):
        here = slice(first, first + chunk)
        field = lines_ref[here, :]
        count = min(chunk, rows - first)
        height = mie_ref.shape[1]
        mie = mie_ref[first // height : (first + count) // height].reshape(count, columns)
        if count < chunk:
            mie = jnp.concatenate([mie, jnp.zeros((chunk - count, columns), F32)], axis=0)
        left = iota(mie.shape, 1) < half
        other = pltpu.roll(mie, half, axis=1)
        product = jnp.where(left, mie, other) * field + jnp.where(left, -other, mie) * pltpu.roll(field, half, axis=1)
        last = (vectors - 1) % 2 * rows + first
        image = blocks_ref[(vectors - 1) // 2, last : last + chunk, :] - product
        image_ref[here, :] = image
        turned = pltpu.roll(image, half, axis=1)
        for k in range(vectors):
            start = k % 2 * rows + first
            values = blocks_ref[k // 2, start : start + chunk, :]
            totals[2 * k] += folded(values * image)
            totals[2 * k + 1] += folded(values * turned)
        totals[2 * vectors] += folded(image * image)
    lane = iota(gram_ref.shape, 1)
    line = gram_ref[...]
    left = iota((8, columns), 1) < half
    for index, total in enumerate(totals):
        if index % 2 and index < 2 * vectors:
            total = jnp.where(left, total, -total)
        line = jnp.where(lane == vectors * vectors + index, jnp.sum(total, axis=(0, 1), keepdims=True), line)
    sums_ref[...] = jnp.broadcast_to(line[None], sums_ref.shape)


def remainder_kernel(quarter, modes, mean_scale, sums_ref, blocks_ref, image_ref, dots_ref, out_ref):
    vectors = 2 * blocks_ref.shape[0]
    full, columns = image_ref.shape
    rows = quarter * modes
    total = jnp.sum(sums_ref[...], axis=0)
    lane = iota(total.shape, 1)

    def lane_at(index):
        return jnp.sum(jnp.where(lane == index, total, 0.0), axis=1, keepdims=True)

    def on_lanes(parts, places):
        line = jnp.zeros(total.shape, F32)
        for k in range(vectors):
            line = jnp.where(places == k, parts[k], line)
        return line

    start = vectors * vectors
    real = [lane_at(start + 2 * k) * mean_scale for k in range(vectors)]
    imag = [lane_at(start + 2 * k + 1) * mean_scale for k in range(vectors)]
    real_line, imag_line = on_lanes(real, lane), on_lanes(imag, lane)
    dots_ref[0:1, :] = real_line[:, :vectors]
    dots_ref[1:2, :] = imag_line[:, :vectors]
    first_index, last_index = lax.div(lane, vectors), lax.rem(lane, vectors)
    real_first, real_last = on_lanes(real, first_index), on_lanes(real, last_index)
    imag_first, imag_last = on_lanes(imag, first_index), on_lanes(imag, last_index)
    same = real_first * real_last + imag_first * imag_last
    cross = imag_last * real_first - real_last * imag_first
    often = jnp.where(first_index == last_index, 1.0, 2.0)
    spread = jnp.where(lane < start, total * often * jnp.where(first_index <= last_index, same, cross), 0.0)
    spread = jnp.sum(spread, axis=1, keepdims=True)
    inside = jnp.sum(real_line * real_line + imag_line * imag_line, axis=1, keepdims=True)
    norm_square = (lane_at(start + 2 * vectors) + spread) * mean_scale - 2.0 * inside
    scale = lax.rsqrt(norm_square)
    image_scale = jnp.broadcast_to(scale, (8, columns))
    reals = [jnp.broadcast_to(real[k] * scale, (8, columns)) for k in range(vectors)]
    imags = [jnp.broadcast_to(imag[k] * scale, (8, columns)) for k in range(vectors)]
    chunk = 64
    for first in range(0, full, chunk):
        here = slice(first, first + chunk)
        values = []
        for k in range(vectors):
            start = k % 2 * rows + first
            values.append(blocks_ref[k // 2, start : start + chunk, :].reshape(chunk // 8, 8, columns))
        along = image_ref[here, :].reshape(chunk // 8, 8, columns) * image_scale
        turned = jnp.zeros_like(along)
        for k in range(vectors):
            along -= reals[k] * values[k]
            turned += imags[k] * values[k]
        result = along.reshape(chunk, columns) - lane_swap(turned.reshape(chunk, columns))
        count = min(chunk, rows - first)
        height = out_ref.shape[1]
        out_ref[first // height : (first + count) // height] = result.reshape(chunk // height, height, columns)[: count // height]


def exchanged(value):
    return lax.all_to_all(value, "pair", split_axis=0, concat_axis=0, tiled=True)


def neighbours(value):
    count = lax.axis_size("blk")
    up = [(i, i + 1) for i in range(count - 1)]
    down = [(j, i) for i, j in up]
    return lax.ppermute(value, "blk", up), lax.ppermute(value, "blk", down)


def shards(basis, mie_coeffs, rot_table, axial_table, pair_table, pair_count):
    vectors, quarter, modes, columns = basis.shape
    ways = lax.axis_size("pair")
    blk_ways = lax.axis_size("blk")
    tables = rot_table.shape[0]
    slots = pair_table.shape[1]
    own = quarter * ways
    part = columns // 2 // ways
    group = own * part
    size = rounded_up(modes, 128)
    rows = quarter * modes
    full = rounded_up(rows, 8)
    pairs_of_vectors = vectors // 2

    basis_rows = in_hbm(basis.transpose(0, 2, 1, 3).reshape(pairs_of_vectors, 2 * rows, columns))
    mie_rows = in_hbm(mie_coeffs.transpose(1, 0, 2).reshape(rows // 4, 4, columns))
    rot_rows = in_hbm(rot_table.transpose(1, 0, 2).reshape(modes * tables, modes))
    axial_rows = in_hbm(axial_table.transpose(0, 2, 1, 3))
    pair_rows = in_hbm(pair_table.transpose(2, 0, 1))

    octets = part * quarter // 16
    pieces = pl.pallas_call(
        functools.partial(pack_kernel, quarter, modes, ways, own),
        in_specs=[hbm(), pl.BlockSpec(memory_space=pltpu.SMEM), hbm()],
        out_specs=whole(),
        out_shape=jax.ShapeDtypeStruct((ways, 2, octets, 16, size), BF16),
        scratch_shapes=[
            pltpu.VMEM(pair_rows.shape, jnp.int32),
            pltpu.VMEM((full, columns), F32),
            pltpu.VMEM((size, columns), F32),
            pltpu.VMEM((2 * slots, slots), F32),
            pltpu.SemaphoreType.DMA((2,)),
        ],
        compiler_params=params(16),
        name="pack",
    )(pair_rows, pair_count, basis_rows)
    tall = rounded_up(rows + full, 8)
    pieces, basis_later = lax.optimization_barrier((pieces, basis_rows))
    own_pieces = exchanged(pieces)
    line = pl.pallas_call(
        functools.partial(gram_kernel, quarter, modes),
        grid=(1,),
        in_specs=[hbm()],
        out_specs=pl.BlockSpec((1, 128), lambda i: (0, 0)),
        out_shape=pltpu.HBM((1, 128), F32),
        scratch_shapes=[
            pltpu.VMEM((pairs_of_vectors, tall, columns), F32),
            pltpu.VMEM((vectors, vectors, 8, columns), F32),
            pltpu.SemaphoreType.DMA((4, pairs_of_vectors, 2)),
        ],
        compiler_params=params(16),
        name="gram",
    )(basis_later)
    own_pieces, line, *inputs = lax.optimization_barrier((own_pieces, line, basis_rows, mie_rows, rot_rows, axial_rows))
    basis_rows, mie_rows, rot_rows, axial_rows = inputs
    below, above = neighbours(own_pieces)

    rotations, axials = pl.pallas_call(
        functools.partial(tables_kernel, modes, tables),
        grid=(tables,),
        in_specs=[
            pl.BlockSpec((1, modes, 2, modes), lambda g: (g, 0, 0, 0)),
            pl.BlockSpec((size, modes), lambda g: (g, 0)),
        ],
        out_specs=[
            pl.BlockSpec((tables, size // tables, size), lambda g: (0, g, 0)),
            pl.BlockSpec((1, 2 * size, size), lambda g: (g, 0, 0)),
        ],
        out_shape=[
            jax.ShapeDtypeStruct((tables, size, size), BF16),
            jax.ShapeDtypeStruct((tables, 2 * size, size), BF16),
        ],
        scratch_shapes=[pltpu.VMEM((2 * size, size), BF16)],
        compiler_params=params(32),
        cost_estimate=pl.CostEstimate(flops=tables * 8 * 256 * 256 * size, bytes_accessed=6 * tables * size * size * 2, transcendentals=0),
        name="tables",
    )(axial_rows, rot_rows)

    below, above, rotations, axials = lax.optimization_barrier((below, above, rotations, axials))

    together = 2 if tables % 2 == 0 else 1
    *field, blocks, mies = pl.pallas_call(
        functools.partial(field_kernel, own, modes, together),
        in_specs=[whole()] * 5 + [hbm()] * 2,
        out_specs=[whole()] * (ways + 2),
        out_shape=[jax.ShapeDtypeStruct((2, quarter, part, size), BF16)] * ways
        + [
            jax.ShapeDtypeStruct((pairs_of_vectors, tall, columns), F32),
            jax.ShapeDtypeStruct(mie_rows.shape, F32),
        ],
        scratch_shapes=[
            pltpu.VMEM((tables, 4 * group, size), BF16),
            pltpu.VMEM((2 * group, size), F32),
            pltpu.SemaphoreType.DMA((pairs_of_vectors + 1,)),
        ],
        compiler_params=params(20),
        name="field",
    )(rotations, axials, below, own_pieces, above, basis_rows, mie_rows)
    field_pieces = [field[0]]
    for i in range(1, ways):
        field_pieces.append(lax.ppermute(field[i], "pair", [(p, p ^ i) for p in range(ways)]))

    image, sums = pl.pallas_call(
        functools.partial(image_kernel, quarter, modes),
        in_specs=[whole()] * (ways + 3),
        out_specs=[whole()] * 2,
        out_shape=[jax.ShapeDtypeStruct((full, columns), F32), jax.ShapeDtypeStruct((ways * blk_ways, 1, 128), F32)],
        scratch_shapes=[pltpu.VMEM((full, columns), F32), pltpu.VMEM((quarter, columns, size), BF16)],
        compiler_params=params(8),
        name="image",
    )(blocks, mies, line, *field_pieces)
    sums = lax.all_to_all(sums, ("blk", "pair"), split_axis=0, concat_axis=0, tiled=True)

    height = 4
    mean_scale = 1.0 / (own * blk_ways * modes * columns)
    dots, next_rows = pl.pallas_call(
        functools.partial(remainder_kernel, quarter, modes, mean_scale),
        in_specs=[whole()] * 3,
        out_specs=[whole(), whole()],
        out_shape=[jax.ShapeDtypeStruct((2, vectors), F32), jax.ShapeDtypeStruct((rows // height, height, columns), F32)],
        compiler_params=params(16),
        name="remainder",
    )(sums, blocks, image)
    return dots, next_rows.reshape(modes, quarter, columns).transpose(1, 0, 2)


def solution(mesh):
    placed = (
        P(None, ("blk", "pair"), None, None),
        P(("blk", "pair"), None, None),
        P(),
        P(),
        P("blk", None, None),
        P("blk"),
    )
    return jax.shard_map(
        shards,
        mesh=mesh,
        in_specs=placed,
        out_specs=(P(), P(("blk", "pair"), None, None)),
        check_vma=False,
    )
```

```python
import functools

import jax
import jax.numpy as jnp
from jax import lax
from jax.experimental import pallas as pl
from jax.experimental.pallas import tpu as pltpu
from jax.sharding import PartitionSpec as P

MIB = 1024 * 1024
F32 = jnp.float32
BF16 = jnp.bfloat16


def params(mib):
    return pltpu.CompilerParams(vmem_limit_bytes=mib * MIB)


def hbm():
    return pl.BlockSpec(memory_space=pltpu.HBM)


def whole():
    return pl.BlockSpec(memory_space=pltpu.VMEM)


def in_hbm(value):
    return pltpu.with_memory_space_constraint(value, pltpu.HBM)


def rounded_up(value, unit):
    return (value + unit - 1) // unit * unit


def iota(shape, dim):
    return lax.broadcasted_iota(jnp.int32, shape, dim)


def dot_nn(left, right):
    return lax.dot_general(left, right, (((1,), (0,)), ((), ())), preferred_element_type=F32)


def dot_nt(left, right):
    return lax.dot_general(left, right, (((1,), (1,)), ((), ())), preferred_element_type=F32)


def pack_kernel(quarter, modes, ways, own, list_ref, count_ref, basis_ref, *rest):
    outs, (pair_rows_ref, lines_ref, pad_ref, codes_ref, turned_ref, sems) = rest[:ways], rest[ways:]
    full, columns = lines_ref.shape
    rows = quarter * modes
    part = columns // 2 // ways
    copy = pltpu.make_async_copy(basis_ref.at[basis_ref.shape[0] - 1, pl.ds(2 * rows - full, full)], lines_ref, sems.at[0])
    copy.start()
    list_copy = pltpu.make_async_copy(list_ref, pair_rows_ref, sems.at[1])
    list_copy.start()
    pad_ref[...] = jnp.zeros_like(pad_ref)
    list_copy.wait()
    slots = pair_rows_ref.shape[2]
    live = iota((1, slots), 1) < count_ref[0]
    marks = jnp.where(live, own * (pair_rows_ref[2] + 1) + pair_rows_ref[0], 0)
    line = iota((slots, slots), 0)
    stacked = jnp.where(line == 0, marks, jnp.where(line == 1, pair_rows_ref[1], 0))
    turned = jnp.transpose(stacked.astype(F32))
    codes_ref[0:slots, :] = turned
    codes_ref[slots : 2 * slots, :] = pltpu.roll(turned, slots - 1, axis=1)
    share = 2 * quarter * part
    mine = codes_ref[pl.ds(pl.multiple_of(lax.axis_index("pair") * share, share), share), :][:, 0:1]
    copy.wait()
    for j in range(quarter):
        pad_ref[0:modes, :] = lines_ref[pl.ds(full - rows + j, modes, quarter), :]
        turned_ref[j] = jnp.transpose(pad_ref[...])
    _, octets, height, size = outs[0].shape
    each = height // quarter
    for i, out_ref in enumerate(outs):
        place = (lax.axis_index("pair") ^ i) * part
        for c in range(2):
            for o in range(octets):
                first = (c * octets + o) * height
                here = pl.ds(pl.multiple_of(c * (columns // 2) + place + o * each, each), each)
                piece = jnp.concatenate([turned_ref[j, here, :] for j in range(quarter)], axis=0)
                piece = jnp.where(iota(piece.shape, 1) == modes, mine[first : first + height], piece)
                out_ref[c, o] = piece.astype(BF16)


def join_kernel(*refs):
    out_ref = refs[-1]
    for i, ref in enumerate(refs[:-1]):
        out_ref[lax.axis_index("pair") ^ i] = ref[...]


def added_kernel(*refs):
    values = [ref[...] for ref in refs[:-1]]
    while len(values) > 1:
        values = [values[i] + values[i + 1] for i in range(0, len(values), 2)]
    refs[-1][...] = values[0]


def tables_kernel(modes, tables, axial_ref, rot_ref, rot_out_ref, axial_out_ref, lines_ref):
    step = pl.program_id(0)
    size = rot_out_ref.shape[2]
    chunk = 256

    @pl.when(step == 0)
    def _():
        lines_ref[...] = jnp.zeros_like(lines_ref)

    out_row, in_row = iota((chunk, chunk), 0), iota((chunk, chunk), 1)
    each = chunk // 2
    halves = (in_row == 2 * lax.rem(out_row, each) + lax.div(out_row, each)).astype(F32).astype(BF16)
    lines_ref[0 : 2 * modes, 0:modes] = axial_ref[0].reshape(2 * modes, modes)
    for q in range(2 * size // chunk):
        sorted_rows = dot_nn(halves, lines_ref[q * chunk : (q + 1) * chunk, :]).astype(BF16)
        for c in range(2):
            axial_out_ref[0, c * size + q * each : c * size + (q + 1) * each, :] = sorted_rows[c * each : (c + 1) * each]
    each = chunk // tables
    entries = (in_row == tables * lax.rem(out_row, each) + lax.div(out_row, each)).astype(F32).astype(BF16)
    block = rot_ref.shape[0]
    left = tables * modes - step * block
    rows = jnp.where(iota((block, modes), 0) < left, rot_ref[...], jnp.zeros((), BF16))
    rot_out_ref[:, :, size - 128 : size] = jnp.zeros((tables, block // tables, 128), BF16)
    for q in range(block // chunk):
        sorted_rows = dot_nn(entries, rows[q * chunk : (q + 1) * chunk]).astype(BF16)
        for g in range(tables):
            rot_out_ref[g, q * each : (q + 1) * each, 0:modes] = sorted_rows[g * each : (g + 1) * each]


def swapped(value):
    half = value.shape[0] // 2
    return jnp.concatenate([-value[half:], value[:half]], axis=0)


def pair_counts(own, tables, lane, refs):
    ways, parts, octets, height, size = refs[0].shape
    group = ways * octets * height
    wanted = iota((tables * own, group), 0) + own

    def one_hot(hit):
        return jnp.where(hit, 1.0, 0.0).astype(BF16)

    even = lax.rem(lax.axis_index("blk"), 2) == 0
    near, far = jnp.where(even, 2, 0), jnp.where(even, 0, 2)
    forward, backward = None, []
    for order, (window, ref) in enumerate(zip((near, 1, far), refs)):
        values = ref[:, :, :, :, size - 128 : size].reshape(2 * group, 128).astype(F32)
        marks_column, sources_column = (values[h * group : (h + 1) * group, lane : lane + 1].astype(jnp.int32) for h in range(2))
        marks, sources = (jnp.transpose(values[h * group : (h + 1) * group])[lane : lane + 1].astype(jnp.int32) for h in range(2))
        if order == 1:
            turned = (2 - lax.div(sources_column, own)) * own + lax.rem(sources_column, own)
            sources_column = jnp.where(even, turned, sources_column)
            forward = dot_nn(one_hot(marks == wanted), one_hot(sources_column == iota((group, 3 * own), 1)))
        block = sources - (2 - window) * own
        inside = (block >= 0) & (block < own) & (marks >= own)
        hits = one_hot(jnp.where(inside, lax.div(marks, own) * own + block, -1) == wanted)
        place = lax.rem(marks_column, own) + order * own
        backward.append(dot_nn(hits, one_hot(place == iota((group, 3 * own), 1))))
    return jnp.concatenate([forward, sum(backward)], axis=0).astype(BF16)


def folded(value):
    return jnp.sum(value.reshape(value.shape[0] // 8, 8, value.shape[1]), axis=0)


def field_kernel(
    own, modes, together, rot_ref, axial_ref, near_ref, own_ref, far_ref, *rest
):
    outs, (sums_ref, total_ref) = rest[:-2], rest[-2:]
    tables, _, size = rot_ref.shape
    refs = (near_ref, own_ref, far_ref)
    ways, _, octets, height, _ = own_ref.shape
    quarter = own // ways
    each = height // quarter
    part = octets * each
    group = own * part
    counts = pair_counts(own, tables, modes % 128, refs)
    spread = jnp.where(iota((3 * own, 3 * own * each), 0) == lax.div(iota((3 * own, 3 * own * each), 1), each), 1.0, 0.0)
    counts = dot_nn(counts, spread.astype(BF16))
    sphere = lax.rem(iota(counts.shape, 1), each)
    chosen = jnp.concatenate([jnp.where(sphere == i, counts, 0.0).astype(BF16) for i in range(each)], axis=0)
    kinds = 2 * tables * own
    for c in range(2):
        for o in range(octets):
            blocks = jnp.concatenate([ref[:, c, o].reshape(ways * height, size) for ref in refs], axis=0)
            for i in range(0, each, 2):
                results = dot_nn(chosen[i * kinds : (i + 2) * kinds], blocks)
                for kind in range(2 * tables):
                    direction, g = kind // tables, kind % tables
                    rows = [results[start + kind * own : start + (kind + 1) * own] for start in (0, kinds)]
                    place = (direction * 2 + c) * group + (o * each + i) * own
                    sums_ref[g, place : place + 2 * own, :] = jnp.concatenate(rows, axis=0).astype(BF16)
    total_ref[...] = jnp.zeros_like(total_ref)

    def body(step, carry):
        entries = [step * together + i for i in range(together)]
        turned = [dot_nt(sums_ref[g], rot_ref[g]).astype(BF16) for g in entries]
        moved = []
        for g, both in zip(entries, turned):
            forward, backward = both[: 2 * group], both[2 * group :]
            result = dot_nt(forward, axial_ref[g, :size]) + dot_nt(swapped(forward), axial_ref[g, size:])
            result += dot_nn(jnp.concatenate([backward, swapped(backward)], axis=1), axial_ref[g])
            moved.append(result.astype(BF16))
        total_ref[...] += sum(dot_nn(value, rot_ref[g]) for g, value in zip(entries, moved))
        return carry

    lax.fori_loop(0, tables // together, body, 0)
    row, source = iota((2 * group, 2 * group), 0), iota((2 * group, 2 * group), 1)
    sphere, c = lax.rem(row, part), lax.rem(lax.div(row, quarter * part), 2)
    owner = lax.div(row, 2 * quarter * part) ^ lax.axis_index("pair")
    block = owner * quarter + lax.rem(lax.div(row, part), quarter)
    order = jnp.where(source == c * group + sphere * own + block, 1.0, 0.0).astype(BF16)
    result = dot_nn(order, total_ref[...].astype(BF16)).astype(BF16)
    share = 2 * quarter * part
    for i, out_ref in enumerate(outs):
        out_ref[...] = result[i * share : (i + 1) * share].reshape(out_ref.shape)


def lane_swap(value):
    half = value.shape[1] // 2
    rolled = pltpu.roll(value, half, axis=1)
    return jnp.where(iota(value.shape, 1) < half, -rolled, rolled)


def add_products(blocks_ref, products_ref, rows, first, count):
    vectors = products_ref.shape[0]
    values = []
    for k in range(vectors):
        start = k % 2 * rows + first
        value = blocks_ref[k // 2, start : start + count, :]
        if k % 2 == 0 and first + count > rows:
            value = jnp.where(iota(value.shape, 0) < rows - first, value, 0.0)
        values.append(value)
    for l in range(vectors):
        other = pltpu.roll(values[l], values[l].shape[1] // 2, axis=1)
        for k in range(l + 1):
            products_ref[k, l] += folded(values[k] * values[l])
            if k < l:
                products_ref[l, k] += folded(values[k] * other)


def products_line(products_ref):
    vectors, _, _, columns = products_ref.shape
    pairs = vectors * vectors
    totals = jnp.sum(products_ref[...].reshape(pairs, 8, columns), axis=1)
    pair = iota(totals.shape, 0)
    signed = (lax.div(pair, vectors) > lax.rem(pair, vectors)) & (iota(totals.shape, 1) >= columns // 2)
    totals = jnp.sum(jnp.where(signed, -totals, totals), axis=1, keepdims=True)
    row, lane = iota((vectors, 128), 0), iota((vectors, 128), 1)
    line = jnp.zeros((1, 128), F32)
    for k in range(vectors):
        column = totals[k * vectors : (k + 1) * vectors]
        line += jnp.sum(jnp.where(row + k * vectors == lane, column, 0.0), axis=0, keepdims=True)
    return line


def gram_kernel(quarter, modes, basis_ref, mie_ref, line_ref, blocks_ref, mies_ref, products_ref, mie_sem, sems):
    blocks, _, columns = basis_ref.shape
    rows = quarter * modes
    parts, chunk = 4, 32
    tile_end = rows // 8 * 8
    step = rounded_up(rows, 8 * parts) // parts
    even = [0] + [step * q for q in range(1, parts)] + [tile_end]
    odd = [tile_end] + [rounded_up(rows, 8) + step * q for q in range(1, parts)] + [2 * rows]
    copies = []
    for q in range(parts):
        for i in range(blocks):
            for side, cuts in enumerate((even, odd)):
                here = pl.ds(cuts[q], cuts[q + 1] - cuts[q])
                copies.append(pltpu.make_async_copy(basis_ref.at[i, here], blocks_ref.at[i, here], sems.at[q, i, side]))
    for copy in copies:
        copy.start()
    mie_rows = mie_ref.shape[0]
    mie_copy = pltpu.make_async_copy(mie_ref, mies_ref.at[pl.ds(0, mie_rows)], mie_sem)
    mie_copy.start()
    mies_ref[mie_rows:] = jnp.zeros((mies_ref.shape[0] - mie_rows,) + mies_ref.shape[1:], F32)
    products_ref[...] = jnp.zeros_like(products_ref)
    for i in range(blocks):
        blocks_ref[i, 2 * rows :, :] = jnp.zeros((blocks_ref.shape[1] - 2 * rows, columns), F32)
    for q in range(parts):
        for copy in copies[2 * blocks * q : 2 * blocks * (q + 1)]:
            copy.wait()
        for first in range(step * q, min(step * (q + 1), rows), chunk):
            add_products(blocks_ref, products_ref, rows, first, chunk)
    line_ref[...] = products_line(products_ref)
    mie_copy.wait()


def image_kernel(quarter, modes, blocks_ref, mie_ref, gram_ref, *rest):
    pieces, (image_ref, sums_ref, lines_ref, whole_ref) = rest[:-4], rest[-4:]
    vectors = 2 * blocks_ref.shape[0]
    full, columns = image_ref.shape
    rows = quarter * modes
    part = pieces[0].shape[2]
    for i, piece_ref in enumerate(pieces):
        place = pl.multiple_of((lax.axis_index("pair") ^ i) * part, part)
        for j in range(quarter):
            for c in range(2):
                whole_ref[j, pl.ds(c * (columns // 2) + place, part), :] = piece_ref[c, j]
    lines_ref[rows:full, :] = jnp.zeros((full - rows, columns), F32)
    for j in range(quarter):
        lines_ref[pl.ds(j, modes, quarter), :] = jnp.transpose(whole_ref[j].astype(F32))[:modes]
    half = columns // 2
    chunk = 64
    totals = [jnp.zeros((8, columns), F32) for _ in range(2 * vectors + 1)]
    for first in range(0, full, chunk):
        here = slice(first, first + chunk)
        field = lines_ref[here, :]
        count = min(chunk, rows - first)
        height = mie_ref.shape[1]
        mie = mie_ref[first // height : (first + count) // height].reshape(count, columns)
        if count < chunk:
            mie = jnp.concatenate([mie, jnp.zeros((chunk - count, columns), F32)], axis=0)
        left = iota(mie.shape, 1) < half
        other = pltpu.roll(mie, half, axis=1)
        product = jnp.where(left, mie, other) * field + jnp.where(left, -other, mie) * pltpu.roll(field, half, axis=1)
        last = (vectors - 1) % 2 * rows + first
        image = blocks_ref[(vectors - 1) // 2, last : last + chunk, :] - product
        image_ref[here, :] = image
        turned = pltpu.roll(image, half, axis=1)
        for k in range(vectors):
            start = k % 2 * rows + first
            values = blocks_ref[k // 2, start : start + chunk, :]
            totals[2 * k] += folded(values * image)
            totals[2 * k + 1] += folded(values * turned)
        totals[2 * vectors] += folded(image * image)
    lane = iota(gram_ref.shape, 1)
    line = gram_ref[...]
    left = iota((8, columns), 1) < half
    for index, total in enumerate(totals):
        if index % 2 and index < 2 * vectors:
            total = jnp.where(left, total, -total)
        line = jnp.where(lane == vectors * vectors + index, jnp.sum(total, axis=(0, 1), keepdims=True), line)
    sums_ref[...] = line


def remainder_kernel(quarter, modes, mean_scale, sums_ref, blocks_ref, image_ref, dots_ref, out_ref):
    vectors = 2 * blocks_ref.shape[0]
    full, columns = image_ref.shape
    rows = quarter * modes
    total = sums_ref[...]
    lane = iota(total.shape, 1)

    def lane_at(index):
        return jnp.sum(jnp.where(lane == index, total, 0.0), axis=1, keepdims=True)

    def on_lanes(parts, places):
        line = jnp.zeros(total.shape, F32)
        for k in range(vectors):
            line = jnp.where(places == k, parts[k], line)
        return line

    start = vectors * vectors
    real = [lane_at(start + 2 * k) * mean_scale for k in range(vectors)]
    imag = [lane_at(start + 2 * k + 1) * mean_scale for k in range(vectors)]
    real_line, imag_line = on_lanes(real, lane), on_lanes(imag, lane)
    dots_ref[0:1, :] = real_line[:, :vectors]
    dots_ref[1:2, :] = imag_line[:, :vectors]
    first_index, last_index = lax.div(lane, vectors), lax.rem(lane, vectors)
    real_first, real_last = on_lanes(real, first_index), on_lanes(real, last_index)
    imag_first, imag_last = on_lanes(imag, first_index), on_lanes(imag, last_index)
    same = real_first * real_last + imag_first * imag_last
    cross = imag_last * real_first - real_last * imag_first
    often = jnp.where(first_index == last_index, 1.0, 2.0)
    spread = jnp.where(lane < start, total * often * jnp.where(first_index <= last_index, same, cross), 0.0)
    spread = jnp.sum(spread, axis=1, keepdims=True)
    inside = jnp.sum(real_line * real_line + imag_line * imag_line, axis=1, keepdims=True)
    norm_square = (lane_at(start + 2 * vectors) + spread) * mean_scale - 2.0 * inside
    scale = lax.rsqrt(norm_square)
    image_scale = jnp.broadcast_to(scale, (8, columns))
    reals = [jnp.broadcast_to(real[k] * scale, (8, columns)) for k in range(vectors)]
    imags = [jnp.broadcast_to(imag[k] * scale, (8, columns)) for k in range(vectors)]
    chunk = 64
    for first in range(0, full, chunk):
        here = slice(first, first + chunk)
        values = []
        for k in range(vectors):
            start = k % 2 * rows + first
            values.append(blocks_ref[k // 2, start : start + chunk, :].reshape(chunk // 8, 8, columns))
        along = image_ref[here, :].reshape(chunk // 8, 8, columns) * image_scale
        turned = jnp.zeros_like(along)
        for k in range(vectors):
            along -= reals[k] * values[k]
            turned += imags[k] * values[k]
        result = along.reshape(chunk, columns) - lane_swap(turned.reshape(chunk, columns))
        count = min(chunk, rows - first)
        height = out_ref.shape[1]
        out_ref[first // height : (first + count) // height] = result.reshape(chunk // height, height, columns)[: count // height]


def exchanged(pieces, axis):
    count = lax.axis_size(axis)
    received = [pieces[0]]
    for i in range(1, len(pieces)):
        received.append(lax.ppermute(pieces[i], axis, [(p, p ^ i) for p in range(count)]))
    return received


def summed(value, axis):
    count, done = lax.axis_size(axis), 1
    while done < count:
        ways = min(4, count // done)
        values = [value]
        for i in range(1, ways):
            values.append(lax.ppermute(value, axis, [(p, p ^ (i * done)) for p in range(count)]))
        value = pl.pallas_call(
            added_kernel,
            in_specs=[whole()] * ways,
            out_specs=whole(),
            out_shape=jax.ShapeDtypeStruct(value.shape, F32),
            compiler_params=params(2),
            name="added",
        )(*values)
        done *= ways
    return value


def neighbours(value):
    count = lax.axis_size("blk")
    results = []
    for first in range(2):
        pairs = [(i, i + 1) for i in range(first, count - 1, 2)]
        results.append(lax.ppermute(value, "blk", pairs + [(j, i) for i, j in pairs]))
    return results


def shards(basis, mie_coeffs, rot_table, axial_table, pair_table, pair_count):
    vectors, quarter, modes, columns = basis.shape
    ways = lax.axis_size("pair")
    blk_ways = lax.axis_size("blk")
    tables = rot_table.shape[0]
    slots = pair_table.shape[1]
    own = quarter * ways
    part = columns // 2 // ways
    group = own * part
    size = rounded_up(modes, 128)
    rows = quarter * modes
    full = rounded_up(rows, 8)
    pairs_of_vectors = vectors // 2
    height = 4

    basis_rows = in_hbm(basis.transpose(0, 2, 1, 3).reshape(pairs_of_vectors, 2 * rows, columns))
    mie_rows = in_hbm(mie_coeffs.transpose(1, 0, 2).reshape(rows // 4, 4, columns))
    rot_rows = in_hbm(rot_table.transpose(1, 0, 2).reshape(modes * tables, modes))
    axial_rows = in_hbm(axial_table.transpose(0, 2, 1, 3))
    pair_rows = in_hbm(pair_table.transpose(2, 0, 1))

    octets = part * quarter // 16
    piece = jax.ShapeDtypeStruct((2, octets, 16, size), BF16)
    pieces = pl.pallas_call(
        functools.partial(pack_kernel, quarter, modes, ways, own),
        in_specs=[hbm(), pl.BlockSpec(memory_space=pltpu.SMEM), hbm()],
        out_specs=[whole()] * ways,
        out_shape=[piece] * ways,
        scratch_shapes=[
            pltpu.VMEM(pair_rows.shape, jnp.int32),
            pltpu.VMEM((full, columns), F32),
            pltpu.VMEM((size, columns), F32),
            pltpu.VMEM((2 * slots, slots), F32),
            pltpu.VMEM((quarter, columns, size), F32),
            pltpu.SemaphoreType.DMA((2,)),
        ],
        compiler_params=params(16),
        name="pack",
    )(pair_rows, pair_count, basis_rows)
    tall = rounded_up(rows + full, 8)
    *pieces, basis_rows, mie_rows = lax.optimization_barrier((*pieces, basis_rows, mie_rows))
    received = exchanged(pieces, "pair")
    line, blocks, mies = pl.pallas_call(
        functools.partial(gram_kernel, quarter, modes),
        in_specs=[hbm()] * 2,
        out_specs=[whole()] * 3,
        out_shape=[
            jax.ShapeDtypeStruct((1, 128), F32),
            jax.ShapeDtypeStruct((pairs_of_vectors, tall, columns), F32),
            jax.ShapeDtypeStruct((full // height, height, columns), F32),
        ],
        scratch_shapes=[
            pltpu.VMEM((vectors, vectors, 8, columns), F32),
            pltpu.SemaphoreType.DMA,
            pltpu.SemaphoreType.DMA((4, pairs_of_vectors, 2)),
        ],
        compiler_params=params(8),
        name="gram",
    )(basis_rows, mie_rows)
    *received, line, rot_rows, axial_rows = lax.optimization_barrier((*received, line, rot_rows, axial_rows))
    own_pieces = pl.pallas_call(
        join_kernel,
        in_specs=[whole()] * ways,
        out_specs=whole(),
        out_shape=jax.ShapeDtypeStruct((ways, *piece.shape), BF16),
        compiler_params=params(4),
        name="join",
    )(*received)
    near, far = neighbours(own_pieces)

    rotations, axials = pl.pallas_call(
        functools.partial(tables_kernel, modes, tables),
        grid=(tables,),
        in_specs=[
            pl.BlockSpec((1, modes, 2, modes), lambda g: (g, 0, 0, 0)),
            pl.BlockSpec((size, modes), lambda g: (g, 0)),
        ],
        out_specs=[
            pl.BlockSpec((tables, size // tables, size), lambda g: (0, g, 0)),
            pl.BlockSpec((1, 2 * size, size), lambda g: (g, 0, 0)),
        ],
        out_shape=[
            jax.ShapeDtypeStruct((tables, size, size), BF16),
            jax.ShapeDtypeStruct((tables, 2 * size, size), BF16),
        ],
        scratch_shapes=[pltpu.VMEM((2 * size, size), BF16)],
        compiler_params=params(32),
        cost_estimate=pl.CostEstimate(flops=tables * 8 * 256 * 256 * size, bytes_accessed=6 * tables * size * size * 2, transcendentals=0),
        name="tables",
    )(axial_rows, rot_rows)

    near, far, rotations, axials = lax.optimization_barrier((near, far, rotations, axials))

    together = 2 if tables % 2 == 0 else 1
    field = pl.pallas_call(
        functools.partial(field_kernel, own, modes, together),
        in_specs=[whole()] * 5,
        out_specs=[whole()] * ways,
        out_shape=[jax.ShapeDtypeStruct((2, quarter, part, size), BF16)] * ways,
        scratch_shapes=[pltpu.VMEM((tables, 4 * group, size), BF16), pltpu.VMEM((2 * group, size), F32)],
        compiler_params=params(20),
        name="field",
    )(rotations, axials, near, own_pieces, far)
    field_pieces = exchanged(field, "pair")

    image, sums = pl.pallas_call(
        functools.partial(image_kernel, quarter, modes),
        in_specs=[whole()] * (ways + 3),
        out_specs=[whole()] * 2,
        out_shape=[jax.ShapeDtypeStruct((full, columns), F32), jax.ShapeDtypeStruct((1, 128), F32)],
        scratch_shapes=[pltpu.VMEM((full, columns), F32), pltpu.VMEM((quarter, columns, size), BF16)],
        compiler_params=params(8),
        name="image",
    )(blocks, mies, line, *field_pieces)
    sums = summed(summed(sums, "pair"), "blk")

    mean_scale = 1.0 / (own * blk_ways * modes * columns)
    dots, next_rows = pl.pallas_call(
        functools.partial(remainder_kernel, quarter, modes, mean_scale),
        in_specs=[whole()] * 3,
        out_specs=[whole(), whole()],
        out_shape=[jax.ShapeDtypeStruct((2, vectors), F32), jax.ShapeDtypeStruct((rows // height, height, columns), F32)],
        compiler_params=params(16),
        name="remainder",
    )(sums, blocks, image)
    return dots, next_rows.reshape(modes, quarter, columns).transpose(1, 0, 2)


def solution(mesh):
    placed = (
        P(None, ("blk", "pair"), None, None),
        P(("blk", "pair"), None, None),
        P(),
        P(),
        P("blk", None, None),
        P("blk"),
    )
    return jax.shard_map(
        shards,
        mesh=mesh,
        in_specs=placed,
        out_specs=(P(), P(("blk", "pair"), None, None)),
        check_vma=False,
    )
```

```python
import functools

import jax
import jax.numpy as jnp
from jax import lax
from jax.experimental import pallas as pl
from jax.experimental.pallas import tpu as pltpu
from jax.sharding import PartitionSpec as P

MIB = 1024 * 1024
F32 = jnp.float32
BF16 = jnp.bfloat16


def params(mib):
    return pltpu.CompilerParams(vmem_limit_bytes=mib * MIB)


def hbm():
    return pl.BlockSpec(memory_space=pltpu.HBM)


def whole():
    return pl.BlockSpec(memory_space=pltpu.VMEM)


def in_hbm(value):
    return pltpu.with_memory_space_constraint(value, pltpu.HBM)


def rounded_up(value, unit):
    return (value + unit - 1) // unit * unit


def iota(shape, dim):
    return lax.broadcasted_iota(jnp.int32, shape, dim)


def dot_nn(left, right):
    return lax.dot_general(left, right, (((1,), (0,)), ((), ())), preferred_element_type=F32)


def dot_nt(left, right):
    return lax.dot_general(left, right, (((1,), (1,)), ((), ())), preferred_element_type=F32)


def pack_kernel(quarter, modes, ways, own, list_ref, count_ref, basis_ref, *rest):
    outs, (pair_rows_ref, lines_ref, pad_ref, codes_ref, turned_ref, sems) = rest[:ways], rest[ways:]
    full, columns = lines_ref.shape
    rows = quarter * modes
    part = columns // 2 // ways
    copy = pltpu.make_async_copy(basis_ref.at[basis_ref.shape[0] - 1, pl.ds(2 * rows - full, full)], lines_ref, sems.at[0])
    copy.start()
    list_copy = pltpu.make_async_copy(list_ref, pair_rows_ref, sems.at[1])
    list_copy.start()
    pad_ref[...] = jnp.zeros_like(pad_ref)
    list_copy.wait()
    slots = pair_rows_ref.shape[2]
    live = iota((1, slots), 1) < count_ref[0]
    marks = jnp.where(live, own * (pair_rows_ref[2] + 1) + pair_rows_ref[0], 0)
    line = iota((slots, slots), 0)
    stacked = jnp.where(line == 0, marks, jnp.where(line == 1, pair_rows_ref[1], 0))
    turned = jnp.transpose(stacked.astype(F32))
    codes_ref[0:slots, :] = turned
    codes_ref[slots : 2 * slots, :] = pltpu.roll(turned, slots - 1, axis=1)
    share = 2 * quarter * part
    mine = codes_ref[pl.ds(pl.multiple_of(lax.axis_index("pair") * share, share), share), :][:, 0:1]
    copy.wait()
    for j in range(quarter):
        pad_ref[0:modes, :] = lines_ref[pl.ds(full - rows + j, modes, quarter), :]
        turned_ref[j] = jnp.transpose(pad_ref[...])
    _, octets, height, size = outs[0].shape
    each = height // quarter
    for i, out_ref in enumerate(outs):
        place = (lax.axis_index("pair") ^ i) * part
        for c in range(2):
            for o in range(octets):
                first = (c * octets + o) * height
                here = pl.ds(pl.multiple_of(c * (columns // 2) + place + o * each, each), each)
                piece = jnp.concatenate([turned_ref[j, here, :] for j in range(quarter)], axis=0)
                piece = jnp.where(iota(piece.shape, 1) == modes, mine[first : first + height], piece)
                out_ref[c, o] = piece.astype(BF16)


def join_kernel(*refs):
    out_ref = refs[-1]
    for i, ref in enumerate(refs[:-1]):
        out_ref[lax.axis_index("pair") ^ i] = ref[...]


def tables_kernel(axial_ref, rot_ref, rot_out_ref, axial_out_ref, axials_ref, rots_ref, sems):
    tables, size, _ = rot_out_ref.shape
    modes = axial_ref.shape[1]
    listed = rot_ref.shape[0]

    def fetch(g):
        return pltpu.make_async_copy(axial_ref.at[g], axials_ref.at[g], sems.at[g])

    for g in range(tables):
        fetch(g).start()
    rot_copy = pltpu.make_async_copy(rot_ref, rots_ref.at[pl.ds(0, listed)], sems.at[tables])
    rot_copy.start()
    chunk = 256
    out_row, in_row = iota((chunk, chunk), 0), iota((chunk, chunk), 1)
    each = chunk // 2
    halves = (in_row == 2 * lax.rem(out_row, each) + lax.div(out_row, each)).astype(F32).astype(BF16)
    share = chunk // tables
    entries = (in_row == tables * lax.rem(out_row, share) + lax.div(out_row, share)).astype(F32).astype(BF16)
    for ref in (rot_out_ref, axial_out_ref):
        ref[:, :, size - 128 : size] = jnp.zeros((tables, ref.shape[1], 128), BF16)
    rots_ref[listed:, :] = jnp.zeros((rots_ref.shape[0] - listed, modes), BF16)

    def split(g, carry):
        fetch(g).wait()
        for first in range(0, modes, each):
            count = min(each, modes - first)
            rows = axials_ref[g, first : first + count].reshape(2 * count, modes)
            sorted_rows = dot_nn(halves[:, : 2 * count], rows).astype(BF16)
            for c in range(2):
                axial_out_ref[g, c * size + first : c * size + first + each, 0:modes] = sorted_rows[c * each : (c + 1) * each]
        return carry

    lax.fori_loop(0, tables, split, 0)
    rot_copy.wait()

    def pick(i, carry):
        rows = rots_ref[pl.ds(pl.multiple_of(i * chunk, chunk), chunk), :]
        sorted_rows = dot_nn(entries, rows).astype(BF16)
        for g in range(tables):
            here = pl.ds(pl.multiple_of(i * share, share), share)
            rot_out_ref[g, here, 0:modes] = sorted_rows[g * share : (g + 1) * share]
        return carry

    lax.fori_loop(0, rots_ref.shape[0] // chunk, pick, 0)


def swapped(value):
    half = value.shape[0] // 2
    return jnp.concatenate([-value[half:], value[:half]], axis=0)


def pair_counts(own, tables, lane, refs):
    ways, parts, octets, height, size = refs[0].shape
    group = ways * octets * height
    wanted = iota((tables * own, group), 0) + own

    def one_hot(hit):
        return jnp.where(hit, 1.0, 0.0).astype(BF16)

    forward, backward = None, []
    for window, ref in enumerate(refs):
        values = ref[:, :, :, :, size - 128 : size].reshape(2 * group, 128).astype(F32)
        marks_column, sources_column = (values[h * group : (h + 1) * group, lane : lane + 1].astype(jnp.int32) for h in range(2))
        marks, sources = (jnp.transpose(values[h * group : (h + 1) * group])[lane : lane + 1].astype(jnp.int32) for h in range(2))
        if window == 1:
            forward = dot_nn(one_hot(marks == wanted), one_hot(sources_column == iota((group, 3 * own), 1)))
        block = sources - (2 - window) * own
        inside = (block >= 0) & (block < own) & (marks >= own)
        hits = one_hot(jnp.where(inside, lax.div(marks, own) * own + block, -1) == wanted)
        place = lax.rem(marks_column, own) + window * own
        backward.append(dot_nn(hits, one_hot(place == iota((group, 3 * own), 1))))
    return jnp.concatenate([forward, sum(backward)], axis=0).astype(BF16)


def folded(value):
    return jnp.sum(value.reshape(value.shape[0] // 8, 8, value.shape[1]), axis=0)


def field_kernel(
    own, modes, together, rot_ref, axial_ref, below_ref, own_ref, above_ref, *rest
):
    outs, (sums_ref, total_ref) = rest[:-2], rest[-2:]
    tables, _, size = rot_ref.shape
    refs = (below_ref, own_ref, above_ref)
    ways, _, octets, height, _ = own_ref.shape
    quarter = own // ways
    each = height // quarter
    part = octets * each
    group = own * part
    counts = pair_counts(own, tables, modes % 128, refs)
    spread = jnp.where(iota((3 * own, 3 * own * each), 0) == lax.div(iota((3 * own, 3 * own * each), 1), each), 1.0, 0.0)
    counts = dot_nn(counts, spread.astype(BF16))
    sphere = lax.rem(iota(counts.shape, 1), each)
    chosen = jnp.concatenate([jnp.where(sphere == i, counts, 0.0).astype(BF16) for i in range(each)], axis=0)
    kinds = 2 * tables * own
    for c in range(2):
        for o in range(octets):
            blocks = jnp.concatenate([ref[:, c, o].reshape(ways * height, size) for ref in refs], axis=0)
            for i in range(0, each, 2):
                results = dot_nn(chosen[i * kinds : (i + 2) * kinds], blocks)
                for kind in range(2 * tables):
                    direction, g = kind // tables, kind % tables
                    rows = [results[start + kind * own : start + (kind + 1) * own] for start in (0, kinds)]
                    place = (direction * 2 + c) * group + (o * each + i) * own
                    sums_ref[g, place : place + 2 * own, :] = jnp.concatenate(rows, axis=0).astype(BF16)
    total_ref[...] = jnp.zeros_like(total_ref)

    def body(step, carry):
        entries = [step * together + i for i in range(together)]
        turned = [dot_nt(sums_ref[g], rot_ref[g]).astype(BF16) for g in entries]
        moved = []
        for g, both in zip(entries, turned):
            forward, backward = both[: 2 * group], both[2 * group :]
            result = dot_nt(forward, axial_ref[g, :size]) + dot_nt(swapped(forward), axial_ref[g, size:])
            result += dot_nn(jnp.concatenate([backward, swapped(backward)], axis=1), axial_ref[g])
            moved.append(result.astype(BF16))
        total_ref[...] += sum(dot_nn(value, rot_ref[g]) for g, value in zip(entries, moved))
        return carry

    lax.fori_loop(0, tables // together, body, 0)
    row, source = iota((2 * group, 2 * group), 0), iota((2 * group, 2 * group), 1)
    sphere, c = lax.rem(row, part), lax.rem(lax.div(row, quarter * part), 2)
    owner = lax.div(row, 2 * quarter * part) ^ lax.axis_index("pair")
    block = owner * quarter + lax.rem(lax.div(row, part), quarter)
    order = jnp.where(source == c * group + sphere * own + block, 1.0, 0.0).astype(BF16)
    result = dot_nn(order, total_ref[...].astype(BF16)).astype(BF16)
    share = 2 * quarter * part
    for i, out_ref in enumerate(outs):
        out_ref[...] = result[i * share : (i + 1) * share].reshape(out_ref.shape)


def lane_swap(value):
    half = value.shape[1] // 2
    rolled = pltpu.roll(value, half, axis=1)
    return jnp.where(iota(value.shape, 1) < half, -rolled, rolled)


def add_products(blocks_ref, products_ref, rows, first, count):
    vectors = products_ref.shape[0]
    values = []
    for k in range(vectors):
        start = k % 2 * rows + first
        value = blocks_ref[k // 2, start : start + count, :]
        if k % 2 == 0 and first + count > rows:
            value = jnp.where(iota(value.shape, 0) < rows - first, value, 0.0)
        values.append(value)
    for l in range(vectors):
        other = pltpu.roll(values[l], values[l].shape[1] // 2, axis=1)
        for k in range(l + 1):
            products_ref[k, l] += folded(values[k] * values[l])
            if k < l:
                products_ref[l, k] += folded(values[k] * other)


def products_line(products_ref):
    vectors, _, _, columns = products_ref.shape
    pairs = vectors * vectors
    totals = jnp.sum(products_ref[...].reshape(pairs, 8, columns), axis=1)
    pair = iota(totals.shape, 0)
    signed = (lax.div(pair, vectors) > lax.rem(pair, vectors)) & (iota(totals.shape, 1) >= columns // 2)
    totals = jnp.sum(jnp.where(signed, -totals, totals), axis=1, keepdims=True)
    row, lane = iota((vectors, 128), 0), iota((vectors, 128), 1)
    line = jnp.zeros((1, 128), F32)
    for k in range(vectors):
        column = totals[k * vectors : (k + 1) * vectors]
        line += jnp.sum(jnp.where(row + k * vectors == lane, column, 0.0), axis=0, keepdims=True)
    return line


def gram_kernel(quarter, modes, basis_ref, mie_ref, line_ref, blocks_ref, mies_ref, products_ref, mie_sem, sems):
    blocks, _, columns = basis_ref.shape
    rows = quarter * modes
    parts, chunk = 4, 32
    tile_end = rows // 8 * 8
    step = rounded_up(rows, 8 * parts) // parts
    even = [0] + [step * q for q in range(1, parts)] + [tile_end]
    odd = [tile_end] + [rounded_up(rows, 8) + step * q for q in range(1, parts)] + [2 * rows]
    copies = []
    for q in range(parts):
        for i in range(blocks):
            for side, cuts in enumerate((even, odd)):
                here = pl.ds(cuts[q], cuts[q + 1] - cuts[q])
                copies.append(pltpu.make_async_copy(basis_ref.at[i, here], blocks_ref.at[i, here], sems.at[q, i, side]))
    for copy in copies:
        copy.start()
    mie_rows = mie_ref.shape[0]
    mie_copy = pltpu.make_async_copy(mie_ref, mies_ref.at[pl.ds(0, mie_rows)], mie_sem)
    mie_copy.start()
    mies_ref[mie_rows:] = jnp.zeros((mies_ref.shape[0] - mie_rows,) + mies_ref.shape[1:], F32)
    products_ref[...] = jnp.zeros_like(products_ref)
    for i in range(blocks):
        blocks_ref[i, 2 * rows :, :] = jnp.zeros((blocks_ref.shape[1] - 2 * rows, columns), F32)
    for q in range(parts):
        for copy in copies[2 * blocks * q : 2 * blocks * (q + 1)]:
            copy.wait()
        for first in range(step * q, min(step * (q + 1), rows), chunk):
            add_products(blocks_ref, products_ref, rows, first, chunk)
    line_ref[...] = products_line(products_ref)
    mie_copy.wait()


def image_kernel(quarter, modes, blocks_ref, mie_ref, gram_ref, *rest):
    pieces, (image_ref, sums_ref, lines_ref, whole_ref) = rest[:-4], rest[-4:]
    vectors = 2 * blocks_ref.shape[0]
    full, columns = image_ref.shape
    rows = quarter * modes
    part = pieces[0].shape[2]
    for i, piece_ref in enumerate(pieces):
        place = pl.multiple_of((lax.axis_index("pair") ^ i) * part, part)
        for j in range(quarter):
            for c in range(2):
                whole_ref[j, pl.ds(c * (columns // 2) + place, part), :] = piece_ref[c, j]
    lines_ref[rows:full, :] = jnp.zeros((full - rows, columns), F32)
    for j in range(quarter):
        lines_ref[pl.ds(j, modes, quarter), :] = jnp.transpose(whole_ref[j].astype(F32))[:modes]
    half = columns // 2
    chunk = 64
    totals = [jnp.zeros((8, columns), F32) for _ in range(2 * vectors + 1)]
    for first in range(0, full, chunk):
        here = slice(first, first + chunk)
        field = lines_ref[here, :]
        count = min(chunk, rows - first)
        height = mie_ref.shape[1]
        mie = mie_ref[first // height : (first + count) // height].reshape(count, columns)
        if count < chunk:
            mie = jnp.concatenate([mie, jnp.zeros((chunk - count, columns), F32)], axis=0)
        left = iota(mie.shape, 1) < half
        other = pltpu.roll(mie, half, axis=1)
        product = jnp.where(left, mie, other) * field + jnp.where(left, -other, mie) * pltpu.roll(field, half, axis=1)
        last = (vectors - 1) % 2 * rows + first
        image = blocks_ref[(vectors - 1) // 2, last : last + chunk, :] - product
        image_ref[here, :] = image
        turned = pltpu.roll(image, half, axis=1)
        for k in range(vectors):
            start = k % 2 * rows + first
            values = blocks_ref[k // 2, start : start + chunk, :]
            totals[2 * k] += folded(values * image)
            totals[2 * k + 1] += folded(values * turned)
        totals[2 * vectors] += folded(image * image)
    lane = iota(gram_ref.shape, 1)
    line = gram_ref[...]
    left = iota((8, columns), 1) < half
    for index, total in enumerate(totals):
        if index % 2 and index < 2 * vectors:
            total = jnp.where(left, total, -total)
        line = jnp.where(lane == vectors * vectors + index, jnp.sum(total, axis=(0, 1), keepdims=True), line)
    sums_ref[...] = jnp.broadcast_to(line[None], sums_ref.shape)


def remainder_kernel(quarter, modes, mean_scale, sums_ref, blocks_ref, image_ref, dots_ref, out_ref):
    vectors = 2 * blocks_ref.shape[0]
    full, columns = image_ref.shape
    rows = quarter * modes
    total = jnp.sum(sums_ref[...], axis=0)
    lane = iota(total.shape, 1)

    def lane_at(index):
        return jnp.sum(jnp.where(lane == index, total, 0.0), axis=1, keepdims=True)

    def on_lanes(parts, places):
        line = jnp.zeros(total.shape, F32)
        for k in range(vectors):
            line = jnp.where(places == k, parts[k], line)
        return line

    start = vectors * vectors
    real = [lane_at(start + 2 * k) * mean_scale for k in range(vectors)]
    imag = [lane_at(start + 2 * k + 1) * mean_scale for k in range(vectors)]
    real_line, imag_line = on_lanes(real, lane), on_lanes(imag, lane)
    dots_ref[0:1, :] = real_line[:, :vectors]
    dots_ref[1:2, :] = imag_line[:, :vectors]
    first_index, last_index = lax.div(lane, vectors), lax.rem(lane, vectors)
    real_first, real_last = on_lanes(real, first_index), on_lanes(real, last_index)
    imag_first, imag_last = on_lanes(imag, first_index), on_lanes(imag, last_index)
    same = real_first * real_last + imag_first * imag_last
    cross = imag_last * real_first - real_last * imag_first
    often = jnp.where(first_index == last_index, 1.0, 2.0)
    spread = jnp.where(lane < start, total * often * jnp.where(first_index <= last_index, same, cross), 0.0)
    spread = jnp.sum(spread, axis=1, keepdims=True)
    inside = jnp.sum(real_line * real_line + imag_line * imag_line, axis=1, keepdims=True)
    norm_square = (lane_at(start + 2 * vectors) + spread) * mean_scale - 2.0 * inside
    scale = lax.rsqrt(norm_square)
    image_scale = jnp.broadcast_to(scale, (8, columns))
    reals = [jnp.broadcast_to(real[k] * scale, (8, columns)) for k in range(vectors)]
    imags = [jnp.broadcast_to(imag[k] * scale, (8, columns)) for k in range(vectors)]
    chunk = 64
    for first in range(0, full, chunk):
        here = slice(first, first + chunk)
        values = []
        for k in range(vectors):
            start = k % 2 * rows + first
            values.append(blocks_ref[k // 2, start : start + chunk, :].reshape(chunk // 8, 8, columns))
        along = image_ref[here, :].reshape(chunk // 8, 8, columns) * image_scale
        turned = jnp.zeros_like(along)
        for k in range(vectors):
            along -= reals[k] * values[k]
            turned += imags[k] * values[k]
        result = along.reshape(chunk, columns) - lane_swap(turned.reshape(chunk, columns))
        count = min(chunk, rows - first)
        height = out_ref.shape[1]
        out_ref[first // height : (first + count) // height] = result.reshape(chunk // height, height, columns)[: count // height]


def exchanged(pieces, axis):
    count = lax.axis_size(axis)
    received = [pieces[0]]
    for i in range(1, len(pieces)):
        received.append(lax.ppermute(pieces[i], axis, [(p, p ^ i) for p in range(count)]))
    return received


def neighbours(value):
    count = lax.axis_size("blk")
    up = [(i, i + 1) for i in range(count - 1)]
    down = [(j, i) for i, j in up]
    return lax.ppermute(value, "blk", up), lax.ppermute(value, "blk", down)


def shards(basis, mie_coeffs, rot_table, axial_table, pair_table, pair_count):
    vectors, quarter, modes, columns = basis.shape
    ways = lax.axis_size("pair")
    blk_ways = lax.axis_size("blk")
    tables = rot_table.shape[0]
    slots = pair_table.shape[1]
    own = quarter * ways
    part = columns // 2 // ways
    group = own * part
    size = rounded_up(modes, 128)
    rows = quarter * modes
    full = rounded_up(rows, 8)
    pairs_of_vectors = vectors // 2
    height = 4

    basis_rows = in_hbm(basis.transpose(0, 2, 1, 3).reshape(pairs_of_vectors, 2 * rows, columns))
    mie_rows = in_hbm(mie_coeffs.transpose(1, 0, 2).reshape(rows // 4, 4, columns))
    rot_rows = in_hbm(rot_table.transpose(1, 0, 2).reshape(modes * tables, modes))
    axial_rows = in_hbm(axial_table.transpose(0, 2, 1, 3))
    pair_rows = in_hbm(pair_table.transpose(2, 0, 1))

    octets = part * quarter // 16
    piece = jax.ShapeDtypeStruct((2, octets, 16, size), BF16)
    pieces = pl.pallas_call(
        functools.partial(pack_kernel, quarter, modes, ways, own),
        in_specs=[hbm(), pl.BlockSpec(memory_space=pltpu.SMEM), hbm()],
        out_specs=[whole()] * ways,
        out_shape=[piece] * ways,
        scratch_shapes=[
            pltpu.VMEM(pair_rows.shape, jnp.int32),
            pltpu.VMEM((full, columns), F32),
            pltpu.VMEM((size, columns), F32),
            pltpu.VMEM((2 * slots, slots), F32),
            pltpu.VMEM((quarter, columns, size), F32),
            pltpu.SemaphoreType.DMA((2,)),
        ],
        compiler_params=params(16),
        name="pack",
    )(pair_rows, pair_count, basis_rows)
    tall = rounded_up(rows + full, 8)
    *pieces, basis_rows, mie_rows = lax.optimization_barrier((*pieces, basis_rows, mie_rows))
    received = exchanged(pieces, "pair")
    line, blocks, mies = pl.pallas_call(
        functools.partial(gram_kernel, quarter, modes),
        in_specs=[hbm()] * 2,
        out_specs=[whole()] * 3,
        out_shape=[
            jax.ShapeDtypeStruct((1, 128), F32),
            jax.ShapeDtypeStruct((pairs_of_vectors, tall, columns), F32),
            jax.ShapeDtypeStruct((full // height, height, columns), F32),
        ],
        scratch_shapes=[
            pltpu.VMEM((vectors, vectors, 8, columns), F32),
            pltpu.SemaphoreType.DMA,
            pltpu.SemaphoreType.DMA((4, pairs_of_vectors, 2)),
        ],
        compiler_params=params(8),
        name="gram",
    )(basis_rows, mie_rows)
    *received, line, rot_rows, axial_rows = lax.optimization_barrier((*received, line, rot_rows, axial_rows))
    own_pieces = pl.pallas_call(
        join_kernel,
        in_specs=[whole()] * ways,
        out_specs=whole(),
        out_shape=jax.ShapeDtypeStruct((ways, *piece.shape), BF16),
        compiler_params=params(4),
        name="join",
    )(*received)
    below, above = neighbours(own_pieces)

    rotations, axials = pl.pallas_call(
        tables_kernel,
        in_specs=[hbm()] * 2,
        out_specs=[whole()] * 2,
        out_shape=[
            jax.ShapeDtypeStruct((tables, size, size), BF16),
            jax.ShapeDtypeStruct((tables, 2 * size, size), BF16),
        ],
        scratch_shapes=[
            pltpu.VMEM(axial_rows.shape, BF16),
            pltpu.VMEM((tables * size, modes), BF16),
            pltpu.SemaphoreType.DMA((tables + 1,)),
        ],
        compiler_params=params(20),
        cost_estimate=pl.CostEstimate(flops=tables * 8 * 256 * 256 * size, bytes_accessed=6 * tables * size * size * 2, transcendentals=0),
        name="tables",
    )(axial_rows, rot_rows)
    below, above, rotations, axials = lax.optimization_barrier((below, above, rotations, axials))

    together = 2 if tables % 2 == 0 else 1
    field = pl.pallas_call(
        functools.partial(field_kernel, own, modes, together),
        in_specs=[whole()] * 5,
        out_specs=[whole()] * ways,
        out_shape=[jax.ShapeDtypeStruct((2, quarter, part, size), BF16)] * ways,
        scratch_shapes=[pltpu.VMEM((tables, 4 * group, size), BF16), pltpu.VMEM((2 * group, size), F32)],
        compiler_params=params(20),
        name="field",
    )(rotations, axials, below, own_pieces, above)
    field_pieces = exchanged(field, "pair")

    image, sums = pl.pallas_call(
        functools.partial(image_kernel, quarter, modes),
        in_specs=[whole()] * (ways + 3),
        out_specs=[whole()] * 2,
        out_shape=[jax.ShapeDtypeStruct((full, columns), F32), jax.ShapeDtypeStruct((ways * blk_ways, 1, 128), F32)],
        scratch_shapes=[pltpu.VMEM((full, columns), F32), pltpu.VMEM((quarter, columns, size), BF16)],
        compiler_params=params(8),
        name="image",
    )(blocks, mies, line, *field_pieces)
    sums = lax.all_to_all(sums, ("blk", "pair"), split_axis=0, concat_axis=0, tiled=True)

    mean_scale = 1.0 / (own * blk_ways * modes * columns)
    dots, next_rows = pl.pallas_call(
        functools.partial(remainder_kernel, quarter, modes, mean_scale),
        in_specs=[whole()] * 3,
        out_specs=[whole(), whole()],
        out_shape=[jax.ShapeDtypeStruct((2, vectors), F32), jax.ShapeDtypeStruct((rows // height, height, columns), F32)],
        compiler_params=params(16),
        name="remainder",
    )(sums, blocks, image)
    return dots, next_rows.reshape(modes, quarter, columns).transpose(1, 0, 2)


def solution(mesh):
    placed = (
        P(None, ("blk", "pair"), None, None),
        P(("blk", "pair"), None, None),
        P(),
        P(),
        P("blk", None, None),
        P("blk"),
    )
    return jax.shard_map(
        shards,
        mesh=mesh,
        in_specs=placed,
        out_specs=(P(), P(("blk", "pair"), None, None)),
        check_vma=False,
    )
```

```python
import functools

import jax
import jax.numpy as jnp
from jax import lax
from jax.experimental import pallas as pl
from jax.experimental.pallas import tpu as pltpu
from jax.sharding import PartitionSpec as P

MIB = 1024 * 1024
F32 = jnp.float32
BF16 = jnp.bfloat16


def params(mib):
    return pltpu.CompilerParams(vmem_limit_bytes=mib * MIB)


def hbm():
    return pl.BlockSpec(memory_space=pltpu.HBM)


def whole():
    return pl.BlockSpec(memory_space=pltpu.VMEM)


def in_hbm(value):
    return pltpu.with_memory_space_constraint(value, pltpu.HBM)


def rounded_up(value, unit):
    return (value + unit - 1) // unit * unit


def mask(i):
    return (lax.axis_size("pair") - i) % lax.axis_size("pair")


def iota(shape, dim):
    return lax.broadcasted_iota(jnp.int32, shape, dim)


def dot_nn(left, right):
    return lax.dot_general(left, right, (((1,), (0,)), ((), ())), preferred_element_type=F32)


def dot_nt(left, right):
    return lax.dot_general(left, right, (((1,), (1,)), ((), ())), preferred_element_type=F32)


def pack_kernel(quarter, modes, ways, own, list_ref, count_ref, basis_ref, *rest):
    outs, (pair_rows_ref, lines_ref, pad_ref, codes_ref, turned_ref, sems) = rest[:ways], rest[ways:]
    full, columns = lines_ref.shape
    rows = quarter * modes
    part = columns // 2 // ways
    copy = pltpu.make_async_copy(basis_ref.at[basis_ref.shape[0] - 1, pl.ds(2 * rows - full, full)], lines_ref, sems.at[0])
    copy.start()
    list_copy = pltpu.make_async_copy(list_ref, pair_rows_ref, sems.at[1])
    list_copy.start()
    pad_ref[...] = jnp.zeros_like(pad_ref)
    list_copy.wait()
    slots = pair_rows_ref.shape[2]
    live = iota((1, slots), 1) < count_ref[0]
    marks = jnp.where(live, own * (pair_rows_ref[2] + 1) + pair_rows_ref[0], 0)
    line = iota((slots, slots), 0)
    stacked = jnp.where(line == 0, marks, jnp.where(line == 1, pair_rows_ref[1], 0))
    turned = jnp.transpose(stacked.astype(F32))
    codes_ref[0:slots, :] = turned
    codes_ref[slots : 2 * slots, :] = pltpu.roll(turned, slots - 1, axis=1)
    share = 2 * quarter * part
    mine = codes_ref[pl.ds(pl.multiple_of(lax.axis_index("pair") * share, share), share), :][:, 0:1]
    copy.wait()
    for j in range(quarter):
        pad_ref[0:modes, :] = lines_ref[pl.ds(full - rows + j, modes, quarter), :]
        turned_ref[j] = jnp.transpose(pad_ref[...])
    _, octets, height, size = outs[0].shape
    each = height // quarter
    for i, out_ref in enumerate(outs):
        place = (lax.axis_index("pair") ^ mask(i)) * part
        for c in range(2):
            for o in range(octets):
                first = (c * octets + o) * height
                here = pl.ds(pl.multiple_of(c * (columns // 2) + place + o * each, each), each)
                piece = jnp.concatenate([turned_ref[j, here, :] for j in range(quarter)], axis=0)
                piece = jnp.where(iota(piece.shape, 1) == modes, mine[first : first + height], piece)
                out_ref[c, o] = piece.astype(BF16)


def join_kernel(*refs):
    out_ref = refs[-1]
    for i, ref in enumerate(refs[:-1]):
        out_ref[lax.axis_index("pair") ^ mask(i)] = ref[...]


def tables_kernel(axial_ref, rot_ref, rot_out_ref, axial_out_ref, axials_ref, rots_ref, sems):
    tables, size, _ = rot_out_ref.shape
    modes = axial_ref.shape[1]
    listed = rot_ref.shape[0]

    def fetch(g):
        return pltpu.make_async_copy(axial_ref.at[g], axials_ref.at[g], sems.at[g])

    for g in range(tables):
        fetch(g).start()
    rot_copy = pltpu.make_async_copy(rot_ref, rots_ref.at[pl.ds(0, listed)], sems.at[tables])
    rot_copy.start()
    chunk = 256
    out_row, in_row = iota((chunk, chunk), 0), iota((chunk, chunk), 1)
    each = chunk // 2
    halves = (in_row == 2 * lax.rem(out_row, each) + lax.div(out_row, each)).astype(F32).astype(BF16)
    share = chunk // tables
    entries = (in_row == tables * lax.rem(out_row, share) + lax.div(out_row, share)).astype(F32).astype(BF16)
    for ref in (rot_out_ref, axial_out_ref):
        ref[:, :, size - 128 : size] = jnp.zeros((tables, ref.shape[1], 128), BF16)
    rots_ref[listed:, :] = jnp.zeros((rots_ref.shape[0] - listed, modes), BF16)

    def split(g, carry):
        fetch(g).wait()
        for first in range(0, modes, each):
            count = min(each, modes - first)
            rows = axials_ref[g, first : first + count].reshape(2 * count, modes)
            sorted_rows = dot_nn(halves[:, : 2 * count], rows).astype(BF16)
            for c in range(2):
                axial_out_ref[g, c * size + first : c * size + first + each, 0:modes] = sorted_rows[c * each : (c + 1) * each]
        return carry

    lax.fori_loop(0, tables, split, 0)
    rot_copy.wait()

    def pick(i, carry):
        rows = rots_ref[pl.ds(pl.multiple_of(i * chunk, chunk), chunk), :]
        sorted_rows = dot_nn(entries, rows).astype(BF16)
        for g in range(tables):
            here = pl.ds(pl.multiple_of(i * share, share), share)
            rot_out_ref[g, here, 0:modes] = sorted_rows[g * share : (g + 1) * share]
        return carry

    lax.fori_loop(0, rots_ref.shape[0] // chunk, pick, 0)


def swapped(value):
    half = value.shape[0] // 2
    return jnp.concatenate([-value[half:], value[:half]], axis=0)


def pair_counts(own, tables, lane, refs):
    ways, parts, octets, height, size = refs[0].shape
    group = ways * octets * height
    wanted = iota((tables * own, group), 0) + own

    def one_hot(hit):
        return jnp.where(hit, 1.0, 0.0).astype(BF16)

    forward, backward = None, []
    for window, ref in enumerate(refs):
        values = ref[:, :, :, :, size - 128 : size].reshape(2 * group, 128).astype(F32)
        marks_column, sources_column = (values[h * group : (h + 1) * group, lane : lane + 1].astype(jnp.int32) for h in range(2))
        marks, sources = (jnp.transpose(values[h * group : (h + 1) * group])[lane : lane + 1].astype(jnp.int32) for h in range(2))
        if window == 1:
            forward = dot_nn(one_hot(marks == wanted), one_hot(sources_column == iota((group, 3 * own), 1)))
        block = sources - (2 - window) * own
        inside = (block >= 0) & (block < own) & (marks >= own)
        hits = one_hot(jnp.where(inside, lax.div(marks, own) * own + block, -1) == wanted)
        place = lax.rem(marks_column, own) + window * own
        backward.append(dot_nn(hits, one_hot(place == iota((group, 3 * own), 1))))
    return jnp.concatenate([forward, sum(backward)], axis=0).astype(BF16)


def folded(value):
    return jnp.sum(value.reshape(value.shape[0] // 8, 8, value.shape[1]), axis=0)


def field_kernel(
    own, modes, together, rot_ref, axial_ref, below_ref, own_ref, above_ref, *rest
):
    outs, (sums_ref, total_ref) = rest[:-2], rest[-2:]
    tables, _, size = rot_ref.shape
    refs = (below_ref, own_ref, above_ref)
    ways, _, octets, height, _ = own_ref.shape
    quarter = own // ways
    each = height // quarter
    part = octets * each
    group = own * part
    counts = pair_counts(own, tables, modes % 128, refs)
    spread = jnp.where(iota((3 * own, 3 * own * each), 0) == lax.div(iota((3 * own, 3 * own * each), 1), each), 1.0, 0.0)
    counts = dot_nn(counts, spread.astype(BF16))
    sphere = lax.rem(iota(counts.shape, 1), each)
    chosen = jnp.concatenate([jnp.where(sphere == i, counts, 0.0).astype(BF16) for i in range(each)], axis=0)
    kinds = 2 * tables * own
    for c in range(2):
        for o in range(octets):
            blocks = jnp.concatenate([ref[:, c, o].reshape(ways * height, size) for ref in refs], axis=0)
            for i in range(0, each, 2):
                results = dot_nn(chosen[i * kinds : (i + 2) * kinds], blocks)
                for kind in range(2 * tables):
                    direction, g = kind // tables, kind % tables
                    rows = [results[start + kind * own : start + (kind + 1) * own] for start in (0, kinds)]
                    place = (direction * 2 + c) * group + (o * each + i) * own
                    sums_ref[g, place : place + 2 * own, :] = jnp.concatenate(rows, axis=0).astype(BF16)
    total_ref[...] = jnp.zeros_like(total_ref)

    def body(step, carry):
        entries = [step * together + i for i in range(together)]
        turned = [dot_nt(sums_ref[g], rot_ref[g]).astype(BF16) for g in entries]
        moved = []
        for g, both in zip(entries, turned):
            forward, backward = both[: 2 * group], both[2 * group :]
            result = dot_nt(forward, axial_ref[g, :size]) + dot_nt(swapped(forward), axial_ref[g, size:])
            result += dot_nn(jnp.concatenate([backward, swapped(backward)], axis=1), axial_ref[g])
            moved.append(result.astype(BF16))
        total_ref[...] += sum(dot_nn(value, rot_ref[g]) for g, value in zip(entries, moved))
        return carry

    lax.fori_loop(0, tables // together, body, 0)
    row, source = iota((2 * group, 2 * group), 0), iota((2 * group, 2 * group), 1)
    sphere, c = lax.rem(row, part), lax.rem(lax.div(row, quarter * part), 2)
    owner = lax.rem(ways - lax.div(row, 2 * quarter * part), ways) ^ lax.axis_index("pair")
    block = owner * quarter + lax.rem(lax.div(row, part), quarter)
    order = jnp.where(source == c * group + sphere * own + block, 1.0, 0.0).astype(BF16)
    result = dot_nn(order, total_ref[...].astype(BF16)).astype(BF16)
    share = 2 * quarter * part
    for i, out_ref in enumerate(outs):
        out_ref[...] = result[i * share : (i + 1) * share].reshape(out_ref.shape)


def lane_swap(value):
    half = value.shape[1] // 2
    rolled = pltpu.roll(value, half, axis=1)
    return jnp.where(iota(value.shape, 1) < half, -rolled, rolled)


def add_products(blocks_ref, products_ref, rows, first, count):
    vectors = products_ref.shape[0]
    values = []
    for k in range(vectors):
        start = k % 2 * rows + first
        value = blocks_ref[k // 2, start : start + count, :]
        if k % 2 == 0 and first + count > rows:
            value = jnp.where(iota(value.shape, 0) < rows - first, value, 0.0)
        values.append(value)
    for l in range(vectors):
        other = pltpu.roll(values[l], values[l].shape[1] // 2, axis=1)
        for k in range(l + 1):
            products_ref[k, l] += folded(values[k] * values[l])
            if k < l:
                products_ref[l, k] += folded(values[k] * other)


def products_line(products_ref):
    vectors, _, _, columns = products_ref.shape
    pairs = vectors * vectors
    totals = jnp.sum(products_ref[...].reshape(pairs, 8, columns), axis=1)
    pair = iota(totals.shape, 0)
    signed = (lax.div(pair, vectors) > lax.rem(pair, vectors)) & (iota(totals.shape, 1) >= columns // 2)
    totals = jnp.sum(jnp.where(signed, -totals, totals), axis=1, keepdims=True)
    row, lane = iota((vectors, 128), 0), iota((vectors, 128), 1)
    line = jnp.zeros((1, 128), F32)
    for k in range(vectors):
        column = totals[k * vectors : (k + 1) * vectors]
        line += jnp.sum(jnp.where(row + k * vectors == lane, column, 0.0), axis=0, keepdims=True)
    return line


def gram_kernel(quarter, modes, basis_ref, mie_ref, line_ref, blocks_ref, mies_ref, products_ref, mie_sem, sems):
    blocks, _, columns = basis_ref.shape
    rows = quarter * modes
    parts, chunk = 4, 32
    tile_end = rows // 8 * 8
    step = rounded_up(rows, 8 * parts) // parts
    even = [0] + [step * q for q in range(1, parts)] + [tile_end]
    odd = [tile_end] + [rounded_up(rows, 8) + step * q for q in range(1, parts)] + [2 * rows]
    copies = []
    for q in range(parts):
        for i in range(blocks):
            for side, cuts in enumerate((even, odd)):
                here = pl.ds(cuts[q], cuts[q + 1] - cuts[q])
                copies.append(pltpu.make_async_copy(basis_ref.at[i, here], blocks_ref.at[i, here], sems.at[q, i, side]))
    for copy in copies:
        copy.start()
    mie_rows = mie_ref.shape[0]
    mie_copy = pltpu.make_async_copy(mie_ref, mies_ref.at[pl.ds(0, mie_rows)], mie_sem)
    mie_copy.start()
    mies_ref[mie_rows:] = jnp.zeros((mies_ref.shape[0] - mie_rows,) + mies_ref.shape[1:], F32)
    products_ref[...] = jnp.zeros_like(products_ref)
    for i in range(blocks):
        blocks_ref[i, 2 * rows :, :] = jnp.zeros((blocks_ref.shape[1] - 2 * rows, columns), F32)
    for q in range(parts):
        for copy in copies[2 * blocks * q : 2 * blocks * (q + 1)]:
            copy.wait()
        for first in range(step * q, min(step * (q + 1), rows), chunk):
            add_products(blocks_ref, products_ref, rows, first, chunk)
    line_ref[...] = products_line(products_ref)
    mie_copy.wait()


def image_kernel(quarter, modes, blocks_ref, mie_ref, gram_ref, *rest):
    pieces, (image_ref, sums_ref, lines_ref, whole_ref) = rest[:-4], rest[-4:]
    vectors = 2 * blocks_ref.shape[0]
    full, columns = image_ref.shape
    rows = quarter * modes
    part = pieces[0].shape[2]
    for i, piece_ref in enumerate(pieces):
        place = pl.multiple_of((lax.axis_index("pair") ^ mask(i)) * part, part)
        for j in range(quarter):
            for c in range(2):
                whole_ref[j, pl.ds(c * (columns // 2) + place, part), :] = piece_ref[c, j]
    lines_ref[rows:full, :] = jnp.zeros((full - rows, columns), F32)
    for j in range(quarter):
        lines_ref[pl.ds(j, modes, quarter), :] = jnp.transpose(whole_ref[j].astype(F32))[:modes]
    half = columns // 2
    chunk = 64
    totals = [jnp.zeros((8, columns), F32) for _ in range(2 * vectors + 1)]
    for first in range(0, full, chunk):
        here = slice(first, first + chunk)
        field = lines_ref[here, :]
        count = min(chunk, rows - first)
        height = mie_ref.shape[1]
        mie = mie_ref[first // height : (first + count) // height].reshape(count, columns)
        if count < chunk:
            mie = jnp.concatenate([mie, jnp.zeros((chunk - count, columns), F32)], axis=0)
        left = iota(mie.shape, 1) < half
        other = pltpu.roll(mie, half, axis=1)
        product = jnp.where(left, mie, other) * field + jnp.where(left, -other, mie) * pltpu.roll(field, half, axis=1)
        last = (vectors - 1) % 2 * rows + first
        image = blocks_ref[(vectors - 1) // 2, last : last + chunk, :] - product
        image_ref[here, :] = image
        turned = pltpu.roll(image, half, axis=1)
        for k in range(vectors):
            start = k % 2 * rows + first
            values = blocks_ref[k // 2, start : start + chunk, :]
            totals[2 * k] += folded(values * image)
            totals[2 * k + 1] += folded(values * turned)
        totals[2 * vectors] += folded(image * image)
    lane = iota(gram_ref.shape, 1)
    line = gram_ref[...]
    left = iota((8, columns), 1) < half
    for index, total in enumerate(totals):
        if index % 2 and index < 2 * vectors:
            total = jnp.where(left, total, -total)
        line = jnp.where(lane == vectors * vectors + index, jnp.sum(total, axis=(0, 1), keepdims=True), line)
    sums_ref[...] = jnp.broadcast_to(line[None], sums_ref.shape)


def remainder_kernel(quarter, modes, mean_scale, sums_ref, blocks_ref, image_ref, dots_ref, out_ref):
    vectors = 2 * blocks_ref.shape[0]
    full, columns = image_ref.shape
    rows = quarter * modes
    total = jnp.sum(sums_ref[...], axis=0)
    lane = iota(total.shape, 1)

    def lane_at(index):
        return jnp.sum(jnp.where(lane == index, total, 0.0), axis=1, keepdims=True)

    def on_lanes(parts, places):
        line = jnp.zeros(total.shape, F32)
        for k in range(vectors):
            line = jnp.where(places == k, parts[k], line)
        return line

    start = vectors * vectors
    real = [lane_at(start + 2 * k) * mean_scale for k in range(vectors)]
    imag = [lane_at(start + 2 * k + 1) * mean_scale for k in range(vectors)]
    real_line, imag_line = on_lanes(real, lane), on_lanes(imag, lane)
    dots_ref[0:1, :] = real_line[:, :vectors]
    dots_ref[1:2, :] = imag_line[:, :vectors]
    first_index, last_index = lax.div(lane, vectors), lax.rem(lane, vectors)
    real_first, real_last = on_lanes(real, first_index), on_lanes(real, last_index)
    imag_first, imag_last = on_lanes(imag, first_index), on_lanes(imag, last_index)
    same = real_first * real_last + imag_first * imag_last
    cross = imag_last * real_first - real_last * imag_first
    often = jnp.where(first_index == last_index, 1.0, 2.0)
    spread = jnp.where(lane < start, total * often * jnp.where(first_index <= last_index, same, cross), 0.0)
    spread = jnp.sum(spread, axis=1, keepdims=True)
    inside = jnp.sum(real_line * real_line + imag_line * imag_line, axis=1, keepdims=True)
    norm_square = (lane_at(start + 2 * vectors) + spread) * mean_scale - 2.0 * inside
    scale = lax.rsqrt(norm_square)
    image_scale = jnp.broadcast_to(scale, (8, columns))
    reals = [jnp.broadcast_to(real[k] * scale, (8, columns)) for k in range(vectors)]
    imags = [jnp.broadcast_to(imag[k] * scale, (8, columns)) for k in range(vectors)]
    chunk = 64
    for first in range(0, full, chunk):
        here = slice(first, first + chunk)
        values = []
        for k in range(vectors):
            start = k % 2 * rows + first
            values.append(blocks_ref[k // 2, start : start + chunk, :].reshape(chunk // 8, 8, columns))
        along = image_ref[here, :].reshape(chunk // 8, 8, columns) * image_scale
        turned = jnp.zeros_like(along)
        for k in range(vectors):
            along -= reals[k] * values[k]
            turned += imags[k] * values[k]
        result = along.reshape(chunk, columns) - lane_swap(turned.reshape(chunk, columns))
        count = min(chunk, rows - first)
        height = out_ref.shape[1]
        out_ref[first // height : (first + count) // height] = result.reshape(chunk // height, height, columns)[: count // height]


def exchanged(pieces, axis):
    count = lax.axis_size(axis)
    received = [pieces[0]]
    for i in range(1, len(pieces)):
        received.append(lax.ppermute(pieces[i], axis, [(p, p ^ mask(i)) for p in range(count)]))
    return received


def neighbours(value):
    count = lax.axis_size("blk")
    up = [(i, i + 1) for i in range(count - 1)]
    down = [(j, i) for i, j in up]
    return lax.ppermute(value, "blk", up), lax.ppermute(value, "blk", down)


def shards(basis, mie_coeffs, rot_table, axial_table, pair_table, pair_count):
    vectors, quarter, modes, columns = basis.shape
    ways = lax.axis_size("pair")
    blk_ways = lax.axis_size("blk")
    tables = rot_table.shape[0]
    slots = pair_table.shape[1]
    own = quarter * ways
    part = columns // 2 // ways
    group = own * part
    size = rounded_up(modes, 128)
    rows = quarter * modes
    full = rounded_up(rows, 8)
    pairs_of_vectors = vectors // 2
    height = 4

    basis_rows = in_hbm(basis.transpose(0, 2, 1, 3).reshape(pairs_of_vectors, 2 * rows, columns))
    mie_rows = in_hbm(mie_coeffs.transpose(1, 0, 2).reshape(rows // 4, 4, columns))
    rot_rows = in_hbm(rot_table.transpose(1, 0, 2).reshape(modes * tables, modes))
    axial_rows = in_hbm(axial_table.transpose(0, 2, 1, 3))
    pair_rows = in_hbm(pair_table.transpose(2, 0, 1))

    octets = part * quarter // 16
    piece = jax.ShapeDtypeStruct((2, octets, 16, size), BF16)
    pieces = pl.pallas_call(
        functools.partial(pack_kernel, quarter, modes, ways, own),
        in_specs=[hbm(), pl.BlockSpec(memory_space=pltpu.SMEM), hbm()],
        out_specs=[whole()] * ways,
        out_shape=[piece] * ways,
        scratch_shapes=[
            pltpu.VMEM(pair_rows.shape, jnp.int32),
            pltpu.VMEM((full, columns), F32),
            pltpu.VMEM((size, columns), F32),
            pltpu.VMEM((2 * slots, slots), F32),
            pltpu.VMEM((quarter, columns, size), F32),
            pltpu.SemaphoreType.DMA((2,)),
        ],
        compiler_params=params(16),
        name="pack",
    )(pair_rows, pair_count, basis_rows)
    tall = rounded_up(rows + full, 8)
    *pieces, basis_rows, mie_rows = lax.optimization_barrier((*pieces, basis_rows, mie_rows))
    received = exchanged(pieces, "pair")
    line, blocks, mies = pl.pallas_call(
        functools.partial(gram_kernel, quarter, modes),
        in_specs=[hbm()] * 2,
        out_specs=[whole()] * 3,
        out_shape=[
            jax.ShapeDtypeStruct((1, 128), F32),
            jax.ShapeDtypeStruct((pairs_of_vectors, tall, columns), F32),
            jax.ShapeDtypeStruct((full // height, height, columns), F32),
        ],
        scratch_shapes=[
            pltpu.VMEM((vectors, vectors, 8, columns), F32),
            pltpu.SemaphoreType.DMA,
            pltpu.SemaphoreType.DMA((4, pairs_of_vectors, 2)),
        ],
        compiler_params=params(8),
        name="gram",
    )(basis_rows, mie_rows)
    *received, line, rot_rows, axial_rows = lax.optimization_barrier((*received, line, rot_rows, axial_rows))
    own_pieces = pl.pallas_call(
        join_kernel,
        in_specs=[whole()] * ways,
        out_specs=whole(),
        out_shape=jax.ShapeDtypeStruct((ways, *piece.shape), BF16),
        compiler_params=params(4),
        name="join",
    )(*received)
    below, above = neighbours(own_pieces)

    rotations, axials = pl.pallas_call(
        tables_kernel,
        in_specs=[hbm()] * 2,
        out_specs=[whole()] * 2,
        out_shape=[
            jax.ShapeDtypeStruct((tables, size, size), BF16),
            jax.ShapeDtypeStruct((tables, 2 * size, size), BF16),
        ],
        scratch_shapes=[
            pltpu.VMEM(axial_rows.shape, BF16),
            pltpu.VMEM((tables * size, modes), BF16),
            pltpu.SemaphoreType.DMA((tables + 1,)),
        ],
        compiler_params=params(20),
        cost_estimate=pl.CostEstimate(flops=tables * 8 * 256 * 256 * size, bytes_accessed=6 * tables * size * size * 2, transcendentals=0),
        name="tables",
    )(axial_rows, rot_rows)
    below, above, rotations, axials = lax.optimization_barrier((below, above, rotations, axials))

    together = 2 if tables % 2 == 0 else 1
    field = pl.pallas_call(
        functools.partial(field_kernel, own, modes, together),
        in_specs=[whole()] * 5,
        out_specs=[whole()] * ways,
        out_shape=[jax.ShapeDtypeStruct((2, quarter, part, size), BF16)] * ways,
        scratch_shapes=[pltpu.VMEM((tables, 4 * group, size), BF16), pltpu.VMEM((2 * group, size), F32)],
        compiler_params=params(20),
        name="field",
    )(rotations, axials, below, own_pieces, above)
    field_pieces = exchanged(field, "pair")

    image, sums = pl.pallas_call(
        functools.partial(image_kernel, quarter, modes),
        in_specs=[whole()] * (ways + 3),
        out_specs=[whole()] * 2,
        out_shape=[jax.ShapeDtypeStruct((full, columns), F32), jax.ShapeDtypeStruct((ways * blk_ways, 1, 128), F32)],
        scratch_shapes=[pltpu.VMEM((full, columns), F32), pltpu.VMEM((quarter, columns, size), BF16)],
        compiler_params=params(8),
        name="image",
    )(blocks, mies, line, *field_pieces)
    sums = lax.all_to_all(sums, ("blk", "pair"), split_axis=0, concat_axis=0, tiled=True)

    mean_scale = 1.0 / (own * blk_ways * modes * columns)
    dots, next_rows = pl.pallas_call(
        functools.partial(remainder_kernel, quarter, modes, mean_scale),
        in_specs=[whole()] * 3,
        out_specs=[whole(), whole()],
        out_shape=[jax.ShapeDtypeStruct((2, vectors), F32), jax.ShapeDtypeStruct((rows // height, height, columns), F32)],
        compiler_params=params(16),
        name="remainder",
    )(sums, blocks, image)
    return dots, next_rows.reshape(modes, quarter, columns).transpose(1, 0, 2)


def solution(mesh):
    placed = (
        P(None, ("blk", "pair"), None, None),
        P(("blk", "pair"), None, None),
        P(),
        P(),
        P("blk", None, None),
        P("blk"),
    )
    return jax.shard_map(
        shards,
        mesh=mesh,
        in_specs=placed,
        out_specs=(P(), P(("blk", "pair"), None, None)),
        check_vma=False,
    )
```

```python
import functools

import jax
import jax.numpy as jnp
from jax import lax
from jax.experimental import pallas as pl
from jax.experimental.pallas import tpu as pltpu
from jax.sharding import PartitionSpec as P

MIB = 1024 * 1024
F32 = jnp.float32
BF16 = jnp.bfloat16


def params(mib):
    return pltpu.CompilerParams(vmem_limit_bytes=mib * MIB)


def hbm():
    return pl.BlockSpec(memory_space=pltpu.HBM)


def whole():
    return pl.BlockSpec(memory_space=pltpu.VMEM)


def in_hbm(value):
    return pltpu.with_memory_space_constraint(value, pltpu.HBM)


def rounded_up(value, unit):
    return (value + unit - 1) // unit * unit


def iota(shape, dim):
    return lax.broadcasted_iota(jnp.int32, shape, dim)


def dot_nn(left, right):
    return lax.dot_general(left, right, (((1,), (0,)), ((), ())), preferred_element_type=F32)


def dot_nt(left, right):
    return lax.dot_general(left, right, (((1,), (1,)), ((), ())), preferred_element_type=F32)


def pack_kernel(quarter, modes, ways, own, list_ref, count_ref, basis_ref, *rest):
    outs, (pair_rows_ref, lines_ref, pad_ref, codes_ref, turned_ref, sems) = rest[:ways], rest[ways:]
    full, columns = lines_ref.shape
    rows = quarter * modes
    part = columns // 2 // ways
    copy = pltpu.make_async_copy(basis_ref.at[basis_ref.shape[0] - 1, pl.ds(2 * rows - full, full)], lines_ref, sems.at[0])
    copy.start()
    list_copy = pltpu.make_async_copy(list_ref, pair_rows_ref, sems.at[1])
    list_copy.start()
    pad_ref[...] = jnp.zeros_like(pad_ref)
    list_copy.wait()
    slots = pair_rows_ref.shape[2]
    live = iota((1, slots), 1) < count_ref[0]
    marks = jnp.where(live, own * (pair_rows_ref[2] + 1) + pair_rows_ref[0], 0)
    line = iota((slots, slots), 0)
    stacked = jnp.where(line == 0, marks, jnp.where(line == 1, pair_rows_ref[1], 0))
    turned = jnp.transpose(stacked.astype(F32))
    codes_ref[0:slots, :] = turned
    codes_ref[slots : 2 * slots, :] = pltpu.roll(turned, slots - 1, axis=1)
    share = 2 * quarter * part
    mine = codes_ref[pl.ds(pl.multiple_of(lax.axis_index("pair") * share, share), share), :][:, 0:1]
    copy.wait()
    for j in range(quarter):
        pad_ref[0:modes, :] = lines_ref[pl.ds(full - rows + j, modes, quarter), :]
        turned_ref[j] = jnp.transpose(pad_ref[...])
    _, octets, height, size = outs[0].shape
    each = height // quarter
    for i, out_ref in enumerate(outs):
        place = (lax.axis_index("pair") ^ i) * part
        for c in range(2):
            for o in range(octets):
                first = (c * octets + o) * height
                here = pl.ds(pl.multiple_of(c * (columns // 2) + place + o * each, each), each)
                piece = jnp.concatenate([turned_ref[j, here, :] for j in range(quarter)], axis=0)
                piece = jnp.where(iota(piece.shape, 1) == modes, mine[first : first + height], piece)
                out_ref[c, o] = piece.astype(BF16)


def join_kernel(*refs):
    out_ref = refs[-1]
    for i, ref in enumerate(refs[:-1]):
        out_ref[lax.axis_index("pair") ^ i] = ref[...]


def tables_kernel(axial_ref, rot_ref, rot_out_ref, axial_out_ref, axials_ref, rots_ref, sems):
    tables, size, _ = rot_out_ref.shape
    modes = axial_ref.shape[1]
    listed = rot_ref.shape[0]

    def fetch(g):
        return pltpu.make_async_copy(axial_ref.at[g], axials_ref.at[g], sems.at[g])

    for g in range(tables):
        fetch(g).start()
    rot_copy = pltpu.make_async_copy(rot_ref, rots_ref.at[pl.ds(0, listed)], sems.at[tables])
    rot_copy.start()
    chunk = 256
    out_row, in_row = iota((chunk, chunk), 0), iota((chunk, chunk), 1)
    each = chunk // 2
    halves = (in_row == 2 * lax.rem(out_row, each) + lax.div(out_row, each)).astype(F32).astype(BF16)
    share = chunk // tables
    entries = (in_row == tables * lax.rem(out_row, share) + lax.div(out_row, share)).astype(F32).astype(BF16)
    for ref in (rot_out_ref, axial_out_ref):
        ref[:, :, size - 128 : size] = jnp.zeros((tables, ref.shape[1], 128), BF16)
    rots_ref[listed:, :] = jnp.zeros((rots_ref.shape[0] - listed, modes), BF16)

    def split(g, carry):
        fetch(g).wait()
        for first in range(0, modes, each):
            count = min(each, modes - first)
            rows = axials_ref[g, first : first + count].reshape(2 * count, modes)
            sorted_rows = dot_nn(halves[:, : 2 * count], rows).astype(BF16)
            for c in range(2):
                axial_out_ref[g, c * size + first : c * size + first + each, 0:modes] = sorted_rows[c * each : (c + 1) * each]
        return carry

    lax.fori_loop(0, tables, split, 0)
    rot_copy.wait()

    def pick(i, carry):
        rows = rots_ref[pl.ds(pl.multiple_of(i * chunk, chunk), chunk), :]
        sorted_rows = dot_nn(entries, rows).astype(BF16)
        for g in range(tables):
            here = pl.ds(pl.multiple_of(i * share, share), share)
            rot_out_ref[g, here, 0:modes] = sorted_rows[g * share : (g + 1) * share]
        return carry

    lax.fori_loop(0, rots_ref.shape[0] // chunk, pick, 0)


def swapped(value):
    half = value.shape[0] // 2
    return jnp.concatenate([-value[half:], value[:half]], axis=0)


def pair_counts(own, tables, lane, refs):
    ways, parts, octets, height, size = refs[0].shape
    group = ways * octets * height
    wanted = iota((tables * own, group), 0) + own

    def one_hot(hit):
        return jnp.where(hit, 1.0, 0.0).astype(BF16)

    forward, backward = None, []
    for window, ref in enumerate(refs):
        values = ref[:, :, :, :, size - 128 : size].reshape(2 * group, 128).astype(F32)
        marks_column, sources_column = (values[h * group : (h + 1) * group, lane : lane + 1].astype(jnp.int32) for h in range(2))
        marks, sources = (jnp.transpose(values[h * group : (h + 1) * group])[lane : lane + 1].astype(jnp.int32) for h in range(2))
        if window == 1:
            forward = dot_nn(one_hot(marks == wanted), one_hot(sources_column == iota((group, 3 * own), 1)))
        block = sources - (2 - window) * own
        inside = (block >= 0) & (block < own) & (marks >= own)
        hits = one_hot(jnp.where(inside, lax.div(marks, own) * own + block, -1) == wanted)
        place = lax.rem(marks_column, own) + window * own
        backward.append(dot_nn(hits, one_hot(place == iota((group, 3 * own), 1))))
    return jnp.concatenate([forward, sum(backward)], axis=0).astype(BF16)


def folded(value):
    return jnp.sum(value.reshape(value.shape[0] // 8, 8, value.shape[1]), axis=0)


def field_kernel(
    own, modes, together, rot_ref, axial_ref, below_ref, own_ref, above_ref, *rest
):
    outs, (sums_ref, total_ref) = rest[:-2], rest[-2:]
    tables, _, size = rot_ref.shape
    refs = (below_ref, own_ref, above_ref)
    ways, _, octets, height, _ = own_ref.shape
    quarter = own // ways
    each = height // quarter
    part = octets * each
    group = own * part
    counts = pair_counts(own, tables, modes % 128, refs)
    spread = jnp.where(iota((3 * own, 3 * own * each), 0) == lax.div(iota((3 * own, 3 * own * each), 1), each), 1.0, 0.0)
    counts = dot_nn(counts, spread.astype(BF16))
    sphere = lax.rem(iota(counts.shape, 1), each)
    chosen = jnp.concatenate([jnp.where(sphere == i, counts, 0.0).astype(BF16) for i in range(each)], axis=0)
    kinds = 2 * tables * own
    for c in range(2):
        for o in range(octets):
            blocks = jnp.concatenate([ref[:, c, o].reshape(ways * height, size) for ref in refs], axis=0)
            for i in range(0, each, 2):
                results = dot_nn(chosen[i * kinds : (i + 2) * kinds], blocks)
                for kind in range(2 * tables):
                    direction, g = kind // tables, kind % tables
                    rows = [results[start + kind * own : start + (kind + 1) * own] for start in (0, kinds)]
                    place = (direction * 2 + c) * group + (o * each + i) * own
                    sums_ref[g, place : place + 2 * own, :] = jnp.concatenate(rows, axis=0).astype(BF16)
    total_ref[...] = jnp.zeros_like(total_ref)

    def body(step, carry):
        entries = [step * together + i for i in range(together)]
        turned = [dot_nt(sums_ref[g], rot_ref[g]).astype(BF16) for g in entries]
        moved = []
        for g, both in zip(entries, turned):
            forward, backward = both[: 2 * group], both[2 * group :]
            result = dot_nt(forward, axial_ref[g, :size]) + dot_nt(swapped(forward), axial_ref[g, size:])
            result += dot_nn(jnp.concatenate([backward, swapped(backward)], axis=1), axial_ref[g])
            moved.append(result.astype(BF16))
        total_ref[...] += sum(dot_nn(value, rot_ref[g]) for g, value in zip(entries, moved))
        return carry

    lax.fori_loop(0, tables // together, body, 0)
    row, source = iota((2 * group, 2 * group), 0), iota((2 * group, 2 * group), 1)
    sphere, c = lax.rem(row, part), lax.rem(lax.div(row, quarter * part), 2)
    owner = lax.div(row, 2 * quarter * part) ^ lax.axis_index("pair")
    block = owner * quarter + lax.rem(lax.div(row, part), quarter)
    order = jnp.where(source == c * group + sphere * own + block, 1.0, 0.0).astype(BF16)
    result = dot_nn(order, total_ref[...].astype(BF16)).astype(BF16)
    share = 2 * quarter * part
    for i, out_ref in enumerate(outs):
        out_ref[...] = result[i * share : (i + 1) * share].reshape(out_ref.shape)


def lane_swap(value):
    half = value.shape[1] // 2
    rolled = pltpu.roll(value, half, axis=1)
    return jnp.where(iota(value.shape, 1) < half, -rolled, rolled)


def add_products(blocks_ref, products_ref, rows, first, count):
    vectors = products_ref.shape[0]
    values = []
    for k in range(vectors):
        start = k % 2 * rows + first
        value = blocks_ref[k // 2, start : start + count, :]
        if k % 2 == 0 and first + count > rows:
            value = jnp.where(iota(value.shape, 0) < rows - first, value, 0.0)
        values.append(value)
    for l in range(vectors):
        other = pltpu.roll(values[l], values[l].shape[1] // 2, axis=1)
        for k in range(l + 1):
            products_ref[k, l] += folded(values[k] * values[l])
            if k < l:
                products_ref[l, k] += folded(values[k] * other)


def products_line(products_ref):
    vectors, _, _, columns = products_ref.shape
    pairs = vectors * vectors
    totals = jnp.sum(products_ref[...].reshape(pairs, 8, columns), axis=1)
    pair = iota(totals.shape, 0)
    signed = (lax.div(pair, vectors) > lax.rem(pair, vectors)) & (iota(totals.shape, 1) >= columns // 2)
    totals = jnp.sum(jnp.where(signed, -totals, totals), axis=1, keepdims=True)
    row, lane = iota((vectors, 128), 0), iota((vectors, 128), 1)
    line = jnp.zeros((1, 128), F32)
    for k in range(vectors):
        column = totals[k * vectors : (k + 1) * vectors]
        line += jnp.sum(jnp.where(row + k * vectors == lane, column, 0.0), axis=0, keepdims=True)
    return line


def gram_kernel(quarter, modes, basis_ref, mie_ref, products_ref, blocks_ref, mies_ref, mie_sem, sems):
    blocks, _, columns = basis_ref.shape
    rows = quarter * modes
    parts, chunk = 4, 32
    tile_end = rows // 8 * 8
    step = rounded_up(rows, 8 * parts) // parts
    even = [0] + [step * q for q in range(1, parts)] + [tile_end]
    odd = [tile_end] + [rounded_up(rows, 8) + step * q for q in range(1, parts)] + [2 * rows]
    copies = []
    for q in range(parts):
        for i in range(blocks):
            for side, cuts in enumerate((even, odd)):
                here = pl.ds(cuts[q], cuts[q + 1] - cuts[q])
                copies.append(pltpu.make_async_copy(basis_ref.at[i, here], blocks_ref.at[i, here], sems.at[q, i, side]))
    for copy in copies:
        copy.start()
    mie_rows = mie_ref.shape[0]
    mie_copy = pltpu.make_async_copy(mie_ref, mies_ref.at[pl.ds(0, mie_rows)], mie_sem)
    mie_copy.start()
    mies_ref[mie_rows:] = jnp.zeros((mies_ref.shape[0] - mie_rows,) + mies_ref.shape[1:], F32)
    products_ref[...] = jnp.zeros_like(products_ref)
    for i in range(blocks):
        blocks_ref[i, 2 * rows :, :] = jnp.zeros((blocks_ref.shape[1] - 2 * rows, columns), F32)
    for q in range(parts):
        for copy in copies[2 * blocks * q : 2 * blocks * (q + 1)]:
            copy.wait()
        if q < parts - 1:
            for first in range(step * q, step * (q + 1), chunk):
                add_products(blocks_ref, products_ref, rows, first, chunk)
    mie_copy.wait()


def gram_end_kernel(quarter, modes, products_ref, blocks_ref, line_ref, totals_ref):
    rows = quarter * modes
    parts, chunk = 4, 32
    totals_ref[...] = products_ref[...]
    for first in range(rounded_up(rows, 8 * parts) // parts * (parts - 1), rows, chunk):
        add_products(blocks_ref, totals_ref, rows, first, chunk)
    line_ref[...] = products_line(totals_ref)


def image_kernel(quarter, modes, blocks_ref, mie_ref, gram_ref, *rest):
    pieces, (image_ref, sums_ref, lines_ref, whole_ref) = rest[:-4], rest[-4:]
    vectors = 2 * blocks_ref.shape[0]
    full, columns = image_ref.shape
    rows = quarter * modes
    part = pieces[0].shape[2]
    for i, piece_ref in enumerate(pieces):
        place = pl.multiple_of((lax.axis_index("pair") ^ i) * part, part)
        for j in range(quarter):
            for c in range(2):
                whole_ref[j, pl.ds(c * (columns // 2) + place, part), :] = piece_ref[c, j]
    lines_ref[rows:full, :] = jnp.zeros((full - rows, columns), F32)
    for j in range(quarter):
        lines_ref[pl.ds(j, modes, quarter), :] = jnp.transpose(whole_ref[j].astype(F32))[:modes]
    half = columns // 2
    chunk = 64
    totals = [jnp.zeros((8, columns), F32) for _ in range(2 * vectors + 1)]
    for first in range(0, full, chunk):
        here = slice(first, first + chunk)
        field = lines_ref[here, :]
        count = min(chunk, rows - first)
        height = mie_ref.shape[1]
        mie = mie_ref[first // height : (first + count) // height].reshape(count, columns)
        if count < chunk:
            mie = jnp.concatenate([mie, jnp.zeros((chunk - count, columns), F32)], axis=0)
        left = iota(mie.shape, 1) < half
        other = pltpu.roll(mie, half, axis=1)
        product = jnp.where(left, mie, other) * field + jnp.where(left, -other, mie) * pltpu.roll(field, half, axis=1)
        last = (vectors - 1) % 2 * rows + first
        image = blocks_ref[(vectors - 1) // 2, last : last + chunk, :] - product
        image_ref[here, :] = image
        turned = pltpu.roll(image, half, axis=1)
        for k in range(vectors):
            start = k % 2 * rows + first
            values = blocks_ref[k // 2, start : start + chunk, :]
            totals[2 * k] += folded(values * image)
            totals[2 * k + 1] += folded(values * turned)
        totals[2 * vectors] += folded(image * image)
    lane = iota(gram_ref.shape, 1)
    line = gram_ref[...]
    left = iota((8, columns), 1) < half
    for index, total in enumerate(totals):
        if index % 2 and index < 2 * vectors:
            total = jnp.where(left, total, -total)
        line = jnp.where(lane == vectors * vectors + index, jnp.sum(total, axis=(0, 1), keepdims=True), line)
    sums_ref[...] = jnp.broadcast_to(line[None], sums_ref.shape)


def remainder_kernel(quarter, modes, mean_scale, sums_ref, blocks_ref, image_ref, dots_ref, out_ref, rows_ref, sems):
    vectors = 2 * blocks_ref.shape[0]
    full, columns = image_ref.shape
    rows = quarter * modes
    total = jnp.sum(sums_ref[...], axis=0)
    lane = iota(total.shape, 1)

    def lane_at(index):
        return jnp.sum(jnp.where(lane == index, total, 0.0), axis=1, keepdims=True)

    def on_lanes(parts, places):
        line = jnp.zeros(total.shape, F32)
        for k in range(vectors):
            line = jnp.where(places == k, parts[k], line)
        return line

    start = vectors * vectors
    real = [lane_at(start + 2 * k) * mean_scale for k in range(vectors)]
    imag = [lane_at(start + 2 * k + 1) * mean_scale for k in range(vectors)]
    real_line, imag_line = on_lanes(real, lane), on_lanes(imag, lane)
    dots_ref[0:1, :] = real_line[:, :vectors]
    dots_ref[1:2, :] = imag_line[:, :vectors]
    first_index, last_index = lax.div(lane, vectors), lax.rem(lane, vectors)
    real_first, real_last = on_lanes(real, first_index), on_lanes(real, last_index)
    imag_first, imag_last = on_lanes(imag, first_index), on_lanes(imag, last_index)
    same = real_first * real_last + imag_first * imag_last
    cross = imag_last * real_first - real_last * imag_first
    often = jnp.where(first_index == last_index, 1.0, 2.0)
    spread = jnp.where(lane < start, total * often * jnp.where(first_index <= last_index, same, cross), 0.0)
    spread = jnp.sum(spread, axis=1, keepdims=True)
    inside = jnp.sum(real_line * real_line + imag_line * imag_line, axis=1, keepdims=True)
    norm_square = (lane_at(start + 2 * vectors) + spread) * mean_scale - 2.0 * inside
    scale = lax.rsqrt(norm_square)
    image_scale = jnp.broadcast_to(scale, (8, columns))
    reals = [jnp.broadcast_to(real[k] * scale, (8, columns)) for k in range(vectors)]
    imags = [jnp.broadcast_to(imag[k] * scale, (8, columns)) for k in range(vectors)]
    chunk = 64
    height = out_ref.shape[1]
    copies = []
    for first in range(0, full, chunk):
        here = slice(first, first + chunk)
        values = []
        for k in range(vectors):
            start = k % 2 * rows + first
            values.append(blocks_ref[k // 2, start : start + chunk, :].reshape(chunk // 8, 8, columns))
        along = image_ref[here, :].reshape(chunk // 8, 8, columns) * image_scale
        turned = jnp.zeros_like(along)
        for k in range(vectors):
            along -= reals[k] * values[k]
            turned += imags[k] * values[k]
        result = along.reshape(chunk, columns) - lane_swap(turned.reshape(chunk, columns))
        count = min(chunk, rows - first)
        rows_ref[first // height : (first + count) // height] = result.reshape(chunk // height, height, columns)[: count // height]
        index = first // chunk
        if index % 4 == 3 or first + chunk >= rows:
            here = pl.ds(index // 4 * 4 * chunk // height, (first + count - index // 4 * 4 * chunk) // height)
            copies.append(pltpu.make_async_copy(rows_ref.at[here], out_ref.at[here], sems.at[index // 4]))
            copies[-1].start()
    for copy in copies:
        copy.wait()


def exchanged(pieces, axis):
    count = lax.axis_size(axis)
    received = [pieces[0]]
    for i in range(1, len(pieces)):
        received.append(lax.ppermute(pieces[i], axis, [(p, p ^ i) for p in range(count)]))
    return received


def neighbours(value):
    count = lax.axis_size("blk")
    up = [(i, i + 1) for i in range(count - 1)]
    down = [(j, i) for i, j in up]
    return lax.ppermute(value, "blk", up), lax.ppermute(value, "blk", down)


def shards(basis, mie_coeffs, rot_table, axial_table, pair_table, pair_count):
    vectors, quarter, modes, columns = basis.shape
    ways = lax.axis_size("pair")
    blk_ways = lax.axis_size("blk")
    tables = rot_table.shape[0]
    slots = pair_table.shape[1]
    own = quarter * ways
    part = columns // 2 // ways
    group = own * part
    size = rounded_up(modes, 128)
    rows = quarter * modes
    full = rounded_up(rows, 8)
    pairs_of_vectors = vectors // 2
    height = 4

    basis_rows = in_hbm(basis.transpose(0, 2, 1, 3).reshape(pairs_of_vectors, 2 * rows, columns))
    mie_rows = in_hbm(mie_coeffs.transpose(1, 0, 2).reshape(rows // 4, 4, columns))
    rot_rows = in_hbm(rot_table.transpose(1, 0, 2).reshape(modes * tables, modes))
    axial_rows = in_hbm(axial_table.transpose(0, 2, 1, 3))
    pair_rows = in_hbm(pair_table.transpose(2, 0, 1))

    octets = part * quarter // 16
    piece = jax.ShapeDtypeStruct((2, octets, 16, size), BF16)
    pieces = pl.pallas_call(
        functools.partial(pack_kernel, quarter, modes, ways, own),
        in_specs=[hbm(), pl.BlockSpec(memory_space=pltpu.SMEM), hbm()],
        out_specs=[whole()] * ways,
        out_shape=[piece] * ways,
        scratch_shapes=[
            pltpu.VMEM(pair_rows.shape, jnp.int32),
            pltpu.VMEM((full, columns), F32),
            pltpu.VMEM((size, columns), F32),
            pltpu.VMEM((2 * slots, slots), F32),
            pltpu.VMEM((quarter, columns, size), F32),
            pltpu.SemaphoreType.DMA((2,)),
        ],
        compiler_params=params(16),
        name="pack",
    )(pair_rows, pair_count, basis_rows)
    tall = rounded_up(rows + full, 8)
    *pieces, basis_rows, mie_rows = lax.optimization_barrier((*pieces, basis_rows, mie_rows))
    received = exchanged(pieces, "pair")
    products, blocks, mies = pl.pallas_call(
        functools.partial(gram_kernel, quarter, modes),
        in_specs=[hbm()] * 2,
        out_specs=[whole()] * 3,
        out_shape=[
            jax.ShapeDtypeStruct((vectors, vectors, 8, columns), F32),
            jax.ShapeDtypeStruct((pairs_of_vectors, tall, columns), F32),
            jax.ShapeDtypeStruct((full // height, height, columns), F32),
        ],
        scratch_shapes=[
            pltpu.SemaphoreType.DMA,
            pltpu.SemaphoreType.DMA((4, pairs_of_vectors, 2)),
        ],
        compiler_params=params(8),
        name="gram",
    )(basis_rows, mie_rows)
    *received, products, rot_rows, axial_rows = lax.optimization_barrier((*received, products, rot_rows, axial_rows))
    own_pieces = pl.pallas_call(
        join_kernel,
        in_specs=[whole()] * ways,
        out_specs=whole(),
        out_shape=jax.ShapeDtypeStruct((ways, *piece.shape), BF16),
        compiler_params=params(4),
        name="join",
    )(*received)
    below, above = neighbours(own_pieces)

    rotations, axials = pl.pallas_call(
        tables_kernel,
        in_specs=[hbm()] * 2,
        out_specs=[whole()] * 2,
        out_shape=[
            jax.ShapeDtypeStruct((tables, size, size), BF16),
            jax.ShapeDtypeStruct((tables, 2 * size, size), BF16),
        ],
        scratch_shapes=[
            pltpu.VMEM(axial_rows.shape, BF16),
            pltpu.VMEM((tables * size, modes), BF16),
            pltpu.SemaphoreType.DMA((tables + 1,)),
        ],
        compiler_params=params(20),
        cost_estimate=pl.CostEstimate(flops=tables * 8 * 256 * 256 * size, bytes_accessed=6 * tables * size * size * 2, transcendentals=0),
        name="tables",
    )(axial_rows, rot_rows)
    own_pieces, products = lax.optimization_barrier((own_pieces, products))
    line = pl.pallas_call(
        functools.partial(gram_end_kernel, quarter, modes),
        in_specs=[whole()] * 2,
        out_specs=whole(),
        out_shape=jax.ShapeDtypeStruct((1, 128), F32),
        scratch_shapes=[pltpu.VMEM((vectors, vectors, 8, columns), F32)],
        compiler_params=params(4),
        name="gram_end",
    )(products, blocks)
    below, above, rotations, axials, line = lax.optimization_barrier((below, above, rotations, axials, line))

    together = 1
    field = pl.pallas_call(
        functools.partial(field_kernel, own, modes, together),
        in_specs=[whole()] * 5,
        out_specs=[whole()] * ways,
        out_shape=[jax.ShapeDtypeStruct((2, quarter, part, size), BF16)] * ways,
        scratch_shapes=[pltpu.VMEM((tables, 4 * group, size), BF16), pltpu.VMEM((2 * group, size), F32)],
        compiler_params=params(20),
        name="field",
    )(rotations, axials, below, own_pieces, above)
    field_pieces = exchanged(field, "pair")

    image, sums = pl.pallas_call(
        functools.partial(image_kernel, quarter, modes),
        in_specs=[whole()] * (ways + 3),
        out_specs=[whole()] * 2,
        out_shape=[jax.ShapeDtypeStruct((full, columns), F32), jax.ShapeDtypeStruct((ways * blk_ways, 1, 128), F32)],
        scratch_shapes=[pltpu.VMEM((full, columns), F32), pltpu.VMEM((quarter, columns, size), BF16)],
        compiler_params=params(8),
        name="image",
    )(blocks, mies, line, *field_pieces)
    sums = lax.all_to_all(sums, ("blk", "pair"), split_axis=0, concat_axis=0, tiled=True)

    mean_scale = 1.0 / (own * blk_ways * modes * columns)
    dots, next_rows = pl.pallas_call(
        functools.partial(remainder_kernel, quarter, modes, mean_scale),
        in_specs=[whole()] * 3,
        out_specs=[whole(), hbm()],
        out_shape=[jax.ShapeDtypeStruct((2, vectors), F32), jax.ShapeDtypeStruct((rows // height, height, columns), F32)],
        scratch_shapes=[pltpu.VMEM((rows // height, height, columns), F32), pltpu.SemaphoreType.DMA((rounded_up(full, 256) // 256,))],
        compiler_params=params(16),
        name="remainder",
    )(sums, blocks, image)
    return dots, next_rows.reshape(modes, quarter, columns).transpose(1, 0, 2)


def solution(mesh):
    placed = (
        P(None, ("blk", "pair"), None, None),
        P(("blk", "pair"), None, None),
        P(),
        P(),
        P("blk", None, None),
        P("blk"),
    )
    return jax.shard_map(
        shards,
        mesh=mesh,
        in_specs=placed,
        out_specs=(P(), P(("blk", "pair"), None, None)),
        check_vma=False,
    )
```

```python
import functools

import jax
import jax.numpy as jnp
from jax import lax
from jax.experimental import pallas as pl
from jax.experimental.pallas import tpu as pltpu
from jax.sharding import PartitionSpec as P

MIB = 1024 * 1024
F32 = jnp.float32
BF16 = jnp.bfloat16


def params(mib):
    return pltpu.CompilerParams(vmem_limit_bytes=mib * MIB)


def hbm():
    return pl.BlockSpec(memory_space=pltpu.HBM)


def whole():
    return pl.BlockSpec(memory_space=pltpu.VMEM)


def in_hbm(value):
    return pltpu.with_memory_space_constraint(value, pltpu.HBM)


def rounded_up(value, unit):
    return (value + unit - 1) // unit * unit


def iota(shape, dim):
    return lax.broadcasted_iota(jnp.int32, shape, dim)


def dot_nn(left, right):
    return lax.dot_general(left, right, (((1,), (0,)), ((), ())), preferred_element_type=F32)


def dot_nt(left, right):
    return lax.dot_general(left, right, (((1,), (1,)), ((), ())), preferred_element_type=F32)


def pack_kernel(quarter, modes, ways, own, list_ref, count_ref, basis_ref, *rest):
    outs, (pair_rows_ref, lines_ref, pad_ref, codes_ref, turned_ref, sems) = rest[:ways], rest[ways:]
    full, columns = lines_ref.shape
    rows = quarter * modes
    part = columns // 2 // ways
    copy = pltpu.make_async_copy(basis_ref.at[basis_ref.shape[0] - 1, pl.ds(2 * rows - full, full)], lines_ref, sems.at[0])
    copy.start()
    list_copy = pltpu.make_async_copy(list_ref, pair_rows_ref, sems.at[1])
    list_copy.start()
    pad_ref[...] = jnp.zeros_like(pad_ref)
    list_copy.wait()
    slots = pair_rows_ref.shape[2]
    live = iota((1, slots), 1) < count_ref[0]
    marks = jnp.where(live, own * (pair_rows_ref[2] + 1) + pair_rows_ref[0], 0)
    line = iota((slots, slots), 0)
    stacked = jnp.where(line == 0, marks, jnp.where(line == 1, pair_rows_ref[1], 0))
    turned = jnp.transpose(stacked.astype(F32))
    codes_ref[0:slots, :] = turned
    codes_ref[slots : 2 * slots, :] = pltpu.roll(turned, slots - 1, axis=1)
    share = 2 * quarter * part
    mine = codes_ref[pl.ds(pl.multiple_of(lax.axis_index("pair") * share, share), share), :][:, 0:1]
    copy.wait()
    for j in range(quarter):
        pad_ref[0:modes, :] = lines_ref[pl.ds(full - rows + j, modes, quarter), :]
        turned_ref[j] = jnp.transpose(pad_ref[...])
    _, octets, height, size = outs[0].shape
    each = height // quarter
    for i, out_ref in enumerate(outs):
        place = (lax.axis_index("pair") ^ i) * part
        for c in range(2):
            for o in range(octets):
                first = (c * octets + o) * height
                here = pl.ds(pl.multiple_of(c * (columns // 2) + place + o * each, each), each)
                piece = jnp.concatenate([turned_ref[j, here, :] for j in range(quarter)], axis=0)
                piece = jnp.where(iota(piece.shape, 1) == modes, mine[first : first + height], piece)
                out_ref[c, o] = piece.astype(BF16)


def join_kernel(*refs):
    out_ref = refs[-1]
    for i, ref in enumerate(refs[:-1]):
        out_ref[lax.axis_index("pair") ^ i] = ref[...]


def tables_kernel(axial_ref, rot_ref, rot_out_ref, axial_out_ref, axials_ref, rots_ref, sems):
    tables, size, _ = rot_out_ref.shape
    modes = axial_ref.shape[1]
    listed = rot_ref.shape[0]

    def fetch(g):
        return pltpu.make_async_copy(axial_ref.at[g], axials_ref.at[g], sems.at[g])

    for g in range(tables):
        fetch(g).start()
    rot_copy = pltpu.make_async_copy(rot_ref, rots_ref.at[pl.ds(0, listed)], sems.at[tables])
    rot_copy.start()
    chunk = 256
    out_row, in_row = iota((chunk, chunk), 0), iota((chunk, chunk), 1)
    each = chunk // 2
    halves = (in_row == 2 * lax.rem(out_row, each) + lax.div(out_row, each)).astype(F32).astype(BF16)
    share = chunk // tables
    entries = (in_row == tables * lax.rem(out_row, share) + lax.div(out_row, share)).astype(F32).astype(BF16)
    for ref in (rot_out_ref, axial_out_ref):
        ref[:, :, size - 128 : size] = jnp.zeros((tables, ref.shape[1], 128), BF16)
    rots_ref[listed:, :] = jnp.zeros((rots_ref.shape[0] - listed, modes), BF16)

    def split(g, carry):
        fetch(g).wait()
        for first in range(0, modes, each):
            count = min(each, modes - first)
            rows = axials_ref[g, first : first + count].reshape(2 * count, modes)
            sorted_rows = dot_nn(halves[:, : 2 * count], rows).astype(BF16)
            for c in range(2):
                axial_out_ref[g, c * size + first : c * size + first + each, 0:modes] = sorted_rows[c * each : (c + 1) * each]
        return carry

    lax.fori_loop(0, tables, split, 0)
    rot_copy.wait()

    def pick(i, carry):
        rows = rots_ref[pl.ds(pl.multiple_of(i * chunk, chunk), chunk), :]
        sorted_rows = dot_nn(entries, rows).astype(BF16)
        for g in range(tables):
            here = pl.ds(pl.multiple_of(i * share, share), share)
            rot_out_ref[g, here, 0:modes] = sorted_rows[g * share : (g + 1) * share]
        return carry

    lax.fori_loop(0, rots_ref.shape[0] // chunk, pick, 0)


def swapped(value):
    half = value.shape[0] // 2
    return jnp.concatenate([-value[half:], value[:half]], axis=0)


def pair_counts(own, tables, lane, refs):
    ways, parts, octets, height, size = refs[0].shape
    group = ways * octets * height
    wanted = iota((tables * own, group), 0) + own

    def one_hot(hit):
        return jnp.where(hit, 1.0, 0.0).astype(BF16)

    forward, backward = None, []
    for window, ref in enumerate(refs):
        values = ref[:, :, :, :, size - 128 : size].reshape(2 * group, 128).astype(F32)
        marks_column, sources_column = (values[h * group : (h + 1) * group, lane : lane + 1].astype(jnp.int32) for h in range(2))
        marks, sources = (jnp.transpose(values[h * group : (h + 1) * group])[lane : lane + 1].astype(jnp.int32) for h in range(2))
        if window == 1:
            forward = dot_nn(one_hot(marks == wanted), one_hot(sources_column == iota((group, 3 * own), 1)))
        block = sources - (2 - window) * own
        inside = (block >= 0) & (block < own) & (marks >= own)
        hits = one_hot(jnp.where(inside, lax.div(marks, own) * own + block, -1) == wanted)
        place = lax.rem(marks_column, own) + window * own
        backward.append(dot_nn(hits, one_hot(place == iota((group, 3 * own), 1))))
    return jnp.concatenate([forward, sum(backward)], axis=0).astype(BF16)


def folded(value):
    return jnp.sum(value.reshape(value.shape[0] // 8, 8, value.shape[1]), axis=0)


def field_kernel(
    own, modes, together, rot_ref, axial_ref, below_ref, own_ref, above_ref, *rest
):
    outs, (sums_ref, total_ref) = rest[:-2], rest[-2:]
    tables, _, size = rot_ref.shape
    refs = (below_ref, own_ref, above_ref)
    ways, _, octets, height, _ = own_ref.shape
    quarter = own // ways
    each = height // quarter
    part = octets * each
    group = own * part
    counts = pair_counts(own, tables, modes % 128, refs)
    spread = jnp.where(iota((3 * own, 3 * own * each), 0) == lax.div(iota((3 * own, 3 * own * each), 1), each), 1.0, 0.0)
    counts = dot_nn(counts, spread.astype(BF16))
    sphere = lax.rem(iota(counts.shape, 1), each)
    chosen = jnp.concatenate([jnp.where(sphere == i, counts, 0.0).astype(BF16) for i in range(each)], axis=0)
    kinds = 2 * tables * own
    for c in range(2):
        for o in range(octets):
            blocks = jnp.concatenate([ref[:, c, o].reshape(ways * height, size) for ref in refs], axis=0)
            for i in range(0, each, 2):
                results = dot_nn(chosen[i * kinds : (i + 2) * kinds], blocks)
                for kind in range(2 * tables):
                    direction, g = kind // tables, kind % tables
                    rows = [results[start + kind * own : start + (kind + 1) * own] for start in (0, kinds)]
                    place = (direction * 2 + c) * group + (o * each + i) * own
                    sums_ref[g, place : place + 2 * own, :] = jnp.concatenate(rows, axis=0).astype(BF16)
    total_ref[...] = jnp.zeros_like(total_ref)

    def body(step, carry):
        entries = [step * together + i for i in range(together)]
        turned = [dot_nt(sums_ref[g], rot_ref[g]).astype(BF16) for g in entries]
        moved = []
        for g, both in zip(entries, turned):
            forward, backward = both[: 2 * group], both[2 * group :]
            result = dot_nt(forward, axial_ref[g, :size]) + dot_nt(swapped(forward), axial_ref[g, size:])
            result += dot_nn(jnp.concatenate([backward, swapped(backward)], axis=1), axial_ref[g])
            moved.append(result.astype(BF16))
        total_ref[...] += sum(dot_nn(value, rot_ref[g]) for g, value in zip(entries, moved))
        return carry

    lax.fori_loop(0, tables // together, body, 0)
    row, source = iota((2 * group, 2 * group), 0), iota((2 * group, 2 * group), 1)
    sphere, c = lax.rem(row, part), lax.rem(lax.div(row, quarter * part), 2)
    owner = lax.div(row, 2 * quarter * part) ^ lax.axis_index("pair")
    block = owner * quarter + lax.rem(lax.div(row, part), quarter)
    order = jnp.where(source == c * group + sphere * own + block, 1.0, 0.0).astype(BF16)
    result = dot_nn(order, total_ref[...].astype(BF16)).astype(BF16)
    share = 2 * quarter * part
    for i, out_ref in enumerate(outs):
        out_ref[...] = result[i * share : (i + 1) * share].reshape(out_ref.shape)


def lane_swap(value):
    half = value.shape[1] // 2
    rolled = pltpu.roll(value, half, axis=1)
    return jnp.where(iota(value.shape, 1) < half, -rolled, rolled)


def add_products(blocks_ref, products_ref, rows, first, count):
    vectors = products_ref.shape[0]
    values = []
    for k in range(vectors):
        start = k % 2 * rows + first
        value = blocks_ref[k // 2, start : start + count, :]
        if k % 2 == 0 and first + count > rows:
            value = jnp.where(iota(value.shape, 0) < rows - first, value, 0.0)
        values.append(value)
    for l in range(vectors):
        other = pltpu.roll(values[l], values[l].shape[1] // 2, axis=1)
        for k in range(l + 1):
            products_ref[k, l] += folded(values[k] * values[l])
            if k < l:
                products_ref[l, k] += folded(values[k] * other)


def products_line(products_ref):
    vectors, _, _, columns = products_ref.shape
    pairs = vectors * vectors
    totals = jnp.sum(products_ref[...].reshape(pairs, 8, columns), axis=1)
    pair = iota(totals.shape, 0)
    signed = (lax.div(pair, vectors) > lax.rem(pair, vectors)) & (iota(totals.shape, 1) >= columns // 2)
    totals = jnp.sum(jnp.where(signed, -totals, totals), axis=1, keepdims=True)
    row, lane = iota((vectors, 128), 0), iota((vectors, 128), 1)
    line = jnp.zeros((1, 128), F32)
    for k in range(vectors):
        column = totals[k * vectors : (k + 1) * vectors]
        line += jnp.sum(jnp.where(row + k * vectors == lane, column, 0.0), axis=0, keepdims=True)
    return line


def gram_kernel(quarter, modes, basis_ref, mie_ref, products_ref, blocks_ref, mies_ref, mie_sem, sems):
    blocks, _, columns = basis_ref.shape
    rows = quarter * modes
    parts, chunk = 4, 32
    tile_end = rows // 8 * 8
    step = rounded_up(rows, 8 * parts) // parts
    even = [0] + [step * q for q in range(1, parts)] + [tile_end]
    odd = [tile_end] + [rounded_up(rows, 8) + step * q for q in range(1, parts)] + [2 * rows]
    copies = []
    for q in range(parts):
        for i in range(blocks):
            for side, cuts in enumerate((even, odd)):
                here = pl.ds(cuts[q], cuts[q + 1] - cuts[q])
                copies.append(pltpu.make_async_copy(basis_ref.at[i, here], blocks_ref.at[i, here], sems.at[q, i, side]))
    for copy in copies:
        copy.start()
    mie_rows = mie_ref.shape[0]
    mie_copy = pltpu.make_async_copy(mie_ref, mies_ref.at[pl.ds(0, mie_rows)], mie_sem)
    mie_copy.start()
    mies_ref[mie_rows:] = jnp.zeros((mies_ref.shape[0] - mie_rows,) + mies_ref.shape[1:], F32)
    products_ref[...] = jnp.zeros_like(products_ref)
    for i in range(blocks):
        blocks_ref[i, 2 * rows :, :] = jnp.zeros((blocks_ref.shape[1] - 2 * rows, columns), F32)
    for q in range(parts):
        for copy in copies[2 * blocks * q : 2 * blocks * (q + 1)]:
            copy.wait()
        if q < parts - 1:
            for first in range(step * q, step * (q + 1), chunk):
                add_products(blocks_ref, products_ref, rows, first, chunk)
    mie_copy.wait()


def gram_end_kernel(quarter, modes, products_ref, blocks_ref, line_ref, totals_ref):
    rows = quarter * modes
    parts, chunk = 4, 32
    totals_ref[...] = products_ref[...]
    for first in range(rounded_up(rows, 8 * parts) // parts * (parts - 1), rows, chunk):
        add_products(blocks_ref, totals_ref, rows, first, chunk)
    line_ref[...] = products_line(totals_ref)


def image_kernel(quarter, modes, blocks_ref, mie_ref, gram_ref, *rest):
    pieces, (image_ref, sums_ref, lines_ref, whole_ref) = rest[:-4], rest[-4:]
    vectors = 2 * blocks_ref.shape[0]
    full, columns = image_ref.shape
    rows = quarter * modes
    part = pieces[0].shape[2]
    for i, piece_ref in enumerate(pieces):
        place = pl.multiple_of((lax.axis_index("pair") ^ i) * part, part)
        for j in range(quarter):
            for c in range(2):
                whole_ref[j, pl.ds(c * (columns // 2) + place, part), :] = piece_ref[c, j]
    lines_ref[rows:full, :] = jnp.zeros((full - rows, columns), F32)
    for j in range(quarter):
        lines_ref[pl.ds(j, modes, quarter), :] = jnp.transpose(whole_ref[j].astype(F32))[:modes]
    half = columns // 2
    chunk = 64
    totals = [jnp.zeros((8, columns), F32) for _ in range(2 * vectors + 1)]
    for first in range(0, full, chunk):
        here = slice(first, first + chunk)
        field = lines_ref[here, :]
        count = min(chunk, rows - first)
        height = mie_ref.shape[1]
        mie = mie_ref[first // height : (first + count) // height].reshape(count, columns)
        if count < chunk:
            mie = jnp.concatenate([mie, jnp.zeros((chunk - count, columns), F32)], axis=0)
        left = iota(mie.shape, 1) < half
        other = pltpu.roll(mie, half, axis=1)
        product = jnp.where(left, mie, other) * field + jnp.where(left, -other, mie) * pltpu.roll(field, half, axis=1)
        last = (vectors - 1) % 2 * rows + first
        image = blocks_ref[(vectors - 1) // 2, last : last + chunk, :] - product
        image_ref[here, :] = image
        turned = pltpu.roll(image, half, axis=1)
        for k in range(vectors):
            start = k % 2 * rows + first
            values = blocks_ref[k // 2, start : start + chunk, :]
            totals[2 * k] += folded(values * image)
            totals[2 * k + 1] += folded(values * turned)
        totals[2 * vectors] += folded(image * image)
    lane = iota(gram_ref.shape, 1)
    line = gram_ref[...]
    left = iota((8, columns), 1) < half
    for index, total in enumerate(totals):
        if index % 2 and index < 2 * vectors:
            total = jnp.where(left, total, -total)
        line = jnp.where(lane == vectors * vectors + index, jnp.sum(total, axis=(0, 1), keepdims=True), line)
    sums_ref[...] = jnp.broadcast_to(line[None], sums_ref.shape)


def remainder_kernel(quarter, modes, mean_scale, sums_ref, blocks_ref, image_ref, dots_ref, out_ref):
    vectors = 2 * blocks_ref.shape[0]
    full, columns = image_ref.shape
    rows = quarter * modes
    total = jnp.sum(sums_ref[...], axis=0)
    lane = iota(total.shape, 1)

    def lane_at(index):
        return jnp.sum(jnp.where(lane == index, total, 0.0), axis=1, keepdims=True)

    def on_lanes(parts, places):
        line = jnp.zeros(total.shape, F32)
        for k in range(vectors):
            line = jnp.where(places == k, parts[k], line)
        return line

    start = vectors * vectors
    real = [lane_at(start + 2 * k) * mean_scale for k in range(vectors)]
    imag = [lane_at(start + 2 * k + 1) * mean_scale for k in range(vectors)]
    real_line, imag_line = on_lanes(real, lane), on_lanes(imag, lane)
    dots_ref[0:1, :] = real_line[:, :vectors]
    dots_ref[1:2, :] = imag_line[:, :vectors]
    first_index, last_index = lax.div(lane, vectors), lax.rem(lane, vectors)
    real_first, real_last = on_lanes(real, first_index), on_lanes(real, last_index)
    imag_first, imag_last = on_lanes(imag, first_index), on_lanes(imag, last_index)
    same = real_first * real_last + imag_first * imag_last
    cross = imag_last * real_first - real_last * imag_first
    often = jnp.where(first_index == last_index, 1.0, 2.0)
    spread = jnp.where(lane < start, total * often * jnp.where(first_index <= last_index, same, cross), 0.0)
    spread = jnp.sum(spread, axis=1, keepdims=True)
    inside = jnp.sum(real_line * real_line + imag_line * imag_line, axis=1, keepdims=True)
    norm_square = (lane_at(start + 2 * vectors) + spread) * mean_scale - 2.0 * inside
    scale = lax.rsqrt(norm_square)
    image_scale = jnp.broadcast_to(scale, (8, columns))
    reals = [jnp.broadcast_to(real[k] * scale, (8, columns)) for k in range(vectors)]
    imags = [jnp.broadcast_to(imag[k] * scale, (8, columns)) for k in range(vectors)]
    chunk = 64
    for first in range(0, full, chunk):
        here = slice(first, first + chunk)
        values = []
        for k in range(vectors):
            start = k % 2 * rows + first
            values.append(blocks_ref[k // 2, start : start + chunk, :].reshape(chunk // 8, 8, columns))
        along = image_ref[here, :].reshape(chunk // 8, 8, columns) * image_scale
        turned = jnp.zeros_like(along)
        for k in range(vectors):
            along -= reals[k] * values[k]
            turned += imags[k] * values[k]
        result = along.reshape(chunk, columns) - lane_swap(turned.reshape(chunk, columns))
        count = min(chunk, rows - first)
        height = out_ref.shape[1]
        out_ref[first // height : (first + count) // height] = result.reshape(chunk // height, height, columns)[: count // height]


def exchanged(pieces, axis):
    count = lax.axis_size(axis)
    received = [pieces[0]]
    for i in range(1, len(pieces)):
        received.append(lax.ppermute(pieces[i], axis, [(p, p ^ i) for p in range(count)]))
    return received


def neighbours(value):
    count = lax.axis_size("blk")
    up = [(i, i + 1) for i in range(count - 1)]
    down = [(j, i) for i, j in up]
    return lax.ppermute(value, "blk", up), lax.ppermute(value, "blk", down)


def shards(basis, mie_coeffs, rot_table, axial_table, pair_table, pair_count):
    vectors, quarter, modes, columns = basis.shape
    ways = lax.axis_size("pair")
    blk_ways = lax.axis_size("blk")
    tables = rot_table.shape[0]
    slots = pair_table.shape[1]
    own = quarter * ways
    part = columns // 2 // ways
    group = own * part
    size = rounded_up(modes, 128)
    rows = quarter * modes
    full = rounded_up(rows, 8)
    pairs_of_vectors = vectors // 2
    height = 4

    basis_rows = in_hbm(basis.transpose(0, 2, 1, 3).reshape(pairs_of_vectors, 2 * rows, columns))
    mie_rows = in_hbm(mie_coeffs.transpose(1, 0, 2).reshape(rows // 4, 4, columns))
    rot_rows = in_hbm(rot_table.transpose(1, 0, 2).reshape(modes * tables, modes))
    axial_rows = in_hbm(axial_table.transpose(0, 2, 1, 3))
    pair_rows = in_hbm(pair_table.transpose(2, 0, 1))

    octets = part * quarter // 16
    piece = jax.ShapeDtypeStruct((2, octets, 16, size), BF16)
    pieces = pl.pallas_call(
        functools.partial(pack_kernel, quarter, modes, ways, own),
        in_specs=[hbm(), pl.BlockSpec(memory_space=pltpu.SMEM), hbm()],
        out_specs=[whole()] * ways,
        out_shape=[piece] * ways,
        scratch_shapes=[
            pltpu.VMEM(pair_rows.shape, jnp.int32),
            pltpu.VMEM((full, columns), F32),
            pltpu.VMEM((size, columns), F32),
            pltpu.VMEM((2 * slots, slots), F32),
            pltpu.VMEM((quarter, columns, size), F32),
            pltpu.SemaphoreType.DMA((2,)),
        ],
        compiler_params=params(16),
        name="pack",
    )(pair_rows, pair_count, basis_rows)
    tall = rounded_up(rows + full, 8)
    *pieces, basis_rows, mie_rows = lax.optimization_barrier((*pieces, basis_rows, mie_rows))
    received = exchanged(pieces, "pair")
    products, blocks, mies = pl.pallas_call(
        functools.partial(gram_kernel, quarter, modes),
        in_specs=[hbm()] * 2,
        out_specs=[whole()] * 3,
        out_shape=[
            jax.ShapeDtypeStruct((vectors, vectors, 8, columns), F32),
            jax.ShapeDtypeStruct((pairs_of_vectors, tall, columns), F32),
            jax.ShapeDtypeStruct((full // height, height, columns), F32),
        ],
        scratch_shapes=[
            pltpu.SemaphoreType.DMA,
            pltpu.SemaphoreType.DMA((4, pairs_of_vectors, 2)),
        ],
        compiler_params=params(8),
        name="gram",
    )(basis_rows, mie_rows)
    *received, products, rot_rows, axial_rows = lax.optimization_barrier((*received, products, rot_rows, axial_rows))
    own_pieces = pl.pallas_call(
        join_kernel,
        in_specs=[whole()] * ways,
        out_specs=whole(),
        out_shape=jax.ShapeDtypeStruct((ways, *piece.shape), BF16),
        compiler_params=params(4),
        name="join",
    )(*received)
    below, above = neighbours(own_pieces)

    rotations, axials = pl.pallas_call(
        tables_kernel,
        in_specs=[hbm()] * 2,
        out_specs=[whole()] * 2,
        out_shape=[
            jax.ShapeDtypeStruct((tables, size, size), BF16),
            jax.ShapeDtypeStruct((tables, 2 * size, size), BF16),
        ],
        scratch_shapes=[
            pltpu.VMEM(axial_rows.shape, BF16),
            pltpu.VMEM((tables * size, modes), BF16),
            pltpu.SemaphoreType.DMA((tables + 1,)),
        ],
        compiler_params=params(20),
        cost_estimate=pl.CostEstimate(flops=tables * 8 * 256 * 256 * size, bytes_accessed=6 * tables * size * size * 2, transcendentals=0),
        name="tables",
    )(axial_rows, rot_rows)
    own_pieces, products = lax.optimization_barrier((own_pieces, products))
    line = pl.pallas_call(
        functools.partial(gram_end_kernel, quarter, modes),
        in_specs=[whole()] * 2,
        out_specs=whole(),
        out_shape=jax.ShapeDtypeStruct((1, 128), F32),
        scratch_shapes=[pltpu.VMEM((vectors, vectors, 8, columns), F32)],
        compiler_params=params(4),
        name="gram_end",
    )(products, blocks)
    below, above, rotations, axials, line = lax.optimization_barrier((below, above, rotations, axials, line))

    together = 4 if tables % 4 == 0 else 1
    field = pl.pallas_call(
        functools.partial(field_kernel, own, modes, together),
        in_specs=[whole()] * 5,
        out_specs=[whole()] * ways,
        out_shape=[jax.ShapeDtypeStruct((2, quarter, part, size), BF16)] * ways,
        scratch_shapes=[pltpu.VMEM((tables, 4 * group, size), BF16), pltpu.VMEM((2 * group, size), F32)],
        compiler_params=params(20),
        name="field",
    )(rotations, axials, below, own_pieces, above)
    field_pieces = exchanged(field, "pair")

    image, sums = pl.pallas_call(
        functools.partial(image_kernel, quarter, modes),
        in_specs=[whole()] * (ways + 3),
        out_specs=[whole()] * 2,
        out_shape=[jax.ShapeDtypeStruct((full, columns), F32), jax.ShapeDtypeStruct((ways * blk_ways, 1, 128), F32)],
        scratch_shapes=[pltpu.VMEM((full, columns), F32), pltpu.VMEM((quarter, columns, size), BF16)],
        compiler_params=params(8),
        name="image",
    )(blocks, mies, line, *field_pieces)
    sums = lax.all_to_all(sums, ("blk", "pair"), split_axis=0, concat_axis=0, tiled=True)

    mean_scale = 1.0 / (own * blk_ways * modes * columns)
    dots, next_rows = pl.pallas_call(
        functools.partial(remainder_kernel, quarter, modes, mean_scale),
        in_specs=[whole()] * 3,
        out_specs=[whole(), whole()],
        out_shape=[jax.ShapeDtypeStruct((2, vectors), F32), jax.ShapeDtypeStruct((rows // height, height, columns), F32)],
        compiler_params=params(16),
        name="remainder",
    )(sums, blocks, image)
    return dots, next_rows.reshape(modes, quarter, columns).transpose(1, 0, 2)


def solution(mesh):
    placed = (
        P(None, ("blk", "pair"), None, None),
        P(("blk", "pair"), None, None),
        P(),
        P(),
        P("blk", None, None),
        P("blk"),
    )
    return jax.shard_map(
        shards,
        mesh=mesh,
        in_specs=placed,
        out_specs=(P(), P(("blk", "pair"), None, None)),
        check_vma=False,
    )
```

```python
import functools

import jax
import jax.numpy as jnp
from jax import lax
from jax.experimental import pallas as pl
from jax.experimental.pallas import tpu as pltpu
from jax.sharding import PartitionSpec as P

MIB = 1024 * 1024
F32 = jnp.float32
BF16 = jnp.bfloat16


def params(mib):
    return pltpu.CompilerParams(vmem_limit_bytes=mib * MIB)


def hbm():
    return pl.BlockSpec(memory_space=pltpu.HBM)


def whole():
    return pl.BlockSpec(memory_space=pltpu.VMEM)


def in_hbm(value):
    return pltpu.with_memory_space_constraint(value, pltpu.HBM)


def rounded_up(value, unit):
    return (value + unit - 1) // unit * unit


def iota(shape, dim):
    return lax.broadcasted_iota(jnp.int32, shape, dim)


def dot_nn(left, right):
    return lax.dot_general(left, right, (((1,), (0,)), ((), ())), preferred_element_type=F32)


def dot_nt(left, right):
    return lax.dot_general(left, right, (((1,), (1,)), ((), ())), preferred_element_type=F32)


def pack_kernel(quarter, modes, ways, own, list_ref, count_ref, basis_ref, *rest):
    outs, (pair_rows_ref, lines_ref, pad_ref, codes_ref, turned_ref, sems) = rest[:ways], rest[ways:]
    full, columns = lines_ref.shape
    rows = quarter * modes
    part = columns // 2 // ways
    copy = pltpu.make_async_copy(basis_ref.at[basis_ref.shape[0] - 1, pl.ds(2 * rows - full, full)], lines_ref, sems.at[0])
    copy.start()
    list_copy = pltpu.make_async_copy(list_ref, pair_rows_ref, sems.at[1])
    list_copy.start()
    pad_ref[...] = jnp.zeros_like(pad_ref)
    list_copy.wait()
    slots = pair_rows_ref.shape[2]
    live = iota((1, slots), 1) < count_ref[0]
    marks = jnp.where(live, own * (pair_rows_ref[2] + 1) + pair_rows_ref[0], 0)
    line = iota((slots, slots), 0)
    stacked = jnp.where(line == 0, marks, jnp.where(line == 1, pair_rows_ref[1], 0))
    turned = jnp.transpose(stacked.astype(F32))
    codes_ref[0:slots, :] = turned
    codes_ref[slots : 2 * slots, :] = pltpu.roll(turned, slots - 1, axis=1)
    share = 2 * quarter * part
    mine = codes_ref[pl.ds(pl.multiple_of(lax.axis_index("pair") * share, share), share), :][:, 0:1]
    copy.wait()
    for j in range(quarter):
        pad_ref[0:modes, :] = lines_ref[pl.ds(full - rows + j, modes, quarter), :]
        turned_ref[j] = jnp.transpose(pad_ref[...])
    _, octets, height, size = outs[0].shape
    each = height // quarter
    for i, out_ref in enumerate(outs):
        place = (lax.axis_index("pair") ^ i) * part
        for c in range(2):
            for o in range(octets):
                first = (c * octets + o) * height
                here = pl.ds(pl.multiple_of(c * (columns // 2) + place + o * each, each), each)
                piece = jnp.concatenate([turned_ref[j, here, :] for j in range(quarter)], axis=0)
                piece = jnp.where(iota(piece.shape, 1) == modes, mine[first : first + height], piece)
                out_ref[c, o] = piece.astype(BF16)


def join_kernel(*refs):
    out_ref = refs[-1]
    for i, ref in enumerate(refs[:-1]):
        out_ref[lax.axis_index("pair") ^ i] = ref[...]


def tables_kernel(axial_ref, rot_ref, rot_out_ref, axial_out_ref, axials_ref, rots_ref, sems):
    tables, size, _ = rot_out_ref.shape
    modes = axial_ref.shape[1]
    listed = rot_ref.shape[0]

    def fetch(g):
        return pltpu.make_async_copy(axial_ref.at[g], axials_ref.at[g], sems.at[g])

    for g in range(tables):
        fetch(g).start()
    rot_copy = pltpu.make_async_copy(rot_ref, rots_ref.at[pl.ds(0, listed)], sems.at[tables])
    rot_copy.start()
    chunk = 256
    out_row, in_row = iota((chunk, chunk), 0), iota((chunk, chunk), 1)
    each = chunk // 2
    halves = (in_row == 2 * lax.rem(out_row, each) + lax.div(out_row, each)).astype(F32).astype(BF16)
    share = chunk // tables
    entries = (in_row == tables * lax.rem(out_row, share) + lax.div(out_row, share)).astype(F32).astype(BF16)
    for ref in (rot_out_ref, axial_out_ref):
        ref[:, :, size - 128 : size] = jnp.zeros((tables, ref.shape[1], 128), BF16)
    rots_ref[listed:, :] = jnp.zeros((rots_ref.shape[0] - listed, modes), BF16)

    def split(g, carry):
        fetch(g).wait()
        for first in range(0, modes, each):
            count = min(each, modes - first)
            rows = axials_ref[g, first : first + count].reshape(2 * count, modes)
            sorted_rows = dot_nn(halves[:, : 2 * count], rows).astype(BF16)
            for c in range(2):
                axial_out_ref[g, c * size + first : c * size + first + each, 0:modes] = sorted_rows[c * each : (c + 1) * each]
        return carry

    lax.fori_loop(0, tables, split, 0)
    rot_copy.wait()

    def pick(i, carry):
        rows = rots_ref[pl.ds(pl.multiple_of(i * chunk, chunk), chunk), :]
        sorted_rows = dot_nn(entries, rows).astype(BF16)
        for g in range(tables):
            here = pl.ds(pl.multiple_of(i * share, share), share)
            rot_out_ref[g, here, 0:modes] = sorted_rows[g * share : (g + 1) * share]
        return carry

    lax.fori_loop(0, rots_ref.shape[0] // chunk, pick, 0)


def swapped(value):
    half = value.shape[0] // 2
    return jnp.concatenate([-value[half:], value[:half]], axis=0)


def pair_counts(own, tables, lane, refs):
    ways, parts, octets, height, size = refs[0].shape
    group = ways * octets * height
    wanted = iota((tables * own, group), 0) + own

    def one_hot(hit):
        return jnp.where(hit, 1.0, 0.0).astype(BF16)

    forward, backward = None, []
    for window, ref in enumerate(refs):
        values = ref[:, :, :, :, size - 128 : size].reshape(2 * group, 128).astype(F32)
        marks_column, sources_column = (values[h * group : (h + 1) * group, lane : lane + 1].astype(jnp.int32) for h in range(2))
        marks, sources = (jnp.transpose(values[h * group : (h + 1) * group])[lane : lane + 1].astype(jnp.int32) for h in range(2))
        if window == 1:
            forward = dot_nn(one_hot(marks == wanted), one_hot(sources_column == iota((group, 3 * own), 1)))
        block = sources - (2 - window) * own
        inside = (block >= 0) & (block < own) & (marks >= own)
        hits = one_hot(jnp.where(inside, lax.div(marks, own) * own + block, -1) == wanted)
        place = lax.rem(marks_column, own) + window * own
        backward.append(dot_nn(hits, one_hot(place == iota((group, 3 * own), 1))))
    return jnp.concatenate([forward, sum(backward)], axis=0).astype(BF16)


def folded(value):
    return jnp.sum(value.reshape(value.shape[0] // 8, 8, value.shape[1]), axis=0)


def field_kernel(
    own, modes, together, rot_ref, axial_ref, below_ref, own_ref, above_ref, *rest
):
    outs, (sums_ref, total_ref) = rest[:-2], rest[-2:]
    tables, _, size = rot_ref.shape
    refs = (below_ref, own_ref, above_ref)
    ways, _, octets, height, _ = own_ref.shape
    quarter = own // ways
    each = height // quarter
    part = octets * each
    group = own * part
    counts = pair_counts(own, tables, modes % 128, refs)
    spread = jnp.where(iota((3 * own, 3 * own * each), 0) == lax.div(iota((3 * own, 3 * own * each), 1), each), 1.0, 0.0)
    counts = dot_nn(counts, spread.astype(BF16))
    sphere = lax.rem(iota(counts.shape, 1), each)
    chosen = jnp.concatenate([jnp.where(sphere == i, counts, 0.0).astype(BF16) for i in range(each)], axis=0)
    kinds = 2 * tables * own
    for c in range(2):
        for o in range(octets):
            blocks = jnp.concatenate([ref[:, c, o].reshape(ways * height, size) for ref in refs], axis=0)
            for i in range(0, each, 2):
                results = dot_nn(chosen[i * kinds : (i + 2) * kinds], blocks)
                for kind in range(2 * tables):
                    direction, g = kind // tables, kind % tables
                    rows = [results[start + kind * own : start + (kind + 1) * own] for start in (0, kinds)]
                    place = (direction * 2 + c) * group + (o * each + i) * own
                    sums_ref[g, place : place + 2 * own, :] = jnp.concatenate(rows, axis=0).astype(BF16)
    total_ref[...] = jnp.zeros_like(total_ref)

    def body(step, carry):
        entries = [step * together + i for i in range(together)]
        turned = [dot_nt(sums_ref[g], rot_ref[g]).astype(BF16) for g in entries]
        moved = []
        for g, both in zip(entries, turned):
            forward, backward = both[: 2 * group], both[2 * group :]
            result = dot_nt(forward, axial_ref[g, :size]) + dot_nt(swapped(forward), axial_ref[g, size:])
            result += dot_nn(jnp.concatenate([backward, swapped(backward)], axis=1), axial_ref[g])
            moved.append(result.astype(BF16))
        total_ref[...] += sum(dot_nn(value, rot_ref[g]) for g, value in zip(entries, moved))
        return carry

    if together == tables:
        body(0, 0)
    else:
        lax.fori_loop(0, tables // together, body, 0)
    row, source = iota((2 * group, 2 * group), 0), iota((2 * group, 2 * group), 1)
    sphere, c = lax.rem(row, part), lax.rem(lax.div(row, quarter * part), 2)
    owner = lax.div(row, 2 * quarter * part) ^ lax.axis_index("pair")
    block = owner * quarter + lax.rem(lax.div(row, part), quarter)
    order = jnp.where(source == c * group + sphere * own + block, 1.0, 0.0).astype(BF16)
    result = dot_nn(order, total_ref[...].astype(BF16)).astype(BF16)
    share = 2 * quarter * part
    for i, out_ref in enumerate(outs):
        out_ref[...] = result[i * share : (i + 1) * share].reshape(out_ref.shape)


def lane_swap(value):
    half = value.shape[1] // 2
    rolled = pltpu.roll(value, half, axis=1)
    return jnp.where(iota(value.shape, 1) < half, -rolled, rolled)


def add_products(blocks_ref, products_ref, rows, first, count):
    vectors = products_ref.shape[0]
    values = []
    for k in range(vectors):
        start = k % 2 * rows + first
        value = blocks_ref[k // 2, start : start + count, :]
        if k % 2 == 0 and first + count > rows:
            value = jnp.where(iota(value.shape, 0) < rows - first, value, 0.0)
        values.append(value)
    for l in range(vectors):
        other = pltpu.roll(values[l], values[l].shape[1] // 2, axis=1)
        for k in range(l + 1):
            products_ref[k, l] += folded(values[k] * values[l])
            if k < l:
                products_ref[l, k] += folded(values[k] * other)


def products_line(products_ref):
    vectors, _, _, columns = products_ref.shape
    pairs = vectors * vectors
    totals = jnp.sum(products_ref[...].reshape(pairs, 8, columns), axis=1)
    pair = iota(totals.shape, 0)
    signed = (lax.div(pair, vectors) > lax.rem(pair, vectors)) & (iota(totals.shape, 1) >= columns // 2)
    totals = jnp.sum(jnp.where(signed, -totals, totals), axis=1, keepdims=True)
    row, lane = iota((vectors, 128), 0), iota((vectors, 128), 1)
    line = jnp.zeros((1, 128), F32)
    for k in range(vectors):
        column = totals[k * vectors : (k + 1) * vectors]
        line += jnp.sum(jnp.where(row + k * vectors == lane, column, 0.0), axis=0, keepdims=True)
    return line


def gram_kernel(quarter, modes, basis_ref, mie_ref, products_ref, blocks_ref, mies_ref, mie_sem, sems):
    blocks, _, columns = basis_ref.shape
    rows = quarter * modes
    parts, chunk = 4, 32
    tile_end = rows // 8 * 8
    step = rounded_up(rows, 8 * parts) // parts
    even = [0] + [step * q for q in range(1, parts)] + [tile_end]
    odd = [tile_end] + [rounded_up(rows, 8) + step * q for q in range(1, parts)] + [2 * rows]
    copies = []
    for q in range(parts):
        for i in range(blocks):
            for side, cuts in enumerate((even, odd)):
                here = pl.ds(cuts[q], cuts[q + 1] - cuts[q])
                copies.append(pltpu.make_async_copy(basis_ref.at[i, here], blocks_ref.at[i, here], sems.at[q, i, side]))
    for copy in copies:
        copy.start()
    mie_rows = mie_ref.shape[0]
    mie_copy = pltpu.make_async_copy(mie_ref, mies_ref.at[pl.ds(0, mie_rows)], mie_sem)
    mie_copy.start()
    mies_ref[mie_rows:] = jnp.zeros((mies_ref.shape[0] - mie_rows,) + mies_ref.shape[1:], F32)
    products_ref[...] = jnp.zeros_like(products_ref)
    for i in range(blocks):
        blocks_ref[i, 2 * rows :, :] = jnp.zeros((blocks_ref.shape[1] - 2 * rows, columns), F32)
    for q in range(parts):
        for copy in copies[2 * blocks * q : 2 * blocks * (q + 1)]:
            copy.wait()
        if q < parts - 1:
            for first in range(step * q, step * (q + 1), chunk):
                add_products(blocks_ref, products_ref, rows, first, chunk)
    mie_copy.wait()


def gram_end_kernel(quarter, modes, products_ref, blocks_ref, line_ref, totals_ref):
    rows = quarter * modes
    parts, chunk = 4, 32
    totals_ref[...] = products_ref[...]
    for first in range(rounded_up(rows, 8 * parts) // parts * (parts - 1), rows, chunk):
        add_products(blocks_ref, totals_ref, rows, first, chunk)
    line_ref[...] = products_line(totals_ref)


def image_kernel(quarter, modes, blocks_ref, mie_ref, gram_ref, *rest):
    pieces, (image_ref, sums_ref, lines_ref, whole_ref) = rest[:-4], rest[-4:]
    vectors = 2 * blocks_ref.shape[0]
    full, columns = image_ref.shape
    rows = quarter * modes
    part = pieces[0].shape[2]
    for i, piece_ref in enumerate(pieces):
        place = pl.multiple_of((lax.axis_index("pair") ^ i) * part, part)
        for j in range(quarter):
            for c in range(2):
                whole_ref[j, pl.ds(c * (columns // 2) + place, part), :] = piece_ref[c, j]
    lines_ref[rows:full, :] = jnp.zeros((full - rows, columns), F32)
    for j in range(quarter):
        lines_ref[pl.ds(j, modes, quarter), :] = jnp.transpose(whole_ref[j].astype(F32))[:modes]
    half = columns // 2
    chunk = 64
    totals = [jnp.zeros((8, columns), F32) for _ in range(2 * vectors + 1)]
    for first in range(0, full, chunk):
        here = slice(first, first + chunk)
        field = lines_ref[here, :]
        count = min(chunk, rows - first)
        height = mie_ref.shape[1]
        mie = mie_ref[first // height : (first + count) // height].reshape(count, columns)
        if count < chunk:
            mie = jnp.concatenate([mie, jnp.zeros((chunk - count, columns), F32)], axis=0)
        left = iota(mie.shape, 1) < half
        other = pltpu.roll(mie, half, axis=1)
        product = jnp.where(left, mie, other) * field + jnp.where(left, -other, mie) * pltpu.roll(field, half, axis=1)
        last = (vectors - 1) % 2 * rows + first
        image = blocks_ref[(vectors - 1) // 2, last : last + chunk, :] - product
        image_ref[here, :] = image
        turned = pltpu.roll(product, half, axis=1)
        for k in range(vectors):
            start = k % 2 * rows + first
            values = blocks_ref[k // 2, start : start + chunk, :]
            totals[2 * k] += folded(values * product)
            totals[2 * k + 1] += folded(values * turned)
        totals[2 * vectors] += folded(product * product)
    lane = iota(gram_ref.shape, 1)
    line = gram_ref[...]
    left = iota((8, columns), 1) < half
    for index, total in enumerate(totals):
        if index % 2 and index < 2 * vectors:
            total = jnp.where(left, total, -total)
        line = jnp.where(lane == vectors * vectors + index, jnp.sum(total, axis=(0, 1), keepdims=True), line)
    sums_ref[...] = jnp.broadcast_to(line[None], sums_ref.shape)


def remainder_kernel(quarter, modes, mean_scale, sums_ref, blocks_ref, image_ref, dots_ref, out_ref):
    vectors = 2 * blocks_ref.shape[0]
    full, columns = image_ref.shape
    rows = quarter * modes
    total = jnp.sum(sums_ref[...], axis=0)
    lane = iota(total.shape, 1)

    def lane_at(index):
        return jnp.sum(jnp.where(lane == index, total, 0.0), axis=1, keepdims=True)

    def on_lanes(parts, places):
        line = jnp.zeros(total.shape, F32)
        for k in range(vectors):
            line = jnp.where(places == k, parts[k], line)
        return line

    start = vectors * vectors
    last = vectors - 1
    taken_real = [lane_at(start + 2 * k) * mean_scale for k in range(vectors)]
    taken_imag = [lane_at(start + 2 * k + 1) * mean_scale for k in range(vectors)]
    real = [lane_at(k * vectors + last) * mean_scale - taken_real[k] for k in range(vectors)]
    imag = [lane_at(last * vectors + k) * mean_scale - taken_imag[k] for k in range(last)] + [-taken_imag[last]]
    dots_ref[0:1, :] = on_lanes(real, lane)[:, :vectors]
    dots_ref[1:2, :] = on_lanes(imag, lane)[:, :vectors]
    kept_real = [-value for value in real[:last]] + [1.0 - real[last]]
    kept_imag = [-value for value in imag]
    first_index, last_index = lax.div(lane, vectors), lax.rem(lane, vectors)
    real_first, real_last = on_lanes(kept_real, first_index), on_lanes(kept_real, last_index)
    imag_first, imag_last = on_lanes(kept_imag, first_index), on_lanes(kept_imag, last_index)
    same = real_first * real_last + imag_first * imag_last
    cross = imag_last * real_first - real_last * imag_first
    often = jnp.where(first_index == last_index, 1.0, 2.0)
    spread = jnp.where(lane < start, total * often * jnp.where(first_index <= last_index, same, cross), 0.0)
    spread = jnp.sum(spread, axis=1, keepdims=True)
    both = sum(kept_real[k] * taken_real[k] + kept_imag[k] * taken_imag[k] for k in range(vectors))
    norm_square = (lane_at(start + 2 * vectors) + spread) * mean_scale - 2.0 * both
    scale = lax.rsqrt(norm_square)
    image_scale = jnp.broadcast_to(scale, (8, columns))
    reals = [jnp.broadcast_to(real[k] * scale, (8, columns)) for k in range(vectors)]
    imags = [jnp.broadcast_to(imag[k] * scale, (8, columns)) for k in range(vectors)]
    chunk = 64
    for first in range(0, full, chunk):
        here = slice(first, first + chunk)
        values = []
        for k in range(vectors):
            start = k % 2 * rows + first
            values.append(blocks_ref[k // 2, start : start + chunk, :].reshape(chunk // 8, 8, columns))
        along = image_ref[here, :].reshape(chunk // 8, 8, columns) * image_scale
        turned = jnp.zeros_like(along)
        for k in range(vectors):
            along -= reals[k] * values[k]
            turned += imags[k] * values[k]
        result = along.reshape(chunk, columns) - lane_swap(turned.reshape(chunk, columns))
        count = min(chunk, rows - first)
        height = out_ref.shape[1]
        out_ref[first // height : (first + count) // height] = result.reshape(chunk // height, height, columns)[: count // height]


def exchanged(pieces, axis):
    count = lax.axis_size(axis)
    received = [pieces[0]]
    for i in range(1, len(pieces)):
        received.append(lax.ppermute(pieces[i], axis, [(p, p ^ i) for p in range(count)]))
    return received


def neighbours(value):
    count = lax.axis_size("blk")
    up = [(i, i + 1) for i in range(count - 1)]
    down = [(j, i) for i, j in up]
    return lax.ppermute(value, "blk", up), lax.ppermute(value, "blk", down)


def shards(basis, mie_coeffs, rot_table, axial_table, pair_table, pair_count):
    vectors, quarter, modes, columns = basis.shape
    ways = lax.axis_size("pair")
    blk_ways = lax.axis_size("blk")
    tables = rot_table.shape[0]
    slots = pair_table.shape[1]
    own = quarter * ways
    part = columns // 2 // ways
    group = own * part
    size = rounded_up(modes, 128)
    rows = quarter * modes
    full = rounded_up(rows, 8)
    pairs_of_vectors = vectors // 2
    height = 4

    basis_rows = in_hbm(basis.transpose(0, 2, 1, 3).reshape(pairs_of_vectors, 2 * rows, columns))
    mie_rows = in_hbm(mie_coeffs.transpose(1, 0, 2).reshape(rows // 4, 4, columns))
    rot_rows = in_hbm(rot_table.transpose(1, 0, 2).reshape(modes * tables, modes))
    axial_rows = in_hbm(axial_table.transpose(0, 2, 1, 3))
    pair_rows = in_hbm(pair_table.transpose(2, 0, 1))

    octets = part * quarter // 16
    piece = jax.ShapeDtypeStruct((2, octets, 16, size), BF16)
    pieces = pl.pallas_call(
        functools.partial(pack_kernel, quarter, modes, ways, own),
        in_specs=[hbm(), pl.BlockSpec(memory_space=pltpu.SMEM), hbm()],
        out_specs=[whole()] * ways,
        out_shape=[piece] * ways,
        scratch_shapes=[
            pltpu.VMEM(pair_rows.shape, jnp.int32),
            pltpu.VMEM((full, columns), F32),
            pltpu.VMEM((size, columns), F32),
            pltpu.VMEM((2 * slots, slots), F32),
            pltpu.VMEM((quarter, columns, size), F32),
            pltpu.SemaphoreType.DMA((2,)),
        ],
        compiler_params=params(16),
        name="pack",
    )(pair_rows, pair_count, basis_rows)
    tall = rounded_up(rows + full, 8)
    *pieces, basis_rows, mie_rows = lax.optimization_barrier((*pieces, basis_rows, mie_rows))
    received = exchanged(pieces, "pair")
    products, blocks, mies = pl.pallas_call(
        functools.partial(gram_kernel, quarter, modes),
        in_specs=[hbm()] * 2,
        out_specs=[whole()] * 3,
        out_shape=[
            jax.ShapeDtypeStruct((vectors, vectors, 8, columns), F32),
            jax.ShapeDtypeStruct((pairs_of_vectors, tall, columns), F32),
            jax.ShapeDtypeStruct((full // height, height, columns), F32),
        ],
        scratch_shapes=[
            pltpu.SemaphoreType.DMA,
            pltpu.SemaphoreType.DMA((4, pairs_of_vectors, 2)),
        ],
        compiler_params=params(8),
        name="gram",
    )(basis_rows, mie_rows)
    *received, products, rot_rows, axial_rows = lax.optimization_barrier((*received, products, rot_rows, axial_rows))
    own_pieces = pl.pallas_call(
        join_kernel,
        in_specs=[whole()] * ways,
        out_specs=whole(),
        out_shape=jax.ShapeDtypeStruct((ways, *piece.shape), BF16),
        compiler_params=params(4),
        name="join",
    )(*received)
    below, above = neighbours(own_pieces)

    rotations, axials = pl.pallas_call(
        tables_kernel,
        in_specs=[hbm()] * 2,
        out_specs=[whole()] * 2,
        out_shape=[
            jax.ShapeDtypeStruct((tables, size, size), BF16),
            jax.ShapeDtypeStruct((tables, 2 * size, size), BF16),
        ],
        scratch_shapes=[
            pltpu.VMEM(axial_rows.shape, BF16),
            pltpu.VMEM((tables * size, modes), BF16),
            pltpu.SemaphoreType.DMA((tables + 1,)),
        ],
        compiler_params=params(20),
        cost_estimate=pl.CostEstimate(flops=tables * 8 * 256 * 256 * size, bytes_accessed=6 * tables * size * size * 2, transcendentals=0),
        name="tables",
    )(axial_rows, rot_rows)
    own_pieces, products = lax.optimization_barrier((own_pieces, products))
    line = pl.pallas_call(
        functools.partial(gram_end_kernel, quarter, modes),
        in_specs=[whole()] * 2,
        out_specs=whole(),
        out_shape=jax.ShapeDtypeStruct((1, 128), F32),
        scratch_shapes=[pltpu.VMEM((vectors, vectors, 8, columns), F32)],
        compiler_params=params(4),
        name="gram_end",
    )(products, blocks)
    below, above, rotations, axials, line = lax.optimization_barrier((below, above, rotations, axials, line))

    together = tables
    field = pl.pallas_call(
        functools.partial(field_kernel, own, modes, together),
        in_specs=[whole()] * 5,
        out_specs=[whole()] * ways,
        out_shape=[jax.ShapeDtypeStruct((2, quarter, part, size), BF16)] * ways,
        scratch_shapes=[pltpu.VMEM((tables, 4 * group, size), BF16), pltpu.VMEM((2 * group, size), F32)],
        compiler_params=params(28),
        name="field",
    )(rotations, axials, below, own_pieces, above)
    field_pieces = exchanged(field, "pair")

    image, sums = pl.pallas_call(
        functools.partial(image_kernel, quarter, modes),
        in_specs=[whole()] * (ways + 3),
        out_specs=[whole()] * 2,
        out_shape=[jax.ShapeDtypeStruct((full, columns), F32), jax.ShapeDtypeStruct((ways * blk_ways, 1, 128), F32)],
        scratch_shapes=[pltpu.VMEM((full, columns), F32), pltpu.VMEM((quarter, columns, size), BF16)],
        compiler_params=params(8),
        name="image",
    )(blocks, mies, line, *field_pieces)
    sums = lax.all_to_all(sums, ("blk", "pair"), split_axis=0, concat_axis=0, tiled=True)

    mean_scale = 1.0 / (own * blk_ways * modes * columns)
    dots, next_rows = pl.pallas_call(
        functools.partial(remainder_kernel, quarter, modes, mean_scale),
        in_specs=[whole()] * 3,
        out_specs=[whole(), whole()],
        out_shape=[jax.ShapeDtypeStruct((2, vectors), F32), jax.ShapeDtypeStruct((rows // height, height, columns), F32)],
        compiler_params=params(16),
        name="remainder",
    )(sums, blocks, image)
    return dots, next_rows.reshape(modes, quarter, columns).transpose(1, 0, 2)


def solution(mesh):
    placed = (
        P(None, ("blk", "pair"), None, None),
        P(("blk", "pair"), None, None),
        P(),
        P(),
        P("blk", None, None),
        P("blk"),
    )
    return jax.shard_map(
        shards,
        mesh=mesh,
        in_specs=placed,
        out_specs=(P(), P(("blk", "pair"), None, None)),
        check_vma=False,
    )
```

```python
import functools

import jax
import jax.numpy as jnp
from jax import lax
from jax.experimental import pallas as pl
from jax.experimental.pallas import tpu as pltpu
from jax.sharding import PartitionSpec as P

MIB = 1024 * 1024
F32 = jnp.float32
BF16 = jnp.bfloat16


def params(mib):
    return pltpu.CompilerParams(vmem_limit_bytes=mib * MIB)


def hbm():
    return pl.BlockSpec(memory_space=pltpu.HBM)


def whole():
    return pl.BlockSpec(memory_space=pltpu.VMEM)


def in_hbm(value):
    return pltpu.with_memory_space_constraint(value, pltpu.HBM)


def rounded_up(value, unit):
    return (value + unit - 1) // unit * unit


def iota(shape, dim):
    return lax.broadcasted_iota(jnp.int32, shape, dim)


def dot_nn(left, right):
    return lax.dot_general(left, right, (((1,), (0,)), ((), ())), preferred_element_type=F32)


def dot_nt(left, right):
    return lax.dot_general(left, right, (((1,), (1,)), ((), ())), preferred_element_type=F32)


def pack_kernel(quarter, modes, ways, own, list_ref, count_ref, basis_ref, *rest):
    outs, (pair_rows_ref, lines_ref, pad_ref, codes_ref, turned_ref, sems) = rest[:ways], rest[ways:]
    full, columns = lines_ref.shape
    rows = quarter * modes
    part = columns // 2 // ways
    copy = pltpu.make_async_copy(basis_ref.at[basis_ref.shape[0] - 1, pl.ds(2 * rows - full, full)], lines_ref, sems.at[0])
    copy.start()
    list_copy = pltpu.make_async_copy(list_ref, pair_rows_ref, sems.at[1])
    list_copy.start()
    pad_ref[...] = jnp.zeros_like(pad_ref)
    list_copy.wait()
    slots = pair_rows_ref.shape[2]
    live = iota((1, slots), 1) < count_ref[0]
    marks = jnp.where(live, own * (pair_rows_ref[2] + 1) + pair_rows_ref[0], 0)
    line = iota((slots, slots), 0)
    stacked = jnp.where(line == 0, marks, jnp.where(line == 1, pair_rows_ref[1], 0))
    turned = jnp.transpose(stacked.astype(F32))
    codes_ref[0:slots, :] = turned
    codes_ref[slots : 2 * slots, :] = pltpu.roll(turned, slots - 1, axis=1)
    share = 2 * quarter * part
    mine = codes_ref[pl.ds(pl.multiple_of(lax.axis_index("pair") * share, share), share), :][:, 0:1]
    copy.wait()
    for j in range(quarter):
        pad_ref[0:modes, :] = lines_ref[pl.ds(full - rows + j, modes, quarter), :]
        turned_ref[j] = jnp.transpose(pad_ref[...])
    _, octets, height, size = outs[0].shape
    each = height // quarter
    for i, out_ref in enumerate(outs):
        place = (lax.axis_index("pair") ^ i) * part
        for c in range(2):
            for o in range(octets):
                first = (c * octets + o) * height
                here = pl.ds(pl.multiple_of(c * (columns // 2) + place + o * each, each), each)
                piece = jnp.concatenate([turned_ref[j, here, :] for j in range(quarter)], axis=0)
                piece = jnp.where(iota(piece.shape, 1) == modes, mine[first : first + height], piece)
                out_ref[c, o] = piece.astype(BF16)


def join_kernel(*refs):
    out_ref = refs[-1]
    for i, ref in enumerate(refs[:-1]):
        out_ref[lax.axis_index("pair") ^ i] = ref[...]


def rotations_kernel(rot_ref, out_ref, rots_ref, sems):
    tables, size, _ = out_ref.shape
    listed, modes = rot_ref.shape
    chunk = 256
    copies = []
    for i, first in enumerate(range(0, listed, 4 * chunk)):
        here = pl.ds(first, min(4 * chunk, listed - first))
        copies.append(pltpu.make_async_copy(rot_ref.at[here], rots_ref.at[here], sems.at[i]))
        copies[-1].start()
    out_row, in_row = iota((chunk, chunk), 0), iota((chunk, chunk), 1)
    share = chunk // tables
    entries = (in_row == tables * lax.rem(out_row, share) + lax.div(out_row, share)).astype(F32).astype(BF16)
    out_ref[:, :, size - 128 : size] = jnp.zeros((tables, size, 128), BF16)
    rots_ref[listed:, :] = jnp.zeros((rots_ref.shape[0] - listed, modes), BF16)

    def pick(i, carry):
        rows = rots_ref[pl.ds(pl.multiple_of(i * chunk, chunk), chunk), :]
        sorted_rows = dot_nn(entries, rows).astype(BF16)
        for g in range(tables):
            here = pl.ds(pl.multiple_of(i * share, share), share)
            out_ref[g, here, 0:modes] = sorted_rows[g * share : (g + 1) * share]
        return carry

    for i, copy in enumerate(copies):
        copy.wait()
        lax.fori_loop(4 * i, min(4 * (i + 1), rots_ref.shape[0] // chunk), pick, 0)


def axials_kernel(axial_ref, out_ref, axials_ref, sems):
    tables, double, size = out_ref.shape
    modes = axial_ref.shape[1]

    def fetch(g):
        return pltpu.make_async_copy(axial_ref.at[g], axials_ref.at[g], sems.at[g])

    for g in range(tables):
        fetch(g).start()
    chunk = 256
    out_row, in_row = iota((chunk, chunk), 0), iota((chunk, chunk), 1)
    each = chunk // 2
    halves = (in_row == 2 * lax.rem(out_row, each) + lax.div(out_row, each)).astype(F32).astype(BF16)
    out_ref[:, :, size - 128 : size] = jnp.zeros((tables, double, 128), BF16)

    def split(g, carry):
        fetch(g).wait()
        for first in range(0, modes, each):
            count = min(each, modes - first)
            rows = axials_ref[g, first : first + count].reshape(2 * count, modes)
            sorted_rows = dot_nn(halves[:, : 2 * count], rows).astype(BF16)
            for c in range(2):
                out_ref[g, c * size + first : c * size + first + each, 0:modes] = sorted_rows[c * each : (c + 1) * each]
        return carry

    lax.fori_loop(0, tables, split, 0)


def swapped(value):
    half = value.shape[0] // 2
    return jnp.concatenate([-value[half:], value[:half]], axis=0)


def pair_counts(own, tables, lane, refs):
    ways, parts, octets, height, size = refs[0].shape
    group = ways * octets * height
    wanted = iota((tables * own, group), 0) + own

    def one_hot(hit):
        return jnp.where(hit, 1.0, 0.0).astype(BF16)

    forward, backward = None, []
    for window, ref in enumerate(refs):
        values = ref[:, :, :, :, size - 128 : size].reshape(2 * group, 128).astype(F32)
        marks_column, sources_column = (values[h * group : (h + 1) * group, lane : lane + 1].astype(jnp.int32) for h in range(2))
        marks, sources = (jnp.transpose(values[h * group : (h + 1) * group])[lane : lane + 1].astype(jnp.int32) for h in range(2))
        if window == 1:
            forward = dot_nn(one_hot(marks == wanted), one_hot(sources_column == iota((group, 3 * own), 1)))
        block = sources - (2 - window) * own
        inside = (block >= 0) & (block < own) & (marks >= own)
        hits = one_hot(jnp.where(inside, lax.div(marks, own) * own + block, -1) == wanted)
        place = lax.rem(marks_column, own) + window * own
        backward.append(dot_nn(hits, one_hot(place == iota((group, 3 * own), 1))))
    return jnp.concatenate([forward, sum(backward)], axis=0).astype(BF16)


def folded(value):
    return jnp.sum(value.reshape(value.shape[0] // 8, 8, value.shape[1]), axis=0)


def field_kernel(
    own, modes, together, rot_ref, axial_ref, below_ref, own_ref, above_ref, *rest
):
    outs, (sums_ref, total_ref) = rest[:-2], rest[-2:]
    tables, _, size = rot_ref.shape
    refs = (below_ref, own_ref, above_ref)
    ways, _, octets, height, _ = own_ref.shape
    quarter = own // ways
    each = height // quarter
    part = octets * each
    group = own * part
    counts = pair_counts(own, tables, modes % 128, refs)
    spread = jnp.where(iota((3 * own, 3 * own * each), 0) == lax.div(iota((3 * own, 3 * own * each), 1), each), 1.0, 0.0)
    counts = dot_nn(counts, spread.astype(BF16))
    sphere = lax.rem(iota(counts.shape, 1), each)
    chosen = jnp.concatenate([jnp.where(sphere == i, counts, 0.0).astype(BF16) for i in range(each)], axis=0)
    kinds = 2 * tables * own
    for c in range(2):
        for o in range(octets):
            blocks = jnp.concatenate([ref[:, c, o].reshape(ways * height, size) for ref in refs], axis=0)
            for i in range(0, each, 2):
                results = dot_nn(chosen[i * kinds : (i + 2) * kinds], blocks)
                for kind in range(2 * tables):
                    direction, g = kind // tables, kind % tables
                    rows = [results[start + kind * own : start + (kind + 1) * own] for start in (0, kinds)]
                    place = (direction * 2 + c) * group + (o * each + i) * own
                    sums_ref[g, place : place + 2 * own, :] = jnp.concatenate(rows, axis=0).astype(BF16)
    total_ref[...] = jnp.zeros_like(total_ref)

    def body(step, carry):
        entries = [step * together + i for i in range(together)]
        turned = [dot_nt(sums_ref[g], rot_ref[g]).astype(BF16) for g in entries]
        moved = []
        for g, both in zip(entries, turned):
            forward, backward = both[: 2 * group], both[2 * group :]
            result = dot_nt(forward, axial_ref[g, :size]) + dot_nt(swapped(forward), axial_ref[g, size:])
            result += dot_nn(jnp.concatenate([backward, swapped(backward)], axis=1), axial_ref[g])
            moved.append(result.astype(BF16))
        total_ref[...] += sum(dot_nn(value, rot_ref[g]) for g, value in zip(entries, moved))
        return carry

    if together == tables:
        body(0, 0)
    else:
        lax.fori_loop(0, tables // together, body, 0)
    row, source = iota((2 * group, 2 * group), 0), iota((2 * group, 2 * group), 1)
    sphere, c = lax.rem(row, part), lax.rem(lax.div(row, quarter * part), 2)
    owner = lax.div(row, 2 * quarter * part) ^ lax.axis_index("pair")
    block = owner * quarter + lax.rem(lax.div(row, part), quarter)
    order = jnp.where(source == c * group + sphere * own + block, 1.0, 0.0).astype(BF16)
    result = dot_nn(order, total_ref[...].astype(BF16)).astype(BF16)
    share = 2 * quarter * part
    for i, out_ref in enumerate(outs):
        out_ref[...] = result[i * share : (i + 1) * share].reshape(out_ref.shape)


def lane_swap(value):
    half = value.shape[1] // 2
    rolled = pltpu.roll(value, half, axis=1)
    return jnp.where(iota(value.shape, 1) < half, -rolled, rolled)


def add_products(blocks_ref, products_ref, rows, first, count):
    vectors = products_ref.shape[0]
    values = []
    for k in range(vectors):
        start = k % 2 * rows + first
        value = blocks_ref[k // 2, start : start + count, :]
        if k % 2 == 0 and first + count > rows:
            value = jnp.where(iota(value.shape, 0) < rows - first, value, 0.0)
        values.append(value)
    for l in range(vectors):
        other = pltpu.roll(values[l], values[l].shape[1] // 2, axis=1)
        for k in range(l + 1):
            products_ref[k, l] += folded(values[k] * values[l])
            if k < l:
                products_ref[l, k] += folded(values[k] * other)


def products_line(products_ref):
    vectors, _, _, columns = products_ref.shape
    pairs = vectors * vectors
    totals = jnp.sum(products_ref[...].reshape(pairs, 8, columns), axis=1)
    pair = iota(totals.shape, 0)
    signed = (lax.div(pair, vectors) > lax.rem(pair, vectors)) & (iota(totals.shape, 1) >= columns // 2)
    totals = jnp.sum(jnp.where(signed, -totals, totals), axis=1, keepdims=True)
    row, lane = iota((vectors, 128), 0), iota((vectors, 128), 1)
    line = jnp.zeros((1, 128), F32)
    for k in range(vectors):
        column = totals[k * vectors : (k + 1) * vectors]
        line += jnp.sum(jnp.where(row + k * vectors == lane, column, 0.0), axis=0, keepdims=True)
    return line


def gram_kernel(quarter, modes, basis_ref, mie_ref, products_ref, blocks_ref, mies_ref, mie_sem, sems):
    blocks, _, columns = basis_ref.shape
    rows = quarter * modes
    parts, chunk = 4, 32
    tile_end = rows // 8 * 8
    step = rounded_up(rows, 8 * parts) // parts
    even = [0] + [step * q for q in range(1, parts)] + [tile_end]
    odd = [tile_end] + [rounded_up(rows, 8) + step * q for q in range(1, parts)] + [2 * rows]
    copies = []
    for q in range(parts):
        for i in range(blocks):
            for side, cuts in enumerate((even, odd)):
                here = pl.ds(cuts[q], cuts[q + 1] - cuts[q])
                copies.append(pltpu.make_async_copy(basis_ref.at[i, here], blocks_ref.at[i, here], sems.at[q, i, side]))
    for copy in copies:
        copy.start()
    mie_rows = mie_ref.shape[0]
    mie_copy = pltpu.make_async_copy(mie_ref, mies_ref.at[pl.ds(0, mie_rows)], mie_sem)
    mie_copy.start()
    mies_ref[mie_rows:] = jnp.zeros((mies_ref.shape[0] - mie_rows,) + mies_ref.shape[1:], F32)
    products_ref[...] = jnp.zeros_like(products_ref)
    for i in range(blocks):
        blocks_ref[i, 2 * rows :, :] = jnp.zeros((blocks_ref.shape[1] - 2 * rows, columns), F32)
    for q in range(parts):
        for copy in copies[2 * blocks * q : 2 * blocks * (q + 1)]:
            copy.wait()
        if q < parts - 1:
            for first in range(step * q, step * (q + 1), chunk):
                add_products(blocks_ref, products_ref, rows, first, chunk)
    mie_copy.wait()


def gram_end_kernel(quarter, modes, products_ref, blocks_ref, line_ref, totals_ref):
    rows = quarter * modes
    parts, chunk = 4, 32
    totals_ref[...] = products_ref[...]
    for first in range(rounded_up(rows, 8 * parts) // parts * (parts - 1), rows, chunk):
        add_products(blocks_ref, totals_ref, rows, first, chunk)
    line_ref[...] = products_line(totals_ref)


def image_kernel(quarter, modes, blocks_ref, mie_ref, gram_ref, *rest):
    pieces, (image_ref, sums_ref, lines_ref, whole_ref) = rest[:-4], rest[-4:]
    vectors = 2 * blocks_ref.shape[0]
    full, columns = image_ref.shape
    rows = quarter * modes
    part = pieces[0].shape[2]
    for i, piece_ref in enumerate(pieces):
        place = pl.multiple_of((lax.axis_index("pair") ^ i) * part, part)
        for j in range(quarter):
            for c in range(2):
                whole_ref[j, pl.ds(c * (columns // 2) + place, part), :] = piece_ref[c, j]
    lines_ref[rows:full, :] = jnp.zeros((full - rows, columns), F32)
    for j in range(quarter):
        lines_ref[pl.ds(j, modes, quarter), :] = jnp.transpose(whole_ref[j].astype(F32))[:modes]
    half = columns // 2
    chunk = 64
    totals = [jnp.zeros((8, columns), F32) for _ in range(2 * vectors + 1)]
    for first in range(0, full, chunk):
        here = slice(first, first + chunk)
        field = lines_ref[here, :]
        count = min(chunk, rows - first)
        height = mie_ref.shape[1]
        mie = mie_ref[first // height : (first + count) // height].reshape(count, columns)
        if count < chunk:
            mie = jnp.concatenate([mie, jnp.zeros((chunk - count, columns), F32)], axis=0)
        left = iota(mie.shape, 1) < half
        other = pltpu.roll(mie, half, axis=1)
        product = jnp.where(left, mie, other) * field + jnp.where(left, -other, mie) * pltpu.roll(field, half, axis=1)
        last = (vectors - 1) % 2 * rows + first
        image = blocks_ref[(vectors - 1) // 2, last : last + chunk, :] - product
        image_ref[here, :] = image
        turned = pltpu.roll(product, half, axis=1)
        for k in range(vectors):
            start = k % 2 * rows + first
            values = blocks_ref[k // 2, start : start + chunk, :]
            totals[2 * k] += folded(values * product)
            totals[2 * k + 1] += folded(values * turned)
        totals[2 * vectors] += folded(product * product)
    lane = iota(gram_ref.shape, 1)
    line = gram_ref[...]
    left = iota((8, columns), 1) < half
    for index, total in enumerate(totals):
        if index % 2 and index < 2 * vectors:
            total = jnp.where(left, total, -total)
        line = jnp.where(lane == vectors * vectors + index, jnp.sum(total, axis=(0, 1), keepdims=True), line)
    sums_ref[...] = jnp.broadcast_to(line[None], sums_ref.shape)


def remainder_kernel(quarter, modes, mean_scale, sums_ref, blocks_ref, image_ref, dots_ref, out_ref):
    vectors = 2 * blocks_ref.shape[0]
    full, columns = image_ref.shape
    rows = quarter * modes
    total = jnp.sum(sums_ref[...], axis=0)
    lane = iota(total.shape, 1)

    def lane_at(index):
        return jnp.sum(jnp.where(lane == index, total, 0.0), axis=1, keepdims=True)

    def on_lanes(parts, places):
        line = jnp.zeros(total.shape, F32)
        for k in range(vectors):
            line = jnp.where(places == k, parts[k], line)
        return line

    start = vectors * vectors
    last = vectors - 1
    taken_real = [lane_at(start + 2 * k) * mean_scale for k in range(vectors)]
    taken_imag = [lane_at(start + 2 * k + 1) * mean_scale for k in range(vectors)]
    real = [lane_at(k * vectors + last) * mean_scale - taken_real[k] for k in range(vectors)]
    imag = [lane_at(last * vectors + k) * mean_scale - taken_imag[k] for k in range(last)] + [-taken_imag[last]]
    dots_ref[0:1, :] = on_lanes(real, lane)[:, :vectors]
    dots_ref[1:2, :] = on_lanes(imag, lane)[:, :vectors]
    kept_real = [-value for value in real[:last]] + [1.0 - real[last]]
    kept_imag = [-value for value in imag]
    first_index, last_index = lax.div(lane, vectors), lax.rem(lane, vectors)
    real_first, real_last = on_lanes(kept_real, first_index), on_lanes(kept_real, last_index)
    imag_first, imag_last = on_lanes(kept_imag, first_index), on_lanes(kept_imag, last_index)
    same = real_first * real_last + imag_first * imag_last
    cross = imag_last * real_first - real_last * imag_first
    often = jnp.where(first_index == last_index, 1.0, 2.0)
    spread = jnp.where(lane < start, total * often * jnp.where(first_index <= last_index, same, cross), 0.0)
    spread = jnp.sum(spread, axis=1, keepdims=True)
    both = sum(kept_real[k] * taken_real[k] + kept_imag[k] * taken_imag[k] for k in range(vectors))
    norm_square = (lane_at(start + 2 * vectors) + spread) * mean_scale - 2.0 * both
    scale = lax.rsqrt(norm_square)
    image_scale = jnp.broadcast_to(scale, (8, columns))
    reals = [jnp.broadcast_to(real[k] * scale, (8, columns)) for k in range(vectors)]
    imags = [jnp.broadcast_to(imag[k] * scale, (8, columns)) for k in range(vectors)]
    chunk = 64
    for first in range(0, full, chunk):
        here = slice(first, first + chunk)
        values = []
        for k in range(vectors):
            start = k % 2 * rows + first
            values.append(blocks_ref[k // 2, start : start + chunk, :].reshape(chunk // 8, 8, columns))
        along = image_ref[here, :].reshape(chunk // 8, 8, columns) * image_scale
        turned = jnp.zeros_like(along)
        for k in range(vectors):
            along -= reals[k] * values[k]
            turned += imags[k] * values[k]
        result = along.reshape(chunk, columns) - lane_swap(turned.reshape(chunk, columns))
        count = min(chunk, rows - first)
        height = out_ref.shape[1]
        out_ref[first // height : (first + count) // height] = result.reshape(chunk // height, height, columns)[: count // height]


def exchanged(pieces, axis):
    count = lax.axis_size(axis)
    received = [pieces[0]]
    for i in range(1, len(pieces)):
        received.append(lax.ppermute(pieces[i], axis, [(p, p ^ i) for p in range(count)]))
    return received


def from_neighbour(value, up):
    pairs = [(i, i + 1) for i in range(lax.axis_size("blk") - 1)]
    return lax.ppermute(value, "blk", pairs if up else [(j, i) for i, j in pairs])


def shards(basis, mie_coeffs, rot_table, axial_table, pair_table, pair_count):
    vectors, quarter, modes, columns = basis.shape
    ways = lax.axis_size("pair")
    blk_ways = lax.axis_size("blk")
    tables = rot_table.shape[0]
    slots = pair_table.shape[1]
    own = quarter * ways
    part = columns // 2 // ways
    group = own * part
    size = rounded_up(modes, 128)
    rows = quarter * modes
    full = rounded_up(rows, 8)
    pairs_of_vectors = vectors // 2
    height = 4

    basis_rows = in_hbm(basis.transpose(0, 2, 1, 3).reshape(pairs_of_vectors, 2 * rows, columns))
    mie_rows = in_hbm(mie_coeffs.transpose(1, 0, 2).reshape(rows // 4, 4, columns))
    rot_rows = in_hbm(rot_table.transpose(1, 0, 2).reshape(modes * tables, modes))
    axial_rows = in_hbm(axial_table.transpose(0, 2, 1, 3))
    pair_rows = in_hbm(pair_table.transpose(2, 0, 1))

    octets = part * quarter // 16
    piece = jax.ShapeDtypeStruct((2, octets, 16, size), BF16)
    pieces = pl.pallas_call(
        functools.partial(pack_kernel, quarter, modes, ways, own),
        in_specs=[hbm(), pl.BlockSpec(memory_space=pltpu.SMEM), hbm()],
        out_specs=[whole()] * ways,
        out_shape=[piece] * ways,
        scratch_shapes=[
            pltpu.VMEM(pair_rows.shape, jnp.int32),
            pltpu.VMEM((full, columns), F32),
            pltpu.VMEM((size, columns), F32),
            pltpu.VMEM((2 * slots, slots), F32),
            pltpu.VMEM((quarter, columns, size), F32),
            pltpu.SemaphoreType.DMA((2,)),
        ],
        compiler_params=params(16),
        name="pack",
    )(pair_rows, pair_count, basis_rows)
    tall = rounded_up(rows + full, 8)
    *pieces, basis_rows, mie_rows = lax.optimization_barrier((*pieces, basis_rows, mie_rows))
    received = exchanged(pieces, "pair")
    products, blocks, mies = pl.pallas_call(
        functools.partial(gram_kernel, quarter, modes),
        in_specs=[hbm()] * 2,
        out_specs=[whole()] * 3,
        out_shape=[
            jax.ShapeDtypeStruct((vectors, vectors, 8, columns), F32),
            jax.ShapeDtypeStruct((pairs_of_vectors, tall, columns), F32),
            jax.ShapeDtypeStruct((full // height, height, columns), F32),
        ],
        scratch_shapes=[
            pltpu.SemaphoreType.DMA,
            pltpu.SemaphoreType.DMA((4, pairs_of_vectors, 2)),
        ],
        compiler_params=params(8),
        name="gram",
    )(basis_rows, mie_rows)
    *received, products, rot_rows, axial_rows = lax.optimization_barrier((*received, products, rot_rows, axial_rows))
    own_pieces = pl.pallas_call(
        join_kernel,
        in_specs=[whole()] * ways,
        out_specs=whole(),
        out_shape=jax.ShapeDtypeStruct((ways, *piece.shape), BF16),
        compiler_params=params(4),
        name="join",
    )(*received)
    own_pieces, products, rot_rows = lax.optimization_barrier((own_pieces, products, rot_rows))
    above = from_neighbour(own_pieces, False)
    line = pl.pallas_call(
        functools.partial(gram_end_kernel, quarter, modes),
        in_specs=[whole()] * 2,
        out_specs=whole(),
        out_shape=jax.ShapeDtypeStruct((1, 128), F32),
        scratch_shapes=[pltpu.VMEM((vectors, vectors, 8, columns), F32)],
        compiler_params=params(4),
        name="gram_end",
    )(products, blocks)
    rotations = pl.pallas_call(
        rotations_kernel,
        in_specs=[hbm()],
        out_specs=whole(),
        out_shape=jax.ShapeDtypeStruct((tables, size, size), BF16),
        scratch_shapes=[
            pltpu.VMEM((tables * size, modes), BF16),
            pltpu.SemaphoreType.DMA((rounded_up(modes * tables, 1024) // 1024,)),
        ],
        compiler_params=params(8),
        name="rotations",
    )(rot_rows)
    own_pieces, line, rotations, axial_rows = lax.optimization_barrier((own_pieces, line, rotations, axial_rows))
    below = from_neighbour(own_pieces, True)
    axials = pl.pallas_call(
        axials_kernel,
        in_specs=[hbm()],
        out_specs=whole(),
        out_shape=jax.ShapeDtypeStruct((tables, 2 * size, size), BF16),
        scratch_shapes=[pltpu.VMEM(axial_rows.shape, BF16), pltpu.SemaphoreType.DMA((tables,))],
        compiler_params=params(16),
        cost_estimate=pl.CostEstimate(flops=tables * 8 * 256 * 256 * size, bytes_accessed=4 * tables * size * size * 2, transcendentals=0),
        name="axials",
    )(axial_rows)
    below, above, axials = lax.optimization_barrier((below, above, axials))

    together = tables
    field = pl.pallas_call(
        functools.partial(field_kernel, own, modes, together),
        in_specs=[whole()] * 5,
        out_specs=[whole()] * ways,
        out_shape=[jax.ShapeDtypeStruct((2, quarter, part, size), BF16)] * ways,
        scratch_shapes=[pltpu.VMEM((tables, 4 * group, size), BF16), pltpu.VMEM((2 * group, size), F32)],
        compiler_params=params(28),
        name="field",
    )(rotations, axials, below, own_pieces, above)
    field_pieces = exchanged(field, "pair")

    image, sums = pl.pallas_call(
        functools.partial(image_kernel, quarter, modes),
        in_specs=[whole()] * (ways + 3),
        out_specs=[whole()] * 2,
        out_shape=[jax.ShapeDtypeStruct((full, columns), F32), jax.ShapeDtypeStruct((ways * blk_ways, 1, 128), F32)],
        scratch_shapes=[pltpu.VMEM((full, columns), F32), pltpu.VMEM((quarter, columns, size), BF16)],
        compiler_params=params(8),
        name="image",
    )(blocks, mies, line, *field_pieces)
    sums = lax.all_to_all(sums, ("blk", "pair"), split_axis=0, concat_axis=0, tiled=True)

    mean_scale = 1.0 / (own * blk_ways * modes * columns)
    dots, next_rows = pl.pallas_call(
        functools.partial(remainder_kernel, quarter, modes, mean_scale),
        in_specs=[whole()] * 3,
        out_specs=[whole(), whole()],
        out_shape=[jax.ShapeDtypeStruct((2, vectors), F32), jax.ShapeDtypeStruct((rows // height, height, columns), F32)],
        compiler_params=params(16),
        name="remainder",
    )(sums, blocks, image)
    return dots, next_rows.reshape(modes, quarter, columns).transpose(1, 0, 2)


def solution(mesh):
    placed = (
        P(None, ("blk", "pair"), None, None),
        P(("blk", "pair"), None, None),
        P(),
        P(),
        P("blk", None, None),
        P("blk"),
    )
    return jax.shard_map(
        shards,
        mesh=mesh,
        in_specs=placed,
        out_specs=(P(), P(("blk", "pair"), None, None)),
        check_vma=False,
    )
```

```python
import functools

import jax
import jax.numpy as jnp
from jax import lax
from jax.experimental import pallas as pl
from jax.experimental.pallas import tpu as pltpu
from jax.sharding import PartitionSpec as P

MIB = 1024 * 1024
F32 = jnp.float32
BF16 = jnp.bfloat16


def params(mib):
    return pltpu.CompilerParams(vmem_limit_bytes=mib * MIB)


def hbm():
    return pl.BlockSpec(memory_space=pltpu.HBM)


def whole():
    return pl.BlockSpec(memory_space=pltpu.VMEM)


def in_hbm(value):
    return pltpu.with_memory_space_constraint(value, pltpu.HBM)


def rounded_up(value, unit):
    return (value + unit - 1) // unit * unit


def iota(shape, dim):
    return lax.broadcasted_iota(jnp.int32, shape, dim)


def dot_nn(left, right):
    return lax.dot_general(left, right, (((1,), (0,)), ((), ())), preferred_element_type=F32)


def dot_nt(left, right):
    return lax.dot_general(left, right, (((1,), (1,)), ((), ())), preferred_element_type=F32)


def pack_kernel(quarter, modes, ways, own, list_ref, count_ref, basis_ref, *rest):
    outs, (pair_rows_ref, lines_ref, pad_ref, codes_ref, turned_ref, sems) = rest[:ways], rest[ways:]
    full, columns = lines_ref.shape
    rows = quarter * modes
    part = columns // 2 // ways
    copy = pltpu.make_async_copy(basis_ref.at[basis_ref.shape[0] - 1, pl.ds(2 * rows - full, full)], lines_ref, sems.at[0])
    copy.start()
    list_copy = pltpu.make_async_copy(list_ref, pair_rows_ref, sems.at[1])
    list_copy.start()
    pad_ref[...] = jnp.zeros_like(pad_ref)
    list_copy.wait()
    slots = pair_rows_ref.shape[2]
    live = iota((1, slots), 1) < count_ref[0]
    marks = jnp.where(live, own * (pair_rows_ref[2] + 1) + pair_rows_ref[0], 0)
    line = iota((slots, slots), 0)
    stacked = jnp.where(line == 0, marks, jnp.where(line == 1, pair_rows_ref[1], 0))
    turned = jnp.transpose(stacked.astype(F32))
    codes_ref[0:slots, :] = turned
    codes_ref[slots : 2 * slots, :] = pltpu.roll(turned, slots - 1, axis=1)
    share = 2 * quarter * part
    mine = codes_ref[pl.ds(pl.multiple_of(lax.axis_index("pair") * share, share), share), :][:, 0:1]
    copy.wait()
    for j in range(quarter):
        pad_ref[0:modes, :] = lines_ref[pl.ds(full - rows + j, modes, quarter), :]
        turned_ref[j] = jnp.transpose(pad_ref[...])
    _, octets, height, size = outs[0].shape
    each = height // quarter
    for i, out_ref in enumerate(outs):
        place = (lax.axis_index("pair") ^ i) * part
        for c in range(2):
            for o in range(octets):
                first = (c * octets + o) * height
                here = pl.ds(pl.multiple_of(c * (columns // 2) + place + o * each, each), each)
                piece = jnp.concatenate([turned_ref[j, here, :] for j in range(quarter)], axis=0)
                piece = jnp.where(iota(piece.shape, 1) == modes, mine[first : first + height], piece)
                out_ref[c, o] = piece.astype(BF16)


def join_kernel(*refs):
    out_ref = refs[-1]
    for i, ref in enumerate(refs[:-1]):
        out_ref[lax.axis_index("pair") ^ i] = ref[...]


def rotations_kernel(rot_ref, out_ref, rots_ref, sems):
    tables, size, _ = out_ref.shape
    listed, modes = rot_ref.shape
    chunk = 256
    copies = []
    for i, first in enumerate(range(0, listed, 4 * chunk)):
        here = pl.ds(first, min(4 * chunk, listed - first))
        copies.append(pltpu.make_async_copy(rot_ref.at[here], rots_ref.at[here], sems.at[i]))
        copies[-1].start()
    out_row, in_row = iota((chunk, chunk), 0), iota((chunk, chunk), 1)
    share = chunk // tables
    entries = (in_row == tables * lax.rem(out_row, share) + lax.div(out_row, share)).astype(F32).astype(BF16)
    out_ref[:, :, size - 128 : size] = jnp.zeros((tables, size, 128), BF16)
    rots_ref[listed:, :] = jnp.zeros((rots_ref.shape[0] - listed, modes), BF16)

    for i, copy in enumerate(copies):
        copy.wait()
        chunks = range(4 * i, min(4 * (i + 1), rots_ref.shape[0] // chunk))
        rows = [rots_ref[q * chunk : (q + 1) * chunk, :] for q in chunks]
        results = [dot_nn(entries, value).astype(BF16) for value in rows]
        for q, result in zip(chunks, results):
            for g in range(tables):
                out_ref[g, q * share : (q + 1) * share, 0:modes] = result[g * share : (g + 1) * share]


def axials_kernel(axial_ref, out_ref, axials_ref, sems):
    tables, double, size = out_ref.shape
    modes = axial_ref.shape[1]

    def fetch(g):
        return pltpu.make_async_copy(axial_ref.at[g], axials_ref.at[g], sems.at[g])

    for g in range(tables):
        fetch(g).start()
    chunk = 256
    out_row, in_row = iota((chunk, chunk), 0), iota((chunk, chunk), 1)
    each = chunk // 2
    halves = (in_row == 2 * lax.rem(out_row, each) + lax.div(out_row, each)).astype(F32).astype(BF16)
    out_ref[:, :, size - 128 : size] = jnp.zeros((tables, double, 128), BF16)

    together = 2 if tables % 2 == 0 else 1

    def split(step, carry):
        entries = [step * together + i for i in range(together)]
        for g in entries:
            fetch(g).wait()
        places = [(g, first) for g in entries for first in range(0, modes, each)]
        results = []
        for g, first in places:
            count = min(each, modes - first)
            rows = axials_ref[g, first : first + count].reshape(2 * count, modes)
            results.append(dot_nn(halves[:, : 2 * count], rows).astype(BF16))
        for (g, first), result in zip(places, results):
            for c in range(2):
                out_ref[g, c * size + first : c * size + first + each, 0:modes] = result[c * each : (c + 1) * each]
        return carry

    lax.fori_loop(0, tables // together, split, 0)


def swapped(value):
    half = value.shape[0] // 2
    return jnp.concatenate([-value[half:], value[:half]], axis=0)


def pair_counts(own, tables, lane, refs):
    ways, parts, octets, height, size = refs[0].shape
    group = ways * octets * height
    wanted = iota((tables * own, group), 0) + own

    def one_hot(hit):
        return jnp.where(hit, 1.0, 0.0).astype(BF16)

    forward, backward = None, []
    for window, ref in enumerate(refs):
        values = ref[:, :, :, :, size - 128 : size].reshape(2 * group, 128).astype(F32)
        marks_column, sources_column = (values[h * group : (h + 1) * group, lane : lane + 1].astype(jnp.int32) for h in range(2))
        marks, sources = (jnp.transpose(values[h * group : (h + 1) * group])[lane : lane + 1].astype(jnp.int32) for h in range(2))
        if window == 1:
            forward = dot_nn(one_hot(marks == wanted), one_hot(sources_column == iota((group, 3 * own), 1)))
        block = sources - (2 - window) * own
        inside = (block >= 0) & (block < own) & (marks >= own)
        hits = one_hot(jnp.where(inside, lax.div(marks, own) * own + block, -1) == wanted)
        place = lax.rem(marks_column, own) + window * own
        backward.append(dot_nn(hits, one_hot(place == iota((group, 3 * own), 1))))
    return jnp.concatenate([forward, sum(backward)], axis=0).astype(BF16)


def folded(value):
    return jnp.sum(value.reshape(value.shape[0] // 8, 8, value.shape[1]), axis=0)


def field_kernel(
    own, modes, together, rot_ref, axial_ref, below_ref, own_ref, above_ref, *rest
):
    outs, (sums_ref, total_ref) = rest[:-2], rest[-2:]
    tables, _, size = rot_ref.shape
    refs = (below_ref, own_ref, above_ref)
    ways, _, octets, height, _ = own_ref.shape
    quarter = own // ways
    each = height // quarter
    part = octets * each
    group = own * part
    counts = pair_counts(own, tables, modes % 128, refs)
    spread = jnp.where(iota((3 * own, 3 * own * each), 0) == lax.div(iota((3 * own, 3 * own * each), 1), each), 1.0, 0.0)
    counts = dot_nn(counts, spread.astype(BF16))
    sphere = lax.rem(iota(counts.shape, 1), each)
    chosen = jnp.concatenate([jnp.where(sphere == i, counts, 0.0).astype(BF16) for i in range(each)], axis=0)
    kinds = 2 * tables * own
    for c in range(2):
        for o in range(octets):
            blocks = jnp.concatenate([ref[:, c, o].reshape(ways * height, size) for ref in refs], axis=0)
            for i in range(0, each, 2):
                results = dot_nn(chosen[i * kinds : (i + 2) * kinds], blocks)
                for kind in range(2 * tables):
                    direction, g = kind // tables, kind % tables
                    rows = [results[start + kind * own : start + (kind + 1) * own] for start in (0, kinds)]
                    place = (direction * 2 + c) * group + (o * each + i) * own
                    sums_ref[g, place : place + 2 * own, :] = jnp.concatenate(rows, axis=0).astype(BF16)
    total_ref[...] = jnp.zeros_like(total_ref)

    def body(step, carry):
        entries = [step * together + i for i in range(together)]
        turned = [dot_nt(sums_ref[g], rot_ref[g]).astype(BF16) for g in entries]
        moved = []
        for g, both in zip(entries, turned):
            forward, backward = both[: 2 * group], both[2 * group :]
            result = dot_nt(forward, axial_ref[g, :size]) + dot_nt(swapped(forward), axial_ref[g, size:])
            result += dot_nn(jnp.concatenate([backward, swapped(backward)], axis=1), axial_ref[g])
            moved.append(result.astype(BF16))
        total_ref[...] += sum(dot_nn(value, rot_ref[g]) for g, value in zip(entries, moved))
        return carry

    if together == tables:
        body(0, 0)
    else:
        lax.fori_loop(0, tables // together, body, 0)
    row, source = iota((2 * group, 2 * group), 0), iota((2 * group, 2 * group), 1)
    sphere, c = lax.rem(row, part), lax.rem(lax.div(row, quarter * part), 2)
    owner = lax.div(row, 2 * quarter * part) ^ lax.axis_index("pair")
    block = owner * quarter + lax.rem(lax.div(row, part), quarter)
    order = jnp.where(source == c * group + sphere * own + block, 1.0, 0.0).astype(BF16)
    result = dot_nn(order, total_ref[...].astype(BF16)).astype(BF16)
    share = 2 * quarter * part
    for i, out_ref in enumerate(outs):
        out_ref[...] = result[i * share : (i + 1) * share].reshape(out_ref.shape)


def lane_swap(value):
    half = value.shape[1] // 2
    rolled = pltpu.roll(value, half, axis=1)
    return jnp.where(iota(value.shape, 1) < half, -rolled, rolled)


def add_products(blocks_ref, products_ref, rows, first, count):
    vectors = products_ref.shape[0]
    values = []
    for k in range(vectors):
        start = k % 2 * rows + first
        value = blocks_ref[k // 2, start : start + count, :]
        if k % 2 == 0 and first + count > rows:
            value = jnp.where(iota(value.shape, 0) < rows - first, value, 0.0)
        values.append(value)
    for l in range(vectors):
        other = pltpu.roll(values[l], values[l].shape[1] // 2, axis=1)
        for k in range(l + 1):
            products_ref[k, l] += folded(values[k] * values[l])
            if k < l:
                products_ref[l, k] += folded(values[k] * other)


def products_line(products_ref):
    vectors, _, _, columns = products_ref.shape
    pairs = vectors * vectors
    totals = jnp.sum(products_ref[...].reshape(pairs, 8, columns), axis=1)
    pair = iota(totals.shape, 0)
    signed = (lax.div(pair, vectors) > lax.rem(pair, vectors)) & (iota(totals.shape, 1) >= columns // 2)
    totals = jnp.sum(jnp.where(signed, -totals, totals), axis=1, keepdims=True)
    row, lane = iota((vectors, 128), 0), iota((vectors, 128), 1)
    line = jnp.zeros((1, 128), F32)
    for k in range(vectors):
        column = totals[k * vectors : (k + 1) * vectors]
        line += jnp.sum(jnp.where(row + k * vectors == lane, column, 0.0), axis=0, keepdims=True)
    return line


def gram_kernel(quarter, modes, basis_ref, mie_ref, products_ref, blocks_ref, mies_ref, mie_sem, sems):
    blocks, _, columns = basis_ref.shape
    rows = quarter * modes
    parts, chunk = 4, 32
    tile_end = rows // 8 * 8
    step = rounded_up(rows, 8 * parts) // parts
    even = [0] + [step * q for q in range(1, parts)] + [tile_end]
    odd = [tile_end] + [rounded_up(rows, 8) + step * q for q in range(1, parts)] + [2 * rows]
    copies = []
    for q in range(parts):
        for i in range(blocks):
            for side, cuts in enumerate((even, odd)):
                here = pl.ds(cuts[q], cuts[q + 1] - cuts[q])
                copies.append(pltpu.make_async_copy(basis_ref.at[i, here], blocks_ref.at[i, here], sems.at[q, i, side]))
    for copy in copies:
        copy.start()
    mie_rows = mie_ref.shape[0]
    mie_copy = pltpu.make_async_copy(mie_ref, mies_ref.at[pl.ds(0, mie_rows)], mie_sem)
    mie_copy.start()
    mies_ref[mie_rows:] = jnp.zeros((mies_ref.shape[0] - mie_rows,) + mies_ref.shape[1:], F32)
    products_ref[...] = jnp.zeros_like(products_ref)
    for i in range(blocks):
        blocks_ref[i, 2 * rows :, :] = jnp.zeros((blocks_ref.shape[1] - 2 * rows, columns), F32)
    for q in range(parts):
        for copy in copies[2 * blocks * q : 2 * blocks * (q + 1)]:
            copy.wait()
        if q < parts - 1:
            for first in range(step * q, step * (q + 1), chunk):
                add_products(blocks_ref, products_ref, rows, first, chunk)
    mie_copy.wait()


def gram_end_kernel(quarter, modes, products_ref, blocks_ref, line_ref, totals_ref):
    rows = quarter * modes
    parts, chunk = 4, 32
    totals_ref[...] = products_ref[...]
    for first in range(rounded_up(rows, 8 * parts) // parts * (parts - 1), rows, chunk):
        add_products(blocks_ref, totals_ref, rows, first, chunk)
    line_ref[...] = products_line(totals_ref)


def image_kernel(quarter, modes, blocks_ref, mie_ref, gram_ref, *rest):
    pieces, (image_ref, sums_ref, lines_ref, whole_ref) = rest[:-4], rest[-4:]
    vectors = 2 * blocks_ref.shape[0]
    full, columns = image_ref.shape
    rows = quarter * modes
    part = pieces[0].shape[2]
    for i, piece_ref in enumerate(pieces):
        place = pl.multiple_of((lax.axis_index("pair") ^ i) * part, part)
        for j in range(quarter):
            for c in range(2):
                whole_ref[j, pl.ds(c * (columns // 2) + place, part), :] = piece_ref[c, j]
    lines_ref[rows:full, :] = jnp.zeros((full - rows, columns), F32)
    for j in range(quarter):
        lines_ref[pl.ds(j, modes, quarter), :] = jnp.transpose(whole_ref[j].astype(F32))[:modes]
    half = columns // 2
    chunk = 64
    totals = [jnp.zeros((8, columns), F32) for _ in range(2 * vectors + 1)]
    for first in range(0, full, chunk):
        here = slice(first, first + chunk)
        field = lines_ref[here, :]
        count = min(chunk, rows - first)
        height = mie_ref.shape[1]
        mie = mie_ref[first // height : (first + count) // height].reshape(count, columns)
        if count < chunk:
            mie = jnp.concatenate([mie, jnp.zeros((chunk - count, columns), F32)], axis=0)
        left = iota(mie.shape, 1) < half
        other = pltpu.roll(mie, half, axis=1)
        product = jnp.where(left, mie, other) * field + jnp.where(left, -other, mie) * pltpu.roll(field, half, axis=1)
        last = (vectors - 1) % 2 * rows + first
        image = blocks_ref[(vectors - 1) // 2, last : last + chunk, :] - product
        image_ref[here, :] = image
        turned = pltpu.roll(product, half, axis=1)
        for k in range(vectors):
            start = k % 2 * rows + first
            values = blocks_ref[k // 2, start : start + chunk, :]
            totals[2 * k] += folded(values * product)
            totals[2 * k + 1] += folded(values * turned)
        totals[2 * vectors] += folded(product * product)
    lane = iota(gram_ref.shape, 1)
    line = gram_ref[...]
    left = iota((8, columns), 1) < half
    for index, total in enumerate(totals):
        if index % 2 and index < 2 * vectors:
            total = jnp.where(left, total, -total)
        line = jnp.where(lane == vectors * vectors + index, jnp.sum(total, axis=(0, 1), keepdims=True), line)
    sums_ref[...] = jnp.broadcast_to(line[None], sums_ref.shape)


def remainder_kernel(quarter, modes, mean_scale, sums_ref, blocks_ref, image_ref, dots_ref, out_ref):
    vectors = 2 * blocks_ref.shape[0]
    full, columns = image_ref.shape
    rows = quarter * modes
    total = jnp.sum(sums_ref[...], axis=0)
    lane = iota(total.shape, 1)

    def lane_at(index):
        return jnp.sum(jnp.where(lane == index, total, 0.0), axis=1, keepdims=True)

    def on_lanes(parts, places):
        line = jnp.zeros(total.shape, F32)
        for k in range(vectors):
            line = jnp.where(places == k, parts[k], line)
        return line

    start = vectors * vectors
    last = vectors - 1
    taken_real = [lane_at(start + 2 * k) * mean_scale for k in range(vectors)]
    taken_imag = [lane_at(start + 2 * k + 1) * mean_scale for k in range(vectors)]
    real = [lane_at(k * vectors + last) * mean_scale - taken_real[k] for k in range(vectors)]
    imag = [lane_at(last * vectors + k) * mean_scale - taken_imag[k] for k in range(last)] + [-taken_imag[last]]
    dots_ref[0:1, :] = on_lanes(real, lane)[:, :vectors]
    dots_ref[1:2, :] = on_lanes(imag, lane)[:, :vectors]
    kept_real = [-value for value in real[:last]] + [1.0 - real[last]]
    kept_imag = [-value for value in imag]
    first_index, last_index = lax.div(lane, vectors), lax.rem(lane, vectors)
    real_first, real_last = on_lanes(kept_real, first_index), on_lanes(kept_real, last_index)
    imag_first, imag_last = on_lanes(kept_imag, first_index), on_lanes(kept_imag, last_index)
    same = real_first * real_last + imag_first * imag_last
    cross = imag_last * real_first - real_last * imag_first
    often = jnp.where(first_index == last_index, 1.0, 2.0)
    spread = jnp.where(lane < start, total * often * jnp.where(first_index <= last_index, same, cross), 0.0)
    spread = jnp.sum(spread, axis=1, keepdims=True)
    both = sum(kept_real[k] * taken_real[k] + kept_imag[k] * taken_imag[k] for k in range(vectors))
    norm_square = (lane_at(start + 2 * vectors) + spread) * mean_scale - 2.0 * both
    scale = lax.rsqrt(norm_square)
    image_scale = jnp.broadcast_to(scale, (8, columns))
    reals = [jnp.broadcast_to(real[k] * scale, (8, columns)) for k in range(vectors)]
    imags = [jnp.broadcast_to(imag[k] * scale, (8, columns)) for k in range(vectors)]
    chunk = 64
    for first in range(0, full, chunk):
        here = slice(first, first + chunk)
        values = []
        for k in range(vectors):
            start = k % 2 * rows + first
            values.append(blocks_ref[k // 2, start : start + chunk, :].reshape(chunk // 8, 8, columns))
        along = image_ref[here, :].reshape(chunk // 8, 8, columns) * image_scale
        turned = jnp.zeros_like(along)
        for k in range(vectors):
            along -= reals[k] * values[k]
            turned += imags[k] * values[k]
        result = along.reshape(chunk, columns) - lane_swap(turned.reshape(chunk, columns))
        count = min(chunk, rows - first)
        height = out_ref.shape[1]
        out_ref[first // height : (first + count) // height] = result.reshape(chunk // height, height, columns)[: count // height]


def exchanged(pieces, axis):
    count = lax.axis_size(axis)
    received = [pieces[0]]
    for i in range(1, len(pieces)):
        received.append(lax.ppermute(pieces[i], axis, [(p, p ^ i) for p in range(count)]))
    return received


def from_neighbour(value, up):
    pairs = [(i, i + 1) for i in range(lax.axis_size("blk") - 1)]
    return lax.ppermute(value, "blk", pairs if up else [(j, i) for i, j in pairs])


def shards(basis, mie_coeffs, rot_table, axial_table, pair_table, pair_count):
    vectors, quarter, modes, columns = basis.shape
    ways = lax.axis_size("pair")
    blk_ways = lax.axis_size("blk")
    tables = rot_table.shape[0]
    slots = pair_table.shape[1]
    own = quarter * ways
    part = columns // 2 // ways
    group = own * part
    size = rounded_up(modes, 128)
    rows = quarter * modes
    full = rounded_up(rows, 8)
    pairs_of_vectors = vectors // 2
    height = 4

    basis_rows = in_hbm(basis.transpose(0, 2, 1, 3).reshape(pairs_of_vectors, 2 * rows, columns))
    mie_rows = in_hbm(mie_coeffs.transpose(1, 0, 2).reshape(rows // 4, 4, columns))
    rot_rows = in_hbm(rot_table.transpose(1, 0, 2).reshape(modes * tables, modes))
    axial_rows = in_hbm(axial_table.transpose(0, 2, 1, 3))
    pair_rows = in_hbm(pair_table.transpose(2, 0, 1))

    octets = part * quarter // 16
    piece = jax.ShapeDtypeStruct((2, octets, 16, size), BF16)
    pieces = pl.pallas_call(
        functools.partial(pack_kernel, quarter, modes, ways, own),
        in_specs=[hbm(), pl.BlockSpec(memory_space=pltpu.SMEM), hbm()],
        out_specs=[whole()] * ways,
        out_shape=[piece] * ways,
        scratch_shapes=[
            pltpu.VMEM(pair_rows.shape, jnp.int32),
            pltpu.VMEM((full, columns), F32),
            pltpu.VMEM((size, columns), F32),
            pltpu.VMEM((2 * slots, slots), F32),
            pltpu.VMEM((quarter, columns, size), F32),
            pltpu.SemaphoreType.DMA((2,)),
        ],
        compiler_params=params(16),
        name="pack",
    )(pair_rows, pair_count, basis_rows)
    tall = rounded_up(rows + full, 8)
    *pieces, basis_rows, mie_rows = lax.optimization_barrier((*pieces, basis_rows, mie_rows))
    received = exchanged(pieces, "pair")
    products, blocks, mies = pl.pallas_call(
        functools.partial(gram_kernel, quarter, modes),
        in_specs=[hbm()] * 2,
        out_specs=[whole()] * 3,
        out_shape=[
            jax.ShapeDtypeStruct((vectors, vectors, 8, columns), F32),
            jax.ShapeDtypeStruct((pairs_of_vectors, tall, columns), F32),
            jax.ShapeDtypeStruct((full // height, height, columns), F32),
        ],
        scratch_shapes=[
            pltpu.SemaphoreType.DMA,
            pltpu.SemaphoreType.DMA((4, pairs_of_vectors, 2)),
        ],
        compiler_params=params(8),
        name="gram",
    )(basis_rows, mie_rows)
    *received, products, rot_rows, axial_rows = lax.optimization_barrier((*received, products, rot_rows, axial_rows))
    own_pieces = pl.pallas_call(
        join_kernel,
        in_specs=[whole()] * ways,
        out_specs=whole(),
        out_shape=jax.ShapeDtypeStruct((ways, *piece.shape), BF16),
        compiler_params=params(4),
        name="join",
    )(*received)
    own_pieces, products, rot_rows = lax.optimization_barrier((own_pieces, products, rot_rows))
    above = from_neighbour(own_pieces, False)
    line = pl.pallas_call(
        functools.partial(gram_end_kernel, quarter, modes),
        in_specs=[whole()] * 2,
        out_specs=whole(),
        out_shape=jax.ShapeDtypeStruct((1, 128), F32),
        scratch_shapes=[pltpu.VMEM((vectors, vectors, 8, columns), F32)],
        compiler_params=params(4),
        name="gram_end",
    )(products, blocks)
    rotations = pl.pallas_call(
        rotations_kernel,
        in_specs=[hbm()],
        out_specs=whole(),
        out_shape=jax.ShapeDtypeStruct((tables, size, size), BF16),
        scratch_shapes=[
            pltpu.VMEM((tables * size, modes), BF16),
            pltpu.SemaphoreType.DMA((rounded_up(modes * tables, 1024) // 1024,)),
        ],
        compiler_params=params(8),
        name="rotations",
    )(rot_rows)
    own_pieces, line, rotations, axial_rows = lax.optimization_barrier((own_pieces, line, rotations, axial_rows))
    below = from_neighbour(own_pieces, True)
    axials = pl.pallas_call(
        axials_kernel,
        in_specs=[hbm()],
        out_specs=whole(),
        out_shape=jax.ShapeDtypeStruct((tables, 2 * size, size), BF16),
        scratch_shapes=[pltpu.VMEM(axial_rows.shape, BF16), pltpu.SemaphoreType.DMA((tables,))],
        compiler_params=params(16),
        cost_estimate=pl.CostEstimate(flops=tables * 8 * 256 * 256 * size, bytes_accessed=4 * tables * size * size * 2, transcendentals=0),
        name="axials",
    )(axial_rows)
    below, above, axials = lax.optimization_barrier((below, above, axials))

    together = tables
    field = pl.pallas_call(
        functools.partial(field_kernel, own, modes, together),
        in_specs=[whole()] * 5,
        out_specs=[whole()] * ways,
        out_shape=[jax.ShapeDtypeStruct((2, quarter, part, size), BF16)] * ways,
        scratch_shapes=[pltpu.VMEM((tables, 4 * group, size), BF16), pltpu.VMEM((2 * group, size), F32)],
        compiler_params=params(28),
        name="field",
    )(rotations, axials, below, own_pieces, above)
    field_pieces = exchanged(field, "pair")

    image, sums = pl.pallas_call(
        functools.partial(image_kernel, quarter, modes),
        in_specs=[whole()] * (ways + 3),
        out_specs=[whole()] * 2,
        out_shape=[jax.ShapeDtypeStruct((full, columns), F32), jax.ShapeDtypeStruct((ways * blk_ways, 1, 128), F32)],
        scratch_shapes=[pltpu.VMEM((full, columns), F32), pltpu.VMEM((quarter, columns, size), BF16)],
        compiler_params=params(8),
        name="image",
    )(blocks, mies, line, *field_pieces)
    sums = lax.all_to_all(sums, ("blk", "pair"), split_axis=0, concat_axis=0, tiled=True)

    mean_scale = 1.0 / (own * blk_ways * modes * columns)
    dots, next_rows = pl.pallas_call(
        functools.partial(remainder_kernel, quarter, modes, mean_scale),
        in_specs=[whole()] * 3,
        out_specs=[whole(), whole()],
        out_shape=[jax.ShapeDtypeStruct((2, vectors), F32), jax.ShapeDtypeStruct((rows // height, height, columns), F32)],
        compiler_params=params(16),
        name="remainder",
    )(sums, blocks, image)
    return dots, next_rows.reshape(modes, quarter, columns).transpose(1, 0, 2)


def solution(mesh):
    placed = (
        P(None, ("blk", "pair"), None, None),
        P(("blk", "pair"), None, None),
        P(),
        P(),
        P("blk", None, None),
        P("blk"),
    )
    return jax.shard_map(
        shards,
        mesh=mesh,
        in_specs=placed,
        out_specs=(P(), P(("blk", "pair"), None, None)),
        check_vma=False,
    )
```

```python
import functools

import jax
import jax.numpy as jnp
from jax import lax
from jax.experimental import pallas as pl
from jax.experimental.pallas import tpu as pltpu
from jax.sharding import PartitionSpec as P

MIB = 1024 * 1024
F32 = jnp.float32
BF16 = jnp.bfloat16


def params(mib):
    return pltpu.CompilerParams(vmem_limit_bytes=mib * MIB)


def hbm():
    return pl.BlockSpec(memory_space=pltpu.HBM)


def whole():
    return pl.BlockSpec(memory_space=pltpu.VMEM)


def in_hbm(value):
    return pltpu.with_memory_space_constraint(value, pltpu.HBM)


def rounded_up(value, unit):
    return (value + unit - 1) // unit * unit


def iota(shape, dim):
    return lax.broadcasted_iota(jnp.int32, shape, dim)


def dot_nn(left, right):
    return lax.dot_general(left, right, (((1,), (0,)), ((), ())), preferred_element_type=F32)


def dot_nt(left, right):
    return lax.dot_general(left, right, (((1,), (1,)), ((), ())), preferred_element_type=F32)


def pack_kernel(quarter, modes, ways, own, list_ref, count_ref, basis_ref, *rest):
    outs, (pair_rows_ref, lines_ref, pad_ref, codes_ref, turned_ref, sems) = rest[:ways], rest[ways:]
    full, columns = lines_ref.shape
    rows = quarter * modes
    part = columns // 2 // ways
    copy = pltpu.make_async_copy(basis_ref.at[basis_ref.shape[0] - 1, pl.ds(2 * rows - full, full)], lines_ref, sems.at[0])
    copy.start()
    list_copy = pltpu.make_async_copy(list_ref, pair_rows_ref, sems.at[1])
    list_copy.start()
    pad_ref[...] = jnp.zeros_like(pad_ref)
    list_copy.wait()
    slots = pair_rows_ref.shape[2]
    live = iota((1, slots), 1) < count_ref[0]
    marks = jnp.where(live, own * (pair_rows_ref[2] + 1) + pair_rows_ref[0], 0)
    line = iota((slots, slots), 0)
    stacked = jnp.where(line == 0, marks, jnp.where(line == 1, pair_rows_ref[1], 0))
    turned = jnp.transpose(stacked.astype(F32))
    codes_ref[0:slots, :] = turned
    codes_ref[slots : 2 * slots, :] = pltpu.roll(turned, slots - 1, axis=1)
    share = 2 * quarter * part
    mine = codes_ref[pl.ds(pl.multiple_of(lax.axis_index("pair") * share, share), share), :][:, 0:1]
    copy.wait()
    for j in range(quarter):
        pad_ref[0:modes, :] = lines_ref[pl.ds(full - rows + j, modes, quarter), :]
        turned_ref[j] = jnp.transpose(pad_ref[...])
    _, octets, height, size = outs[0].shape
    each = height // quarter
    for i, out_ref in enumerate(outs):
        place = (lax.axis_index("pair") ^ i) * part
        for c in range(2):
            for o in range(octets):
                first = (c * octets + o) * height
                here = pl.ds(pl.multiple_of(c * (columns // 2) + place + o * each, each), each)
                piece = jnp.concatenate([turned_ref[j, here, :] for j in range(quarter)], axis=0)
                piece = jnp.where(iota(piece.shape, 1) == modes, mine[first : first + height], piece)
                out_ref[c, o] = piece.astype(BF16)


def join_kernel(*refs):
    out_ref = refs[-1]
    for i, ref in enumerate(refs[:-1]):
        out_ref[lax.axis_index("pair") ^ i] = ref[...]


def tables_kernel(
    quarter, modes, rot_ref, axial_ref, products_ref, blocks_ref, rot_out_ref, axial_out_ref, line_ref, rots_ref, axials_ref, totals_ref, sems,
):
    tables, size, _ = rot_out_ref.shape
    listed = rot_ref.shape[0]
    chunk = 256
    rot_copies = []
    for i, first in enumerate(range(0, listed, 4 * chunk)):
        here = pl.ds(first, min(4 * chunk, listed - first))
        rot_copies.append(pltpu.make_async_copy(rot_ref.at[here], rots_ref.at[here], sems.at[tables + i]))
        rot_copies[-1].start()

    def fetch(g):
        return pltpu.make_async_copy(axial_ref.at[g], axials_ref.at[g], sems.at[g])

    for g in range(tables):
        fetch(g).start()
    for ref in (rot_out_ref, axial_out_ref):
        ref[:, :, size - 128 : size] = jnp.zeros((tables, ref.shape[1], 128), BF16)
    rots_ref[listed:, :] = jnp.zeros((rots_ref.shape[0] - listed, modes), BF16)
    gram_end(quarter * modes, products_ref, blocks_ref, line_ref, totals_ref)

    out_row, in_row = iota((chunk, chunk), 0), iota((chunk, chunk), 1)
    share = chunk // tables
    entries = (in_row == tables * lax.rem(out_row, share) + lax.div(out_row, share)).astype(F32).astype(BF16)
    for i, copy in enumerate(rot_copies):
        copy.wait()
        chunks = range(4 * i, min(4 * (i + 1), rots_ref.shape[0] // chunk))
        rows = [rots_ref[q * chunk : (q + 1) * chunk, :] for q in chunks]
        results = [dot_nn(entries, value).astype(BF16) for value in rows]
        for q, result in zip(chunks, results):
            for g in range(tables):
                rot_out_ref[g, q * share : (q + 1) * share, 0:modes] = result[g * share : (g + 1) * share]

    each = chunk // 2
    halves = (in_row == 2 * lax.rem(out_row, each) + lax.div(out_row, each)).astype(F32).astype(BF16)
    together = 2 if tables % 2 == 0 else 1

    def split(step, carry):
        members = [step * together + i for i in range(together)]
        for g in members:
            fetch(g).wait()
        places = [(g, first) for g in members for first in range(0, modes, each)]
        results = []
        for g, first in places:
            count = min(each, modes - first)
            rows = axials_ref[g, first : first + count].reshape(2 * count, modes)
            results.append(dot_nn(halves[:, : 2 * count], rows).astype(BF16))
        for (g, first), result in zip(places, results):
            for c in range(2):
                axial_out_ref[g, c * size + first : c * size + first + each, 0:modes] = result[c * each : (c + 1) * each]
        return carry

    lax.fori_loop(0, tables // together, split, 0)


def swapped(value):
    half = value.shape[0] // 2
    return jnp.concatenate([-value[half:], value[:half]], axis=0)


def pair_counts(own, tables, lane, refs):
    ways, parts, octets, height, size = refs[0].shape
    group = ways * octets * height
    wanted = iota((tables * own, group), 0) + own

    def one_hot(hit):
        return jnp.where(hit, 1.0, 0.0).astype(BF16)

    forward, backward = None, []
    for window, ref in enumerate(refs):
        values = ref[:, :, :, :, size - 128 : size].reshape(2 * group, 128).astype(F32)
        marks_column, sources_column = (values[h * group : (h + 1) * group, lane : lane + 1].astype(jnp.int32) for h in range(2))
        marks, sources = (jnp.transpose(values[h * group : (h + 1) * group])[lane : lane + 1].astype(jnp.int32) for h in range(2))
        if window == 1:
            forward = dot_nn(one_hot(marks == wanted), one_hot(sources_column == iota((group, 3 * own), 1)))
        block = sources - (2 - window) * own
        inside = (block >= 0) & (block < own) & (marks >= own)
        hits = one_hot(jnp.where(inside, lax.div(marks, own) * own + block, -1) == wanted)
        place = lax.rem(marks_column, own) + window * own
        backward.append(dot_nn(hits, one_hot(place == iota((group, 3 * own), 1))))
    return jnp.concatenate([forward, sum(backward)], axis=0).astype(BF16)


def folded(value):
    return jnp.sum(value.reshape(value.shape[0] // 8, 8, value.shape[1]), axis=0)


def field_kernel(
    own, modes, together, rot_ref, axial_ref, below_ref, own_ref, above_ref, *rest
):
    outs, (sums_ref, total_ref) = rest[:-2], rest[-2:]
    tables, _, size = rot_ref.shape
    refs = (below_ref, own_ref, above_ref)
    ways, _, octets, height, _ = own_ref.shape
    quarter = own // ways
    each = height // quarter
    part = octets * each
    group = own * part
    counts = pair_counts(own, tables, modes % 128, refs)
    spread = jnp.where(iota((3 * own, 3 * own * each), 0) == lax.div(iota((3 * own, 3 * own * each), 1), each), 1.0, 0.0)
    counts = dot_nn(counts, spread.astype(BF16))
    sphere = lax.rem(iota(counts.shape, 1), each)
    chosen = jnp.concatenate([jnp.where(sphere == i, counts, 0.0).astype(BF16) for i in range(each)], axis=0)
    kinds = 2 * tables * own
    for c in range(2):
        for o in range(octets):
            blocks = jnp.concatenate([ref[:, c, o].reshape(ways * height, size) for ref in refs], axis=0)
            for i in range(0, each, 2):
                results = dot_nn(chosen[i * kinds : (i + 2) * kinds], blocks)
                for kind in range(2 * tables):
                    direction, g = kind // tables, kind % tables
                    rows = [results[start + kind * own : start + (kind + 1) * own] for start in (0, kinds)]
                    place = (direction * 2 + c) * group + (o * each + i) * own
                    sums_ref[g, place : place + 2 * own, :] = jnp.concatenate(rows, axis=0).astype(BF16)
    total_ref[...] = jnp.zeros_like(total_ref)

    def body(step, carry):
        entries = [step * together + i for i in range(together)]
        turned = [dot_nt(sums_ref[g], rot_ref[g]).astype(BF16) for g in entries]
        moved = []
        for g, both in zip(entries, turned):
            forward, backward = both[: 2 * group], both[2 * group :]
            result = dot_nt(forward, axial_ref[g, :size]) + dot_nt(swapped(forward), axial_ref[g, size:])
            result += dot_nn(jnp.concatenate([backward, swapped(backward)], axis=1), axial_ref[g])
            moved.append(result.astype(BF16))
        total_ref[...] += sum(dot_nn(value, rot_ref[g]) for g, value in zip(entries, moved))
        return carry

    if together == tables:
        body(0, 0)
    else:
        lax.fori_loop(0, tables // together, body, 0)
    row, source = iota((2 * group, 2 * group), 0), iota((2 * group, 2 * group), 1)
    sphere, c = lax.rem(row, part), lax.rem(lax.div(row, quarter * part), 2)
    owner = lax.div(row, 2 * quarter * part) ^ lax.axis_index("pair")
    block = owner * quarter + lax.rem(lax.div(row, part), quarter)
    order = jnp.where(source == c * group + sphere * own + block, 1.0, 0.0).astype(BF16)
    result = dot_nn(order, total_ref[...].astype(BF16)).astype(BF16)
    share = 2 * quarter * part
    for i, out_ref in enumerate(outs):
        out_ref[...] = result[i * share : (i + 1) * share].reshape(out_ref.shape)


def lane_swap(value):
    half = value.shape[1] // 2
    rolled = pltpu.roll(value, half, axis=1)
    return jnp.where(iota(value.shape, 1) < half, -rolled, rolled)


def add_products(blocks_ref, products_ref, rows, first, count):
    vectors = products_ref.shape[0]
    values = []
    for k in range(vectors):
        start = k % 2 * rows + first
        value = blocks_ref[k // 2, start : start + count, :]
        if k % 2 == 0 and first + count > rows:
            value = jnp.where(iota(value.shape, 0) < rows - first, value, 0.0)
        values.append(value)
    for l in range(vectors):
        other = pltpu.roll(values[l], values[l].shape[1] // 2, axis=1)
        for k in range(l + 1):
            products_ref[k, l] += folded(values[k] * values[l])
            if k < l:
                products_ref[l, k] += folded(values[k] * other)


def products_line(products_ref):
    vectors, _, _, columns = products_ref.shape
    pairs = vectors * vectors
    totals = jnp.sum(products_ref[...].reshape(pairs, 8, columns), axis=1)
    pair = iota(totals.shape, 0)
    signed = (lax.div(pair, vectors) > lax.rem(pair, vectors)) & (iota(totals.shape, 1) >= columns // 2)
    totals = jnp.sum(jnp.where(signed, -totals, totals), axis=1, keepdims=True)
    row, lane = iota((vectors, 128), 0), iota((vectors, 128), 1)
    line = jnp.zeros((1, 128), F32)
    for k in range(vectors):
        column = totals[k * vectors : (k + 1) * vectors]
        line += jnp.sum(jnp.where(row + k * vectors == lane, column, 0.0), axis=0, keepdims=True)
    return line


def gram_kernel(quarter, modes, basis_ref, mie_ref, products_ref, blocks_ref, mies_ref, mie_sem, sems):
    blocks, _, columns = basis_ref.shape
    rows = quarter * modes
    parts, chunk = 4, 32
    tile_end = rows // 8 * 8
    step = rounded_up(rows, 8 * parts) // parts
    even = [0] + [step * q for q in range(1, parts)] + [tile_end]
    odd = [tile_end] + [rounded_up(rows, 8) + step * q for q in range(1, parts)] + [2 * rows]
    copies = []
    for q in range(parts):
        for i in range(blocks):
            for side, cuts in enumerate((even, odd)):
                here = pl.ds(cuts[q], cuts[q + 1] - cuts[q])
                copies.append(pltpu.make_async_copy(basis_ref.at[i, here], blocks_ref.at[i, here], sems.at[q, i, side]))
    for copy in copies:
        copy.start()
    mie_rows = mie_ref.shape[0]
    mie_copy = pltpu.make_async_copy(mie_ref, mies_ref.at[pl.ds(0, mie_rows)], mie_sem)
    mie_copy.start()
    mies_ref[mie_rows:] = jnp.zeros((mies_ref.shape[0] - mie_rows,) + mies_ref.shape[1:], F32)
    products_ref[...] = jnp.zeros_like(products_ref)
    for i in range(blocks):
        blocks_ref[i, 2 * rows :, :] = jnp.zeros((blocks_ref.shape[1] - 2 * rows, columns), F32)
    for q in range(parts):
        for copy in copies[2 * blocks * q : 2 * blocks * (q + 1)]:
            copy.wait()
        if q < parts - 1:
            for first in range(step * q, step * (q + 1), chunk):
                add_products(blocks_ref, products_ref, rows, first, chunk)
    mie_copy.wait()


def gram_end(rows, products_ref, blocks_ref, line_ref, totals_ref):
    parts, chunk = 4, 32
    totals_ref[...] = products_ref[...]
    for first in range(rounded_up(rows, 8 * parts) // parts * (parts - 1), rows, chunk):
        add_products(blocks_ref, totals_ref, rows, first, chunk)
    line_ref[...] = products_line(totals_ref)


def image_kernel(quarter, modes, blocks_ref, mie_ref, gram_ref, *rest):
    pieces, (image_ref, sums_ref, lines_ref, whole_ref) = rest[:-4], rest[-4:]
    vectors = 2 * blocks_ref.shape[0]
    full, columns = image_ref.shape
    rows = quarter * modes
    part = pieces[0].shape[2]
    for i, piece_ref in enumerate(pieces):
        place = pl.multiple_of((lax.axis_index("pair") ^ i) * part, part)
        for j in range(quarter):
            for c in range(2):
                whole_ref[j, pl.ds(c * (columns // 2) + place, part), :] = piece_ref[c, j]
    lines_ref[rows:full, :] = jnp.zeros((full - rows, columns), F32)
    for j in range(quarter):
        lines_ref[pl.ds(j, modes, quarter), :] = jnp.transpose(whole_ref[j].astype(F32))[:modes]
    half = columns // 2
    chunk = 64
    totals = [jnp.zeros((8, columns), F32) for _ in range(2 * vectors + 1)]
    for first in range(0, full, chunk):
        here = slice(first, first + chunk)
        field = lines_ref[here, :]
        count = min(chunk, rows - first)
        height = mie_ref.shape[1]
        mie = mie_ref[first // height : (first + count) // height].reshape(count, columns)
        if count < chunk:
            mie = jnp.concatenate([mie, jnp.zeros((chunk - count, columns), F32)], axis=0)
        left = iota(mie.shape, 1) < half
        other = pltpu.roll(mie, half, axis=1)
        product = jnp.where(left, mie, other) * field + jnp.where(left, -other, mie) * pltpu.roll(field, half, axis=1)
        last = (vectors - 1) % 2 * rows + first
        image = blocks_ref[(vectors - 1) // 2, last : last + chunk, :] - product
        image_ref[here, :] = image
        turned = pltpu.roll(product, half, axis=1)
        for k in range(vectors):
            start = k % 2 * rows + first
            values = blocks_ref[k // 2, start : start + chunk, :]
            totals[2 * k] += folded(values * product)
            totals[2 * k + 1] += folded(values * turned)
        totals[2 * vectors] += folded(product * product)
    lane = iota(gram_ref.shape, 1)
    line = gram_ref[...]
    left = iota((8, columns), 1) < half
    for index, total in enumerate(totals):
        if index % 2 and index < 2 * vectors:
            total = jnp.where(left, total, -total)
        line = jnp.where(lane == vectors * vectors + index, jnp.sum(total, axis=(0, 1), keepdims=True), line)
    sums_ref[...] = jnp.broadcast_to(line[None], sums_ref.shape)


def remainder_kernel(quarter, modes, mean_scale, sums_ref, blocks_ref, image_ref, dots_ref, out_ref):
    vectors = 2 * blocks_ref.shape[0]
    full, columns = image_ref.shape
    rows = quarter * modes
    total = jnp.sum(sums_ref[...], axis=0)
    lane = iota(total.shape, 1)

    def lane_at(index):
        return jnp.sum(jnp.where(lane == index, total, 0.0), axis=1, keepdims=True)

    def on_lanes(parts, places):
        line = jnp.zeros(total.shape, F32)
        for k in range(vectors):
            line = jnp.where(places == k, parts[k], line)
        return line

    start = vectors * vectors
    last = vectors - 1
    taken_real = [lane_at(start + 2 * k) * mean_scale for k in range(vectors)]
    taken_imag = [lane_at(start + 2 * k + 1) * mean_scale for k in range(vectors)]
    real = [lane_at(k * vectors + last) * mean_scale - taken_real[k] for k in range(vectors)]
    imag = [lane_at(last * vectors + k) * mean_scale - taken_imag[k] for k in range(last)] + [-taken_imag[last]]
    dots_ref[0:1, :] = on_lanes(real, lane)[:, :vectors]
    dots_ref[1:2, :] = on_lanes(imag, lane)[:, :vectors]
    kept_real = [-value for value in real[:last]] + [1.0 - real[last]]
    kept_imag = [-value for value in imag]
    first_index, last_index = lax.div(lane, vectors), lax.rem(lane, vectors)
    real_first, real_last = on_lanes(kept_real, first_index), on_lanes(kept_real, last_index)
    imag_first, imag_last = on_lanes(kept_imag, first_index), on_lanes(kept_imag, last_index)
    same = real_first * real_last + imag_first * imag_last
    cross = imag_last * real_first - real_last * imag_first
    often = jnp.where(first_index == last_index, 1.0, 2.0)
    spread = jnp.where(lane < start, total * often * jnp.where(first_index <= last_index, same, cross), 0.0)
    spread = jnp.sum(spread, axis=1, keepdims=True)
    both = sum(kept_real[k] * taken_real[k] + kept_imag[k] * taken_imag[k] for k in range(vectors))
    norm_square = (lane_at(start + 2 * vectors) + spread) * mean_scale - 2.0 * both
    scale = lax.rsqrt(norm_square)
    image_scale = jnp.broadcast_to(scale, (8, columns))
    reals = [jnp.broadcast_to(real[k] * scale, (8, columns)) for k in range(vectors)]
    imags = [jnp.broadcast_to(imag[k] * scale, (8, columns)) for k in range(vectors)]
    chunk = 64
    for first in range(0, full, chunk):
        here = slice(first, first + chunk)
        values = []
        for k in range(vectors):
            start = k % 2 * rows + first
            values.append(blocks_ref[k // 2, start : start + chunk, :].reshape(chunk // 8, 8, columns))
        along = image_ref[here, :].reshape(chunk // 8, 8, columns) * image_scale
        turned = jnp.zeros_like(along)
        for k in range(vectors):
            along -= reals[k] * values[k]
            turned += imags[k] * values[k]
        result = along.reshape(chunk, columns) - lane_swap(turned.reshape(chunk, columns))
        count = min(chunk, rows - first)
        height = out_ref.shape[1]
        out_ref[first // height : (first + count) // height] = result.reshape(chunk // height, height, columns)[: count // height]


def exchanged(pieces, axis):
    count = lax.axis_size(axis)
    received = [pieces[0]]
    for i in range(1, len(pieces)):
        received.append(lax.ppermute(pieces[i], axis, [(p, p ^ i) for p in range(count)]))
    return received


def neighbours(value):
    count = lax.axis_size("blk")
    up = [(i, i + 1) for i in range(count - 1)]
    down = [(j, i) for i, j in up]
    return lax.ppermute(value, "blk", up), lax.ppermute(value, "blk", down)


def shards(basis, mie_coeffs, rot_table, axial_table, pair_table, pair_count):
    vectors, quarter, modes, columns = basis.shape
    ways = lax.axis_size("pair")
    blk_ways = lax.axis_size("blk")
    tables = rot_table.shape[0]
    slots = pair_table.shape[1]
    own = quarter * ways
    part = columns // 2 // ways
    group = own * part
    size = rounded_up(modes, 128)
    rows = quarter * modes
    full = rounded_up(rows, 8)
    pairs_of_vectors = vectors // 2
    height = 4

    basis_rows = in_hbm(basis.transpose(0, 2, 1, 3).reshape(pairs_of_vectors, 2 * rows, columns))
    mie_rows = in_hbm(mie_coeffs.transpose(1, 0, 2).reshape(rows // 4, 4, columns))
    rot_rows = in_hbm(rot_table.transpose(1, 0, 2).reshape(modes * tables, modes))
    axial_rows = in_hbm(axial_table.transpose(0, 2, 1, 3))
    pair_rows = in_hbm(pair_table.transpose(2, 0, 1))

    octets = part * quarter // 16
    piece = jax.ShapeDtypeStruct((2, octets, 16, size), BF16)
    pieces = pl.pallas_call(
        functools.partial(pack_kernel, quarter, modes, ways, own),
        in_specs=[hbm(), pl.BlockSpec(memory_space=pltpu.SMEM), hbm()],
        out_specs=[whole()] * ways,
        out_shape=[piece] * ways,
        scratch_shapes=[
            pltpu.VMEM(pair_rows.shape, jnp.int32),
            pltpu.VMEM((full, columns), F32),
            pltpu.VMEM((size, columns), F32),
            pltpu.VMEM((2 * slots, slots), F32),
            pltpu.VMEM((quarter, columns, size), F32),
            pltpu.SemaphoreType.DMA((2,)),
        ],
        compiler_params=params(16),
        name="pack",
    )(pair_rows, pair_count, basis_rows)
    tall = rounded_up(rows + full, 8)
    *pieces, basis_rows, mie_rows = lax.optimization_barrier((*pieces, basis_rows, mie_rows))
    received = exchanged(pieces, "pair")
    products, blocks, mies = pl.pallas_call(
        functools.partial(gram_kernel, quarter, modes),
        in_specs=[hbm()] * 2,
        out_specs=[whole()] * 3,
        out_shape=[
            jax.ShapeDtypeStruct((vectors, vectors, 8, columns), F32),
            jax.ShapeDtypeStruct((pairs_of_vectors, tall, columns), F32),
            jax.ShapeDtypeStruct((full // height, height, columns), F32),
        ],
        scratch_shapes=[
            pltpu.SemaphoreType.DMA,
            pltpu.SemaphoreType.DMA((4, pairs_of_vectors, 2)),
        ],
        compiler_params=params(8),
        name="gram",
    )(basis_rows, mie_rows)
    *received, products, rot_rows, axial_rows = lax.optimization_barrier((*received, products, rot_rows, axial_rows))
    own_pieces = pl.pallas_call(
        join_kernel,
        in_specs=[whole()] * ways,
        out_specs=whole(),
        out_shape=jax.ShapeDtypeStruct((ways, *piece.shape), BF16),
        compiler_params=params(4),
        name="join",
    )(*received)
    below, above = neighbours(own_pieces)
    own_pieces, products, rot_rows, axial_rows = lax.optimization_barrier((own_pieces, products, rot_rows, axial_rows))
    rotations, axials, line = pl.pallas_call(
        functools.partial(tables_kernel, quarter, modes),
        in_specs=[hbm()] * 2 + [whole()] * 2,
        out_specs=[whole()] * 3,
        out_shape=[
            jax.ShapeDtypeStruct((tables, size, size), BF16),
            jax.ShapeDtypeStruct((tables, 2 * size, size), BF16),
            jax.ShapeDtypeStruct((1, 128), F32),
        ],
        scratch_shapes=[
            pltpu.VMEM((tables * size, modes), BF16),
            pltpu.VMEM(axial_rows.shape, BF16),
            pltpu.VMEM((vectors, vectors, 8, columns), F32),
            pltpu.SemaphoreType.DMA((tables + rounded_up(modes * tables, 1024) // 1024,)),
        ],
        compiler_params=params(20),
        cost_estimate=pl.CostEstimate(flops=tables * 8 * 256 * 256 * size, bytes_accessed=6 * tables * size * size * 2, transcendentals=0),
        name="tables",
    )(rot_rows, axial_rows, products, blocks)
    below, above, rotations, axials, line = lax.optimization_barrier((below, above, rotations, axials, line))

    together = tables
    field = pl.pallas_call(
        functools.partial(field_kernel, own, modes, together),
        in_specs=[whole()] * 5,
        out_specs=[whole()] * ways,
        out_shape=[jax.ShapeDtypeStruct((2, quarter, part, size), BF16)] * ways,
        scratch_shapes=[pltpu.VMEM((tables, 4 * group, size), BF16), pltpu.VMEM((2 * group, size), F32)],
        compiler_params=params(28),
        name="field",
    )(rotations, axials, below, own_pieces, above)
    field_pieces = exchanged(field, "pair")

    image, sums = pl.pallas_call(
        functools.partial(image_kernel, quarter, modes),
        in_specs=[whole()] * (ways + 3),
        out_specs=[whole()] * 2,
        out_shape=[jax.ShapeDtypeStruct((full, columns), F32), jax.ShapeDtypeStruct((ways * blk_ways, 1, 128), F32)],
        scratch_shapes=[pltpu.VMEM((full, columns), F32), pltpu.VMEM((quarter, columns, size), BF16)],
        compiler_params=params(8),
        name="image",
    )(blocks, mies, line, *field_pieces)
    sums = lax.all_to_all(sums, ("blk", "pair"), split_axis=0, concat_axis=0, tiled=True)

    mean_scale = 1.0 / (own * blk_ways * modes * columns)
    dots, next_rows = pl.pallas_call(
        functools.partial(remainder_kernel, quarter, modes, mean_scale),
        in_specs=[whole()] * 3,
        out_specs=[whole(), whole()],
        out_shape=[jax.ShapeDtypeStruct((2, vectors), F32), jax.ShapeDtypeStruct((rows // height, height, columns), F32)],
        compiler_params=params(16),
        name="remainder",
    )(sums, blocks, image)
    return dots, next_rows.reshape(modes, quarter, columns).transpose(1, 0, 2)


def solution(mesh):
    placed = (
        P(None, ("blk", "pair"), None, None),
        P(("blk", "pair"), None, None),
        P(),
        P(),
        P("blk", None, None),
        P("blk"),
    )
    return jax.shard_map(
        shards,
        mesh=mesh,
        in_specs=placed,
        out_specs=(P(), P(("blk", "pair"), None, None)),
        check_vma=False,
    )
```

```python
import functools

import jax
import jax.numpy as jnp
from jax import lax
from jax.experimental import pallas as pl
from jax.experimental.pallas import tpu as pltpu
from jax.sharding import PartitionSpec as P

MIB = 1024 * 1024
F32 = jnp.float32
BF16 = jnp.bfloat16


def params(mib):
    return pltpu.CompilerParams(vmem_limit_bytes=mib * MIB)


def hbm():
    return pl.BlockSpec(memory_space=pltpu.HBM)


def whole():
    return pl.BlockSpec(memory_space=pltpu.VMEM)


def in_hbm(value):
    return pltpu.with_memory_space_constraint(value, pltpu.HBM)


def rounded_up(value, unit):
    return (value + unit - 1) // unit * unit


def iota(shape, dim):
    return lax.broadcasted_iota(jnp.int32, shape, dim)


def dot_nn(left, right):
    return lax.dot_general(left, right, (((1,), (0,)), ((), ())), preferred_element_type=F32)


def dot_nt(left, right):
    return lax.dot_general(left, right, (((1,), (1,)), ((), ())), preferred_element_type=F32)


def pack_kernel(quarter, modes, ways, own, list_ref, count_ref, basis_ref, *rest):
    outs, (pair_rows_ref, lines_ref, pad_ref, codes_ref, turned_ref, sems) = rest[:ways], rest[ways:]
    full, columns = lines_ref.shape
    rows = quarter * modes
    part = columns // 2 // ways
    copy = pltpu.make_async_copy(basis_ref.at[basis_ref.shape[0] - 1, pl.ds(2 * rows - full, full)], lines_ref, sems.at[0])
    copy.start()
    list_copy = pltpu.make_async_copy(list_ref, pair_rows_ref, sems.at[1])
    list_copy.start()
    pad_ref[...] = jnp.zeros_like(pad_ref)
    list_copy.wait()
    slots = pair_rows_ref.shape[2]
    live = iota((1, slots), 1) < count_ref[0]
    marks = jnp.where(live, own * (pair_rows_ref[2] + 1) + pair_rows_ref[0], 0)
    line = iota((slots, slots), 0)
    stacked = jnp.where(line == 0, marks, jnp.where(line == 1, pair_rows_ref[1], 0))
    turned = jnp.transpose(stacked.astype(F32))
    codes_ref[0:slots, :] = turned
    codes_ref[slots : 2 * slots, :] = pltpu.roll(turned, slots - 1, axis=1)
    share = 2 * quarter * part
    mine = codes_ref[pl.ds(pl.multiple_of(lax.axis_index("pair") * share, share), share), :][:, 0:1]
    copy.wait()
    for j in range(quarter):
        pad_ref[0:modes, :] = lines_ref[pl.ds(full - rows + j, modes, quarter), :]
        turned_ref[j] = jnp.transpose(pad_ref[...])
    _, octets, height, size = outs[0].shape
    each = height // quarter
    for i, out_ref in enumerate(outs):
        place = (lax.axis_index("pair") ^ i) * part
        for c in range(2):
            for o in range(octets):
                first = (c * octets + o) * height
                here = pl.ds(pl.multiple_of(c * (columns // 2) + place + o * each, each), each)
                piece = jnp.concatenate([turned_ref[j, here, :] for j in range(quarter)], axis=0)
                piece = jnp.where(iota(piece.shape, 1) == modes, mine[first : first + height], piece)
                out_ref[c, o] = piece.astype(BF16)


def join_kernel(*refs):
    for i, ref in enumerate(refs[:-2]):
        for c, out_ref in enumerate(refs[-2:]):
            out_ref[lax.axis_index("pair") ^ i] = ref[c]


def rotations_kernel(quarter, modes, rot_ref, products_ref, blocks_ref, out_ref, line_ref, rots_ref, totals_ref, sems):
    tables, size, _ = out_ref.shape
    listed = rot_ref.shape[0]
    chunk = 256
    copies = []
    for i, first in enumerate(range(0, listed, 4 * chunk)):
        here = pl.ds(first, min(4 * chunk, listed - first))
        copies.append(pltpu.make_async_copy(rot_ref.at[here], rots_ref.at[here], sems.at[i]))
        copies[-1].start()
    out_ref[:, :, size - 128 : size] = jnp.zeros((tables, size, 128), BF16)
    rots_ref[listed:, :] = jnp.zeros((rots_ref.shape[0] - listed, modes), BF16)
    gram_end(quarter * modes, products_ref, blocks_ref, line_ref, totals_ref)
    out_row, in_row = iota((chunk, chunk), 0), iota((chunk, chunk), 1)
    share = chunk // tables
    entries = (in_row == tables * lax.rem(out_row, share) + lax.div(out_row, share)).astype(F32).astype(BF16)
    for i, copy in enumerate(copies):
        copy.wait()
        chunks = range(4 * i, min(4 * (i + 1), rots_ref.shape[0] // chunk))
        rows = [rots_ref[q * chunk : (q + 1) * chunk, :] for q in chunks]
        results = [dot_nn(entries, value).astype(BF16) for value in rows]
        for q, result in zip(chunks, results):
            for g in range(tables):
                out_ref[g, q * share : (q + 1) * share, 0:modes] = result[g * share : (g + 1) * share]


def axials_kernel(axial_ref, out_ref, axials_ref, sems):
    tables, double, size = out_ref.shape
    modes = axial_ref.shape[1]

    def fetch(g):
        return pltpu.make_async_copy(axial_ref.at[g], axials_ref.at[g], sems.at[g])

    for g in range(tables):
        fetch(g).start()
    out_ref[:, :, size - 128 : size] = jnp.zeros((tables, double, 128), BF16)
    chunk = 256
    out_row, in_row = iota((chunk, chunk), 0), iota((chunk, chunk), 1)
    each = chunk // 2
    halves = (in_row == 2 * lax.rem(out_row, each) + lax.div(out_row, each)).astype(F32).astype(BF16)
    together = 2 if tables % 2 == 0 else 1

    def split(step, carry):
        members = [step * together + i for i in range(together)]
        for g in members:
            fetch(g).wait()
        places = [(g, first) for g in members for first in range(0, modes, each)]
        results = []
        for g, first in places:
            count = min(each, modes - first)
            rows = axials_ref[g, first : first + count].reshape(2 * count, modes)
            results.append(dot_nn(halves[:, : 2 * count], rows).astype(BF16))
        for (g, first), result in zip(places, results):
            for c in range(2):
                out_ref[g, c * size + first : c * size + first + each, 0:modes] = result[c * each : (c + 1) * each]
        return carry

    lax.fori_loop(0, tables // together, split, 0)


def swapped(value):
    half = value.shape[0] // 2
    return jnp.concatenate([-value[half:], value[:half]], axis=0)


def pair_counts(own, tables, lane, refs):
    ways, octets, height, size = refs[0][0].shape
    group = ways * octets * height
    wanted = iota((tables * own, group), 0) + own

    def one_hot(hit):
        return jnp.where(hit, 1.0, 0.0).astype(BF16)

    even = lax.rem(lax.axis_index("blk"), 2) == 0
    windows = (jnp.where(even, 2, 0), 1, jnp.where(even, 0, 2))
    forward, backward = None, []
    for order, (window, halves) in enumerate(zip(windows, refs)):
        values = jnp.stack([ref[:, :, :, size - 128 : size] for ref in halves], axis=1).reshape(2 * group, 128).astype(F32)
        marks_column, sources_column = (values[h * group : (h + 1) * group, lane : lane + 1].astype(jnp.int32) for h in range(2))
        marks, sources = (jnp.transpose(values[h * group : (h + 1) * group])[lane : lane + 1].astype(jnp.int32) for h in range(2))
        if order == 1:
            turned = (2 - lax.div(sources_column, own)) * own + lax.rem(sources_column, own)
            sources_column = jnp.where(even, turned, sources_column)
            forward = dot_nn(one_hot(marks == wanted), one_hot(sources_column == iota((group, 3 * own), 1)))
        block = sources - (2 - window) * own
        inside = (block >= 0) & (block < own) & (marks >= own)
        hits = one_hot(jnp.where(inside, lax.div(marks, own) * own + block, -1) == wanted)
        place = lax.rem(marks_column, own) + order * own
        backward.append(dot_nn(hits, one_hot(place == iota((group, 3 * own), 1))))
    return jnp.concatenate([forward, sum(backward)], axis=0).astype(BF16)


def folded(value):
    return jnp.sum(value.reshape(value.shape[0] // 8, 8, value.shape[1]), axis=0)


def field_kernel(
    own, modes, together, rot_ref, axial_ref, near0, near1, own0, own1, far0, far1, *rest
):
    outs, (sums_ref, total_ref) = rest[:-2], rest[-2:]
    tables, _, size = rot_ref.shape
    refs = ((near0, near1), (own0, own1), (far0, far1))
    ways, octets, height, _ = own0.shape
    quarter = own // ways
    each = height // quarter
    part = octets * each
    group = own * part
    counts = pair_counts(own, tables, modes % 128, refs)
    spread = jnp.where(iota((3 * own, 3 * own * each), 0) == lax.div(iota((3 * own, 3 * own * each), 1), each), 1.0, 0.0)
    counts = dot_nn(counts, spread.astype(BF16))
    sphere = lax.rem(iota(counts.shape, 1), each)
    chosen = jnp.concatenate([jnp.where(sphere == i, counts, 0.0).astype(BF16) for i in range(each)], axis=0)
    kinds = 2 * tables * own
    for c in range(2):
        for o in range(octets):
            blocks = jnp.concatenate([halves[c][:, o].reshape(ways * height, size) for halves in refs], axis=0)
            for i in range(0, each, 2):
                results = dot_nn(chosen[i * kinds : (i + 2) * kinds], blocks)
                for kind in range(2 * tables):
                    direction, g = kind // tables, kind % tables
                    rows = [results[start + kind * own : start + (kind + 1) * own] for start in (0, kinds)]
                    place = (direction * 2 + c) * group + (o * each + i) * own
                    sums_ref[g, place : place + 2 * own, :] = jnp.concatenate(rows, axis=0).astype(BF16)
    total_ref[...] = jnp.zeros_like(total_ref)

    def body(step, carry):
        entries = [step * together + i for i in range(together)]
        turned = [dot_nt(sums_ref[g], rot_ref[g]).astype(BF16) for g in entries]
        moved = []
        for g, both in zip(entries, turned):
            forward, backward = both[: 2 * group], both[2 * group :]
            result = dot_nt(forward, axial_ref[g, :size]) + dot_nt(swapped(forward), axial_ref[g, size:])
            result += dot_nn(jnp.concatenate([backward, swapped(backward)], axis=1), axial_ref[g])
            moved.append(result.astype(BF16))
        total_ref[...] += sum(dot_nn(value, rot_ref[g]) for g, value in zip(entries, moved))
        return carry

    if together == tables:
        body(0, 0)
    else:
        lax.fori_loop(0, tables // together, body, 0)
    row, source = iota((2 * group, 2 * group), 0), iota((2 * group, 2 * group), 1)
    sphere, c = lax.rem(row, part), lax.rem(lax.div(row, quarter * part), 2)
    owner = lax.div(row, 2 * quarter * part) ^ lax.axis_index("pair")
    block = owner * quarter + lax.rem(lax.div(row, part), quarter)
    order = jnp.where(source == c * group + sphere * own + block, 1.0, 0.0).astype(BF16)
    result = dot_nn(order, total_ref[...].astype(BF16)).astype(BF16)
    share = 2 * quarter * part
    for i, out_ref in enumerate(outs):
        out_ref[...] = result[i * share : (i + 1) * share].reshape(out_ref.shape)


def lane_swap(value):
    half = value.shape[1] // 2
    rolled = pltpu.roll(value, half, axis=1)
    return jnp.where(iota(value.shape, 1) < half, -rolled, rolled)


def add_products(blocks_ref, products_ref, rows, first, count):
    vectors = products_ref.shape[0]
    values = []
    for k in range(vectors):
        start = k % 2 * rows + first
        value = blocks_ref[k // 2, start : start + count, :]
        if k % 2 == 0 and first + count > rows:
            value = jnp.where(iota(value.shape, 0) < rows - first, value, 0.0)
        values.append(value)
    for l in range(vectors):
        other = pltpu.roll(values[l], values[l].shape[1] // 2, axis=1)
        for k in range(l + 1):
            products_ref[k, l] += folded(values[k] * values[l])
            if k < l:
                products_ref[l, k] += folded(values[k] * other)


def products_line(products_ref):
    vectors, _, _, columns = products_ref.shape
    pairs = vectors * vectors
    totals = jnp.sum(products_ref[...].reshape(pairs, 8, columns), axis=1)
    pair = iota(totals.shape, 0)
    signed = (lax.div(pair, vectors) > lax.rem(pair, vectors)) & (iota(totals.shape, 1) >= columns // 2)
    totals = jnp.sum(jnp.where(signed, -totals, totals), axis=1, keepdims=True)
    row, lane = iota((vectors, 128), 0), iota((vectors, 128), 1)
    line = jnp.zeros((1, 128), F32)
    for k in range(vectors):
        column = totals[k * vectors : (k + 1) * vectors]
        line += jnp.sum(jnp.where(row + k * vectors == lane, column, 0.0), axis=0, keepdims=True)
    return line


def gram_kernel(quarter, modes, basis_ref, mie_ref, products_ref, blocks_ref, mies_ref, mie_sem, sems):
    blocks, _, columns = basis_ref.shape
    rows = quarter * modes
    parts, chunk = 4, 32
    tile_end = rows // 8 * 8
    step = rounded_up(rows, 8 * parts) // parts
    even = [0] + [step * q for q in range(1, parts)] + [tile_end]
    odd = [tile_end] + [rounded_up(rows, 8) + step * q for q in range(1, parts)] + [2 * rows]
    copies = []
    for q in range(parts):
        for i in range(blocks):
            for side, cuts in enumerate((even, odd)):
                here = pl.ds(cuts[q], cuts[q + 1] - cuts[q])
                copies.append(pltpu.make_async_copy(basis_ref.at[i, here], blocks_ref.at[i, here], sems.at[q, i, side]))
    for copy in copies:
        copy.start()
    mie_rows = mie_ref.shape[0]
    mie_copy = pltpu.make_async_copy(mie_ref, mies_ref.at[pl.ds(0, mie_rows)], mie_sem)
    mie_copy.start()
    mies_ref[mie_rows:] = jnp.zeros((mies_ref.shape[0] - mie_rows,) + mies_ref.shape[1:], F32)
    products_ref[...] = jnp.zeros_like(products_ref)
    for i in range(blocks):
        blocks_ref[i, 2 * rows :, :] = jnp.zeros((blocks_ref.shape[1] - 2 * rows, columns), F32)
    for q in range(parts):
        for copy in copies[2 * blocks * q : 2 * blocks * (q + 1)]:
            copy.wait()
        if q < parts - 1:
            for first in range(step * q, step * (q + 1), chunk):
                add_products(blocks_ref, products_ref, rows, first, chunk)
    mie_copy.wait()


def gram_end(rows, products_ref, blocks_ref, line_ref, totals_ref):
    parts, chunk = 4, 32
    totals_ref[...] = products_ref[...]
    for first in range(rounded_up(rows, 8 * parts) // parts * (parts - 1), rows, chunk):
        add_products(blocks_ref, totals_ref, rows, first, chunk)
    line_ref[...] = products_line(totals_ref)


def image_kernel(quarter, modes, blocks_ref, mie_ref, gram_ref, *rest):
    pieces, (image_ref, sums_ref, lines_ref, whole_ref) = rest[:-4], rest[-4:]
    vectors = 2 * blocks_ref.shape[0]
    full, columns = image_ref.shape
    rows = quarter * modes
    part = pieces[0].shape[2]
    for i, piece_ref in enumerate(pieces):
        place = pl.multiple_of((lax.axis_index("pair") ^ i) * part, part)
        for j in range(quarter):
            for c in range(2):
                whole_ref[j, pl.ds(c * (columns // 2) + place, part), :] = piece_ref[c, j]
    lines_ref[rows:full, :] = jnp.zeros((full - rows, columns), F32)
    for j in range(quarter):
        lines_ref[pl.ds(j, modes, quarter), :] = jnp.transpose(whole_ref[j].astype(F32))[:modes]
    half = columns // 2
    chunk = 64
    totals = [jnp.zeros((8, columns), F32) for _ in range(2 * vectors + 1)]
    for first in range(0, full, chunk):
        here = slice(first, first + chunk)
        field = lines_ref[here, :]
        count = min(chunk, rows - first)
        height = mie_ref.shape[1]
        mie = mie_ref[first // height : (first + count) // height].reshape(count, columns)
        if count < chunk:
            mie = jnp.concatenate([mie, jnp.zeros((chunk - count, columns), F32)], axis=0)
        left = iota(mie.shape, 1) < half
        other = pltpu.roll(mie, half, axis=1)
        product = jnp.where(left, mie, other) * field + jnp.where(left, -other, mie) * pltpu.roll(field, half, axis=1)
        last = (vectors - 1) % 2 * rows + first
        image = blocks_ref[(vectors - 1) // 2, last : last + chunk, :] - product
        image_ref[here, :] = image
        turned = pltpu.roll(product, half, axis=1)
        for k in range(vectors):
            start = k % 2 * rows + first
            values = blocks_ref[k // 2, start : start + chunk, :]
            totals[2 * k] += folded(values * product)
            totals[2 * k + 1] += folded(values * turned)
        totals[2 * vectors] += folded(product * product)
    lane = iota(gram_ref.shape, 1)
    line = gram_ref[...]
    left = iota((8, columns), 1) < half
    for index, total in enumerate(totals):
        if index % 2 and index < 2 * vectors:
            total = jnp.where(left, total, -total)
        line = jnp.where(lane == vectors * vectors + index, jnp.sum(total, axis=(0, 1), keepdims=True), line)
    sums_ref[...] = jnp.broadcast_to(line[None], sums_ref.shape)


def remainder_kernel(quarter, modes, mean_scale, sums_ref, blocks_ref, image_ref, dots_ref, out_ref):
    vectors = 2 * blocks_ref.shape[0]
    full, columns = image_ref.shape
    rows = quarter * modes
    total = jnp.sum(sums_ref[...], axis=0)
    lane = iota(total.shape, 1)

    def lane_at(index):
        return jnp.sum(jnp.where(lane == index, total, 0.0), axis=1, keepdims=True)

    def on_lanes(parts, places):
        line = jnp.zeros(total.shape, F32)
        for k in range(vectors):
            line = jnp.where(places == k, parts[k], line)
        return line

    start = vectors * vectors
    last = vectors - 1
    taken_real = [lane_at(start + 2 * k) * mean_scale for k in range(vectors)]
    taken_imag = [lane_at(start + 2 * k + 1) * mean_scale for k in range(vectors)]
    real = [lane_at(k * vectors + last) * mean_scale - taken_real[k] for k in range(vectors)]
    imag = [lane_at(last * vectors + k) * mean_scale - taken_imag[k] for k in range(last)] + [-taken_imag[last]]
    dots_ref[0:1, :] = on_lanes(real, lane)[:, :vectors]
    dots_ref[1:2, :] = on_lanes(imag, lane)[:, :vectors]
    kept_real = [-value for value in real[:last]] + [1.0 - real[last]]
    kept_imag = [-value for value in imag]
    first_index, last_index = lax.div(lane, vectors), lax.rem(lane, vectors)
    real_first, real_last = on_lanes(kept_real, first_index), on_lanes(kept_real, last_index)
    imag_first, imag_last = on_lanes(kept_imag, first_index), on_lanes(kept_imag, last_index)
    same = real_first * real_last + imag_first * imag_last
    cross = imag_last * real_first - real_last * imag_first
    often = jnp.where(first_index == last_index, 1.0, 2.0)
    spread = jnp.where(lane < start, total * often * jnp.where(first_index <= last_index, same, cross), 0.0)
    spread = jnp.sum(spread, axis=1, keepdims=True)
    both = sum(kept_real[k] * taken_real[k] + kept_imag[k] * taken_imag[k] for k in range(vectors))
    norm_square = (lane_at(start + 2 * vectors) + spread) * mean_scale - 2.0 * both
    scale = lax.rsqrt(norm_square)
    image_scale = jnp.broadcast_to(scale, (8, columns))
    reals = [jnp.broadcast_to(real[k] * scale, (8, columns)) for k in range(vectors)]
    imags = [jnp.broadcast_to(imag[k] * scale, (8, columns)) for k in range(vectors)]
    chunk = 64
    for first in range(0, full, chunk):
        here = slice(first, first + chunk)
        values = []
        for k in range(vectors):
            start = k % 2 * rows + first
            values.append(blocks_ref[k // 2, start : start + chunk, :].reshape(chunk // 8, 8, columns))
        along = image_ref[here, :].reshape(chunk // 8, 8, columns) * image_scale
        turned = jnp.zeros_like(along)
        for k in range(vectors):
            along -= reals[k] * values[k]
            turned += imags[k] * values[k]
        result = along.reshape(chunk, columns) - lane_swap(turned.reshape(chunk, columns))
        count = min(chunk, rows - first)
        height = out_ref.shape[1]
        out_ref[first // height : (first + count) // height] = result.reshape(chunk // height, height, columns)[: count // height]


def exchanged(pieces, axis):
    count = lax.axis_size(axis)
    received = [pieces[0]]
    for i in range(1, len(pieces)):
        received.append(lax.ppermute(pieces[i], axis, [(p, p ^ i) for p in range(count)]))
    return received


def from_near(value):
    count = lax.axis_size("blk")
    return lax.ppermute(value, "blk", [(i, i ^ 1) for i in range(count) if i ^ 1 < count])


def from_far(value):
    count = lax.axis_size("blk")
    steps = [(i, i - 2 if i % 2 else i + 2) for i in range(count)]
    return lax.ppermute(value, "blk", [(i, j) for i, j in steps if 0 <= j < count])


def shards(basis, mie_coeffs, rot_table, axial_table, pair_table, pair_count):
    vectors, quarter, modes, columns = basis.shape
    ways = lax.axis_size("pair")
    blk_ways = lax.axis_size("blk")
    tables = rot_table.shape[0]
    slots = pair_table.shape[1]
    own = quarter * ways
    part = columns // 2 // ways
    group = own * part
    size = rounded_up(modes, 128)
    rows = quarter * modes
    full = rounded_up(rows, 8)
    pairs_of_vectors = vectors // 2
    height = 4

    basis_rows = in_hbm(basis.transpose(0, 2, 1, 3).reshape(pairs_of_vectors, 2 * rows, columns))
    mie_rows = in_hbm(mie_coeffs.transpose(1, 0, 2).reshape(rows // 4, 4, columns))
    rot_rows = in_hbm(rot_table.transpose(1, 0, 2).reshape(modes * tables, modes))
    axial_rows = in_hbm(axial_table.transpose(0, 2, 1, 3))
    pair_rows = in_hbm(pair_table.transpose(2, 0, 1))

    octets = part * quarter // 16
    piece = jax.ShapeDtypeStruct((2, octets, 16, size), BF16)
    pieces = pl.pallas_call(
        functools.partial(pack_kernel, quarter, modes, ways, own),
        in_specs=[hbm(), pl.BlockSpec(memory_space=pltpu.SMEM), hbm()],
        out_specs=[whole()] * ways,
        out_shape=[piece] * ways,
        scratch_shapes=[
            pltpu.VMEM(pair_rows.shape, jnp.int32),
            pltpu.VMEM((full, columns), F32),
            pltpu.VMEM((size, columns), F32),
            pltpu.VMEM((2 * slots, slots), F32),
            pltpu.VMEM((quarter, columns, size), F32),
            pltpu.SemaphoreType.DMA((2,)),
        ],
        compiler_params=params(16),
        name="pack",
    )(pair_rows, pair_count, basis_rows)
    tall = rounded_up(rows + full, 8)
    *pieces, basis_rows, mie_rows = lax.optimization_barrier((*pieces, basis_rows, mie_rows))
    received = exchanged(pieces, "pair")
    products, blocks, mies = pl.pallas_call(
        functools.partial(gram_kernel, quarter, modes),
        in_specs=[hbm()] * 2,
        out_specs=[whole()] * 3,
        out_shape=[
            jax.ShapeDtypeStruct((vectors, vectors, 8, columns), F32),
            jax.ShapeDtypeStruct((pairs_of_vectors, tall, columns), F32),
            jax.ShapeDtypeStruct((full // height, height, columns), F32),
        ],
        scratch_shapes=[
            pltpu.SemaphoreType.DMA,
            pltpu.SemaphoreType.DMA((4, pairs_of_vectors, 2)),
        ],
        compiler_params=params(8),
        name="gram",
    )(basis_rows, mie_rows)
    *received, products, rot_rows, axial_rows = lax.optimization_barrier((*received, products, rot_rows, axial_rows))
    half = jax.ShapeDtypeStruct((ways, *piece.shape[1:]), BF16)
    own0, own1 = pl.pallas_call(
        join_kernel,
        in_specs=[whole()] * ways,
        out_specs=[whole()] * 2,
        out_shape=[half] * 2,
        compiler_params=params(4),
        name="join",
    )(*received)
    near0, near1 = from_near(own0), from_near(own1)
    own0, own1, products, rot_rows = lax.optimization_barrier((own0, own1, products, rot_rows))
    rotations, line = pl.pallas_call(
        functools.partial(rotations_kernel, quarter, modes),
        in_specs=[hbm()] + [whole()] * 2,
        out_specs=[whole()] * 2,
        out_shape=[jax.ShapeDtypeStruct((tables, size, size), BF16), jax.ShapeDtypeStruct((1, 128), F32)],
        scratch_shapes=[
            pltpu.VMEM((tables * size, modes), BF16),
            pltpu.VMEM((vectors, vectors, 8, columns), F32),
            pltpu.SemaphoreType.DMA((rounded_up(modes * tables, 1024) // 1024,)),
        ],
        compiler_params=params(12),
        name="rotations",
    )(rot_rows, products, blocks)
    near0, rotations, line = lax.optimization_barrier((near0, rotations, line))
    far0 = from_far(near0)
    near1, rotations, axial_rows = lax.optimization_barrier((near1, rotations, axial_rows))
    far1 = from_far(near1)
    axials = pl.pallas_call(
        axials_kernel,
        in_specs=[hbm()],
        out_specs=whole(),
        out_shape=jax.ShapeDtypeStruct((tables, 2 * size, size), BF16),
        scratch_shapes=[pltpu.VMEM(axial_rows.shape, BF16), pltpu.SemaphoreType.DMA((tables,))],
        compiler_params=params(16),
        cost_estimate=pl.CostEstimate(flops=tables * 8 * 256 * 256 * size, bytes_accessed=4 * tables * size * size * 2, transcendentals=0),
        name="axials",
    )(axial_rows)
    far0, far1, axials = lax.optimization_barrier((far0, far1, axials))

    together = tables
    field = pl.pallas_call(
        functools.partial(field_kernel, own, modes, together),
        in_specs=[whole()] * 8,
        out_specs=[whole()] * ways,
        out_shape=[jax.ShapeDtypeStruct((2, quarter, part, size), BF16)] * ways,
        scratch_shapes=[pltpu.VMEM((tables, 4 * group, size), BF16), pltpu.VMEM((2 * group, size), F32)],
        compiler_params=params(28),
        name="field",
    )(rotations, axials, near0, near1, own0, own1, far0, far1)
    field_pieces = exchanged(field, "pair")

    image, sums = pl.pallas_call(
        functools.partial(image_kernel, quarter, modes),
        in_specs=[whole()] * (ways + 3),
        out_specs=[whole()] * 2,
        out_shape=[jax.ShapeDtypeStruct((full, columns), F32), jax.ShapeDtypeStruct((ways * blk_ways, 1, 128), F32)],
        scratch_shapes=[pltpu.VMEM((full, columns), F32), pltpu.VMEM((quarter, columns, size), BF16)],
        compiler_params=params(8),
        name="image",
    )(blocks, mies, line, *field_pieces)
    sums = lax.all_to_all(sums, ("blk", "pair"), split_axis=0, concat_axis=0, tiled=True)

    mean_scale = 1.0 / (own * blk_ways * modes * columns)
    dots, next_rows = pl.pallas_call(
        functools.partial(remainder_kernel, quarter, modes, mean_scale),
        in_specs=[whole()] * 3,
        out_specs=[whole(), whole()],
        out_shape=[jax.ShapeDtypeStruct((2, vectors), F32), jax.ShapeDtypeStruct((rows // height, height, columns), F32)],
        compiler_params=params(16),
        name="remainder",
    )(sums, blocks, image)
    return dots, next_rows.reshape(modes, quarter, columns).transpose(1, 0, 2)


def solution(mesh):
    placed = (
        P(None, ("blk", "pair"), None, None),
        P(("blk", "pair"), None, None),
        P(),
        P(),
        P("blk", None, None),
        P("blk"),
    )
    return jax.shard_map(
        shards,
        mesh=mesh,
        in_specs=placed,
        out_specs=(P(), P(("blk", "pair"), None, None)),
        check_vma=False,
    )
```

```python
import functools

import jax
import jax.numpy as jnp
from jax import lax
from jax.experimental import pallas as pl
from jax.experimental.pallas import tpu as pltpu
from jax.sharding import PartitionSpec as P

MIB = 1024 * 1024
F32 = jnp.float32
BF16 = jnp.bfloat16


def params(mib):
    return pltpu.CompilerParams(vmem_limit_bytes=mib * MIB)


def hbm():
    return pl.BlockSpec(memory_space=pltpu.HBM)


def whole():
    return pl.BlockSpec(memory_space=pltpu.VMEM)


def in_hbm(value):
    return pltpu.with_memory_space_constraint(value, pltpu.HBM)


def rounded_up(value, unit):
    return (value + unit - 1) // unit * unit


def iota(shape, dim):
    return lax.broadcasted_iota(jnp.int32, shape, dim)


def dot_nn(left, right):
    return lax.dot_general(left, right, (((1,), (0,)), ((), ())), preferred_element_type=F32)


def dot_nt(left, right):
    return lax.dot_general(left, right, (((1,), (1,)), ((), ())), preferred_element_type=F32)


def pack_kernel(quarter, modes, ways, own, list_ref, count_ref, basis_ref, *rest):
    outs, (pair_rows_ref, lines_ref, pad_ref, codes_ref, turned_ref, sems) = rest[:ways], rest[ways:]
    full, columns = lines_ref.shape
    rows = quarter * modes
    part = columns // 2 // ways
    copy = pltpu.make_async_copy(basis_ref.at[basis_ref.shape[0] - 1, pl.ds(2 * rows - full, full)], lines_ref, sems.at[0])
    copy.start()
    list_copy = pltpu.make_async_copy(list_ref, pair_rows_ref, sems.at[1])
    list_copy.start()
    pad_ref[...] = jnp.zeros_like(pad_ref)
    list_copy.wait()
    slots = pair_rows_ref.shape[2]
    live = iota((1, slots), 1) < count_ref[0]
    marks = jnp.where(live, own * (pair_rows_ref[2] + 1) + pair_rows_ref[0], 0)
    line = iota((slots, slots), 0)
    stacked = jnp.where(line == 0, marks, jnp.where(line == 1, pair_rows_ref[1], 0))
    turned = jnp.transpose(stacked.astype(F32))
    codes_ref[0:slots, :] = turned
    codes_ref[slots : 2 * slots, :] = pltpu.roll(turned, slots - 1, axis=1)
    share = 2 * quarter * part
    mine = codes_ref[pl.ds(pl.multiple_of(lax.axis_index("pair") * share, share), share), :][:, 0:1]
    copy.wait()
    for j in range(quarter):
        pad_ref[0:modes, :] = lines_ref[pl.ds(full - rows + j, modes, quarter), :]
        turned_ref[j] = jnp.transpose(pad_ref[...])
    _, octets, height, size = outs[0].shape
    each = height // quarter
    for i, out_ref in enumerate(outs):
        place = (lax.axis_index("pair") ^ i) * part
        for c in range(2):
            for o in range(octets):
                first = (c * octets + o) * height
                here = pl.ds(pl.multiple_of(c * (columns // 2) + place + o * each, each), each)
                piece = jnp.concatenate([turned_ref[j, here, :] for j in range(quarter)], axis=0)
                piece = jnp.where(iota(piece.shape, 1) == modes, mine[first : first + height], piece)
                out_ref[c, o] = piece.astype(BF16)


def join_kernel(*refs):
    out_ref = refs[-1]
    for i, ref in enumerate(refs[:-1]):
        out_ref[lax.axis_index("pair") ^ i] = ref[...]


def tables_kernel(
    quarter, modes, rot_ref, axial_ref, products_ref, blocks_ref, rot_out_ref, axial_out_ref, line_ref, rots_ref, axials_ref, totals_ref, sems,
):
    tables, size, _ = rot_out_ref.shape
    listed = rot_ref.shape[0]
    chunk = 256
    rot_copies = []
    for i, first in enumerate(range(0, listed, 4 * chunk)):
        here = pl.ds(first, min(4 * chunk, listed - first))
        rot_copies.append(pltpu.make_async_copy(rot_ref.at[here], rots_ref.at[here], sems.at[tables + i]))
        rot_copies[-1].start()

    def fetch(g):
        return pltpu.make_async_copy(axial_ref.at[g], axials_ref.at[g], sems.at[g])

    for g in range(tables):
        fetch(g).start()
    for ref in (rot_out_ref, axial_out_ref):
        ref[:, :, size - 128 : size] = jnp.zeros((tables, ref.shape[1], 128), BF16)
    rots_ref[listed:, :] = jnp.zeros((rots_ref.shape[0] - listed, modes), BF16)
    gram_end(quarter * modes, products_ref, blocks_ref, line_ref, totals_ref)

    out_row, in_row = iota((chunk, chunk), 0), iota((chunk, chunk), 1)
    share = chunk // tables
    entries = (in_row == tables * lax.rem(out_row, share) + lax.div(out_row, share)).astype(F32).astype(BF16)
    for i, copy in enumerate(rot_copies):
        copy.wait()
        chunks = range(4 * i, min(4 * (i + 1), rots_ref.shape[0] // chunk))
        rows = [rots_ref[q * chunk : (q + 1) * chunk, :] for q in chunks]
        results = [dot_nn(entries, value).astype(BF16) for value in rows]
        for q, result in zip(chunks, results):
            for g in range(tables):
                rot_out_ref[g, q * share : (q + 1) * share, 0:modes] = result[g * share : (g + 1) * share]

    each = chunk // 2
    halves = (in_row == 2 * lax.rem(out_row, each) + lax.div(out_row, each)).astype(F32).astype(BF16)
    together = 2 if tables % 2 == 0 else 1

    def split(step, carry):
        members = [step * together + i for i in range(together)]
        for g in members:
            fetch(g).wait()
        places = [(g, first) for g in members for first in range(0, modes, each)]
        results = []
        for g, first in places:
            count = min(each, modes - first)
            rows = axials_ref[g, first : first + count].reshape(2 * count, modes)
            results.append(dot_nn(halves[:, : 2 * count], rows).astype(BF16))
        for (g, first), result in zip(places, results):
            for c in range(2):
                axial_out_ref[g, c * size + first : c * size + first + each, 0:modes] = result[c * each : (c + 1) * each]
        return carry

    lax.fori_loop(0, tables // together, split, 0)


def swapped(value):
    half = value.shape[0] // 2
    return jnp.concatenate([-value[half:], value[:half]], axis=0)


def pair_counts(own, tables, lane, refs):
    ways, parts, octets, height, size = refs[0].shape
    group = ways * octets * height
    wanted = iota((tables * own, group), 0) + own

    def one_hot(hit):
        return jnp.where(hit, 1.0, 0.0).astype(BF16)

    forward, backward = None, []
    for window, ref in enumerate(refs):
        values = ref[:, :, :, :, size - 128 : size].reshape(2 * group, 128).astype(F32)
        marks_column, sources_column = (values[h * group : (h + 1) * group, lane : lane + 1].astype(jnp.int32) for h in range(2))
        marks, sources = (jnp.transpose(values[h * group : (h + 1) * group])[lane : lane + 1].astype(jnp.int32) for h in range(2))
        if window == 1:
            forward = dot_nn(one_hot(marks == wanted), one_hot(sources_column == iota((group, 3 * own), 1)))
        block = sources - (2 - window) * own
        inside = (block >= 0) & (block < own) & (marks >= own)
        hits = one_hot(jnp.where(inside, lax.div(marks, own) * own + block, -1) == wanted)
        place = lax.rem(marks_column, own) + window * own
        backward.append(dot_nn(hits, one_hot(place == iota((group, 3 * own), 1))))
    return jnp.concatenate([forward, sum(backward)], axis=0).astype(BF16)


def folded(value):
    return jnp.sum(value.reshape(value.shape[0] // 8, 8, value.shape[1]), axis=0)


def field_kernel(
    own, modes, together, rot_ref, axial_ref, below_ref, own_ref, above_ref, *rest
):
    outs, (sums_ref, total_ref) = rest[:-2], rest[-2:]
    tables, _, size = rot_ref.shape
    refs = (below_ref, own_ref, above_ref)
    ways, _, octets, height, _ = own_ref.shape
    quarter = own // ways
    each = height // quarter
    part = octets * each
    group = own * part
    counts = pair_counts(own, tables, modes % 128, refs)
    spread = jnp.where(iota((3 * own, 3 * own * each), 0) == lax.div(iota((3 * own, 3 * own * each), 1), each), 1.0, 0.0)
    counts = dot_nn(counts, spread.astype(BF16))
    sphere = lax.rem(iota(counts.shape, 1), each)
    chosen = jnp.concatenate([jnp.where(sphere == i, counts, 0.0).astype(BF16) for i in range(each)], axis=0)
    kinds = 2 * tables * own
    for c in range(2):
        for o in range(octets):
            blocks = jnp.concatenate([ref[:, c, o].reshape(ways * height, size) for ref in refs], axis=0)
            for i in range(0, each, 2):
                results = dot_nn(chosen[i * kinds : (i + 2) * kinds], blocks)
                for kind in range(2 * tables):
                    direction, g = kind // tables, kind % tables
                    rows = [results[start + kind * own : start + (kind + 1) * own] for start in (0, kinds)]
                    place = (direction * 2 + c) * group + (o * each + i) * own
                    sums_ref[g, place : place + 2 * own, :] = jnp.concatenate(rows, axis=0).astype(BF16)
    total_ref[...] = jnp.zeros_like(total_ref)

    def body(step, carry):
        entries = [step * together + i for i in range(together)]
        turned = [dot_nt(sums_ref[g], rot_ref[g]).astype(BF16) for g in entries]
        moved = []
        for g, both in zip(entries, turned):
            forward, backward = both[: 2 * group], both[2 * group :]
            result = dot_nt(forward, axial_ref[g, :size]) + dot_nt(swapped(forward), axial_ref[g, size:])
            result += dot_nn(jnp.concatenate([backward, swapped(backward)], axis=1), axial_ref[g])
            moved.append(result.astype(BF16))
        total_ref[...] += sum(dot_nn(value, rot_ref[g]) for g, value in zip(entries, moved))
        return carry

    if together == tables:
        body(0, 0)
    else:
        lax.fori_loop(0, tables // together, body, 0)
    row, source = iota((2 * group, 2 * group), 0), iota((2 * group, 2 * group), 1)
    sphere, c = lax.rem(row, part), lax.rem(lax.div(row, quarter * part), 2)
    owner = lax.div(row, 2 * quarter * part) ^ lax.axis_index("pair")
    block = owner * quarter + lax.rem(lax.div(row, part), quarter)
    order = jnp.where(source == c * group + sphere * own + block, 1.0, 0.0).astype(BF16)
    result = dot_nn(order, total_ref[...].astype(BF16)).astype(BF16)
    share = 2 * quarter * part
    for i, out_ref in enumerate(outs):
        out_ref[...] = result[i * share : (i + 1) * share].reshape(out_ref.shape)


def lane_swap(value):
    half = value.shape[1] // 2
    rolled = pltpu.roll(value, half, axis=1)
    return jnp.where(iota(value.shape, 1) < half, -rolled, rolled)


def add_products(blocks_ref, products_ref, rows, first, count):
    vectors = products_ref.shape[0]
    values = []
    for k in range(vectors):
        start = k % 2 * rows + first
        value = blocks_ref[k // 2, start : start + count, :]
        if k % 2 == 0 and first + count > rows:
            value = jnp.where(iota(value.shape, 0) < rows - first, value, 0.0)
        values.append(value)
    for l in range(vectors):
        other = pltpu.roll(values[l], values[l].shape[1] // 2, axis=1)
        for k in range(l + 1):
            products_ref[k, l] += folded(values[k] * values[l])
            if k < l:
                products_ref[l, k] += folded(values[k] * other)


def products_line(products_ref):
    vectors, _, _, columns = products_ref.shape
    pairs = vectors * vectors
    totals = jnp.sum(products_ref[...].reshape(pairs, 8, columns), axis=1)
    pair = iota(totals.shape, 0)
    signed = (lax.div(pair, vectors) > lax.rem(pair, vectors)) & (iota(totals.shape, 1) >= columns // 2)
    totals = jnp.sum(jnp.where(signed, -totals, totals), axis=1, keepdims=True)
    row, lane = iota((vectors, 128), 0), iota((vectors, 128), 1)
    line = jnp.zeros((1, 128), F32)
    for k in range(vectors):
        column = totals[k * vectors : (k + 1) * vectors]
        line += jnp.sum(jnp.where(row + k * vectors == lane, column, 0.0), axis=0, keepdims=True)
    return line


def gram_kernel(quarter, modes, basis_ref, mie_ref, products_ref, blocks_ref, mies_ref, mie_sem, sems):
    blocks, _, columns = basis_ref.shape
    rows = quarter * modes
    parts, chunk = 4, 32
    tile_end = rows // 8 * 8
    step = rounded_up(rows, 8 * parts) // parts
    even = [0] + [step * q for q in range(1, parts)] + [tile_end]
    odd = [tile_end] + [rounded_up(rows, 8) + step * q for q in range(1, parts)] + [2 * rows]
    copies = []
    for q in range(parts):
        for i in range(blocks):
            for side, cuts in enumerate((even, odd)):
                here = pl.ds(cuts[q], cuts[q + 1] - cuts[q])
                copies.append(pltpu.make_async_copy(basis_ref.at[i, here], blocks_ref.at[i, here], sems.at[q, i, side]))
    for copy in copies:
        copy.start()
    mie_rows = mie_ref.shape[0]
    mie_copy = pltpu.make_async_copy(mie_ref, mies_ref.at[pl.ds(0, mie_rows)], mie_sem)
    mie_copy.start()
    mies_ref[mie_rows:] = jnp.zeros((mies_ref.shape[0] - mie_rows,) + mies_ref.shape[1:], F32)
    products_ref[...] = jnp.zeros_like(products_ref)
    for i in range(blocks):
        blocks_ref[i, 2 * rows :, :] = jnp.zeros((blocks_ref.shape[1] - 2 * rows, columns), F32)
    for q in range(parts):
        for copy in copies[2 * blocks * q : 2 * blocks * (q + 1)]:
            copy.wait()
        if q < parts - 2:
            for first in range(step * q, step * (q + 1), chunk):
                add_products(blocks_ref, products_ref, rows, first, chunk)
    mie_copy.wait()


def gram_end(rows, products_ref, blocks_ref, line_ref, totals_ref):
    parts, chunk = 4, 32
    totals_ref[...] = products_ref[...]
    for first in range(rounded_up(rows, 8 * parts) // parts * (parts - 2), rows, chunk):
        add_products(blocks_ref, totals_ref, rows, first, chunk)
    line_ref[...] = products_line(totals_ref)


def image_kernel(quarter, modes, blocks_ref, mie_ref, gram_ref, *rest):
    pieces, (image_ref, sums_ref, lines_ref, whole_ref) = rest[:-4], rest[-4:]
    vectors = 2 * blocks_ref.shape[0]
    full, columns = image_ref.shape
    rows = quarter * modes
    part = pieces[0].shape[2]
    for i, piece_ref in enumerate(pieces):
        place = pl.multiple_of((lax.axis_index("pair") ^ i) * part, part)
        for j in range(quarter):
            for c in range(2):
                whole_ref[j, pl.ds(c * (columns // 2) + place, part), :] = piece_ref[c, j]
    lines_ref[rows:full, :] = jnp.zeros((full - rows, columns), F32)
    for j in range(quarter):
        lines_ref[pl.ds(j, modes, quarter), :] = jnp.transpose(whole_ref[j].astype(F32))[:modes]
    half = columns // 2
    chunk = 64
    totals = [jnp.zeros((8, columns), F32) for _ in range(2 * vectors + 1)]
    for first in range(0, full, chunk):
        here = slice(first, first + chunk)
        field = lines_ref[here, :]
        count = min(chunk, rows - first)
        height = mie_ref.shape[1]
        mie = mie_ref[first // height : (first + count) // height].reshape(count, columns)
        if count < chunk:
            mie = jnp.concatenate([mie, jnp.zeros((chunk - count, columns), F32)], axis=0)
        left = iota(mie.shape, 1) < half
        other = pltpu.roll(mie, half, axis=1)
        product = jnp.where(left, mie, other) * field + jnp.where(left, -other, mie) * pltpu.roll(field, half, axis=1)
        last = (vectors - 1) % 2 * rows + first
        image = blocks_ref[(vectors - 1) // 2, last : last + chunk, :] - product
        image_ref[here, :] = image
        turned = pltpu.roll(product, half, axis=1)
        for k in range(vectors):
            start = k % 2 * rows + first
            values = blocks_ref[k // 2, start : start + chunk, :]
            totals[2 * k] += folded(values * product)
            totals[2 * k + 1] += folded(values * turned)
        totals[2 * vectors] += folded(product * product)
    lane = iota(gram_ref.shape, 1)
    line = gram_ref[...]
    left = iota((8, columns), 1) < half
    for index, total in enumerate(totals):
        if index % 2 and index < 2 * vectors:
            total = jnp.where(left, total, -total)
        line = jnp.where(lane == vectors * vectors + index, jnp.sum(total, axis=(0, 1), keepdims=True), line)
    sums_ref[...] = jnp.broadcast_to(line[None], sums_ref.shape)


def remainder_kernel(quarter, modes, mean_scale, sums_ref, blocks_ref, image_ref, dots_ref, out_ref):
    vectors = 2 * blocks_ref.shape[0]
    full, columns = image_ref.shape
    rows = quarter * modes
    total = jnp.sum(sums_ref[...], axis=0)
    lane = iota(total.shape, 1)

    def lane_at(index):
        return jnp.sum(jnp.where(lane == index, total, 0.0), axis=1, keepdims=True)

    def on_lanes(parts, places):
        line = jnp.zeros(total.shape, F32)
        for k in range(vectors):
            line = jnp.where(places == k, parts[k], line)
        return line

    start = vectors * vectors
    last = vectors - 1
    taken_real = [lane_at(start + 2 * k) * mean_scale for k in range(vectors)]
    taken_imag = [lane_at(start + 2 * k + 1) * mean_scale for k in range(vectors)]
    real = [lane_at(k * vectors + last) * mean_scale - taken_real[k] for k in range(vectors)]
    imag = [lane_at(last * vectors + k) * mean_scale - taken_imag[k] for k in range(last)] + [-taken_imag[last]]
    dots_ref[0:1, :] = on_lanes(real, lane)[:, :vectors]
    dots_ref[1:2, :] = on_lanes(imag, lane)[:, :vectors]
    kept_real = [-value for value in real[:last]] + [1.0 - real[last]]
    kept_imag = [-value for value in imag]
    first_index, last_index = lax.div(lane, vectors), lax.rem(lane, vectors)
    real_first, real_last = on_lanes(kept_real, first_index), on_lanes(kept_real, last_index)
    imag_first, imag_last = on_lanes(kept_imag, first_index), on_lanes(kept_imag, last_index)
    same = real_first * real_last + imag_first * imag_last
    cross = imag_last * real_first - real_last * imag_first
    often = jnp.where(first_index == last_index, 1.0, 2.0)
    spread = jnp.where(lane < start, total * often * jnp.where(first_index <= last_index, same, cross), 0.0)
    spread = jnp.sum(spread, axis=1, keepdims=True)
    both = sum(kept_real[k] * taken_real[k] + kept_imag[k] * taken_imag[k] for k in range(vectors))
    norm_square = (lane_at(start + 2 * vectors) + spread) * mean_scale - 2.0 * both
    scale = lax.rsqrt(norm_square)
    image_scale = jnp.broadcast_to(scale, (8, columns))
    reals = [jnp.broadcast_to(real[k] * scale, (8, columns)) for k in range(vectors)]
    imags = [jnp.broadcast_to(imag[k] * scale, (8, columns)) for k in range(vectors)]
    chunk = 64
    for first in range(0, full, chunk):
        here = slice(first, first + chunk)
        values = []
        for k in range(vectors):
            start = k % 2 * rows + first
            values.append(blocks_ref[k // 2, start : start + chunk, :].reshape(chunk // 8, 8, columns))
        along = image_ref[here, :].reshape(chunk // 8, 8, columns) * image_scale
        turned = jnp.zeros_like(along)
        for k in range(vectors):
            along -= reals[k] * values[k]
            turned += imags[k] * values[k]
        result = along.reshape(chunk, columns) - lane_swap(turned.reshape(chunk, columns))
        count = min(chunk, rows - first)
        height = out_ref.shape[1]
        out_ref[first // height : (first + count) // height] = result.reshape(chunk // height, height, columns)[: count // height]


def exchanged(pieces, axis):
    count = lax.axis_size(axis)
    received = [pieces[0]]
    for i in range(1, len(pieces)):
        received.append(lax.ppermute(pieces[i], axis, [(p, p ^ i) for p in range(count)]))
    return received


def neighbours(value):
    count = lax.axis_size("blk")
    up = [(i, i + 1) for i in range(count - 1)]
    down = [(j, i) for i, j in up]
    return lax.ppermute(value, "blk", up), lax.ppermute(value, "blk", down)


def shards(basis, mie_coeffs, rot_table, axial_table, pair_table, pair_count):
    vectors, quarter, modes, columns = basis.shape
    ways = lax.axis_size("pair")
    blk_ways = lax.axis_size("blk")
    tables = rot_table.shape[0]
    slots = pair_table.shape[1]
    own = quarter * ways
    part = columns // 2 // ways
    group = own * part
    size = rounded_up(modes, 128)
    rows = quarter * modes
    full = rounded_up(rows, 8)
    pairs_of_vectors = vectors // 2
    height = 4

    basis_rows = in_hbm(basis.transpose(0, 2, 1, 3).reshape(pairs_of_vectors, 2 * rows, columns))
    mie_rows = in_hbm(mie_coeffs.transpose(1, 0, 2).reshape(rows // 4, 4, columns))
    rot_rows = in_hbm(rot_table.transpose(1, 0, 2).reshape(modes * tables, modes))
    axial_rows = in_hbm(axial_table.transpose(0, 2, 1, 3))
    pair_rows = in_hbm(pair_table.transpose(2, 0, 1))

    octets = part * quarter // 16
    piece = jax.ShapeDtypeStruct((2, octets, 16, size), BF16)
    pieces = pl.pallas_call(
        functools.partial(pack_kernel, quarter, modes, ways, own),
        in_specs=[hbm(), pl.BlockSpec(memory_space=pltpu.SMEM), hbm()],
        out_specs=[whole()] * ways,
        out_shape=[piece] * ways,
        scratch_shapes=[
            pltpu.VMEM(pair_rows.shape, jnp.int32),
            pltpu.VMEM((full, columns), F32),
            pltpu.VMEM((size, columns), F32),
            pltpu.VMEM((2 * slots, slots), F32),
            pltpu.VMEM((quarter, columns, size), F32),
            pltpu.SemaphoreType.DMA((2,)),
        ],
        compiler_params=params(16),
        name="pack",
    )(pair_rows, pair_count, basis_rows)
    tall = rounded_up(rows + full, 8)
    *pieces, basis_rows, mie_rows = lax.optimization_barrier((*pieces, basis_rows, mie_rows))
    received = exchanged(pieces, "pair")
    products, blocks, mies = pl.pallas_call(
        functools.partial(gram_kernel, quarter, modes),
        in_specs=[hbm()] * 2,
        out_specs=[whole()] * 3,
        out_shape=[
            jax.ShapeDtypeStruct((vectors, vectors, 8, columns), F32),
            jax.ShapeDtypeStruct((pairs_of_vectors, tall, columns), F32),
            jax.ShapeDtypeStruct((full // height, height, columns), F32),
        ],
        scratch_shapes=[
            pltpu.SemaphoreType.DMA,
            pltpu.SemaphoreType.DMA((4, pairs_of_vectors, 2)),
        ],
        compiler_params=params(8),
        name="gram",
    )(basis_rows, mie_rows)
    *received, products, rot_rows, axial_rows = lax.optimization_barrier((*received, products, rot_rows, axial_rows))
    own_pieces = pl.pallas_call(
        join_kernel,
        in_specs=[whole()] * ways,
        out_specs=whole(),
        out_shape=jax.ShapeDtypeStruct((ways, *piece.shape), BF16),
        compiler_params=params(4),
        name="join",
    )(*received)
    below, above = neighbours(own_pieces)
    own_pieces, products, rot_rows, axial_rows = lax.optimization_barrier((own_pieces, products, rot_rows, axial_rows))
    rotations, axials, line = pl.pallas_call(
        functools.partial(tables_kernel, quarter, modes),
        in_specs=[hbm()] * 2 + [whole()] * 2,
        out_specs=[whole()] * 3,
        out_shape=[
            jax.ShapeDtypeStruct((tables, size, size), BF16),
            jax.ShapeDtypeStruct((tables, 2 * size, size), BF16),
            jax.ShapeDtypeStruct((1, 128), F32),
        ],
        scratch_shapes=[
            pltpu.VMEM((tables * size, modes), BF16),
            pltpu.VMEM(axial_rows.shape, BF16),
            pltpu.VMEM((vectors, vectors, 8, columns), F32),
            pltpu.SemaphoreType.DMA((tables + rounded_up(modes * tables, 1024) // 1024,)),
        ],
        compiler_params=params(20),
        cost_estimate=pl.CostEstimate(flops=tables * 8 * 256 * 256 * size, bytes_accessed=6 * tables * size * size * 2, transcendentals=0),
        name="tables",
    )(rot_rows, axial_rows, products, blocks)
    below, above, rotations, axials, line = lax.optimization_barrier((below, above, rotations, axials, line))

    together = tables
    field = pl.pallas_call(
        functools.partial(field_kernel, own, modes, together),
        in_specs=[whole()] * 5,
        out_specs=[whole()] * ways,
        out_shape=[jax.ShapeDtypeStruct((2, quarter, part, size), BF16)] * ways,
        scratch_shapes=[pltpu.VMEM((tables, 4 * group, size), BF16), pltpu.VMEM((2 * group, size), F32)],
        compiler_params=params(28),
        name="field",
    )(rotations, axials, below, own_pieces, above)
    field_pieces = exchanged(field, "pair")

    image, sums = pl.pallas_call(
        functools.partial(image_kernel, quarter, modes),
        in_specs=[whole()] * (ways + 3),
        out_specs=[whole()] * 2,
        out_shape=[jax.ShapeDtypeStruct((full, columns), F32), jax.ShapeDtypeStruct((ways * blk_ways, 1, 128), F32)],
        scratch_shapes=[pltpu.VMEM((full, columns), F32), pltpu.VMEM((quarter, columns, size), BF16)],
        compiler_params=params(8),
        name="image",
    )(blocks, mies, line, *field_pieces)
    sums = lax.all_to_all(sums, ("blk", "pair"), split_axis=0, concat_axis=0, tiled=True)

    mean_scale = 1.0 / (own * blk_ways * modes * columns)
    dots, next_rows = pl.pallas_call(
        functools.partial(remainder_kernel, quarter, modes, mean_scale),
        in_specs=[whole()] * 3,
        out_specs=[whole(), whole()],
        out_shape=[jax.ShapeDtypeStruct((2, vectors), F32), jax.ShapeDtypeStruct((rows // height, height, columns), F32)],
        compiler_params=params(16),
        name="remainder",
    )(sums, blocks, image)
    return dots, next_rows.reshape(modes, quarter, columns).transpose(1, 0, 2)


def solution(mesh):
    placed = (
        P(None, ("blk", "pair"), None, None),
        P(("blk", "pair"), None, None),
        P(),
        P(),
        P("blk", None, None),
        P("blk"),
    )
    return jax.shard_map(
        shards,
        mesh=mesh,
        in_specs=placed,
        out_specs=(P(), P(("blk", "pair"), None, None)),
        check_vma=False,
    )
```

```python
import functools

import jax
import jax.numpy as jnp
from jax import lax
from jax.experimental import pallas as pl
from jax.experimental.pallas import tpu as pltpu
from jax.sharding import PartitionSpec as P

MIB = 1024 * 1024
F32 = jnp.float32
BF16 = jnp.bfloat16


def params(mib):
    return pltpu.CompilerParams(vmem_limit_bytes=mib * MIB)


def hbm():
    return pl.BlockSpec(memory_space=pltpu.HBM)


def whole():
    return pl.BlockSpec(memory_space=pltpu.VMEM)


def in_hbm(value):
    return pltpu.with_memory_space_constraint(value, pltpu.HBM)


def rounded_up(value, unit):
    return (value + unit - 1) // unit * unit


def iota(shape, dim):
    return lax.broadcasted_iota(jnp.int32, shape, dim)


def dot_nn(left, right):
    return lax.dot_general(left, right, (((1,), (0,)), ((), ())), preferred_element_type=F32)


def dot_nt(left, right):
    return lax.dot_general(left, right, (((1,), (1,)), ((), ())), preferred_element_type=F32)


def pack_kernel(quarter, modes, ways, own, list_ref, count_ref, basis_ref, *rest):
    outs, (pair_rows_ref, lines_ref, pad_ref, codes_ref, turned_ref, sems) = rest[:ways], rest[ways:]
    full, columns = lines_ref.shape
    rows = quarter * modes
    part = columns // 2 // ways
    copy = pltpu.make_async_copy(basis_ref.at[basis_ref.shape[0] - 1, pl.ds(2 * rows - full, full)], lines_ref, sems.at[0])
    copy.start()
    list_copy = pltpu.make_async_copy(list_ref, pair_rows_ref, sems.at[1])
    list_copy.start()
    pad_ref[...] = jnp.zeros_like(pad_ref)
    list_copy.wait()
    slots = pair_rows_ref.shape[2]
    live = iota((1, slots), 1) < count_ref[0]
    marks = jnp.where(live, own * (pair_rows_ref[2] + 1) + pair_rows_ref[0], 0)
    line = iota((slots, slots), 0)
    stacked = jnp.where(line == 0, marks, jnp.where(line == 1, pair_rows_ref[1], 0))
    turned = jnp.transpose(stacked.astype(F32))
    codes_ref[0:slots, :] = turned
    codes_ref[slots : 2 * slots, :] = pltpu.roll(turned, slots - 1, axis=1)
    share = 2 * quarter * part
    mine = codes_ref[pl.ds(pl.multiple_of(lax.axis_index("pair") * share, share), share), :][:, 0:1]
    copy.wait()
    for j in range(quarter):
        pad_ref[0:modes, :] = lines_ref[pl.ds(full - rows + j, modes, quarter), :]
        turned_ref[j] = jnp.transpose(pad_ref[...])
    _, octets, height, size = outs[0].shape
    each = height // quarter
    for i, out_ref in enumerate(outs):
        place = (lax.axis_index("pair") ^ i) * part
        for c in range(2):
            for o in range(octets):
                first = (c * octets + o) * height
                here = pl.ds(pl.multiple_of(c * (columns // 2) + place + o * each, each), each)
                piece = jnp.concatenate([turned_ref[j, here, :] for j in range(quarter)], axis=0)
                piece = jnp.where(iota(piece.shape, 1) == modes, mine[first : first + height], piece)
                out_ref[c, o] = piece.astype(BF16)


def join_kernel(*refs):
    out_ref = refs[-1]
    for i, ref in enumerate(refs[:-1]):
        out_ref[lax.axis_index("pair") ^ i] = ref[...]


def tables_kernel(
    quarter, modes, rot_ref, axial_ref, products_ref, blocks_ref, rot_out_ref, axial_out_ref, line_ref, rots_ref, axials_ref, totals_ref, sems,
):
    tables, size, _ = rot_out_ref.shape
    listed = rot_ref.shape[0]
    chunk = 256
    rot_copies = []
    for i, first in enumerate(range(0, listed, 4 * chunk)):
        here = pl.ds(first, min(4 * chunk, listed - first))
        rot_copies.append(pltpu.make_async_copy(rot_ref.at[here], rots_ref.at[here], sems.at[tables + i]))
        rot_copies[-1].start()

    def fetch(g):
        return pltpu.make_async_copy(axial_ref.at[g], axials_ref.at[g], sems.at[g])

    for g in range(tables):
        fetch(g).start()
    for ref in (rot_out_ref, axial_out_ref):
        ref[:, :, size - 128 : size] = jnp.zeros((tables, ref.shape[1], 128), BF16)
    rots_ref[listed:, :] = jnp.zeros((rots_ref.shape[0] - listed, modes), BF16)
    gram_end(quarter * modes, products_ref, blocks_ref, line_ref, totals_ref)

    out_row, in_row = iota((chunk, chunk), 0), iota((chunk, chunk), 1)
    share = chunk // tables
    entries = (in_row == tables * lax.rem(out_row, share) + lax.div(out_row, share)).astype(F32).astype(BF16)
    for i, copy in enumerate(rot_copies):
        copy.wait()
        chunks = range(4 * i, min(4 * (i + 1), rots_ref.shape[0] // chunk))
        rows = [rots_ref[q * chunk : (q + 1) * chunk, :] for q in chunks]
        results = [dot_nn(entries, value).astype(BF16) for value in rows]
        for q, result in zip(chunks, results):
            for g in range(tables):
                rot_out_ref[g, q * share : (q + 1) * share, 0:modes] = result[g * share : (g + 1) * share]

    each = chunk // 2
    halves = (in_row == 2 * lax.rem(out_row, each) + lax.div(out_row, each)).astype(F32).astype(BF16)
    together = 2 if tables % 2 == 0 else 1

    def split(step, carry):
        members = [step * together + i for i in range(together)]
        for g in members:
            fetch(g).wait()
        places = [(g, first) for g in members for first in range(0, modes, each)]
        results = []
        for g, first in places:
            count = min(each, modes - first)
            rows = axials_ref[g, first : first + count].reshape(2 * count, modes)
            results.append(dot_nn(halves[:, : 2 * count], rows).astype(BF16))
        for (g, first), result in zip(places, results):
            for c in range(2):
                axial_out_ref[g, c * size + first : c * size + first + each, 0:modes] = result[c * each : (c + 1) * each]
        return carry

    lax.fori_loop(0, tables // together, split, 0)


def swapped(value):
    half = value.shape[0] // 2
    return jnp.concatenate([-value[half:], value[:half]], axis=0)


def pair_counts(own, tables, lane, refs):
    ways, parts, octets, height, size = refs[0].shape
    group = ways * octets * height
    wanted = iota((tables * own, group), 0) + own

    def one_hot(hit):
        return jnp.where(hit, 1.0, 0.0).astype(BF16)

    forward, backward = None, []
    for window, ref in enumerate(refs):
        values = ref[:, :, :, :, size - 128 : size].reshape(2 * group, 128).astype(F32)
        marks_column, sources_column = (values[h * group : (h + 1) * group, lane : lane + 1].astype(jnp.int32) for h in range(2))
        marks, sources = (jnp.transpose(values[h * group : (h + 1) * group])[lane : lane + 1].astype(jnp.int32) for h in range(2))
        if window == 1:
            forward = dot_nn(one_hot(marks == wanted), one_hot(sources_column == iota((group, 3 * own), 1)))
        block = sources - (2 - window) * own
        inside = (block >= 0) & (block < own) & (marks >= own)
        hits = one_hot(jnp.where(inside, lax.div(marks, own) * own + block, -1) == wanted)
        place = lax.rem(marks_column, own) + window * own
        backward.append(dot_nn(hits, one_hot(place == iota((group, 3 * own), 1))))
    return jnp.concatenate([forward, sum(backward)], axis=0).astype(BF16)


def folded(value):
    return jnp.sum(value.reshape(value.shape[0] // 8, 8, value.shape[1]), axis=0)


def field_kernel(
    own, modes, together, rot_ref, axial_ref, below_ref, own_ref, above_ref, *rest
):
    outs, (sums_ref, total_ref) = rest[:-2], rest[-2:]
    tables, _, size = rot_ref.shape
    refs = (below_ref, own_ref, above_ref)
    ways, _, octets, height, _ = own_ref.shape
    quarter = own // ways
    each = height // quarter
    part = octets * each
    group = own * part
    counts = pair_counts(own, tables, modes % 128, refs)
    spread = jnp.where(iota((3 * own, 3 * own * each), 0) == lax.div(iota((3 * own, 3 * own * each), 1), each), 1.0, 0.0)
    counts = dot_nn(counts, spread.astype(BF16))
    sphere = lax.rem(iota(counts.shape, 1), each)
    chosen = jnp.concatenate([jnp.where(sphere == i, counts, 0.0).astype(BF16) for i in range(each)], axis=0)
    kinds = 2 * tables * own
    for c in range(2):
        for o in range(octets):
            blocks = jnp.concatenate([ref[:, c, o].reshape(ways * height, size) for ref in refs], axis=0)
            for i in range(0, each, 2):
                results = dot_nn(chosen[i * kinds : (i + 2) * kinds], blocks)
                for kind in range(2 * tables):
                    direction, g = kind // tables, kind % tables
                    rows = [results[start + kind * own : start + (kind + 1) * own] for start in (0, kinds)]
                    place = (direction * 2 + c) * group + (o * each + i) * own
                    sums_ref[g, place : place + 2 * own, :] = jnp.concatenate(rows, axis=0).astype(BF16)
    total_ref[...] = jnp.zeros_like(total_ref)

    def body(step, carry):
        entries = [step * together + i for i in range(together)]
        turned = [dot_nt(sums_ref[g], rot_ref[g]).astype(BF16) for g in entries]
        moved = []
        for g, both in zip(entries, turned):
            forward, backward = both[: 2 * group], both[2 * group :]
            result = dot_nt(forward, axial_ref[g, :size]) + dot_nt(swapped(forward), axial_ref[g, size:])
            result += dot_nn(jnp.concatenate([backward, swapped(backward)], axis=1), axial_ref[g])
            moved.append(result.astype(BF16))
        total_ref[...] += sum(dot_nn(value, rot_ref[g]) for g, value in zip(entries, moved))
        return carry

    if together == tables:
        body(0, 0)
    else:
        lax.fori_loop(0, tables // together, body, 0)
    row, source = iota((2 * group, 2 * group), 0), iota((2 * group, 2 * group), 1)
    sphere, c = lax.rem(row, part), lax.rem(lax.div(row, quarter * part), 2)
    owner = lax.div(row, 2 * quarter * part) ^ lax.axis_index("pair")
    block = owner * quarter + lax.rem(lax.div(row, part), quarter)
    order = jnp.where(source == c * group + sphere * own + block, 1.0, 0.0).astype(BF16)
    result = dot_nn(order, total_ref[...].astype(BF16)).astype(BF16)
    share = 2 * quarter * part
    for i, out_ref in enumerate(outs):
        out_ref[...] = result[i * share : (i + 1) * share].reshape(out_ref.shape)


def lane_swap(value):
    half = value.shape[1] // 2
    rolled = pltpu.roll(value, half, axis=1)
    return jnp.where(iota(value.shape, 1) < half, -rolled, rolled)


def add_products(blocks_ref, products_ref, rows, first, count):
    vectors = products_ref.shape[0]
    values = []
    for k in range(vectors):
        start = k % 2 * rows + first
        value = blocks_ref[k // 2, start : start + count, :]
        if k % 2 == 0 and first + count > rows:
            value = jnp.where(iota(value.shape, 0) < rows - first, value, 0.0)
        values.append(value)
    for l in range(vectors):
        other = pltpu.roll(values[l], values[l].shape[1] // 2, axis=1)
        for k in range(l + 1):
            products_ref[k, l] += folded(values[k] * values[l])
            if k < l:
                products_ref[l, k] += folded(values[k] * other)


def products_line(products_ref):
    vectors, _, _, columns = products_ref.shape
    pairs = vectors * vectors
    totals = jnp.sum(products_ref[...].reshape(pairs, 8, columns), axis=1)
    pair = iota(totals.shape, 0)
    signed = (lax.div(pair, vectors) > lax.rem(pair, vectors)) & (iota(totals.shape, 1) >= columns // 2)
    totals = jnp.sum(jnp.where(signed, -totals, totals), axis=1, keepdims=True)
    row, lane = iota((vectors, 128), 0), iota((vectors, 128), 1)
    line = jnp.zeros((1, 128), F32)
    for k in range(vectors):
        column = totals[k * vectors : (k + 1) * vectors]
        line += jnp.sum(jnp.where(row + k * vectors == lane, column, 0.0), axis=0, keepdims=True)
    return line


def gram_kernel(quarter, modes, basis_ref, mie_ref, products_ref, blocks_ref, mies_ref, mie_sem, sems):
    blocks, _, columns = basis_ref.shape
    rows = quarter * modes
    parts, chunk = 4, 32
    tile_end = rows // 8 * 8
    step = rounded_up(rows, 8 * parts) // parts
    even = [0] + [step * q for q in range(1, parts)] + [tile_end]
    odd = [tile_end] + [rounded_up(rows, 8) + step * q for q in range(1, parts)] + [2 * rows]
    copies = []
    for q in range(parts):
        for i in range(blocks):
            for side, cuts in enumerate((even, odd)):
                here = pl.ds(cuts[q], cuts[q + 1] - cuts[q])
                copies.append(pltpu.make_async_copy(basis_ref.at[i, here], blocks_ref.at[i, here], sems.at[q, i, side]))
    for copy in copies:
        copy.start()
    mie_rows = mie_ref.shape[0]
    mie_copy = pltpu.make_async_copy(mie_ref, mies_ref.at[pl.ds(0, mie_rows)], mie_sem)
    mie_copy.start()
    mies_ref[mie_rows:] = jnp.zeros((mies_ref.shape[0] - mie_rows,) + mies_ref.shape[1:], F32)
    products_ref[...] = jnp.zeros_like(products_ref)
    for i in range(blocks):
        blocks_ref[i, 2 * rows :, :] = jnp.zeros((blocks_ref.shape[1] - 2 * rows, columns), F32)
    for q in range(parts):
        for copy in copies[2 * blocks * q : 2 * blocks * (q + 1)]:
            copy.wait()
        if q < parts - 1:
            for first in range(step * q, step * (q + 1), chunk):
                add_products(blocks_ref, products_ref, rows, first, chunk)
    mie_copy.wait()


def gram_end(rows, products_ref, blocks_ref, line_ref, totals_ref):
    parts, chunk = 4, 32
    totals_ref[...] = products_ref[...]
    for first in range(rounded_up(rows, 8 * parts) // parts * (parts - 1), rows, chunk):
        add_products(blocks_ref, totals_ref, rows, first, chunk)
    line_ref[...] = products_line(totals_ref)


def image_kernel(quarter, modes, blocks_ref, mie_ref, gram_ref, *rest):
    pieces, (image_ref, sums_ref, lines_ref, whole_ref) = rest[:-4], rest[-4:]
    vectors = 2 * blocks_ref.shape[0]
    full, columns = image_ref.shape
    rows = quarter * modes
    part = pieces[0].shape[2]
    for i, piece_ref in enumerate(pieces):
        place = pl.multiple_of((lax.axis_index("pair") ^ i) * part, part)
        for j in range(quarter):
            for c in range(2):
                whole_ref[j, pl.ds(c * (columns // 2) + place, part), :] = piece_ref[c, j]
    lines_ref[rows:full, :] = jnp.zeros((full - rows, columns), F32)
    for j in range(quarter):
        lines_ref[pl.ds(j, modes, quarter), :] = jnp.transpose(whole_ref[j].astype(F32))[:modes]
    half = columns // 2
    chunk = 64
    totals = [jnp.zeros((8, columns), F32) for _ in range(2 * vectors + 1)]
    for first in range(0, full, chunk):
        here = slice(first, first + chunk)
        field = lines_ref[here, :]
        count = min(chunk, rows - first)
        height = mie_ref.shape[1]
        mie = mie_ref[first // height : (first + count) // height].reshape(count, columns)
        if count < chunk:
            mie = jnp.concatenate([mie, jnp.zeros((chunk - count, columns), F32)], axis=0)
        left = iota(mie.shape, 1) < half
        other = pltpu.roll(mie, half, axis=1)
        product = jnp.where(left, mie, other) * field + jnp.where(left, -other, mie) * pltpu.roll(field, half, axis=1)
        last = (vectors - 1) % 2 * rows + first
        image = blocks_ref[(vectors - 1) // 2, last : last + chunk, :] - product
        image_ref[here, :] = image
        turned = pltpu.roll(product, half, axis=1)
        for k in range(vectors):
            start = k % 2 * rows + first
            values = blocks_ref[k // 2, start : start + chunk, :]
            totals[2 * k] += folded(values * product)
            totals[2 * k + 1] += folded(values * turned)
        totals[2 * vectors] += folded(product * product)
    lane = iota(gram_ref.shape, 1)
    line = gram_ref[...]
    left = iota((8, columns), 1) < half
    for index, total in enumerate(totals):
        if index % 2 and index < 2 * vectors:
            total = jnp.where(left, total, -total)
        line = jnp.where(lane == vectors * vectors + index, jnp.sum(total, axis=(0, 1), keepdims=True), line)
    sums_ref[...] = jnp.broadcast_to(line[None], sums_ref.shape)


def remainder_kernel(quarter, modes, mean_scale, sums_ref, blocks_ref, image_ref, dots_ref, out_ref):
    vectors = 2 * blocks_ref.shape[0]
    full, columns = image_ref.shape
    rows = quarter * modes
    total = jnp.sum(sums_ref[...], axis=0)
    lane = iota(total.shape, 1)

    def lane_at(index):
        return jnp.sum(jnp.where(lane == index, total, 0.0), axis=1, keepdims=True)

    def on_lanes(parts, places):
        line = jnp.zeros(total.shape, F32)
        for k in range(vectors):
            line = jnp.where(places == k, parts[k], line)
        return line

    start = vectors * vectors
    last = vectors - 1
    taken_real = [lane_at(start + 2 * k) * mean_scale for k in range(vectors)]
    taken_imag = [lane_at(start + 2 * k + 1) * mean_scale for k in range(vectors)]
    real = [lane_at(k * vectors + last) * mean_scale - taken_real[k] for k in range(vectors)]
    imag = [lane_at(last * vectors + k) * mean_scale - taken_imag[k] for k in range(last)] + [-taken_imag[last]]
    dots_ref[0:1, :] = on_lanes(real, lane)[:, :vectors]
    dots_ref[1:2, :] = on_lanes(imag, lane)[:, :vectors]
    kept_real = [-value for value in real[:last]] + [1.0 - real[last]]
    kept_imag = [-value for value in imag]
    first_index, last_index = lax.div(lane, vectors), lax.rem(lane, vectors)
    real_first, real_last = on_lanes(kept_real, first_index), on_lanes(kept_real, last_index)
    imag_first, imag_last = on_lanes(kept_imag, first_index), on_lanes(kept_imag, last_index)
    same = real_first * real_last + imag_first * imag_last
    cross = imag_last * real_first - real_last * imag_first
    often = jnp.where(first_index == last_index, 1.0, 2.0)
    spread = jnp.where(lane < start, total * often * jnp.where(first_index <= last_index, same, cross), 0.0)
    spread = jnp.sum(spread, axis=1, keepdims=True)
    both = sum(kept_real[k] * taken_real[k] + kept_imag[k] * taken_imag[k] for k in range(vectors))
    norm_square = (lane_at(start + 2 * vectors) + spread) * mean_scale - 2.0 * both
    scale = lax.rsqrt(norm_square)
    image_scale = jnp.broadcast_to(scale, (8, columns))
    reals = [jnp.broadcast_to(real[k] * scale, (8, columns)) for k in range(vectors)]
    imags = [jnp.broadcast_to(imag[k] * scale, (8, columns)) for k in range(vectors)]
    chunk = 64
    for first in range(0, full, chunk):
        here = slice(first, first + chunk)
        values = []
        for k in range(vectors):
            start = k % 2 * rows + first
            values.append(blocks_ref[k // 2, start : start + chunk, :].reshape(chunk // 8, 8, columns))
        along = image_ref[here, :].reshape(chunk // 8, 8, columns) * image_scale
        turned = jnp.zeros_like(along)
        for k in range(vectors):
            along -= reals[k] * values[k]
            turned += imags[k] * values[k]
        result = along.reshape(chunk, columns) - lane_swap(turned.reshape(chunk, columns))
        count = min(chunk, rows - first)
        height = out_ref.shape[1]
        out_ref[first // height : (first + count) // height] = result.reshape(chunk // height, height, columns)[: count // height]


def exchanged(pieces, axis):
    count = lax.axis_size(axis)
    received = [pieces[0]]
    for i in range(1, len(pieces)):
        received.append(lax.ppermute(pieces[i], axis, [(p, p ^ i) for p in range(count)]))
    return received


def neighbours(value):
    count = lax.axis_size("blk")
    up = [(i, i + 1) for i in range(count - 1)]
    down = [(j, i) for i, j in up]
    above = lax.ppermute(value, "blk", down)
    return lax.ppermute(value, "blk", up), above


def shards(basis, mie_coeffs, rot_table, axial_table, pair_table, pair_count):
    vectors, quarter, modes, columns = basis.shape
    ways = lax.axis_size("pair")
    blk_ways = lax.axis_size("blk")
    tables = rot_table.shape[0]
    slots = pair_table.shape[1]
    own = quarter * ways
    part = columns // 2 // ways
    group = own * part
    size = rounded_up(modes, 128)
    rows = quarter * modes
    full = rounded_up(rows, 8)
    pairs_of_vectors = vectors // 2
    height = 4

    basis_rows = in_hbm(basis.transpose(0, 2, 1, 3).reshape(pairs_of_vectors, 2 * rows, columns))
    mie_rows = in_hbm(mie_coeffs.transpose(1, 0, 2).reshape(rows // 4, 4, columns))
    rot_rows = in_hbm(rot_table.transpose(1, 0, 2).reshape(modes * tables, modes))
    axial_rows = in_hbm(axial_table.transpose(0, 2, 1, 3))
    pair_rows = in_hbm(pair_table.transpose(2, 0, 1))

    octets = part * quarter // 16
    piece = jax.ShapeDtypeStruct((2, octets, 16, size), BF16)
    pieces = pl.pallas_call(
        functools.partial(pack_kernel, quarter, modes, ways, own),
        in_specs=[hbm(), pl.BlockSpec(memory_space=pltpu.SMEM), hbm()],
        out_specs=[whole()] * ways,
        out_shape=[piece] * ways,
        scratch_shapes=[
            pltpu.VMEM(pair_rows.shape, jnp.int32),
            pltpu.VMEM((full, columns), F32),
            pltpu.VMEM((size, columns), F32),
            pltpu.VMEM((2 * slots, slots), F32),
            pltpu.VMEM((quarter, columns, size), F32),
            pltpu.SemaphoreType.DMA((2,)),
        ],
        compiler_params=params(16),
        name="pack",
    )(pair_rows, pair_count, basis_rows)
    tall = rounded_up(rows + full, 8)
    *pieces, basis_rows, mie_rows = lax.optimization_barrier((*pieces, basis_rows, mie_rows))
    received = exchanged(pieces, "pair")
    products, blocks, mies = pl.pallas_call(
        functools.partial(gram_kernel, quarter, modes),
        in_specs=[hbm()] * 2,
        out_specs=[whole()] * 3,
        out_shape=[
            jax.ShapeDtypeStruct((vectors, vectors, 8, columns), F32),
            jax.ShapeDtypeStruct((pairs_of_vectors, tall, columns), F32),
            jax.ShapeDtypeStruct((full // height, height, columns), F32),
        ],
        scratch_shapes=[
            pltpu.SemaphoreType.DMA,
            pltpu.SemaphoreType.DMA((4, pairs_of_vectors, 2)),
        ],
        compiler_params=params(8),
        name="gram",
    )(basis_rows, mie_rows)
    *received, products, rot_rows, axial_rows = lax.optimization_barrier((*received, products, rot_rows, axial_rows))
    own_pieces = pl.pallas_call(
        join_kernel,
        in_specs=[whole()] * ways,
        out_specs=whole(),
        out_shape=jax.ShapeDtypeStruct((ways, *piece.shape), BF16),
        compiler_params=params(4),
        name="join",
    )(*received)
    below, above = neighbours(own_pieces)
    own_pieces, products, rot_rows, axial_rows = lax.optimization_barrier((own_pieces, products, rot_rows, axial_rows))
    rotations, axials, line = pl.pallas_call(
        functools.partial(tables_kernel, quarter, modes),
        in_specs=[hbm()] * 2 + [whole()] * 2,
        out_specs=[whole()] * 3,
        out_shape=[
            jax.ShapeDtypeStruct((tables, size, size), BF16),
            jax.ShapeDtypeStruct((tables, 2 * size, size), BF16),
            jax.ShapeDtypeStruct((1, 128), F32),
        ],
        scratch_shapes=[
            pltpu.VMEM((tables * size, modes), BF16),
            pltpu.VMEM(axial_rows.shape, BF16),
            pltpu.VMEM((vectors, vectors, 8, columns), F32),
            pltpu.SemaphoreType.DMA((tables + rounded_up(modes * tables, 1024) // 1024,)),
        ],
        compiler_params=params(20),
        cost_estimate=pl.CostEstimate(flops=tables * 8 * 256 * 256 * size, bytes_accessed=6 * tables * size * size * 2, transcendentals=0),
        name="tables",
    )(rot_rows, axial_rows, products, blocks)
    above, below, rotations, axials, line = lax.optimization_barrier((above, below, rotations, axials, line))

    together = tables
    field = pl.pallas_call(
        functools.partial(field_kernel, own, modes, together),
        in_specs=[whole()] * 5,
        out_specs=[whole()] * ways,
        out_shape=[jax.ShapeDtypeStruct((2, quarter, part, size), BF16)] * ways,
        scratch_shapes=[pltpu.VMEM((tables, 4 * group, size), BF16), pltpu.VMEM((2 * group, size), F32)],
        compiler_params=params(28),
        name="field",
    )(rotations, axials, below, own_pieces, above)
    field_pieces = exchanged(field, "pair")

    image, sums = pl.pallas_call(
        functools.partial(image_kernel, quarter, modes),
        in_specs=[whole()] * (ways + 3),
        out_specs=[whole()] * 2,
        out_shape=[jax.ShapeDtypeStruct((full, columns), F32), jax.ShapeDtypeStruct((ways * blk_ways, 1, 128), F32)],
        scratch_shapes=[pltpu.VMEM((full, columns), F32), pltpu.VMEM((quarter, columns, size), BF16)],
        compiler_params=params(8),
        name="image",
    )(blocks, mies, line, *field_pieces)
    sums = lax.all_to_all(sums, ("blk", "pair"), split_axis=0, concat_axis=0, tiled=True)

    mean_scale = 1.0 / (own * blk_ways * modes * columns)
    dots, next_rows = pl.pallas_call(
        functools.partial(remainder_kernel, quarter, modes, mean_scale),
        in_specs=[whole()] * 3,
        out_specs=[whole(), whole()],
        out_shape=[jax.ShapeDtypeStruct((2, vectors), F32), jax.ShapeDtypeStruct((rows // height, height, columns), F32)],
        compiler_params=params(16),
        name="remainder",
    )(sums, blocks, image)
    return dots, next_rows.reshape(modes, quarter, columns).transpose(1, 0, 2)


def solution(mesh):
    placed = (
        P(None, ("blk", "pair"), None, None),
        P(("blk", "pair"), None, None),
        P(),
        P(),
        P("blk", None, None),
        P("blk"),
    )
    return jax.shard_map(
        shards,
        mesh=mesh,
        in_specs=placed,
        out_specs=(P(), P(("blk", "pair"), None, None)),
        check_vma=False,
    )
```
